32 devices in a mesh: grp: 2 (over y), mig: 4 (over x, core), pen: 4 (over z).
Axes of the slice: x: 2, y: 2, z: 4, core: 2. Of those that a mesh axis runs over, the one named last changes fastest.
Arguments:
- fields: float32 [1024, 9, 4096], P(('grp', 'mig', 'pen')), may hold values from -6 to 6
- ghosts: float32 [1024, 9, 1536], P(('grp', 'mig', 'pen')), may hold values from -6 to 6
- velocity: float32 [3, 1024], P(None, ('grp', 'mig', 'pen')), may hold values from -1 to 1
- rate_matrix: float32 [9, 9], replicated, may hold values from -2 to 2
- recent_tend: bfloat16 [1024, 9, 4096], P(('grp', 'mig', 'pen')), may hold values from -6 to 6
- older_tend: bfloat16 [1024, 9, 4096], P(('grp', 'mig', 'pen')), may hold values from -6 to 6
- destination: int32 [1024], P(('grp', 'mig', 'pen')), may hold values from 0 to 15, as said below
- target_slot: int32 [1024], P(('grp', 'mig', 'pen')), may hold values from 0 to 32, as said below
- live_counts: int32 [32], P(('grp', 'mig', 'pen')), may hold values from 0 to 32, as said below
- tile_ids: int32 [1024], P(('grp', 'mig', 'pen')), may hold values from 0 to 1023, each once
- sensor: float32 [128, 32768], P('pen', ('grp', 'mig')), may hold values from 0 to 4
- flame_flags: int32 [8, 128], P('pen', ('grp', 'mig')), may hold values 0 or 1
Outputs:
- new_fields: float32 [1024, 9, 4096], P(('grp', 'mig', 'pen'))
- new_tend: bfloat16 [1024, 9, 4096], P(('grp', 'mig', 'pen'))
- filtered: float32 [128, 32768], P('pen', ('grp', 'mig'))
The draws below stay inside these ranges and needn't reach their ends.
Inputs may be any that keep to these rules, and one draw needn't show every extreme that they name: `destination`: index (mig-major) within the old slot's group of devices sharing its grp index; a device names every other device of its group for at most one of its slots; slots whose tile stays, and slots without a tile, name the device itself. `target_slot`: 32 marks an old slot without a tile; at each device the kept and arriving tiles take the slots 0 to its live count - 1, each exactly once. `live_counts`: equals the number of tiles that a device keeps or receives.
All inputs are finite; a program needn't handle non-finite values. No bound on the sum of `flame_flags` on one device may be relied on, other than what follows from the above.
Results may differ from the reference program's by a relative error of at most 0.001.
Values may be sent and summed in bfloat16 or wider, within the bound.
No kernel may reach another device: no remote copies, remote signals or barrier semaphores. Data moves between devices by JAX's collectives and lax.ppermute only.
A program may use at most 320 MiB of HBM per device.

```python
import jax
import jax.numpy as jnp
from jax import lax

S = 9
TE = 16
TZ = 2
TCOL = 16
SLOTS = 32
NTILES = 1024
BZ = 32
NZ = 128
NCOL = 32768
NTZ = 8
NTC = 128
N_GRP = 2
N_MIG = 4
N_PEN = 4


def migration_plan(key):
    peer_count = N_MIG * N_PEN
    groups = N_GRP
    subkeys = jax.random.split(jax.random.fold_in(key, 911), 6)
    members = jnp.arange(peer_count, dtype=jnp.int32)
    rank_list = jnp.arange(SLOTS, dtype=jnp.int32)
    thresholds = jax.random.randint(subkeys[0], (groups, peer_count), 0, 5)
    chosen = jax.random.randint(subkeys[1], (groups,), 0, peer_count)
    is_full = members[None, :] == chosen[:, None]
    is_empty = members[None, :] == (chosen[:, None] + 1) % peer_count
    thresholds = jnp.where(is_full, 4, thresholds)
    throws = jax.random.randint(subkeys[2], (groups, peer_count, peer_count), 0, 4)
    self_link = members[:, None] == members[None, :]
    linkage = ((throws < thresholds[:, None, :]) & jnp.logical_not(self_link)[None]).astype(jnp.int32)
    out_degree = jnp.sum(linkage, axis=2)
    in_degree = jnp.sum(linkage, axis=1)
    headroom = SLOTS - jnp.maximum(out_degree, in_degree)
    staying = jax.random.randint(subkeys[3], (groups, peer_count), 0, headroom + 1)
    staying = jnp.where(is_full, headroom, staying)
    staying = jnp.where(is_empty, 0, staying)
    counts = staying + in_degree
    old_scores = jax.random.randint(subkeys[4], (groups, peer_count, SLOTS), 0, 1 << 20) * SLOTS + rank_list
    old_order = jnp.argsort(old_scores, axis=2)
    rank_of_slot = jnp.argsort(old_order, axis=2)
    receivers = jnp.argsort((1 - linkage) * peer_count + members[None, None, :], axis=2)
    arriving = jnp.cumsum(linkage, axis=1) - linkage
    new_scores = jax.random.randint(subkeys[5], (groups, peer_count, SLOTS), 0, 1 << 20) * SLOTS + rank_list
    new_order = jnp.argsort(new_scores, axis=2)
    sort_key = jnp.where(new_order < counts[:, :, None], rank_list, SLOTS + rank_list)
    layout = jnp.take_along_axis(new_order, jnp.argsort(sort_key, axis=2), axis=2)
    is_send = rank_list[None, None, :] < out_degree[:, :, None]
    is_keep = jnp.logical_not(is_send) & (rank_list[None, None, :] < (out_degree + staying)[:, :, None])
    clipped_rank = jnp.broadcast_to(jnp.minimum(rank_list, peer_count - 1), (groups, peer_count, SLOTS))
    target_peer = jnp.take_along_axis(receivers, clipped_rank, axis=2)
    staying_wide = jnp.broadcast_to(staying[:, None, :], (groups, peer_count, peer_count))
    position = jnp.take_along_axis(arriving, target_peer, axis=2) + jnp.take_along_axis(staying_wide, target_peer, axis=2)
    flat_layout = layout.reshape(groups, peer_count * SLOTS)
    pick_index = (target_peer * SLOTS + jnp.minimum(position, SLOTS - 1)).reshape(groups, peer_count * SLOTS)
    sent_slot = jnp.take_along_axis(flat_layout, pick_index, axis=1).reshape(groups, peer_count, SLOTS)
    kept_rank = jnp.clip(rank_list[None, None, :] - out_degree[:, :, None], 0, SLOTS - 1)
    kept_slot = jnp.take_along_axis(layout, kept_rank, axis=2)
    slot_by_rank = jnp.where(is_send, sent_slot, jnp.where(is_keep, kept_slot, SLOTS))
    peer_by_rank = jnp.where(is_send, target_peer, members[None, :, None])
    destination = jnp.take_along_axis(peer_by_rank, rank_of_slot, axis=2)
    target = jnp.take_along_axis(slot_by_rank, rank_of_slot, axis=2)
    return (destination.reshape(-1).astype(jnp.int32), target.reshape(-1).astype(jnp.int32), counts.reshape(-1).astype(jnp.int32))


def draw_destination(key, part):
    return migration_plan(key)[0]


def draw_target_slot(key, part):
    return migration_plan(key)[1]


def draw_live_counts(key, part):
    return migration_plan(key)[2]


def plant(array, stream_key, least, top_value):
    longest = array.shape.index(max(array.shape))
    spots = []
    for shift in (0, 1):
        where = [jax.random.randint(jax.random.fold_in(stream_key, axis), (), 0, length) for axis, length in enumerate(array.shape)]
        where[longest] = (where[longest] + shift) % array.shape[longest]
        spots.append(tuple(where))
    return array.at[spots[0]].set(least).at[spots[1]].set(top_value)


def block_scale(own_key, dims, cuts, least, top_value):
    loudness, own = 1.0, jax.random.fold_in(own_key, 6)
    for axis_at, parts in cuts:
        steps = jnp.exp(jax.random.uniform(jax.random.fold_in(own, axis_at), (parts,), jnp.float32, least / len(cuts), top_value / len(cuts)))
        loudness = loudness * jnp.repeat(steps, dims[axis_at] // parts).reshape([-1 if axis == axis_at else 1 for axis in range(len(dims))])
    return loudness


def bell_draw(rng, dims, scale, most, cuts=(), kind=jnp.bfloat16):
    array = jax.random.normal(rng, dims, jnp.float32) * scale
    if len(cuts) > 0:
        array = block_scale(rng, dims, cuts, -0.22, 0.18) * array
    return jnp.clip(array, min=-most, max=most).astype(kind)


def setup_inputs(seed: int = 0) -> dict:
    arg_keys = jax.random.split(jax.random.key(seed), 13)
    return {
        "fields": bell_draw(arg_keys[0], (NTILES, S, TE**3), 1.0, 6.0, ((0, 32),), jnp.float32),
        "ghosts": bell_draw(arg_keys[1], (NTILES, S, 6 * TE * TE), 1.0, 6.0, ((0, 32),), jnp.float32),
        "velocity": jnp.clip(jax.random.uniform(arg_keys[2], (3, NTILES), jnp.float32, -1.0, 1.0) * block_scale(arg_keys[2], (3, NTILES), ((1, 32),), -0.4, 0.0), -1.0, 1.0),
        "rate_matrix": bell_draw(arg_keys[3], (S, S), S ** -0.5, 2.0, (), jnp.float32),
        "recent_tend": bell_draw(arg_keys[4], (NTILES, S, TE**3), 1.0, 6.0, ((0, 32),)),
        "older_tend": bell_draw(arg_keys[5], (NTILES, S, TE**3), 1.0, 6.0, ((0, 32),)),
        "destination": draw_destination(jax.random.fold_in(arg_keys[12], 71), 0),
        "target_slot": draw_target_slot(jax.random.fold_in(arg_keys[12], 71), 0),
        "live_counts": draw_live_counts(jax.random.fold_in(arg_keys[12], 71), 0),
        "tile_ids": jax.random.permutation(arg_keys[9], NTILES).astype(jnp.int32),
        "sensor": jnp.clip(4.0 * jax.random.uniform(arg_keys[10], (NZ, NCOL), jnp.float32) ** block_scale(arg_keys[10], (NZ, NCOL), ((0, 4), (1, 8)), -0.2, 0.2), 0.0, 4.0),
        "flame_flags": plant((jax.random.randint(arg_keys[11], (NTZ, NTC), 0, 2) < 1).astype(jnp.int32), jax.random.fold_in(arg_keys[11], 1), 0, 1),
    }


viscous = 0.05
step_size = 0.25
thicken = 5.0


def face_fill(face_values, tile_edge, direction):
    lead = face_values.shape[0]
    species = face_values.shape[1]
    cells = tile_edge ** 3
    if direction == 0:
        spread = jnp.broadcast_to(face_values[:, :, None, :], (lead, species, tile_edge, tile_edge * tile_edge))
    elif direction == 1:
        shaped = face_values.reshape(lead, species, tile_edge, 1, tile_edge)
        spread = jnp.broadcast_to(shaped, (lead, species, tile_edge, tile_edge, tile_edge))
    else:
        shaped = face_values.reshape(lead, species, tile_edge * tile_edge, 1)
        spread = jnp.broadcast_to(shaped, (lead, species, tile_edge * tile_edge, tile_edge))
    return spread.reshape(lead, species, cells)


def tendency(fields, ghosts, velocity, thickening, rate_matrix, tile_edge):
    face_size = tile_edge * tile_edge
    tile_cells = tile_edge ** 3
    cell_index = jnp.arange(tile_cells, dtype=jnp.int32)
    z_index = cell_index % tile_edge
    y_index = (cell_index // tile_edge) % tile_edge
    x_index = cell_index // face_size
    faces = [face_fill(ghosts[:, :, which * face_size:(which + 1) * face_size], tile_edge, which // 2) for which in range(6)]
    x_low = jnp.where(x_index == 0, faces[0], jnp.roll(fields, face_size, axis=2))
    x_high = jnp.where(x_index == tile_edge - 1, faces[1], jnp.roll(fields, -face_size, axis=2))
    y_low = jnp.where(y_index == 0, faces[2], jnp.roll(fields, tile_edge, axis=2))
    y_high = jnp.where(y_index == tile_edge - 1, faces[3], jnp.roll(fields, -tile_edge, axis=2))
    z_low = jnp.where(z_index == 0, faces[4], jnp.roll(fields, 1, axis=2))
    z_high = jnp.where(z_index == tile_edge - 1, faces[5], jnp.roll(fields, -1, axis=2))
    laplace = x_low + x_high + y_low + y_high + z_low + z_high - 6.0 * fields
    advection = 0.5 * (velocity[0][:, None, None] * (x_high - x_low)
                       + velocity[1][:, None, None] * (y_high - y_low)
                       + velocity[2][:, None, None] * (z_high - z_low))
    burning = fields[:, 0] * fields[:, 1]
    reaction = jnp.einsum("sk,nkc->nsc", rate_matrix, fields * burning[:, None, :], precision=lax.Precision.HIGHEST)
    thick_slot = thickening[:, None, None]
    return thick_slot * viscous * laplace - advection + reaction / thick_slot


def gauss_total(reach):
    sigma = reach / 2.0
    offsets = jnp.arange(-reach, reach + 1).astype(jnp.float32)
    return jnp.sum(jnp.exp(-offsets * offsets / (2.0 * sigma * sigma)))


def circulant(length, reach):
    sigma = reach / 2.0
    row_index = jnp.arange(length, dtype=jnp.int32)[:, None]
    col_index = jnp.arange(length, dtype=jnp.int32)[None, :]
    offset = (col_index - row_index) % length
    distance = jnp.minimum(offset, length - offset).astype(jnp.float32)
    weights = jnp.where(distance <= reach, jnp.exp(-distance * distance / (2.0 * sigma * sigma)), 0.0)
    return (weights / gauss_total(reach)).astype(jnp.float32)


def tile_thickening(filtered, tile_edge, tile_rows, tile_cols):
    clipped = jnp.minimum(filtered, 1.0)
    shaped = clipped.reshape(tile_rows, tile_edge, tile_cols, tile_edge * tile_edge)
    return 1.0 + (thicken - 1.0) * jnp.mean(shaped, axis=(1, 3))


def reference(fields, ghosts, velocity, rate_matrix, recent_tend, older_tend, destination, target_slot, live_counts, tile_ids, sensor, flame_flags):
    peer_count = N_MIG * N_PEN
    expand = jnp.repeat(jnp.repeat(flame_flags.astype(jnp.float32), TE, axis=0), TE * TE, axis=1)
    raw_sensor = sensor * expand
    filtered = jnp.dot(circulant(NZ, BZ), raw_sensor, precision=lax.Precision.HIGHEST)
    thick_grid = tile_thickening(filtered, TE, NTZ, NTC)
    thick_table = thick_grid.reshape(N_PEN, TZ, N_GRP * N_MIG, TCOL).transpose(2, 0, 1, 3).reshape(NTILES)
    slot_thick = jnp.take(thick_table, tile_ids)
    old_index = jnp.arange(NTILES, dtype=jnp.int32)
    group_index = old_index // (SLOTS * peer_count)
    target = (group_index * peer_count + destination) * SLOTS + target_slot
    target = jnp.where(target_slot < SLOTS, target, NTILES).astype(jnp.int32)
    moved_recent = jnp.zeros_like(recent_tend).at[target].set(recent_tend, mode="drop")
    moved_older = jnp.zeros_like(older_tend).at[target].set(older_tend, mode="drop")
    live_mask = ((old_index % SLOTS) < jnp.repeat(live_counts, SLOTS)).astype(jnp.float32)
    device_count = NTILES // SLOTS
    tile_cells = TE ** 3

    def per_device(bundle):
        here_fields, here_ghosts, here_velocity, here_thick, here_recent, here_older, here_live = bundle
        tendencies = tendency(here_fields, here_ghosts, here_velocity, here_thick, rate_matrix, TE)
        update = (23.0 / 12.0) * tendencies - (16.0 / 12.0) * here_recent.astype(jnp.float32) + (5.0 / 12.0) * here_older.astype(jnp.float32)
        mask_column = here_live[:, None, None]
        new_fields = (here_fields + step_size * update) * mask_column
        new_tend = (tendencies * mask_column).astype(jnp.bfloat16)
        return new_fields, new_tend

    bundle = (fields.reshape(device_count, SLOTS, S, tile_cells),
              ghosts.reshape(device_count, SLOTS, S, 6 * TE * TE),
              velocity.reshape(3, device_count, SLOTS).transpose(1, 0, 2),
              slot_thick.reshape(device_count, SLOTS),
              moved_recent.reshape(device_count, SLOTS, S, tile_cells),
              moved_older.reshape(device_count, SLOTS, S, tile_cells),
              live_mask.reshape(device_count, SLOTS))
    new_fields, new_tend = lax.map(per_device, bundle)
    return new_fields.reshape(NTILES, S, tile_cells), new_tend.reshape(NTILES, S, tile_cells), filtered
```

```python
import functools

import jax
import jax.numpy as jnp
import numpy as np
from jax import lax
from jax.experimental import pallas as pl
from jax.experimental.pallas import tpu as pltpu
from jax.sharding import PartitionSpec as P

TE = 16
TZ = 2
TCOL = 16
FACE = TE * TE
CELLS = TE**3
LANES = 128
ROWS = CELLS // LANES

viscous = 0.05
step_size = 0.25
thicken = 5.0

SCALE = 4096.0
PLANES = 4

EVERY = ("grp", "mig", "pen")
TEAM = ("mig", "pen")


def passed_along(x, axis, by):
    peers = lax.axis_size(axis)
    return lax.ppermute(x, axis, [(i, (i + by) % peers) for i in range(peers)])


def banded(brick_rows, reach):
    sigma = reach / 2.0
    offsets = np.arange(-reach, reach + 1, dtype=np.float64)
    total = np.sum(np.exp(-offsets * offsets / (2.0 * sigma * sigma)))
    row = np.arange(brick_rows)[:, None]
    col = np.arange(brick_rows + 2 * reach)[None, :]
    offset = (col - reach - row).astype(np.float64)
    weights = np.where(np.abs(offset) <= reach, np.exp(-offset * offset / (2.0 * sigma * sigma)), 0)
    return (weights / total).astype(np.float32)


def raw_kernel(flags_ref, sensor_ref, raw_ref):
    for r in range(TZ):
        for k in range(TCOL):
            rows, cols = slice(r * TE, (r + 1) * TE), slice(k * FACE, (k + 1) * FACE)
            flag = flags_ref[r, k].astype(jnp.float32)
            raw_ref[rows, cols] = (sensor_ref[rows, cols] * flag).astype(jnp.bfloat16)


def filter_kernel(flags_ref, weights_ref, sensor_ref, below_ref, above_ref, notes_ref, filtered_ref, row_ref):
    lane = lax.broadcasted_iota(jnp.int32, (1, LANES), 1)
    row = notes_ref[...]
    brick = sensor_ref.shape[0]
    for k in range(TCOL):
        cols = slice(k * FACE, (k + 1) * FACE)
        own = [
            sensor_ref[r * TE : (r + 1) * TE, cols] * flags_ref[r, k].astype(jnp.float32)
            for r in range(TZ)
        ]
        widened = jnp.concatenate(
            [below_ref[:, cols].astype(jnp.float32)] + own + [above_ref[:, cols].astype(jnp.float32)],
            axis=0,
        )
        filtered = jnp.dot(
            weights_ref[...],
            widened,
            precision=lax.Precision.HIGHEST,
            preferred_element_type=jnp.float32,
        )
        filtered_ref[:, cols] = filtered
        clipped = jnp.minimum(filtered, 1.0)
        for r in range(TZ):
            total = jnp.sum(
                jnp.sum(clipped[r * TE : (r + 1) * TE], axis=0, keepdims=True), axis=1, keepdims=True
            )
            thick = 1.0 + (thicken - 1.0) * (total / float(TE * FACE))
            row = jnp.where(lane == r * TCOL + k, thick, row)
    row_ref[...] = row


def send_kernel(me_ref, destination_ref, recent_ref, older_ref, out_ref):
    peers = out_ref.shape[0]
    slots = recent_ref.shape[1]
    peer = lax.broadcasted_iota(jnp.int32, (peers, slots), 0)
    hot = ((destination_ref[...] == peer) & (peer != me_ref[0])).astype(jnp.bfloat16)
    recent = jnp.dot(hot, recent_ref[0], preferred_element_type=jnp.float32)
    older = jnp.dot(hot, older_ref[0], preferred_element_type=jnp.float32)
    mixed = recent * (-16.0 / 12.0 * SCALE) + older * (5.0 / 12.0 * SCALE)
    flat = out_ref.reshape(peers * ROWS, LANES)
    for k in range(ROWS):
        flat[pl.ds(k, peers, stride=ROWS), :] = mixed[:, k * LANES : (k + 1) * LANES]


def add_kernel(me_ref, live_ref, table_ref, fields_ref, arrived_ref, out_ref):
    peers = arrived_ref.shape[0]
    slots = fields_ref.shape[1]
    me, first = me_ref[0], pl.multiple_of(me_ref[1] * peers, peers)
    notes = table_ref[pl.ds(first, peers), :]
    destination = notes[:, slots : 2 * slots]
    target = notes[:, 2 * slots : 3 * slots]
    peer = lax.broadcasted_iota(jnp.int32, (peers, slots), 0)
    mine = (destination == me.astype(jnp.float32)) & (peer != me)
    slot = jnp.max(jnp.where(mine, target, -1.0), axis=1, keepdims=True)
    index = lax.broadcasted_iota(jnp.int32, (peers, slots), 1)
    hot = (slot == index.astype(jnp.float32)) & (index < live_ref[0])
    hot = jnp.where(hot, step_size / SCALE, 0.0).astype(jnp.bfloat16)
    flat = arrived_ref.reshape(peers * ROWS, LANES)
    arrived = jnp.concatenate(
        [flat[pl.ds(k, peers, stride=ROWS), :] for k in range(ROWS)], axis=1
    )
    high = arrived.astype(jnp.bfloat16)
    low = (arrived - high.astype(jnp.float32)).astype(jnp.bfloat16)
    placed = lax.dot_general(
        jnp.concatenate([hot, hot], axis=0),
        jnp.concatenate([high, low], axis=0),
        (((0,), (0,)), ((), ())),
        preferred_element_type=jnp.float32,
    )
    out_ref[0] = fields_ref[0] + placed


def main_kernel(
    me_ref,
    live_ref,
    rate_ref,
    moves_ref,
    coef_ref,
    fields_ref,
    before_ref,
    after_ref,
    ghosts_ref,
    recent_ref,
    older_ref,
    new_fields_ref,
    new_tend_ref,
    kept_ref,
    wide_ref,
):
    step = pl.program_id(0)
    species, slots, width = fields_ref.shape
    last = pl.num_programs(0) - 1

    @pl.when(step == 0)
    def _():
        coef = coef_ref[...]
        thick = coef[:, 0:1]
        smooth = viscous * thick
        live = lax.broadcasted_iota(jnp.int32, (slots, 1), 0) < live_ref[0]
        parts = []
        for d in range(3):
            carry = 0.5 * coef[:, 1 + d : 2 + d]
            parts += [smooth + carry, smooth - carry]
        parts += [6.0 * smooth, 1.0 / thick, jnp.where(live, 1.0, 0.0)]
        for n, part in enumerate(parts):
            wide_ref[n] = jnp.broadcast_to(part, (slots, LANES))

    slot = lax.broadcasted_iota(jnp.int32, (slots, slots), 0)
    keep = ((moves_ref[0:1, :] == me_ref[0]) & (moves_ref[1:2, :] == slot)).astype(jnp.bfloat16)

    def keep_one(s, carry):
        recent = jnp.dot(keep, recent_ref[s], preferred_element_type=jnp.float32)
        older = jnp.dot(keep, older_ref[s], preferred_element_type=jnp.float32)
        kept_ref[s] = recent * (-16.0 / 12.0 * step_size) + older * (5.0 / 12.0 * step_size)
        return carry

    lax.fori_loop(0, species, keep_one, 0)

    lane = lax.broadcasted_iota(jnp.int32, (8, LANES), 1)
    z_index = lane % TE
    low_end, high_end = lane < TE, lane >= LANES - TE
    z_first, z_last = z_index == 0, z_index == TE - 1
    block = step * PLANES // 8
    inner = step * PLANES % 8

    def group(g, carry):
        for sub in range(2):
            rows = pl.ds(pl.multiple_of(g * 16, 16) + sub * 8, 8)
            xl_c, xh_c, yl_c, yh_c, zl_c, zh_c, six, over, live = [
                wide_ref[n, rows, :] for n in range(9)
            ]
            for p in range(PLANES):
                fields = []
                for half in range(2):
                    lanes = slice(p * FACE + half * LANES, p * FACE + (half + 1) * LANES)
                    fields.append([fields_ref[s, rows, lanes] for s in range(species)])
                burning = [f[0] * f[1] * over for f in fields]
                fuel = [[f[s] * burning[h] for s in range(species)] for h, f in enumerate(fields)]
                shift = (inner + p) * TE
                for s in range(species):
                    face = [
                        ghosts_ref[
                            s, rows, pl.ds(pl.multiple_of(w * FACE + block * LANES, LANES), LANES)
                        ]
                        for w in range(2, 6)
                    ]
                    pair = [fields[0][s], fields[1][s]]
                    up = [pltpu.roll(v, TE, 1) for v in pair]
                    down = [pltpu.roll(v, LANES - TE, 1) for v in pair]
                    y_low = [
                        jnp.where(low_end, pltpu.roll(face[0], (LANES - shift) % LANES, 1), up[0]),
                        jnp.where(low_end, up[0], up[1]),
                    ]
                    y_high = [
                        jnp.where(high_end, down[1], down[0]),
                        jnp.where(high_end, pltpu.roll(face[1], (2 * LANES - TE - shift) % LANES, 1), down[1]),
                    ]
                    for half in range(2):
                        lanes = slice(p * FACE + half * LANES, p * FACE + (half + 1) * LANES)
                        f = pair[half]
                        spread = shift + half * (TE // 2) + lane // TE
                        z_low = jnp.where(
                            z_first,
                            jnp.take_along_axis(face[2], spread, axis=1, mode="promise_in_bounds"),
                            pltpu.roll(f, 1, 1),
                        )
                        z_high = jnp.where(
                            z_last,
                            jnp.take_along_axis(face[3], spread, axis=1, mode="promise_in_bounds"),
                            pltpu.roll(f, LANES - 1, 1),
                        )
                        if p > 0:
                            back = slice(lanes.start - FACE, lanes.stop - FACE)
                            x_low = fields_ref[s, rows, back]
                        else:
                            near = slice(half * LANES, (half + 1) * LANES)
                            x_low = jnp.where(
                                step == 0, ghosts_ref[s, rows, near], before_ref[s, rows, near]
                            )
                        if p < PLANES - 1:
                            ahead = slice(lanes.start + FACE, lanes.stop + FACE)
                            x_high = fields_ref[s, rows, ahead]
                        else:
                            near = slice(half * LANES, (half + 1) * LANES)
                            far = slice(FACE + half * LANES, FACE + (half + 1) * LANES)
                            x_high = jnp.where(
                                step == last, ghosts_ref[s, rows, far], after_ref[s, rows, near]
                            )
                        tend = (xl_c * x_low + xh_c * x_high) + (yl_c * y_low[half] + yh_c * y_high[half])
                        tend += (zl_c * z_low + zh_c * z_high) - six * f
                        react = rate_ref[s, 0] * fuel[half][0]
                        for k in range(1, species):
                            react += rate_ref[s, k] * fuel[half][k]
                        tend += react
                        new = f + (step_size * 23.0 / 12.0) * tend + kept_ref[s, rows, lanes]
                        new_fields_ref[s, rows, lanes] = new * live
                        kept_ref[s, rows, lanes] = tend * live
        return carry

    lax.fori_loop(0, slots // 16, group, 0)

    def narrow(s, carry):
        new_tend_ref[s] = kept_ref[s].astype(jnp.bfloat16)
        return carry

    lax.fori_loop(0, species, narrow, 0)


def smem():
    return pl.BlockSpec(memory_space=pltpu.SMEM)


def whole(shape):
    return pl.BlockSpec(shape, lambda i: (0,) * len(shape))


def params(mib, semantics=None):
    return pltpu.CompilerParams(vmem_limit_bytes=mib << 20, dimension_semantics=semantics)


def local(
    fields,
    ghosts,
    velocity,
    rate_matrix,
    recent_tend,
    older_tend,
    destination,
    target_slot,
    live_counts,
    tile_ids,
    sensor,
    flame_flags,
):
    slots, species, cells = fields.shape
    peers = lax.axis_size(TEAM)
    devices = lax.axis_size(EVERY)
    brick = sensor.shape[0]
    me = jnp.stack([lax.axis_index(TEAM), lax.axis_index("grp")]).astype(jnp.int32)
    fields, ghosts, recent, older = (
        a.transpose(1, 0, 2) for a in (fields, ghosts, recent_tend, older_tend)
    )
    moves = jnp.stack([destination, target_slot])

    raw = pl.pallas_call(
        raw_kernel,
        name="raw_sensor",
        out_shape=jax.ShapeDtypeStruct(sensor.shape, jnp.bfloat16),
        in_specs=[smem(), pl.BlockSpec(memory_space=pltpu.VMEM)],
        out_specs=pl.BlockSpec(memory_space=pltpu.VMEM),
        compiler_params=params(16),
    )(flame_flags, sensor)
    below = passed_along(raw, "pen", 1)
    above = passed_along(raw, "pen", -1)

    outgoing = pl.pallas_call(
        send_kernel,
        name="outgoing_histories",
        grid=(species,),
        out_shape=jax.ShapeDtypeStruct((peers, species * ROWS, LANES), jnp.float32),
        in_specs=[
            smem(),
            whole((1, slots)),
            pl.BlockSpec((1, slots, cells), lambda i: (i, 0, 0)),
            pl.BlockSpec((1, slots, cells), lambda i: (i, 0, 0)),
        ],
        out_specs=pl.BlockSpec((peers, ROWS, LANES), lambda i: (0, i, 0)),
        compiler_params=params(32, ("arbitrary",)),
        cost_estimate=pl.CostEstimate(flops=0, bytes_accessed=8 << 20, transcendentals=0),
    )(me, destination.reshape(1, slots), recent, older)
    arrived = lax.all_to_all(
        outgoing.astype(jnp.float16), TEAM, split_axis=0, concat_axis=0, tiled=True
    ).astype(jnp.float32)

    notes = jnp.concatenate(
        [jnp.zeros((1, slots), jnp.float32), moves.astype(jnp.float32).reshape(1, 2 * slots)], axis=1
    )
    notes = jnp.pad(notes, ((0, 0), (0, LANES - 3 * slots)))
    vmem = pl.BlockSpec(memory_space=pltpu.VMEM)
    filtered, row = pl.pallas_call(
        filter_kernel,
        name="filtered_sensor",
        out_shape=(
            jax.ShapeDtypeStruct(sensor.shape, jnp.float32),
            jax.ShapeDtypeStruct((1, LANES), jnp.float32),
        ),
        in_specs=[smem()] + [vmem] * 5,
        out_specs=(vmem, vmem),
        compiler_params=params(32),
        cost_estimate=pl.CostEstimate(flops=0, bytes_accessed=4 << 20, transcendentals=0),
    )(flame_flags, jnp.asarray(banded(brick, brick)), sensor, below, above, notes)
    table = gathered(row)

    slot_thick = jnp.take(table[:, :slots].reshape(devices * slots), tile_ids)
    coef = jnp.concatenate([slot_thick[:, None], velocity.T, jnp.zeros((slots, 4))], axis=1)
    width = PLANES * FACE
    steps = cells // width
    new_fields, new_tend = pl.pallas_call(
        main_kernel,
        name="tendencies",
        grid=(steps,),
        out_shape=(
            jax.ShapeDtypeStruct((species, slots, cells), jnp.float32),
            jax.ShapeDtypeStruct((species, slots, cells), jnp.bfloat16),
        ),
        in_specs=[
            smem(),
            smem(),
            smem(),
            whole((2, slots)),
            whole((slots, 8)),
            pl.BlockSpec((species, slots, width), lambda i: (0, 0, i)),
            pl.BlockSpec((species, slots, FACE), lambda i: (0, 0, jnp.maximum(i * PLANES - 1, 0))),
            pl.BlockSpec(
                (species, slots, FACE), lambda i: (0, 0, jnp.minimum((i + 1) * PLANES, TE - 1))
            ),
            whole(ghosts.shape),
            pl.BlockSpec((species, slots, width), lambda i: (0, 0, i)),
            pl.BlockSpec((species, slots, width), lambda i: (0, 0, i)),
        ],
        out_specs=(
            pl.BlockSpec((species, slots, width), lambda i: (0, 0, i)),
            pl.BlockSpec((species, slots, width), lambda i: (0, 0, i)),
        ),
        scratch_shapes=[
            pltpu.VMEM((species, slots, width), jnp.float32),
            pltpu.VMEM((9, slots, LANES), jnp.float32),
        ],
        compiler_params=params(48, ("arbitrary",)),
        cost_estimate=pl.CostEstimate(flops=0, bytes_accessed=36 << 20, transcendentals=0),
    )(me, live_counts, rate_matrix, moves, coef, fields, fields, fields, ghosts, recent, older)

    new_fields = pl.pallas_call(
        add_kernel,
        name="arrived_histories",
        grid=(species,),
        out_shape=jax.ShapeDtypeStruct((species, slots, cells), jnp.float32),
        in_specs=[
            smem(),
            smem(),
            whole(table.shape),
            pl.BlockSpec((1, slots, cells), lambda i: (i, 0, 0)),
            pl.BlockSpec((peers, ROWS, LANES), lambda i: (0, i, 0)),
        ],
        out_specs=pl.BlockSpec((1, slots, cells), lambda i: (i, 0, 0)),
        input_output_aliases={3: 0},
        compiler_params=params(32, ("arbitrary",)),
        cost_estimate=pl.CostEstimate(flops=0, bytes_accessed=12 << 20, transcendentals=0),
    )(me, live_counts, table, new_fields, arrived)
    return new_fields.transpose(1, 0, 2), new_tend.transpose(1, 0, 2), filtered


def gathered(row):
    for axis in ("pen", "mig", "grp"):
        count = lax.axis_size(axis)
        here = lax.axis_index(axis)
        rows = [row] + [passed_along(row, axis, by) for by in range(1, count)]
        height = row.shape[0]
        table = jnp.zeros((count,) + row.shape, row.dtype)
        for by, part in enumerate(rows):
            table = lax.dynamic_update_slice(table, part[None], ((here - by) % count, 0, 0))
        row = table.reshape(count * height, row.shape[1])
    return row


def solution(mesh):
    split = P(EVERY, None, None)
    return jax.shard_map(
        local,
        mesh=mesh,
        in_specs=(
            split,
            split,
            P(None, EVERY),
            P(),
            split,
            split,
            P(EVERY),
            P(EVERY),
            P(EVERY),
            P(EVERY),
            P("pen", ("grp", "mig")),
            P("pen", ("grp", "mig")),
        ),
        out_specs=(split, split, P("pen", ("grp", "mig"))),
        check_vma=False,
    )
```

```python
import functools

import jax
import jax.numpy as jnp
import numpy as np
from jax import lax
from jax.experimental import pallas as pl
from jax.experimental.pallas import tpu as pltpu
from jax.sharding import PartitionSpec as P

TE = 16
TZ = 2
TCOL = 16
FACE = TE * TE
CELLS = TE**3
LANES = 128
ROWS = CELLS // LANES

viscous = 0.05
step_size = 0.25
thicken = 5.0

SCALE = 4096.0
PLANES = 4

EVERY = ("grp", "mig", "pen")
TEAM = ("pen", "mig")


def passed_along(x, axis, by):
    peers = lax.axis_size(axis)
    return lax.ppermute(x, axis, [(i, (i + by) % peers) for i in range(peers)])


def banded(brick_rows, reach):
    sigma = reach / 2.0
    offsets = np.arange(-reach, reach + 1, dtype=np.float64)
    total = np.sum(np.exp(-offsets * offsets / (2.0 * sigma * sigma)))
    row = np.arange(brick_rows)[:, None]
    col = np.arange(brick_rows + 2 * reach)[None, :]
    offset = (col - reach - row).astype(np.float64)
    weights = np.where(np.abs(offset) <= reach, np.exp(-offset * offset / (2.0 * sigma * sigma)), 0)
    return (weights / total).astype(np.float32)


def raw_kernel(flags_ref, sensor_ref, raw_ref):
    for r in range(TZ):
        for k in range(TCOL):
            rows, cols = slice(r * TE, (r + 1) * TE), slice(k * FACE, (k + 1) * FACE)
            flag = flags_ref[r, k].astype(jnp.float32)
            raw_ref[rows, cols] = (sensor_ref[rows, cols] * flag).astype(jnp.bfloat16)


def filter_kernel(flags_ref, weights_ref, sensor_ref, below_ref, above_ref, notes_ref, filtered_ref, row_ref):
    lane = lax.broadcasted_iota(jnp.int32, (1, LANES), 1)
    row = notes_ref[...]
    brick = sensor_ref.shape[0]
    for k in range(TCOL):
        cols = slice(k * FACE, (k + 1) * FACE)
        own = [
            sensor_ref[r * TE : (r + 1) * TE, cols] * flags_ref[r, k].astype(jnp.float32)
            for r in range(TZ)
        ]
        widened = jnp.concatenate(
            [below_ref[:, cols].astype(jnp.float32)] + own + [above_ref[:, cols].astype(jnp.float32)],
            axis=0,
        )
        filtered = jnp.dot(
            weights_ref[...],
            widened,
            precision=lax.Precision.HIGHEST,
            preferred_element_type=jnp.float32,
        )
        filtered_ref[:, cols] = filtered
        clipped = jnp.minimum(filtered, 1.0)
        for r in range(TZ):
            total = jnp.sum(
                jnp.sum(clipped[r * TE : (r + 1) * TE], axis=0, keepdims=True), axis=1, keepdims=True
            )
            thick = 1.0 + (thicken - 1.0) * (total / float(TE * FACE))
            row = jnp.where(lane == r * TCOL + k, thick, row)
    row_ref[...] = row


def send_kernel(migs, me_ref, destination_ref, recent_ref, older_ref, out_ref):
    peers = out_ref.shape[0]
    slots = recent_ref.shape[1]
    peer = lax.broadcasted_iota(jnp.int32, (peers, slots), 0)
    named = peer % migs * (peers // migs) + peer // migs
    hot = ((destination_ref[...] == named) & (peer != me_ref[1])).astype(jnp.bfloat16)
    recent = jnp.dot(hot, recent_ref[0], preferred_element_type=jnp.float32)
    older = jnp.dot(hot, older_ref[0], preferred_element_type=jnp.float32)
    mixed = recent * (-16.0 / 12.0 * SCALE) + older * (5.0 / 12.0 * SCALE)
    flat = out_ref.reshape(peers * ROWS, LANES)
    for k in range(ROWS):
        flat[pl.ds(k, peers, stride=ROWS), :] = mixed[:, k * LANES : (k + 1) * LANES]


def parts_kernel(
    me_ref,
    rate_ref,
    moves_ref,
    speed_ref,
    fields_ref,
    before_ref,
    after_ref,
    ghosts_ref,
    recent_ref,
    older_ref,
    laplace_ref,
    carried_ref,
    react_ref,
    base_ref,
):
    step = pl.program_id(0)
    species, slots, width = fields_ref.shape
    last = pl.num_programs(0) - 1

    slot = lax.broadcasted_iota(jnp.int32, (slots, slots), 0)
    keep = ((moves_ref[0:1, :] == me_ref[0]) & (moves_ref[1:2, :] == slot)).astype(jnp.bfloat16)

    def keep_one(s, carry):
        recent = jnp.dot(keep, recent_ref[s], preferred_element_type=jnp.float32)
        older = jnp.dot(keep, older_ref[s], preferred_element_type=jnp.float32)
        kept = recent * (-16.0 / 12.0 * step_size) + older * (5.0 / 12.0 * step_size)
        base_ref[s] = fields_ref[s] + kept
        return carry

    lax.fori_loop(0, species, keep_one, 0)

    lane = lax.broadcasted_iota(jnp.int32, (8, LANES), 1)
    z_index = lane % TE
    low_end, high_end = lane < TE, lane >= LANES - TE
    z_first, z_last = z_index == 0, z_index == TE - 1
    left_half = lane < LANES // 2
    spread = jnp.where(z_last, LANES // 2, 0) + lane // TE
    block = step * PLANES // 8
    turn = step * PLANES % 8 * TE

    def group(g, carry):
        rows = pl.ds(pl.multiple_of(g * 8, 8), 8)
        speed = [jnp.broadcast_to(speed_ref[rows, d : d + 1] * 0.5, (8, LANES)) for d in range(3)]
        for p in range(PLANES):
            spans = [slice(p * FACE + h * LANES, p * FACE + (h + 1) * LANES) for h in range(2)]
            for lanes in spans:
                fuel = [fields_ref[s, rows, lanes] for s in range(species)]
                burning = fuel[0] * fuel[1]
                fuel = [f * burning for f in fuel]
                for s in range(species):
                    total = rate_ref[s, 0] * fuel[0]
                    for k in range(1, species):
                        total += rate_ref[s, k] * fuel[k]
                    react_ref[s, rows, lanes] = total
        for s in range(species):
            face = [
                ghosts_ref[s, rows, pl.ds(pl.multiple_of(w * FACE + block * LANES, LANES), LANES)]
                for w in range(2, 6)
            ]
            z_ends = jnp.where(
                left_half,
                pltpu.roll(face[2], (LANES - turn) % LANES, 1),
                pltpu.roll(face[3], (LANES + LANES // 2 - turn) % LANES, 1),
            )
            for p in range(PLANES):
                spans = [slice(p * FACE + h * LANES, p * FACE + (h + 1) * LANES) for h in range(2)]
                pair = [fields_ref[s, rows, lanes] for lanes in spans]
                shift = turn + p * TE
                up = [pltpu.roll(v, TE, 1) for v in pair]
                down = [pltpu.roll(v, LANES - TE, 1) for v in pair]
                y_low = [
                    jnp.where(low_end, pltpu.roll(face[0], (LANES - shift) % LANES, 1), up[0]),
                    jnp.where(low_end, up[0], up[1]),
                ]
                y_high = [
                    jnp.where(high_end, down[1], down[0]),
                    jnp.where(
                        high_end, pltpu.roll(face[1], (2 * LANES - TE - shift) % LANES, 1), down[1]
                    ),
                ]
                for h, lanes in enumerate(spans):
                    f = pair[h]
                    ends = jnp.take_along_axis(
                        z_ends, spread + (p * TE + h * (TE // 2)), axis=1, mode="promise_in_bounds"
                    )
                    z_low = jnp.where(z_first, ends, pltpu.roll(f, 1, 1))
                    z_high = jnp.where(z_last, ends, pltpu.roll(f, LANES - 1, 1))
                    near = slice(h * LANES, (h + 1) * LANES)
                    far = slice(FACE + h * LANES, FACE + (h + 1) * LANES)
                    if p > 0:
                        x_low = fields_ref[s, rows, lanes.start - FACE : lanes.stop - FACE]
                    else:
                        x_low = jnp.where(
                            step == 0, ghosts_ref[s, rows, near], before_ref[s, rows, near]
                        )
                    if p < PLANES - 1:
                        x_high = fields_ref[s, rows, lanes.start + FACE : lanes.stop + FACE]
                    else:
                        x_high = jnp.where(
                            step == last, ghosts_ref[s, rows, far], after_ref[s, rows, near]
                        )
                    total = (x_low + x_high) + (y_low[h] + y_high[h]) + (z_low + z_high)
                    laplace_ref[s, rows, lanes] = total - 6.0 * f
                    carried_ref[s, rows, lanes] = (
                        speed[0] * (x_high - x_low)
                        + speed[1] * (y_high[h] - y_low[h])
                        + speed[2] * (z_high - z_low)
                    )
        return carry

    lax.fori_loop(0, slots // 8, group, 0)


def final_kernel(
    me_ref,
    live_ref,
    table_ref,
    tile_ref,
    laplace_ref,
    carried_ref,
    react_ref,
    base_ref,
    arrived_ref,
    new_fields_ref,
    new_tend_ref,
    hot_ref,
    wide_ref,
):
    peers = arrived_ref.shape[0]
    slots = base_ref.shape[1]

    @pl.when(pl.program_id(0) == 0)
    def _():
        me, first = me_ref[1], pl.multiple_of(me_ref[2] * LANES, LANES)
        notes = table_ref[:, pl.ds(first, LANES)]
        destination = notes[:, slots : 2 * slots]
        target = notes[:, 2 * slots : 3 * slots]
        peer = lax.broadcasted_iota(jnp.int32, (peers, slots), 0)
        mine = (destination == me_ref[0].astype(jnp.float32)) & (peer != me)
        slot = jnp.max(jnp.where(mine, target, -1.0), axis=1, keepdims=True)
        index = lax.broadcasted_iota(jnp.int32, (peers, slots), 1)
        hot = (slot == index.astype(jnp.float32)) & (index < live_ref[0])
        hot = jnp.where(hot, step_size / SCALE, 0.0)
        hot = jnp.concatenate([hot, hot], axis=0)
        hot_ref[...] = hot.T.astype(jnp.bfloat16)
        wanted = lax.broadcasted_iota(jnp.int32, (slots, peers), 1) == tile_ref[:, 0:1]
        picked = jnp.dot(
            wanted.astype(jnp.float32),
            table_ref[...],
            precision=lax.Precision.HIGHEST,
            preferred_element_type=jnp.float32,
        )
        lane = lax.broadcasted_iota(jnp.int32, picked.shape, 1)
        thick = jnp.sum(jnp.where(lane == tile_ref[:, 1:2], picked, 0.0), axis=1, keepdims=True)
        live = lax.broadcasted_iota(jnp.int32, (slots, 1), 0) < live_ref[0]
        for n, part in enumerate((viscous * thick, 1.0 / thick, jnp.where(live, 1.0, 0.0))):
            wide_ref[n] = jnp.broadcast_to(part, (slots, LANES))

    flat = arrived_ref.reshape(peers * ROWS, LANES)
    smooth, over, live = (wide_ref[n] for n in range(3))
    for c in range(ROWS // 2):
        lanes = slice(c * 2 * LANES, (c + 1) * 2 * LANES)
        arrived = jnp.concatenate(
            [flat[pl.ds(2 * c + k, peers, stride=ROWS), :] for k in range(2)], axis=1
        )
        high = arrived.astype(jnp.bfloat16)
        low = (arrived - high.astype(jnp.float32)).astype(jnp.bfloat16)
        placed = jnp.dot(
            hot_ref[...],
            jnp.concatenate([high, low], axis=0),
            preferred_element_type=jnp.float32,
        )
        tends = []
        for k in range(2):
            here = slice((2 * c + k) * LANES, (2 * c + k + 1) * LANES)
            tend = smooth * laplace_ref[0, :, here] - carried_ref[0, :, here] + over * react_ref[0, :, here]
            new = base_ref[0, :, here] + (step_size * 23.0 / 12.0) * tend
            new_fields_ref[0, :, here] = new * live + placed[:, k * LANES : (k + 1) * LANES]
            tends.append(tend * live)
        new_tend_ref[0, :, lanes] = jnp.concatenate(tends, axis=1).astype(jnp.bfloat16)


def smem():
    return pl.BlockSpec(memory_space=pltpu.SMEM)


def whole(shape):
    return pl.BlockSpec(shape, lambda i: (0,) * len(shape))


def params(mib, semantics=None):
    return pltpu.CompilerParams(vmem_limit_bytes=mib << 20, dimension_semantics=semantics)


def local(
    fields,
    ghosts,
    velocity,
    rate_matrix,
    recent_tend,
    older_tend,
    destination,
    target_slot,
    live_counts,
    tile_ids,
    sensor,
    flame_flags,
):
    slots, species, cells = fields.shape
    peers = lax.axis_size(TEAM)
    brick = sensor.shape[0]
    me = jnp.stack(
        [lax.axis_index(("mig", "pen")), lax.axis_index(TEAM), lax.axis_index("grp")]
    ).astype(jnp.int32)
    fields, ghosts, recent, older = (
        a.transpose(1, 0, 2) for a in (fields, ghosts, recent_tend, older_tend)
    )
    moves = jnp.stack([destination, target_slot])

    raw = pl.pallas_call(
        raw_kernel,
        name="raw_sensor",
        out_shape=jax.ShapeDtypeStruct(sensor.shape, jnp.bfloat16),
        in_specs=[smem(), pl.BlockSpec(memory_space=pltpu.VMEM)],
        out_specs=pl.BlockSpec(memory_space=pltpu.VMEM),
        compiler_params=params(58),
    )(flame_flags, sensor)
    below = passed_along(raw, "pen", 1)
    above = passed_along(raw, "pen", -1)

    outgoing = pl.pallas_call(
        functools.partial(send_kernel, lax.axis_size("mig")),
        name="outgoing_histories",
        grid=(species,),
        out_shape=jax.ShapeDtypeStruct((peers, species * ROWS, LANES), jnp.float32),
        in_specs=[
            smem(),
            whole((1, slots)),
            pl.BlockSpec((1, slots, cells), lambda i: (i, 0, 0)),
            pl.BlockSpec((1, slots, cells), lambda i: (i, 0, 0)),
        ],
        out_specs=pl.BlockSpec((peers, ROWS, LANES), lambda i: (0, i, 0)),
        compiler_params=params(58, ("arbitrary",)),
        cost_estimate=pl.CostEstimate(flops=0, bytes_accessed=8 << 20, transcendentals=0),
    )(me, destination.reshape(1, slots), recent, older)
    arrived = lax.all_to_all(
        outgoing.astype(jnp.float16), TEAM, split_axis=0, concat_axis=0, tiled=True
    ).astype(jnp.float32)

    notes = jnp.concatenate(
        [jnp.zeros((1, slots), jnp.float32), moves.astype(jnp.float32).reshape(1, 2 * slots)], axis=1
    )
    notes = jnp.pad(notes, ((0, 0), (0, LANES - 3 * slots)))
    vmem = pl.BlockSpec(memory_space=pltpu.VMEM)
    filtered, row = pl.pallas_call(
        filter_kernel,
        name="filtered_sensor",
        out_shape=(
            jax.ShapeDtypeStruct(sensor.shape, jnp.float32),
            jax.ShapeDtypeStruct((1, LANES), jnp.float32),
        ),
        in_specs=[smem()] + [vmem] * 5,
        out_specs=(vmem, vmem),
        compiler_params=params(32),
        cost_estimate=pl.CostEstimate(flops=0, bytes_accessed=4 << 20, transcendentals=0),
    )(flame_flags, jnp.asarray(banded(brick, brick)), sensor, below, above, notes)
    table = gathered(row)

    owner, lane = tile_ids // slots, tile_ids % slots
    pens, migs = lax.axis_size("pen"), lax.axis_size("mig")
    tile_place = jnp.stack(
        [owner % pens * migs + owner // pens % migs, owner // peers * LANES + lane], axis=1
    )
    speed = jnp.pad(velocity.T, ((0, 0), (0, 5)))
    width = PLANES * FACE
    moving = pl.BlockSpec((species, slots, width), lambda i: (0, 0, i))
    shape = jax.ShapeDtypeStruct((species, slots, cells), jnp.float32)
    parts = pl.pallas_call(
        parts_kernel,
        name="tendency_parts",
        grid=(cells // width,),
        out_shape=(shape,) * 4,
        in_specs=[
            smem(),
            smem(),
            whole((2, slots)),
            whole((slots, 8)),
            moving,
            pl.BlockSpec((species, slots, FACE), lambda i: (0, 0, jnp.maximum(i * PLANES - 1, 0))),
            pl.BlockSpec(
                (species, slots, FACE), lambda i: (0, 0, jnp.minimum((i + 1) * PLANES, TE - 1))
            ),
            whole(ghosts.shape),
            moving,
            moving,
        ],
        out_specs=(moving,) * 4,
        compiler_params=params(28, ("arbitrary",)),
        cost_estimate=pl.CostEstimate(flops=0, bytes_accessed=40 << 20, transcendentals=0),
    )(me, rate_matrix, moves, speed, fields, fields, fields, ghosts, recent, older)

    each = pl.BlockSpec((1, slots, cells), lambda i: (i, 0, 0))
    new_fields, new_tend = pl.pallas_call(
        final_kernel,
        name="updates",
        grid=(species,),
        out_shape=(shape, jax.ShapeDtypeStruct(shape.shape, jnp.bfloat16)),
        in_specs=[
            smem(),
            smem(),
            whole(table.shape),
            whole((slots, 2)),
            each,
            each,
            each,
            each,
            pl.BlockSpec((peers, ROWS, LANES), lambda i: (0, i, 0)),
        ],
        out_specs=(each, each),
        scratch_shapes=[
            pltpu.VMEM((slots, 2 * peers), jnp.bfloat16),
            pltpu.VMEM((3, slots, LANES), jnp.float32),
        ],
        compiler_params=params(16, ("arbitrary",)),
        cost_estimate=pl.CostEstimate(flops=0, bytes_accessed=28 << 20, transcendentals=0),
    )(me, live_counts, table, tile_place, *parts, arrived)
    return new_fields.transpose(1, 0, 2), new_tend.transpose(1, 0, 2), filtered


def gathered(row):
    for axis in ("grp", "mig", "pen"):
        count = lax.axis_size(axis)
        here = lax.axis_index(axis)
        rows = [row] + [passed_along(row, axis, by) for by in range(1, count)]
        height, width = row.shape
        if axis == "grp":
            table = jnp.zeros((height, count * width), row.dtype)
        else:
            table = jnp.zeros((count * height, width), row.dtype)
        for by, part in enumerate(rows):
            place = (here - by) % count
            place = (0, place * width) if axis == "grp" else (place * height, 0)
            table = lax.dynamic_update_slice(table, part, place)
        row = table
    return row


def solution(mesh):
    split = P(EVERY, None, None)
    return jax.shard_map(
        local,
        mesh=mesh,
        in_specs=(
            split,
            split,
            P(None, EVERY),
            P(),
            split,
            split,
            P(EVERY),
            P(EVERY),
            P(EVERY),
            P(EVERY),
            P("pen", ("grp", "mig")),
            P("pen", ("grp", "mig")),
        ),
        out_specs=(split, split, P("pen", ("grp", "mig"))),
        check_vma=False,
    )
```

```python
import functools

import jax
import jax.numpy as jnp
import numpy as np
from jax import lax
from jax.experimental import pallas as pl
from jax.experimental.pallas import tpu as pltpu
from jax.sharding import PartitionSpec as P

TE = 16
TZ = 2
TCOL = 16
FACE = TE * TE
CELLS = TE**3
LANES = 128
ROWS = CELLS // LANES

viscous = 0.05
step_size = 0.25
thicken = 5.0

SCALE = 4096.0
PLANES = 4

EVERY = ("grp", "mig", "pen")
TEAM = ("pen", "mig")


def passed_along(x, axis, by):
    peers = lax.axis_size(axis)
    return lax.ppermute(x, axis, [(i, (i + by) % peers) for i in range(peers)])


def banded(brick_rows, reach):
    sigma = reach / 2.0
    offsets = np.arange(-reach, reach + 1, dtype=np.float64)
    total = np.sum(np.exp(-offsets * offsets / (2.0 * sigma * sigma)))
    row = np.arange(brick_rows)[:, None]
    col = np.arange(brick_rows + 2 * reach)[None, :]
    offset = (col - reach - row).astype(np.float64)
    weights = np.where(np.abs(offset) <= reach, np.exp(-offset * offset / (2.0 * sigma * sigma)), 0)
    return (weights / total).astype(np.float32)


def raw_kernel(flags_ref, sensor_ref, raw_ref):
    for r in range(TZ):
        for k in range(TCOL):
            rows, cols = slice(r * TE, (r + 1) * TE), slice(k * FACE, (k + 1) * FACE)
            flag = flags_ref[r, k].astype(jnp.float32)
            raw_ref[rows, cols] = (sensor_ref[rows, cols] * flag).astype(jnp.bfloat16)


def filter_kernel(flags_ref, weights_ref, sensor_ref, below_ref, above_ref, notes_ref, filtered_ref, row_ref):
    lane = lax.broadcasted_iota(jnp.int32, (1, LANES), 1)
    row = notes_ref[...]
    brick = sensor_ref.shape[0]
    for k in range(TCOL):
        cols = slice(k * FACE, (k + 1) * FACE)
        own = [
            sensor_ref[r * TE : (r + 1) * TE, cols] * flags_ref[r, k].astype(jnp.float32)
            for r in range(TZ)
        ]
        widened = jnp.concatenate(
            [below_ref[:, cols].astype(jnp.float32)] + own + [above_ref[:, cols].astype(jnp.float32)],
            axis=0,
        )
        filtered = jnp.dot(
            weights_ref[...],
            widened,
            precision=lax.Precision.HIGHEST,
            preferred_element_type=jnp.float32,
        )
        filtered_ref[:, cols] = filtered
        clipped = jnp.minimum(filtered, 1.0)
        for r in range(TZ):
            total = jnp.sum(
                jnp.sum(clipped[r * TE : (r + 1) * TE], axis=0, keepdims=True), axis=1, keepdims=True
            )
            thick = 1.0 + (thicken - 1.0) * (total / float(TE * FACE))
            row = jnp.where(lane == r * TCOL + k, thick, row)
    row_ref[...] = row


def send_kernel(
    migs, me_ref, destination_ref, recent_hbm, older_hbm, out_hbm, recent_ref, older_ref, out_ref, got, sent
):
    species, slots, _ = recent_ref.shape
    peers = out_ref.shape[0]

    def fetches(s):
        return (
            pltpu.make_async_copy(recent_hbm.at[s], recent_ref.at[s], got.at[0, s]),
            pltpu.make_async_copy(older_hbm.at[s], older_ref.at[s], got.at[1, s]),
        )

    def store(s):
        part = pl.ds(s * ROWS, ROWS)
        return pltpu.make_async_copy(out_ref.at[:, part], out_hbm.at[:, part], sent.at[s])

    for s in range(species):
        for copy in fetches(s):
            copy.start()
    peer = lax.broadcasted_iota(jnp.int32, (peers, slots), 0)
    named = peer % migs * (peers // migs) + peer // migs
    hot = ((destination_ref[...] == named) & (peer != me_ref[1])).astype(jnp.bfloat16)
    flat = out_ref.reshape(peers * species * ROWS, LANES)
    for s in range(species):
        for copy in fetches(s):
            copy.wait()
        recent = jnp.dot(hot, recent_ref[s], preferred_element_type=jnp.float32)
        older = jnp.dot(hot, older_ref[s], preferred_element_type=jnp.float32)
        mixed = recent * (-16.0 / 12.0 * SCALE) + older * (5.0 / 12.0 * SCALE)
        for k in range(ROWS):
            flat[pl.ds(s * ROWS + k, peers, stride=species * ROWS), :] = mixed[
                :, k * LANES : (k + 1) * LANES
            ]
        store(s).start()
    for s in range(species):
        store(s).wait()


def base_kernel(
    me_ref, rate_ref, moves_ref, fields_ref, recent_ref, older_ref, react_ref, base_ref
):
    species, slots, width = fields_ref.shape
    slot = lax.broadcasted_iota(jnp.int32, (slots, slots), 0)
    keep = ((moves_ref[0:1, :] == me_ref[0]) & (moves_ref[1:2, :] == slot)).astype(jnp.bfloat16)

    def keep_one(s, carry):
        recent = jnp.dot(keep, recent_ref[s], preferred_element_type=jnp.float32)
        older = jnp.dot(keep, older_ref[s], preferred_element_type=jnp.float32)
        kept = recent * (-16.0 / 12.0 * step_size) + older * (5.0 / 12.0 * step_size)
        base_ref[s] = fields_ref[s] + kept
        return carry

    lax.fori_loop(0, species, keep_one, 0)

    def group(g, carry):
        rows = pl.ds(pl.multiple_of(g * 8, 8), 8)
        for lanes in (slice(c * 2 * LANES, (c + 1) * 2 * LANES) for c in range(width // LANES // 2)):
            fuel = [fields_ref[s, rows, lanes] for s in range(species)]
            burning = fuel[0] * fuel[1]
            fuel = [f * burning for f in fuel]
            for s in range(species):
                total = rate_ref[s, 0] * fuel[0]
                for k in range(1, species):
                    total += rate_ref[s, k] * fuel[k]
                react_ref[s, rows, lanes] = total
        return carry

    lax.fori_loop(0, slots // 8, group, 0)


def stencil_kernel(
    speed_ref, fields_ref, before_ref, after_ref, ghosts_ref, laplace_ref, carried_ref
):
    step = pl.program_id(0)
    species, slots, width = fields_ref.shape
    last = pl.num_programs(0) - 1

    lane = lax.broadcasted_iota(jnp.int32, (8, LANES), 1)
    z_index = lane % TE
    low_end, high_end = lane < TE, lane >= LANES - TE
    z_first, z_last = z_index == 0, z_index == TE - 1
    left_half = lane < LANES // 2
    spread = jnp.where(z_last, LANES // 2, 0) + lane // TE
    block = step * PLANES // 8
    turn = step * PLANES % 8 * TE

    def group(g, carry):
        rows = pl.ds(pl.multiple_of(g * 8, 8), 8)
        speed = [jnp.broadcast_to(speed_ref[rows, d : d + 1] * 0.5, (8, LANES)) for d in range(3)]
        for s in range(species):
            face = [
                ghosts_ref[s, rows, pl.ds(pl.multiple_of(w * FACE + block * LANES, LANES), LANES)]
                for w in range(2, 6)
            ]
            z_ends = jnp.where(
                left_half,
                pltpu.roll(face[2], (LANES - turn) % LANES, 1),
                pltpu.roll(face[3], (LANES + LANES // 2 - turn) % LANES, 1),
            )
            for p in range(PLANES):
                spans = [slice(p * FACE + h * LANES, p * FACE + (h + 1) * LANES) for h in range(2)]
                pair = [fields_ref[s, rows, lanes] for lanes in spans]
                shift = turn + p * TE
                up = [pltpu.roll(v, TE, 1) for v in pair]
                down = [pltpu.roll(v, LANES - TE, 1) for v in pair]
                y_low = [
                    jnp.where(low_end, pltpu.roll(face[0], (LANES - shift) % LANES, 1), up[0]),
                    jnp.where(low_end, up[0], up[1]),
                ]
                y_high = [
                    jnp.where(high_end, down[1], down[0]),
                    jnp.where(
                        high_end, pltpu.roll(face[1], (2 * LANES - TE - shift) % LANES, 1), down[1]
                    ),
                ]
                for h, lanes in enumerate(spans):
                    f = pair[h]
                    ends = jnp.take_along_axis(
                        z_ends, spread + (p * TE + h * (TE // 2)), axis=1, mode="promise_in_bounds"
                    )
                    z_low = jnp.where(z_first, ends, pltpu.roll(f, 1, 1))
                    z_high = jnp.where(z_last, ends, pltpu.roll(f, LANES - 1, 1))
                    near = slice(h * LANES, (h + 1) * LANES)
                    far = slice(FACE + h * LANES, FACE + (h + 1) * LANES)
                    if p > 0:
                        x_low = fields_ref[s, rows, lanes.start - FACE : lanes.stop - FACE]
                    else:
                        x_low = jnp.where(
                            step == 0, ghosts_ref[s, rows, near], before_ref[s, rows, near]
                        )
                    if p < PLANES - 1:
                        x_high = fields_ref[s, rows, lanes.start + FACE : lanes.stop + FACE]
                    else:
                        x_high = jnp.where(
                            step == last, ghosts_ref[s, rows, far], after_ref[s, rows, near]
                        )
                    total = (x_low + x_high) + (y_low[h] + y_high[h]) + (z_low + z_high)
                    laplace_ref[s, rows, lanes] = total - 6.0 * f
                    carried_ref[s, rows, lanes] = (
                        speed[0] * (x_high - x_low)
                        + speed[1] * (y_high[h] - y_low[h])
                        + speed[2] * (z_high - z_low)
                    )
        return carry

    lax.fori_loop(0, slots // 8, group, 0)


def final_kernel(
    me_ref,
    live_ref,
    table_ref,
    tile_ref,
    laplace_hbm,
    carried_hbm,
    react_hbm,
    base_hbm,
    arrived_hbm,
    new_fields_hbm,
    new_tend_hbm,
    parts_ref,
    arrived_ref,
    new_fields_ref,
    new_tend_ref,
    got,
    sent,
):
    species, peers = arrived_ref.shape[:2]
    slots = new_fields_ref.shape[1]
    sources = (laplace_hbm, carried_hbm, react_hbm, base_hbm)

    def fetches(s):
        copies = [
            pltpu.make_async_copy(ref.at[s], parts_ref.at[n, s], got.at[n, s])
            for n, ref in enumerate(sources)
        ]
        part = arrived_hbm.at[:, pl.ds(s * ROWS, ROWS)]
        return copies + [pltpu.make_async_copy(part, arrived_ref.at[s], got.at[4, s])]

    def stores(s):
        return (
            pltpu.make_async_copy(new_fields_ref.at[s], new_fields_hbm.at[s], sent.at[0, s]),
            pltpu.make_async_copy(new_tend_ref.at[s], new_tend_hbm.at[s], sent.at[1, s]),
        )

    for s in range(species):
        for copy in fetches(s):
            copy.start()

    me, first = me_ref[1], pl.multiple_of(me_ref[2] * LANES, LANES)
    notes = table_ref[:, pl.ds(first, LANES)]
    destination = notes[:, slots : 2 * slots]
    target = notes[:, 2 * slots : 3 * slots]
    peer = lax.broadcasted_iota(jnp.int32, (peers, slots), 0)
    mine = (destination == me_ref[0].astype(jnp.float32)) & (peer != me)
    slot = jnp.max(jnp.where(mine, target, -1.0), axis=1, keepdims=True)
    index = lax.broadcasted_iota(jnp.int32, (peers, slots), 1)
    hot = (slot == index.astype(jnp.float32)) & (index < live_ref[0])
    hot = jnp.where(hot, step_size / SCALE, 0.0)
    hot = jnp.concatenate([hot, hot], axis=0).T.astype(jnp.bfloat16)
    wanted = lax.broadcasted_iota(jnp.int32, (slots, peers), 1) == tile_ref[:, 0:1]
    picked = jnp.dot(
        wanted.astype(jnp.float32),
        table_ref[...],
        precision=lax.Precision.HIGHEST,
        preferred_element_type=jnp.float32,
    )
    lane = lax.broadcasted_iota(jnp.int32, picked.shape, 1)
    thick = jnp.sum(jnp.where(lane == tile_ref[:, 1:2], picked, 0.0), axis=1, keepdims=True)
    live = lax.broadcasted_iota(jnp.int32, (slots, 1), 0) < live_ref[0]
    smooth, over, live = (
        jnp.broadcast_to(part, (slots, LANES))
        for part in (viscous * thick, 1.0 / thick, jnp.where(live, 1.0, 0.0))
    )

    for s in range(species):
        for copy in fetches(s):
            copy.wait()
        flat = arrived_ref.at[s].reshape(peers * ROWS, LANES)
        for c in range(ROWS // 2):
            lanes = slice(c * 2 * LANES, (c + 1) * 2 * LANES)
            arrived = jnp.concatenate(
                [flat[pl.ds(2 * c + k, peers, stride=ROWS), :] for k in range(2)], axis=1
            )
            high = arrived.astype(jnp.bfloat16)
            low = (arrived - high.astype(jnp.float32)).astype(jnp.bfloat16)
            placed = jnp.dot(
                hot, jnp.concatenate([high, low], axis=0), preferred_element_type=jnp.float32
            )
            tends = []
            for k in range(2):
                here = slice((2 * c + k) * LANES, (2 * c + k + 1) * LANES)
                tend = smooth * parts_ref[0, s, :, here] - parts_ref[1, s, :, here]
                tend += over * parts_ref[2, s, :, here]
                new = parts_ref[3, s, :, here] + (step_size * 23.0 / 12.0) * tend
                new_fields_ref[s, :, here] = new * live + placed[:, k * LANES : (k + 1) * LANES]
                tends.append(tend * live)
            new_tend_ref[s, :, lanes] = jnp.concatenate(tends, axis=1).astype(jnp.bfloat16)
        for copy in stores(s):
            copy.start()
    for s in range(species):
        for copy in stores(s):
            copy.wait()


def smem():
    return pl.BlockSpec(memory_space=pltpu.SMEM)


def whole(shape):
    return pl.BlockSpec(shape, lambda i: (0,) * len(shape))


def params(mib, semantics=None):
    return pltpu.CompilerParams(vmem_limit_bytes=mib << 20, dimension_semantics=semantics)


def local(
    fields,
    ghosts,
    velocity,
    rate_matrix,
    recent_tend,
    older_tend,
    destination,
    target_slot,
    live_counts,
    tile_ids,
    sensor,
    flame_flags,
):
    slots, species, cells = fields.shape
    peers = lax.axis_size(TEAM)
    brick = sensor.shape[0]
    me = jnp.stack(
        [lax.axis_index(("mig", "pen")), lax.axis_index(TEAM), lax.axis_index("grp")]
    ).astype(jnp.int32)
    fields, ghosts, recent, older = (
        a.transpose(1, 0, 2) for a in (fields, ghosts, recent_tend, older_tend)
    )
    moves = jnp.stack([destination, target_slot])

    raw = pl.pallas_call(
        raw_kernel,
        name="raw_sensor",
        out_shape=jax.ShapeDtypeStruct(sensor.shape, jnp.bfloat16),
        in_specs=[smem(), pl.BlockSpec(memory_space=pltpu.VMEM)],
        out_specs=pl.BlockSpec(memory_space=pltpu.VMEM),
        compiler_params=params(58),
    )(flame_flags, sensor)
    below = passed_along(raw, "pen", 1)
    above = passed_along(raw, "pen", -1)

    anywhere = pl.BlockSpec(memory_space=pl.ANY)
    vmem = pl.BlockSpec(memory_space=pltpu.VMEM)
    outgoing = pl.pallas_call(
        functools.partial(send_kernel, lax.axis_size("mig")),
        name="outgoing_histories",
        out_shape=jax.ShapeDtypeStruct((peers, species * ROWS, LANES), jnp.float32),
        in_specs=[smem(), vmem, anywhere, anywhere],
        out_specs=anywhere,
        scratch_shapes=[
            pltpu.VMEM(recent.shape, jnp.bfloat16),
            pltpu.VMEM(older.shape, jnp.bfloat16),
            pltpu.VMEM((peers, species * ROWS, LANES), jnp.float32),
            pltpu.SemaphoreType.DMA((2, species)),
            pltpu.SemaphoreType.DMA((species,)),
        ],
        compiler_params=params(58),
        cost_estimate=pl.CostEstimate(flops=0, bytes_accessed=8 << 20, transcendentals=0),
    )(me, destination.reshape(1, slots), recent, older)
    outgoing, below, above = lax.optimization_barrier(
        (outgoing.astype(jnp.float16), below, above)
    )
    arrived = lax.all_to_all(outgoing, TEAM, split_axis=0, concat_axis=0, tiled=True)
    arrived = arrived.astype(jnp.float32)

    notes = jnp.concatenate(
        [jnp.zeros((1, slots), jnp.float32), moves.astype(jnp.float32).reshape(1, 2 * slots)], axis=1
    )
    notes = jnp.pad(notes, ((0, 0), (0, LANES - 3 * slots)))
    filtered, row = pl.pallas_call(
        filter_kernel,
        name="filtered_sensor",
        out_shape=(
            jax.ShapeDtypeStruct(sensor.shape, jnp.float32),
            jax.ShapeDtypeStruct((1, LANES), jnp.float32),
        ),
        in_specs=[smem()] + [vmem] * 5,
        out_specs=(vmem, vmem),
        compiler_params=params(32),
        cost_estimate=pl.CostEstimate(flops=0, bytes_accessed=4 << 20, transcendentals=0),
    )(flame_flags, jnp.asarray(banded(brick, brick)), sensor, below, above, notes)
    owner, lane = tile_ids // slots, tile_ids % slots
    pens, migs = lax.axis_size("pen"), lax.axis_size("mig")
    tile_place = jnp.stack(
        [owner % pens * migs + owner // pens % migs, owner // peers * LANES + lane], axis=1
    )
    speed = jnp.pad(velocity.T, ((0, 0), (0, 5)))
    width = PLANES * FACE
    moving = pl.BlockSpec((species, slots, width), lambda i: (0, 0, i))
    shape = jax.ShapeDtypeStruct((species, slots, cells), jnp.float32)
    row, speed, rates = lax.optimization_barrier((row, speed, rate_matrix))
    table = gathered(row)
    react, base = pl.pallas_call(
        base_kernel,
        name="reaction_and_base",
        grid=(cells // width,),
        out_shape=(shape,) * 2,
        in_specs=[smem(), smem(), whole((2, slots)), moving, moving, moving],
        out_specs=(moving,) * 2,
        compiler_params=params(58, ("arbitrary",)),
        cost_estimate=pl.CostEstimate(flops=0, bytes_accessed=30 << 20, transcendentals=0),
    )(me, rates, moves, fields, recent, older)
    laplace, carried = pl.pallas_call(
        stencil_kernel,
        name="neighbour_sums",
        grid=(cells // width,),
        out_shape=(shape,) * 2,
        in_specs=[
            whole((slots, 8)),
            moving,
            pl.BlockSpec((species, slots, FACE), lambda i: (0, 0, jnp.maximum(i * PLANES - 1, 0))),
            pl.BlockSpec(
                (species, slots, FACE), lambda i: (0, 0, jnp.minimum((i + 1) * PLANES, TE - 1))
            ),
            whole(ghosts.shape),
        ],
        out_specs=(moving,) * 2,
        compiler_params=params(58, ("arbitrary",)),
        cost_estimate=pl.CostEstimate(flops=0, bytes_accessed=40 << 20, transcendentals=0),
    )(speed, fields, fields, fields, ghosts)

    new_fields, new_tend = pl.pallas_call(
        final_kernel,
        name="updates",
        out_shape=(shape, jax.ShapeDtypeStruct(shape.shape, jnp.bfloat16)),
        in_specs=[smem(), smem(), vmem, vmem] + [anywhere] * 5,
        out_specs=(anywhere, anywhere),
        scratch_shapes=[
            pltpu.VMEM((4,) + shape.shape, jnp.float32),
            pltpu.VMEM((species, peers, ROWS, LANES), jnp.float32),
            pltpu.VMEM(shape.shape, jnp.float32),
            pltpu.VMEM(shape.shape, jnp.bfloat16),
            pltpu.SemaphoreType.DMA((5, species)),
            pltpu.SemaphoreType.DMA((2, species)),
        ],
        compiler_params=params(58),
        cost_estimate=pl.CostEstimate(flops=0, bytes_accessed=28 << 20, transcendentals=0),
    )(me, live_counts, table, tile_place, laplace, carried, react, base, arrived)
    return new_fields.transpose(1, 0, 2), new_tend.transpose(1, 0, 2), filtered


def gathered(row):
    for axis in ("grp", "mig", "pen"):
        count = lax.axis_size(axis)
        here = lax.axis_index(axis)
        rows = [row] + [passed_along(row, axis, by) for by in range(1, count)]
        height, width = row.shape
        if axis == "grp":
            table = jnp.zeros((height, count * width), row.dtype)
        else:
            table = jnp.zeros((count * height, width), row.dtype)
        for by, part in enumerate(rows):
            place = (here - by) % count
            place = (0, place * width) if axis == "grp" else (place * height, 0)
            table = lax.dynamic_update_slice(table, part, place)
        row = table
    return row


def solution(mesh):
    split = P(EVERY, None, None)
    return jax.shard_map(
        local,
        mesh=mesh,
        in_specs=(
            split,
            split,
            P(None, EVERY),
            P(),
            split,
            split,
            P(EVERY),
            P(EVERY),
            P(EVERY),
            P(EVERY),
            P("pen", ("grp", "mig")),
            P("pen", ("grp", "mig")),
        ),
        out_specs=(split, split, P("pen", ("grp", "mig"))),
        check_vma=False,
    )
```

```python
import functools

import jax
import jax.numpy as jnp
import numpy as np
from jax import lax
from jax.experimental import pallas as pl
from jax.experimental.pallas import tpu as pltpu
from jax.sharding import PartitionSpec as P

TE = 16
TZ = 2
TCOL = 16
FACE = TE * TE
CELLS = TE**3
LANES = 128
ROWS = CELLS // LANES

viscous = 0.05
step_size = 0.25
thicken = 5.0

SCALE = 4096.0
PLANES = 4

EVERY = ("grp", "mig", "pen")
TEAM = ("pen", "mig")


def passed_along(x, axis, by):
    peers = lax.axis_size(axis)
    return lax.ppermute(x, axis, [(i, (i + by) % peers) for i in range(peers)])


def banded(brick_rows, reach):
    sigma = reach / 2.0
    offsets = np.arange(-reach, reach + 1, dtype=np.float64)
    total = np.sum(np.exp(-offsets * offsets / (2.0 * sigma * sigma)))
    row = np.arange(brick_rows)[:, None]
    col = np.arange(brick_rows + 2 * reach)[None, :]
    offset = (col - reach - row).astype(np.float64)
    weights = np.where(np.abs(offset) <= reach, np.exp(-offset * offset / (2.0 * sigma * sigma)), 0)
    return (weights / total).astype(np.float32)


def raw_kernel(flags_ref, sensor_ref, raw_ref):
    for r in range(TZ):
        for k in range(TCOL):
            rows, cols = slice(r * TE, (r + 1) * TE), slice(k * FACE, (k + 1) * FACE)
            flag = flags_ref[r, k].astype(jnp.float32)
            raw_ref[rows, cols] = (sensor_ref[rows, cols] * flag).astype(jnp.bfloat16)


def filter_kernel(flags_ref, weights_ref, sensor_ref, below_ref, above_ref, notes_ref, filtered_ref, row_ref):
    lane = lax.broadcasted_iota(jnp.int32, (1, LANES), 1)
    row = notes_ref[...]
    brick = sensor_ref.shape[0]
    for k in range(TCOL):
        cols = slice(k * FACE, (k + 1) * FACE)
        own = [
            sensor_ref[r * TE : (r + 1) * TE, cols] * flags_ref[r, k].astype(jnp.float32)
            for r in range(TZ)
        ]
        widened = jnp.concatenate(
            [below_ref[:, cols].astype(jnp.float32)] + own + [above_ref[:, cols].astype(jnp.float32)],
            axis=0,
        )
        filtered = jnp.dot(
            weights_ref[...],
            widened,
            precision=lax.Precision.HIGHEST,
            preferred_element_type=jnp.float32,
        )
        filtered_ref[:, cols] = filtered
        clipped = jnp.minimum(filtered, 1.0)
        for r in range(TZ):
            total = jnp.sum(
                jnp.sum(clipped[r * TE : (r + 1) * TE], axis=0, keepdims=True), axis=1, keepdims=True
            )
            thick = 1.0 + (thicken - 1.0) * (total / float(TE * FACE))
            row = jnp.where(lane == r * TCOL + k, thick, row)
    row_ref[...] = row


def send_kernel(
    migs, me_ref, destination_ref, recent_hbm, older_hbm, out_hbm, recent_ref, older_ref, out_ref, got, sent
):
    species, slots, _ = recent_ref.shape
    peers = out_ref.shape[0]

    def fetches(s):
        return (
            pltpu.make_async_copy(recent_hbm.at[s], recent_ref.at[s], got.at[0, s]),
            pltpu.make_async_copy(older_hbm.at[s], older_ref.at[s], got.at[1, s]),
        )

    def store(s):
        part = pl.ds(s * ROWS, ROWS)
        return pltpu.make_async_copy(out_ref.at[:, part], out_hbm.at[:, part], sent.at[s])

    for s in range(species):
        for copy in fetches(s):
            copy.start()
    peer = lax.broadcasted_iota(jnp.int32, (peers, slots), 0)
    named = peer % migs * (peers // migs) + peer // migs
    hot = ((destination_ref[...] == named) & (peer != me_ref[1])).astype(jnp.bfloat16)
    flat = out_ref.reshape(peers * species * ROWS, LANES)
    for s in range(species):
        for copy in fetches(s):
            copy.wait()
        recent = jnp.dot(hot, recent_ref[s], preferred_element_type=jnp.float32)
        older = jnp.dot(hot, older_ref[s], preferred_element_type=jnp.float32)
        mixed = recent * (-16.0 / 12.0 * SCALE) + older * (5.0 / 12.0 * SCALE)
        for k in range(ROWS):
            flat[pl.ds(s * ROWS + k, peers, stride=species * ROWS), :] = mixed[
                :, k * LANES : (k + 1) * LANES
            ]
        store(s).start()
    for s in range(species):
        store(s).wait()


def prepare_kernel(
    me_ref, live_ref, moves_ref, fields_ref, recent_ref, older_ref, ghosts_ref, base_ref, rims_ref
):
    slots = fields_ref.shape[1]
    slot = lax.broadcasted_iota(jnp.int32, (slots, slots), 0)
    keep = (moves_ref[0:1, :] == me_ref[0]) & (moves_ref[1:2, :] == slot)
    keep = keep.astype(jnp.bfloat16)
    live = lax.broadcasted_iota(jnp.int32, (slots, 1), 0) < live_ref[0]
    recent = jnp.dot(keep, recent_ref[0], preferred_element_type=jnp.float32)
    older = jnp.dot(keep, older_ref[0], preferred_element_type=jnp.float32)
    kept = recent * (-16.0 / 12.0 * step_size) + older * (5.0 / 12.0 * step_size)
    base_ref[0] = (fields_ref[0] + kept) * jnp.where(live, 1.0, 0.0)

    quarter = lax.broadcasted_iota(jnp.int32, (slots, LANES), 1) // (2 * TE)
    for block in range(2):
        faces = [
            ghosts_ref[0, :, w * FACE + block * LANES : w * FACE + (block + 1) * LANES]
            for w in (4, 5, 2, 3)
        ]
        for q in range(4):
            rim = faces[0]
            for n in range(4):
                turned = pltpu.roll(faces[n], (n - q) % 4 * 2 * TE, 1) if n != q else faces[n]
                rim = turned if n == 0 else jnp.where(quarter == n, turned, rim)
            high = rim.astype(jnp.bfloat16)
            low = (rim - high.astype(jnp.float32)).astype(jnp.bfloat16)
            start = (block * 4 + q) * 2 * LANES
            rims_ref[0, :, start : start + LANES] = high
            rims_ref[0, :, start + LANES : start + 2 * LANES] = low


def plane_weights():
    weights = np.zeros((2, 6 * LANES, 3 * FACE), np.float32)
    for cell in range(FACE):
        y, z = divmod(cell, TE)
        for d, at, step in ((0, y, TE), (1, z, 1)):
            for way in (-1, 1):
                if 0 <= at + way < TE:
                    rows = [[cell + way * step, FACE + cell + way * step]] * 2
                else:
                    face = (2 + (way > 0)) if d == 0 else (way > 0)
                    spot = z if d == 0 else y
                    spot = [2 * FACE + face * 2 * TE + odd * TE + spot for odd in range(2)]
                    rows = [[spot[odd], spot[odd] + LANES] for odd in range(2)]
                for odd in range(2):
                    weights[odd, rows[odd], cell] += 1.0
                    weights[odd, rows[odd], (1 + d) * FACE + cell] += way
        weights[:, [cell, FACE + cell], cell] -= 6.0
    return weights


def main_kernel(
    me_ref,
    live_ref,
    rate_ref,
    table_ref,
    tile_ref,
    speed_ref,
    weights_hbm,
    fields_hbm,
    ghosts_hbm,
    rims_hbm,
    base_hbm,
    arrived_hbm,
    new_fields_hbm,
    new_tend_hbm,
    weights_ref,
    fields_ref,
    rims_ref,
    base_ref,
    arrived_ref,
    new_fields_ref,
    new_tend_ref,
    rates_ref,
    wide_ref,
    left_even_ref,
    left_odd_ref,
    sums_even_ref,
    sums_odd_ref,
    got,
    sent,
):
    species, slots, cells = new_fields_ref.shape
    peers = arrived_ref.shape[0]
    chunk = PLANES * FACE
    chunks = cells // chunk

    def span(c, length, skipped=0):
        return pl.ds(pl.multiple_of(skipped + c * length, min(length, LANES)), length)

    def arrivals(c):
        rows = span(c, chunk // LANES)
        return pltpu.make_async_copy(
            arrived_hbm.at[:, :, rows], arrived_ref.at[:, :, rows], got.at[3, c]
        )

    def others(c):
        lanes = span(c, chunk)
        return pltpu.make_async_copy(
            base_hbm.at[:, :, lanes], base_ref.at[:, :, lanes], got.at[2, c]
        )

    def cells_in(c):
        lanes, rims = span(c, chunk), span(c, chunk // 2)
        inner = span(c, chunk, FACE)
        return (
            pltpu.make_async_copy(
                fields_hbm.at[:, :, lanes], fields_ref.at[:, :, inner], got.at[0, c]
            ),
            pltpu.make_async_copy(
                rims_hbm.at[:, :, rims], rims_ref.at[:, :, rims], got.at[1, c]
            ),
        )

    def ends():
        return (
            pltpu.make_async_copy(weights_hbm, weights_ref, got.at[4, 0]),
            pltpu.make_async_copy(
                ghosts_hbm.at[:, :, pl.ds(0, FACE)], fields_ref.at[:, :, pl.ds(0, FACE)], got.at[4, 1]
            ),
            pltpu.make_async_copy(
                ghosts_hbm.at[:, :, pl.ds(FACE, FACE)],
                fields_ref.at[:, :, pl.ds(FACE + cells, FACE)],
                got.at[4, 2],
            ),
        )

    def stores(c):
        lanes = span(c, chunk)
        return (
            pltpu.make_async_copy(
                new_fields_ref.at[:, :, lanes], new_fields_hbm.at[:, :, lanes], sent.at[0, c]
            ),
            pltpu.make_async_copy(
                new_tend_ref.at[:, :, lanes], new_tend_hbm.at[:, :, lanes], sent.at[1, c]
            ),
        )

    def all_in(c):
        return (*cells_in(c), others(c), arrivals(c))

    for copy in ends():
        copy.start()
    for c in range(chunks):
        for copy in all_in(c):
            copy.start()

    me, first = me_ref[1], pl.multiple_of(me_ref[2] * LANES, LANES)
    notes = table_ref[:, pl.ds(first, LANES)]
    destination = notes[:, slots : 2 * slots]
    target = notes[:, 2 * slots : 3 * slots]
    peer = lax.broadcasted_iota(jnp.int32, (peers, slots), 0)
    mine = (destination == me_ref[0].astype(jnp.float32)) & (peer != me)
    slot = jnp.max(jnp.where(mine, target, -1.0), axis=1, keepdims=True)
    index = lax.broadcasted_iota(jnp.int32, (peers, slots), 1)
    hot = (slot == index.astype(jnp.float32)) & (index < live_ref[0])
    hot = jnp.where(hot, step_size / SCALE, 0.0)
    hot = jnp.concatenate([hot, hot], axis=0).T.astype(jnp.bfloat16)
    wanted = lax.broadcasted_iota(jnp.int32, (slots, peers), 1) == tile_ref[:, 0:1]
    picked = jnp.dot(
        wanted.astype(jnp.float32),
        table_ref[...],
        precision=lax.Precision.HIGHEST,
        preferred_element_type=jnp.float32,
    )
    lane = lax.broadcasted_iota(jnp.int32, picked.shape, 1)
    thick = jnp.sum(jnp.where(lane == tile_ref[:, 1:2], picked, 0.0), axis=1, keepdims=True)
    live = lax.broadcasted_iota(jnp.int32, (slots, 1), 0) < live_ref[0]
    live = jnp.where(live, 1.0, 0.0)
    parts = [viscous * thick * live, live / thick]
    parts += [0.5 * live * speed_ref[:, d : d + 1] for d in range(3)]
    for n, part in enumerate(parts):
        wide_ref[n] = jnp.broadcast_to(part, (slots, LANES))
    for s in range(species):
        for k in range(species):
            rates_ref[s * species + k] = jnp.full((8, LANES), rate_ref[s, k], jnp.float32)

    flat = arrived_ref.reshape(peers * species * ROWS, LANES)

    def sums(plane, odd):
        left_ref, sums_ref = ((left_even_ref, sums_even_ref), (left_odd_ref, sums_odd_ref))[odd]
        lanes = pl.ds(pl.multiple_of((plane + 1) * FACE, FACE), FACE)
        rims = pl.ds(pl.multiple_of(plane // 2 * FACE, FACE), FACE)
        for s in range(species):
            rows = slice(s * slots, (s + 1) * slots)
            f = fields_ref[s, :, lanes]
            high = f.astype(jnp.bfloat16)
            left_ref[rows, 0:FACE] = high
            left_ref[rows, FACE : 2 * FACE] = (f - high.astype(jnp.float32)).astype(jnp.bfloat16)
            left_ref[rows, 2 * FACE :] = rims_ref[s, :, rims]
        sums_ref[...] = jnp.dot(
            left_ref[...], weights_ref[odd], preferred_element_type=jnp.float32
        )

    def finish(plane, odd):
        sums_ref = (sums_even_ref, sums_odd_ref)[odd]
        for half in range(2):
            inner = pl.ds(pl.multiple_of(plane * FACE, FACE) + half * LANES, LANES)
            before, here, after = (
                pl.ds(pl.multiple_of((plane + n) * FACE, FACE) + half * LANES, LANES)
                for n in range(3)
            )
            placed = []
            for s in range(species):
                arrived = flat[
                    pl.ds(s * ROWS + plane * 2 + half, peers, stride=species * ROWS), :
                ]
                high = arrived.astype(jnp.bfloat16)
                low = (arrived - high.astype(jnp.float32)).astype(jnp.bfloat16)
                placed.append(
                    jnp.dot(
                        hot, jnp.concatenate([high, low], axis=0), preferred_element_type=jnp.float32
                    )
                )
            for g in range(slots // 16):
                rows = slice(g * 16, (g + 1) * 16)
                smooth, over, vx, vy, vz = (wide_ref[n, rows, :] for n in range(5))
                fuel = [fields_ref[s, rows, here] for s in range(species)]
                burning = fuel[0] * fuel[1] * over
                fuel = [f * burning for f in fuel]
                for s in range(species):
                    react = None
                    for k in range(species):
                        rate = rates_ref[s * species + k]
                        term = jnp.concatenate([rate, rate], axis=0) * fuel[k]
                        react = term if react is None else react + term
                    low, high = fields_ref[s, rows, before], fields_ref[s, rows, after]
                    lines = slice(s * slots + g * 16, s * slots + (g + 1) * 16)
                    total, along_y, along_z = (
                        sums_ref[lines, d * FACE + half * LANES : d * FACE + (half + 1) * LANES]
                        for d in range(3)
                    )
                    tend = smooth * (total + (low + high)) - vx * (high - low)
                    tend = (tend - vy * along_y) + (react - vz * along_z)
                    new = base_ref[s, rows, inner] + (step_size * 23.0 / 12.0) * tend
                    new_fields_ref[s, rows, inner] = new + placed[s][rows]
                    new_tend_ref[s, rows, inner] = tend.astype(jnp.bfloat16)

    for copy in (*ends(), *cells_in(0)):
        copy.wait()
    sums(0, 0)

    def pair(q, carry):
        c = q // 2

        @pl.when(q % 2 == 0)
        def _():
            others(c).wait()
            arrivals(c).wait()

        sums(2 * q + 1, 1)
        finish(2 * q, 0)

        @pl.when((q % 2 == 1) & (c + 1 < chunks))
        def _():
            for copy in cells_in(c + 1):
                copy.wait()

        sums(jnp.minimum(2 * q + 2, 2 * (TE // 2 - 1)), 0)
        finish(2 * q + 1, 1)

        @pl.when(q % 2 == 1)
        def _():
            for copy in stores(c):
                copy.start()

        return carry

    lax.fori_loop(0, TE // 2, pair, 0)
    for c in range(chunks):
        for copy in stores(c):
            copy.wait()


def smem():
    return pl.BlockSpec(memory_space=pltpu.SMEM)


def whole(shape):
    return pl.BlockSpec(shape, lambda i: (0,) * len(shape))


def params(mib, semantics=None):
    return pltpu.CompilerParams(vmem_limit_bytes=mib << 20, dimension_semantics=semantics)


def local(
    fields,
    ghosts,
    velocity,
    rate_matrix,
    recent_tend,
    older_tend,
    destination,
    target_slot,
    live_counts,
    tile_ids,
    sensor,
    flame_flags,
):
    slots, species, cells = fields.shape
    peers = lax.axis_size(TEAM)
    brick = sensor.shape[0]
    me = jnp.stack(
        [lax.axis_index(("mig", "pen")), lax.axis_index(TEAM), lax.axis_index("grp")]
    ).astype(jnp.int32)
    fields, ghosts, recent, older = (
        a.transpose(1, 0, 2) for a in (fields, ghosts, recent_tend, older_tend)
    )
    moves = jnp.stack([destination, target_slot])

    raw = pl.pallas_call(
        raw_kernel,
        name="raw_sensor",
        out_shape=jax.ShapeDtypeStruct(sensor.shape, jnp.bfloat16),
        in_specs=[smem(), pl.BlockSpec(memory_space=pltpu.VMEM)],
        out_specs=pl.BlockSpec(memory_space=pltpu.VMEM),
        compiler_params=params(58),
    )(flame_flags, sensor)
    below = passed_along(raw, "pen", 1)
    above = passed_along(raw, "pen", -1)

    anywhere = pl.BlockSpec(memory_space=pl.ANY)
    vmem = pl.BlockSpec(memory_space=pltpu.VMEM)
    outgoing = pl.pallas_call(
        functools.partial(send_kernel, lax.axis_size("mig")),
        name="outgoing_histories",
        out_shape=jax.ShapeDtypeStruct((peers, species * ROWS, LANES), jnp.float32),
        in_specs=[smem(), vmem, anywhere, anywhere],
        out_specs=anywhere,
        scratch_shapes=[
            pltpu.VMEM(recent.shape, jnp.bfloat16),
            pltpu.VMEM(older.shape, jnp.bfloat16),
            pltpu.VMEM((peers, species * ROWS, LANES), jnp.float32),
            pltpu.SemaphoreType.DMA((2, species)),
            pltpu.SemaphoreType.DMA((species,)),
        ],
        compiler_params=params(58),
        cost_estimate=pl.CostEstimate(flops=0, bytes_accessed=8 << 20, transcendentals=0),
    )(me, destination.reshape(1, slots), recent, older)
    arrived = lax.all_to_all(
        outgoing.astype(jnp.float16), TEAM, split_axis=0, concat_axis=0, tiled=True
    )
    arrived = arrived.astype(jnp.float32).reshape(peers, species, ROWS, LANES)

    notes = jnp.concatenate(
        [jnp.zeros((1, slots), jnp.float32), moves.astype(jnp.float32).reshape(1, 2 * slots)], axis=1
    )
    notes = jnp.pad(notes, ((0, 0), (0, LANES - 3 * slots)))
    filtered, row = pl.pallas_call(
        filter_kernel,
        name="filtered_sensor",
        out_shape=(
            jax.ShapeDtypeStruct(sensor.shape, jnp.float32),
            jax.ShapeDtypeStruct((1, LANES), jnp.float32),
        ),
        in_specs=[smem()] + [vmem] * 5,
        out_specs=(vmem, vmem),
        compiler_params=params(32),
        cost_estimate=pl.CostEstimate(flops=0, bytes_accessed=4 << 20, transcendentals=0),
    )(flame_flags, jnp.asarray(banded(brick, brick)), sensor, below, above, notes)
    owner, lane = tile_ids // slots, tile_ids % slots
    pens, migs = lax.axis_size("pen"), lax.axis_size("mig")
    tile_place = jnp.stack(
        [owner % pens * migs + owner // pens % migs, owner // peers * LANES + lane], axis=1
    )
    speed = jnp.pad(velocity.T, ((0, 0), (0, 5)))
    shape = jax.ShapeDtypeStruct((species, slots, cells), jnp.float32)
    each = pl.BlockSpec((1, slots, cells), lambda i: (i, 0, 0))
    rims = (species, slots, TE * LANES)
    row, early = lax.optimization_barrier((row, moves))
    table = gathered(row)
    base, rims = pl.pallas_call(
        prepare_kernel,
        name="base_and_rims",
        grid=(species,),
        out_shape=(shape, jax.ShapeDtypeStruct(rims, jnp.bfloat16)),
        in_specs=[
            smem(),
            smem(),
            whole((2, slots)),
            each,
            each,
            each,
            pl.BlockSpec((1, slots, ghosts.shape[2]), lambda i: (i, 0, 0)),
        ],
        out_specs=(each, pl.BlockSpec((1, slots, rims[2]), lambda i: (i, 0, 0))),
        compiler_params=params(58, ("arbitrary",)),
        cost_estimate=pl.CostEstimate(flops=0, bytes_accessed=30 << 20, transcendentals=0),
    )(me, live_counts, early, fields, recent, older, ghosts)

    weights = jnp.asarray(plane_weights(), jnp.bfloat16)
    left = pltpu.VMEM((species * slots, 6 * LANES), jnp.bfloat16)
    sums = pltpu.VMEM((species * slots, 3 * FACE), jnp.float32)
    new_fields, new_tend = pl.pallas_call(
        main_kernel,
        name="updates",
        out_shape=(shape, jax.ShapeDtypeStruct(shape.shape, jnp.bfloat16)),
        in_specs=[smem()] * 3 + [vmem] * 3 + [anywhere] * 6,
        out_specs=(anywhere, anywhere),
        scratch_shapes=[
            pltpu.VMEM(weights.shape, jnp.bfloat16),
            pltpu.VMEM((species, slots, cells + 2 * FACE), jnp.float32),
            pltpu.VMEM(rims.shape, jnp.bfloat16),
            pltpu.VMEM(shape.shape, jnp.float32),
            pltpu.VMEM(arrived.shape, jnp.float32),
            pltpu.VMEM(shape.shape, jnp.float32),
            pltpu.VMEM(shape.shape, jnp.bfloat16),
            pltpu.VMEM((species * species, 8, LANES), jnp.float32),
            pltpu.VMEM((5, slots, LANES), jnp.float32),
            left,
            left,
            sums,
            sums,
            pltpu.SemaphoreType.DMA((5, TE // PLANES)),
            pltpu.SemaphoreType.DMA((2, TE // PLANES)),
        ],
        compiler_params=params(58),
        cost_estimate=pl.CostEstimate(flops=0, bytes_accessed=28 << 20, transcendentals=0),
    )(
        me,
        live_counts,
        rate_matrix,
        table,
        tile_place,
        speed,
        weights,
        fields,
        ghosts,
        rims,
        base,
        arrived,
    )
    return new_fields.transpose(1, 0, 2), new_tend.transpose(1, 0, 2), filtered


def gathered(row):
    for axis in ("grp", "mig", "pen"):
        count = lax.axis_size(axis)
        here = lax.axis_index(axis)
        rows = [row] + [passed_along(row, axis, by) for by in range(1, count)]
        height, width = row.shape
        if axis == "grp":
            table = jnp.zeros((height, count * width), row.dtype)
        else:
            table = jnp.zeros((count * height, width), row.dtype)
        for by, part in enumerate(rows):
            place = (here - by) % count
            place = (0, place * width) if axis == "grp" else (place * height, 0)
            table = lax.dynamic_update_slice(table, part, place)
        row = table
    return row


def solution(mesh):
    split = P(EVERY, None, None)
    return jax.shard_map(
        local,
        mesh=mesh,
        in_specs=(
            split,
            split,
            P(None, EVERY),
            P(),
            split,
            split,
            P(EVERY),
            P(EVERY),
            P(EVERY),
            P(EVERY),
            P("pen", ("grp", "mig")),
            P("pen", ("grp", "mig")),
        ),
        out_specs=(split, split, P("pen", ("grp", "mig"))),
        check_vma=False,
    )
```

```python
import functools

import jax
import jax.numpy as jnp
import numpy as np
from jax import lax
from jax.experimental import pallas as pl
from jax.experimental.pallas import tpu as pltpu
from jax.sharding import PartitionSpec as P

TE = 16
TZ = 2
TCOL = 16
FACE = TE * TE
CELLS = TE**3
LANES = 128
ROWS = CELLS // LANES

viscous = 0.05
step_size = 0.25
thicken = 5.0

SCALE = 4096.0
PLANES = 4

EVERY = ("grp", "mig", "pen")
TEAM = ("pen", "mig")


def passed_along(x, axis, by):
    peers = lax.axis_size(axis)
    return lax.ppermute(x, axis, [(i, (i + by) % peers) for i in range(peers)])


def banded(brick_rows, reach):
    sigma = reach / 2.0
    offsets = np.arange(-reach, reach + 1, dtype=np.float64)
    total = np.sum(np.exp(-offsets * offsets / (2.0 * sigma * sigma)))
    row = np.arange(brick_rows)[:, None]
    col = np.arange(brick_rows + 2 * reach)[None, :]
    offset = (col - reach - row).astype(np.float64)
    weights = np.where(np.abs(offset) <= reach, np.exp(-offset * offset / (2.0 * sigma * sigma)), 0)
    return (weights / total).astype(np.float32)


def raw_kernel(me_ref, flags_ref, sensor_ref, raw_ref, me_out_ref):
    for n in range(me_ref.shape[0]):
        me_out_ref[n] = me_ref[n]
    for r in range(TZ):
        for k in range(TCOL):
            rows, cols = slice(r * TE, (r + 1) * TE), slice(k * FACE, (k + 1) * FACE)
            flag = flags_ref[r, k].astype(jnp.float32)
            raw_ref[rows, cols] = (sensor_ref[rows, cols] * flag).astype(jnp.bfloat16)


def filter_kernel(flags_ref, weights_ref, sensor_ref, below_ref, above_ref, notes_ref, filtered_ref, row_ref):
    lane = lax.broadcasted_iota(jnp.int32, (1, LANES), 1)
    row = notes_ref[...]
    brick = sensor_ref.shape[0]
    for k in range(TCOL):
        cols = slice(k * FACE, (k + 1) * FACE)
        own = [
            sensor_ref[r * TE : (r + 1) * TE, cols] * flags_ref[r, k].astype(jnp.float32)
            for r in range(TZ)
        ]
        widened = jnp.concatenate(
            [below_ref[:, cols].astype(jnp.float32)] + own + [above_ref[:, cols].astype(jnp.float32)],
            axis=0,
        )
        filtered = jnp.dot(
            weights_ref[...],
            widened,
            precision=lax.Precision.HIGHEST,
            preferred_element_type=jnp.float32,
        )
        filtered_ref[:, cols] = filtered
        clipped = jnp.minimum(filtered, 1.0)
        for r in range(TZ):
            total = jnp.sum(
                jnp.sum(clipped[r * TE : (r + 1) * TE], axis=0, keepdims=True), axis=1, keepdims=True
            )
            thick = 1.0 + (thicken - 1.0) * (total / float(TE * FACE))
            row = jnp.where(lane == r * TCOL + k, thick, row)
    row_ref[...] = row


def send_kernel(
    migs, me_ref, destination_ref, recent_hbm, older_hbm, out_ref, recent_ref, older_ref, got
):
    species, slots, _ = recent_ref.shape
    peers = out_ref.shape[0]

    def fetches(s):
        return (
            pltpu.make_async_copy(recent_hbm.at[s], recent_ref.at[s], got.at[0, s]),
            pltpu.make_async_copy(older_hbm.at[s], older_ref.at[s], got.at[1, s]),
        )

    for s in range(species):
        for copy in fetches(s):
            copy.start()
    peer = lax.broadcasted_iota(jnp.int32, (peers, slots), 0)
    named = peer % migs * (peers // migs) + peer // migs
    hot = ((destination_ref[...] == named) & (peer != me_ref[1])).astype(jnp.bfloat16)
    flat = out_ref.reshape(peers * species * ROWS, LANES)
    for s in range(species):
        for copy in fetches(s):
            copy.wait()
        recent = jnp.dot(hot, recent_ref[s], preferred_element_type=jnp.float32)
        older = jnp.dot(hot, older_ref[s], preferred_element_type=jnp.float32)
        mixed = recent * (-16.0 / 12.0 * SCALE) + older * (5.0 / 12.0 * SCALE)
        for k in range(ROWS):
            flat[pl.ds(s * ROWS + k, peers, stride=species * ROWS), :] = mixed[
                :, k * LANES : (k + 1) * LANES
            ]


def prepare_kernel(
    me_ref, live_ref, moves_ref, fields_ref, recent_ref, older_ref, ghosts_ref, base_ref, rims_ref
):
    slots = fields_ref.shape[1]
    slot = lax.broadcasted_iota(jnp.int32, (slots, slots), 0)
    keep = (moves_ref[0:1, :] == me_ref[0]) & (moves_ref[1:2, :] == slot)
    keep = keep.astype(jnp.bfloat16)
    live = lax.broadcasted_iota(jnp.int32, (slots, 1), 0) < live_ref[0]
    recent = jnp.dot(keep, recent_ref[0], preferred_element_type=jnp.float32)
    older = jnp.dot(keep, older_ref[0], preferred_element_type=jnp.float32)
    kept = recent * (-16.0 / 12.0 * step_size) + older * (5.0 / 12.0 * step_size)
    base_ref[0] = (fields_ref[0] + kept) * jnp.where(live, 1.0, 0.0)

    quarter = lax.broadcasted_iota(jnp.int32, (slots, LANES), 1) // (2 * TE)
    for block in range(2):
        faces = [
            ghosts_ref[0, :, w * FACE + block * LANES : w * FACE + (block + 1) * LANES]
            for w in (4, 5, 2, 3)
        ]
        for q in range(4):
            rim = faces[0]
            for n in range(4):
                turned = pltpu.roll(faces[n], (n - q) % 4 * 2 * TE, 1) if n != q else faces[n]
                rim = turned if n == 0 else jnp.where(quarter == n, turned, rim)
            high = rim.astype(jnp.bfloat16)
            low = (rim - high.astype(jnp.float32)).astype(jnp.bfloat16)
            start = (block * 4 + q) * 2 * LANES
            rims_ref[0, :, start : start + LANES] = high
            rims_ref[0, :, start + LANES : start + 2 * LANES] = low


def plane_weights():
    weights = np.zeros((2, 6 * LANES, 3 * FACE), np.float32)
    for cell in range(FACE):
        y, z = divmod(cell, TE)
        for d, at, step in ((0, y, TE), (1, z, 1)):
            for way in (-1, 1):
                if 0 <= at + way < TE:
                    rows = [[cell + way * step, FACE + cell + way * step]] * 2
                else:
                    face = (2 + (way > 0)) if d == 0 else (way > 0)
                    spot = z if d == 0 else y
                    spot = [2 * FACE + face * 2 * TE + odd * TE + spot for odd in range(2)]
                    rows = [[spot[odd], spot[odd] + LANES] for odd in range(2)]
                for odd in range(2):
                    weights[odd, rows[odd], cell] += 1.0
                    weights[odd, rows[odd], (1 + d) * FACE + cell] += way
        weights[:, [cell, FACE + cell], cell] -= 6.0
    return weights


def main_kernel(
    me_ref,
    live_ref,
    rate_ref,
    table_ref,
    tile_ref,
    speed_ref,
    weights_hbm,
    fields_hbm,
    ghosts_hbm,
    rims_hbm,
    base_hbm,
    arrived_hbm,
    new_fields_hbm,
    new_tend_hbm,
    weights_ref,
    fields_ref,
    rims_ref,
    base_ref,
    arrived_ref,
    new_fields_ref,
    new_tend_ref,
    rates_ref,
    wide_ref,
    left_even_ref,
    left_odd_ref,
    sums_even_ref,
    sums_odd_ref,
    got,
    sent,
):
    species, slots, cells = new_fields_ref.shape
    peers = arrived_ref.shape[0]
    chunk = PLANES * FACE
    chunks = cells // chunk

    def span(c, length, skipped=0):
        return pl.ds(pl.multiple_of(skipped + c * length, min(length, LANES)), length)

    def arrivals(c):
        rows = span(c, chunk // LANES)
        return pltpu.make_async_copy(
            arrived_hbm.at[:, :, rows], arrived_ref.at[:, :, rows], got.at[3, c]
        )

    def others(c):
        lanes = span(c, chunk)
        return pltpu.make_async_copy(
            base_hbm.at[:, :, lanes], base_ref.at[:, :, lanes], got.at[2, c]
        )

    def cells_in(c):
        lanes, rims = span(c, chunk), span(c, chunk // 2)
        inner = span(c, chunk, FACE)
        return (
            pltpu.make_async_copy(
                fields_hbm.at[:, :, lanes], fields_ref.at[:, :, inner], got.at[0, c]
            ),
            pltpu.make_async_copy(
                rims_hbm.at[:, :, rims], rims_ref.at[:, :, rims], got.at[1, c]
            ),
        )

    def ends():
        return (
            pltpu.make_async_copy(weights_hbm, weights_ref, got.at[4, 0]),
            pltpu.make_async_copy(
                ghosts_hbm.at[:, :, pl.ds(0, FACE)], fields_ref.at[:, :, pl.ds(0, FACE)], got.at[4, 1]
            ),
            pltpu.make_async_copy(
                ghosts_hbm.at[:, :, pl.ds(FACE, FACE)],
                fields_ref.at[:, :, pl.ds(FACE + cells, FACE)],
                got.at[4, 2],
            ),
        )

    def stores(c):
        lanes = span(c, chunk)
        return (
            pltpu.make_async_copy(
                new_fields_ref.at[:, :, lanes], new_fields_hbm.at[:, :, lanes], sent.at[0, c]
            ),
            pltpu.make_async_copy(
                new_tend_ref.at[:, :, lanes], new_tend_hbm.at[:, :, lanes], sent.at[1, c]
            ),
        )

    def all_in(c):
        return (*cells_in(c), others(c), arrivals(c))

    for copy in ends():
        copy.start()
    for c in range(chunks):
        for copy in all_in(c):
            copy.start()

    me, first = me_ref[1], pl.multiple_of(me_ref[2] * LANES, LANES)
    notes = table_ref[:, pl.ds(first, LANES)]
    destination = notes[:, slots : 2 * slots]
    target = notes[:, 2 * slots : 3 * slots]
    peer = lax.broadcasted_iota(jnp.int32, (peers, slots), 0)
    mine = (destination == me_ref[0].astype(jnp.float32)) & (peer != me)
    slot = jnp.max(jnp.where(mine, target, -1.0), axis=1, keepdims=True)
    index = lax.broadcasted_iota(jnp.int32, (peers, slots), 1)
    hot = (slot == index.astype(jnp.float32)) & (index < live_ref[0])
    hot = jnp.where(hot, step_size / SCALE, 0.0)
    hot = jnp.concatenate([hot, hot], axis=0).T.astype(jnp.bfloat16)
    wanted = lax.broadcasted_iota(jnp.int32, (slots, peers), 1) == tile_ref[:, 0:1]
    picked = jnp.dot(
        wanted.astype(jnp.float32),
        table_ref[...],
        precision=lax.Precision.HIGHEST,
        preferred_element_type=jnp.float32,
    )
    lane = lax.broadcasted_iota(jnp.int32, picked.shape, 1)
    thick = jnp.sum(jnp.where(lane == tile_ref[:, 1:2], picked, 0.0), axis=1, keepdims=True)
    live = lax.broadcasted_iota(jnp.int32, (slots, 1), 0) < live_ref[0]
    live = jnp.where(live, 1.0, 0.0)
    parts = [viscous * thick * live, live / thick]
    parts += [0.5 * live * speed_ref[:, d : d + 1] for d in range(3)]
    for n, part in enumerate(parts):
        wide_ref[n] = jnp.broadcast_to(part, (slots, LANES))
    for s in range(species):
        for k in range(species):
            rates_ref[s * species + k] = jnp.full((8, LANES), rate_ref[s, k], jnp.float32)

    flat = arrived_ref.reshape(peers * species * ROWS, LANES)

    def sums(plane, odd):
        left_ref, sums_ref = ((left_even_ref, sums_even_ref), (left_odd_ref, sums_odd_ref))[odd]
        lanes = pl.ds(pl.multiple_of((plane + 1) * FACE, FACE), FACE)
        rims = pl.ds(pl.multiple_of(plane // 2 * FACE, FACE), FACE)
        for s in range(species):
            rows = slice(s * slots, (s + 1) * slots)
            f = fields_ref[s, :, lanes]
            high = f.astype(jnp.bfloat16)
            left_ref[rows, 0:FACE] = high
            left_ref[rows, FACE : 2 * FACE] = (f - high.astype(jnp.float32)).astype(jnp.bfloat16)
            left_ref[rows, 2 * FACE :] = rims_ref[s, :, rims]
        sums_ref[...] = jnp.dot(
            left_ref[...], weights_ref[odd], preferred_element_type=jnp.float32
        )

    def arrive(plane):
        lanes = pl.ds(pl.multiple_of(plane * FACE, FACE), FACE)
        for s in range(species):
            arrived = jnp.concatenate(
                [
                    flat[pl.ds(s * ROWS + plane * 2 + half, peers, stride=species * ROWS), :]
                    for half in range(2)
                ],
                axis=1,
            )
            high = arrived.astype(jnp.bfloat16)
            low = (arrived - high.astype(jnp.float32)).astype(jnp.bfloat16)
            base_ref[s, :, lanes] += jnp.dot(
                hot, jnp.concatenate([high, low], axis=0), preferred_element_type=jnp.float32
            )

    def finish(plane, odd):
        sums_ref = (sums_even_ref, sums_odd_ref)[odd]
        for half in range(2):
            inner = pl.ds(pl.multiple_of(plane * FACE, FACE) + half * LANES, LANES)
            before, here, after = (
                pl.ds(pl.multiple_of((plane + n) * FACE, FACE) + half * LANES, LANES)
                for n in range(3)
            )
            for g in range(slots // 16):
                rows = slice(g * 16, (g + 1) * 16)
                smooth, over, vx, vy, vz = (wide_ref[n, rows, :] for n in range(5))
                fuel = [fields_ref[s, rows, here] for s in range(species)]
                burning = fuel[0] * fuel[1] * over
                fuel = [f * burning for f in fuel]
                for s in range(species):
                    react = None
                    for k in range(species):
                        rate = rates_ref[s * species + k]
                        term = jnp.concatenate([rate, rate], axis=0) * fuel[k]
                        react = term if react is None else react + term
                    low, high = fields_ref[s, rows, before], fields_ref[s, rows, after]
                    lines = slice(s * slots + g * 16, s * slots + (g + 1) * 16)
                    total, along_y, along_z = (
                        sums_ref[lines, d * FACE + half * LANES : d * FACE + (half + 1) * LANES]
                        for d in range(3)
                    )
                    tend = smooth * (total + (low + high)) - vx * (high - low)
                    tend = (tend - vy * along_y) + (react - vz * along_z)
                    new = base_ref[s, rows, inner] + (step_size * 23.0 / 12.0) * tend
                    new_fields_ref[s, rows, inner] = new
                    new_tend_ref[s, rows, inner] = tend.astype(jnp.bfloat16)

    for copy in (*ends(), *cells_in(0)):
        copy.wait()
    sums(0, 0)

    def pair(q, carry):
        c = q // 2

        @pl.when(q % 2 == 0)
        def _():
            others(c).wait()
            arrivals(c).wait()

        arrive(2 * q)
        arrive(2 * q + 1)
        sums(2 * q + 1, 1)
        finish(2 * q, 0)

        @pl.when((q % 2 == 1) & (c + 1 < chunks))
        def _():
            for copy in cells_in(c + 1):
                copy.wait()

        sums(jnp.minimum(2 * q + 2, 2 * (TE // 2 - 1)), 0)
        finish(2 * q + 1, 1)

        @pl.when(q % 2 == 1)
        def _():
            for copy in stores(c):
                copy.start()

        return carry

    lax.fori_loop(0, TE // 2, pair, 0)
    for c in range(chunks):
        for copy in stores(c):
            copy.wait()


def smem():
    return pl.BlockSpec(memory_space=pltpu.SMEM)


def whole(shape):
    return pl.BlockSpec(shape, lambda i: (0,) * len(shape))


def params(mib, semantics=None):
    return pltpu.CompilerParams(vmem_limit_bytes=mib << 20, dimension_semantics=semantics)


def local(
    fields,
    ghosts,
    velocity,
    rate_matrix,
    recent_tend,
    older_tend,
    destination,
    target_slot,
    live_counts,
    tile_ids,
    sensor,
    flame_flags,
):
    slots, species, cells = fields.shape
    peers = lax.axis_size(TEAM)
    brick = sensor.shape[0]
    me = jnp.stack(
        [lax.axis_index(("mig", "pen")), lax.axis_index(TEAM), lax.axis_index("grp")]
    ).astype(jnp.int32)
    fields, ghosts, recent, older = (
        a.transpose(1, 0, 2) for a in (fields, ghosts, recent_tend, older_tend)
    )
    moves = jnp.stack([destination, target_slot])

    raw, me = pl.pallas_call(
        raw_kernel,
        name="raw_sensor",
        out_shape=(
            jax.ShapeDtypeStruct(sensor.shape, jnp.bfloat16),
            jax.ShapeDtypeStruct(me.shape, jnp.int32),
        ),
        in_specs=[smem(), smem(), pl.BlockSpec(memory_space=pltpu.VMEM)],
        out_specs=(pl.BlockSpec(memory_space=pltpu.VMEM), smem()),
        compiler_params=params(58),
    )(me, flame_flags, sensor)
    below = passed_along(raw, "pen", 1)
    above = passed_along(raw, "pen", -1)

    anywhere = pl.BlockSpec(memory_space=pl.ANY)
    in_hbm = pl.BlockSpec(memory_space=pltpu.HBM)
    vmem = pl.BlockSpec(memory_space=pltpu.VMEM)
    outgoing = pl.pallas_call(
        functools.partial(send_kernel, lax.axis_size("mig")),
        name="outgoing_histories",
        out_shape=jax.ShapeDtypeStruct((peers, species * ROWS, LANES), jnp.float32),
        in_specs=[smem(), vmem, in_hbm, in_hbm],
        out_specs=vmem,
        scratch_shapes=[
            pltpu.VMEM(recent.shape, jnp.bfloat16),
            pltpu.VMEM(older.shape, jnp.bfloat16),
            pltpu.SemaphoreType.DMA((2, species)),
        ],
        compiler_params=params(50),
        cost_estimate=pl.CostEstimate(flops=0, bytes_accessed=8 << 20, transcendentals=0),
    )(me, destination.reshape(1, slots), recent, older)
    arrived = lax.all_to_all(
        outgoing.astype(jnp.float16), TEAM, split_axis=0, concat_axis=0, tiled=True
    )
    arrived = arrived.astype(jnp.float32).reshape(peers, species, ROWS, LANES)

    notes = jnp.concatenate(
        [jnp.zeros((1, slots), jnp.float32), moves.astype(jnp.float32).reshape(1, 2 * slots)], axis=1
    )
    notes = jnp.pad(notes, ((0, 0), (0, LANES - 3 * slots)))
    filtered, row = pl.pallas_call(
        filter_kernel,
        name="filtered_sensor",
        out_shape=(
            jax.ShapeDtypeStruct(sensor.shape, jnp.float32),
            jax.ShapeDtypeStruct((1, LANES), jnp.float32),
        ),
        in_specs=[smem()] + [vmem] * 5,
        out_specs=(vmem, vmem),
        compiler_params=params(32),
        cost_estimate=pl.CostEstimate(flops=0, bytes_accessed=4 << 20, transcendentals=0),
    )(flame_flags, jnp.asarray(banded(brick, brick)), sensor, below, above, notes)
    owner, lane = tile_ids // slots, tile_ids % slots
    pens, migs = lax.axis_size("pen"), lax.axis_size("mig")
    tile_place = jnp.stack(
        [owner % pens * migs + owner // pens % migs, owner // peers * LANES + lane], axis=1
    )
    speed = jnp.pad(velocity.T, ((0, 0), (0, 5)))
    shape = jax.ShapeDtypeStruct((species, slots, cells), jnp.float32)
    each = pl.BlockSpec((1, slots, cells), lambda i: (i, 0, 0))
    rims = (species, slots, TE * LANES)
    row, early = lax.optimization_barrier((row, moves))
    table = gathered(row)
    base, rims = pl.pallas_call(
        prepare_kernel,
        name="base_and_rims",
        grid=(species,),
        out_shape=(shape, jax.ShapeDtypeStruct(rims, jnp.bfloat16)),
        in_specs=[
            smem(),
            smem(),
            whole((2, slots)),
            each,
            each,
            each,
            pl.BlockSpec((1, slots, ghosts.shape[2]), lambda i: (i, 0, 0)),
        ],
        out_specs=(each, pl.BlockSpec((1, slots, rims[2]), lambda i: (i, 0, 0))),
        compiler_params=params(58, ("arbitrary",)),
        cost_estimate=pl.CostEstimate(flops=0, bytes_accessed=30 << 20, transcendentals=0),
    )(me, live_counts, early, fields, recent, older, ghosts)

    weights = jnp.asarray(plane_weights(), jnp.bfloat16)
    left = pltpu.VMEM((species * slots, 6 * LANES), jnp.bfloat16)
    sums = pltpu.VMEM((species * slots, 3 * FACE), jnp.float32)
    new_fields, new_tend = pl.pallas_call(
        main_kernel,
        name="updates",
        out_shape=(shape, jax.ShapeDtypeStruct(shape.shape, jnp.bfloat16)),
        in_specs=[smem()] * 3 + [vmem] * 3 + [anywhere] * 6,
        out_specs=(anywhere, anywhere),
        scratch_shapes=[
            pltpu.VMEM(weights.shape, jnp.bfloat16),
            pltpu.VMEM((species, slots, cells + 2 * FACE), jnp.float32),
            pltpu.VMEM(rims.shape, jnp.bfloat16),
            pltpu.VMEM(shape.shape, jnp.float32),
            pltpu.VMEM(arrived.shape, jnp.float32),
            pltpu.VMEM(shape.shape, jnp.float32),
            pltpu.VMEM(shape.shape, jnp.bfloat16),
            pltpu.VMEM((species * species, 8, LANES), jnp.float32),
            pltpu.VMEM((5, slots, LANES), jnp.float32),
            left,
            left,
            sums,
            sums,
            pltpu.SemaphoreType.DMA((5, TE // PLANES)),
            pltpu.SemaphoreType.DMA((2, TE // PLANES)),
        ],
        compiler_params=params(58),
        cost_estimate=pl.CostEstimate(flops=0, bytes_accessed=28 << 20, transcendentals=0),
    )(
        me,
        live_counts,
        rate_matrix,
        table,
        tile_place,
        speed,
        weights,
        fields,
        ghosts,
        rims,
        base,
        arrived,
    )
    return new_fields.transpose(1, 0, 2), new_tend.transpose(1, 0, 2), filtered


def gathered(row):
    for axis in ("grp", "mig", "pen"):
        count = lax.axis_size(axis)
        here = lax.axis_index(axis)
        rows = [row] + [passed_along(row, axis, by) for by in range(1, count)]
        height, width = row.shape
        if axis == "grp":
            table = jnp.zeros((height, count * width), row.dtype)
        else:
            table = jnp.zeros((count * height, width), row.dtype)
        for by, part in enumerate(rows):
            place = (here - by) % count
            place = (0, place * width) if axis == "grp" else (place * height, 0)
            table = lax.dynamic_update_slice(table, part, place)
        row = table
    return row


def solution(mesh):
    split = P(EVERY, None, None)
    return jax.shard_map(
        local,
        mesh=mesh,
        in_specs=(
            split,
            split,
            P(None, EVERY),
            P(),
            split,
            split,
            P(EVERY),
            P(EVERY),
            P(EVERY),
            P(EVERY),
            P("pen", ("grp", "mig")),
            P("pen", ("grp", "mig")),
        ),
        out_specs=(split, split, P("pen", ("grp", "mig"))),
        check_vma=False,
    )
```

```python
import jax
import jax.numpy as jnp
import numpy as np
from jax import lax
from jax.experimental import pallas as pl
from jax.experimental.pallas import tpu as pltpu
from jax.sharding import PartitionSpec as P

TE = 16
TZ = 2
TCOL = 16
FACE = TE * TE
CELLS = TE**3
LANES = 128
ROWS = CELLS // LANES

viscous = 0.05
step_size = 0.25
thicken = 5.0

SCALE = 4096.0
PLANES = 4

EVERY = ("grp", "mig", "pen")
TEAM = ("mig", "pen")


def passed_along(x, axis, by):
    peers = lax.axis_size(axis)
    return lax.ppermute(x, axis, [(i, (i + by) % peers) for i in range(peers)])


def banded(brick_rows, reach):
    sigma = reach / 2.0
    offsets = np.arange(-reach, reach + 1, dtype=np.float64)
    total = np.sum(np.exp(-offsets * offsets / (2.0 * sigma * sigma)))
    row = np.arange(brick_rows)[:, None]
    col = np.arange(brick_rows + 2 * reach)[None, :]
    offset = (col - reach - row).astype(np.float64)
    weights = np.where(np.abs(offset) <= reach, np.exp(-offset * offset / (2.0 * sigma * sigma)), 0)
    return (weights / total).astype(np.float32)


def raw_kernel(flags_ref, sensor_ref, raw_ref):
    for r in range(TZ):
        for k in range(TCOL):
            rows, cols = slice(r * TE, (r + 1) * TE), slice(k * FACE, (k + 1) * FACE)
            flag = flags_ref[r, k].astype(jnp.float32)
            raw_ref[rows, cols] = (sensor_ref[rows, cols] * flag).astype(jnp.bfloat16)


def filter_kernel(flags_ref, weights_ref, sensor_ref, below_ref, above_ref, notes_ref, filtered_ref, row_ref):
    lane = lax.broadcasted_iota(jnp.int32, (1, LANES), 1)
    row = notes_ref[...]
    brick = sensor_ref.shape[0]
    for k in range(TCOL):
        cols = slice(k * FACE, (k + 1) * FACE)
        own = [
            sensor_ref[r * TE : (r + 1) * TE, cols] * flags_ref[r, k].astype(jnp.float32)
            for r in range(TZ)
        ]
        widened = jnp.concatenate(
            [below_ref[:, cols].astype(jnp.float32)] + own + [above_ref[:, cols].astype(jnp.float32)],
            axis=0,
        )
        filtered = jnp.dot(
            weights_ref[...],
            widened,
            precision=lax.Precision.HIGHEST,
            preferred_element_type=jnp.float32,
        )
        filtered_ref[:, cols] = filtered
        clipped = jnp.minimum(filtered, 1.0)
        for r in range(TZ):
            total = jnp.sum(
                jnp.sum(clipped[r * TE : (r + 1) * TE], axis=0, keepdims=True), axis=1, keepdims=True
            )
            thick = 1.0 + (thicken - 1.0) * (total / float(TE * FACE))
            row = jnp.where(lane == r * TCOL + k, thick, row)
    row_ref[...] = row


def send_kernel(
    me_ref, destination_ref, recent_hbm, older_hbm, out_ref, recent_ref, older_ref, got
):
    species, slots, _ = recent_ref.shape
    peers = out_ref.shape[0]

    def fetches(s):
        return (
            pltpu.make_async_copy(recent_hbm.at[s], recent_ref.at[s], got.at[0, s]),
            pltpu.make_async_copy(older_hbm.at[s], older_ref.at[s], got.at[1, s]),
        )

    for s in range(species):
        for copy in fetches(s):
            copy.start()
    peer = lax.broadcasted_iota(jnp.int32, (peers, slots), 0)
    hot = ((destination_ref[...] == peer) & (peer != me_ref[0])).astype(jnp.bfloat16)
    flat = out_ref.reshape(peers * species * ROWS, LANES)
    for s in range(species):
        for copy in fetches(s):
            copy.wait()
        recent = jnp.dot(hot, recent_ref[s], preferred_element_type=jnp.float32)
        older = jnp.dot(hot, older_ref[s], preferred_element_type=jnp.float32)
        mixed = recent * (-16.0 / 12.0 * SCALE) + older * (5.0 / 12.0 * SCALE)
        for k in range(ROWS):
            flat[pl.ds(s * ROWS + k, peers, stride=species * ROWS), :] = mixed[
                :, k * LANES : (k + 1) * LANES
            ]


def prepare_kernel(
    me_ref,
    live_ref,
    moves_ref,
    fields_hbm,
    recent_hbm,
    older_hbm,
    ghosts_hbm,
    base_hbm,
    rims_hbm,
    fields_ref,
    recent_ref,
    older_ref,
    ghosts_ref,
    rims_ref,
    got,
    sent,
):
    species, slots, _ = fields_ref.shape

    def fetches(s):
        pairs = (
            (fields_hbm, fields_ref),
            (recent_hbm, recent_ref),
            (older_hbm, older_ref),
            (ghosts_hbm, ghosts_ref),
        )
        return [
            pltpu.make_async_copy(here.at[s], there.at[s], got.at[n, s])
            for n, (here, there) in enumerate(pairs)
        ]

    def stores(s):
        return (
            pltpu.make_async_copy(fields_ref.at[s], base_hbm.at[s], sent.at[0, s]),
            pltpu.make_async_copy(rims_ref.at[s], rims_hbm.at[s], sent.at[1, s]),
        )

    for s in range(species):
        for copy in fetches(s):
            copy.start()
    slot = lax.broadcasted_iota(jnp.int32, (slots, slots), 0)
    keep = (moves_ref[0:1, :] == me_ref[0]) & (moves_ref[1:2, :] == slot)
    keep = keep.astype(jnp.bfloat16)
    live = lax.broadcasted_iota(jnp.int32, (slots, 1), 0) < live_ref[0]
    live = jnp.where(live, 1.0, 0.0)
    quarter = lax.broadcasted_iota(jnp.int32, (slots, LANES), 1) // (2 * TE)

    def one(s, carry):
        for copy in fetches(s):
            copy.wait()
        recent = jnp.dot(keep, recent_ref[s], preferred_element_type=jnp.float32)
        older = jnp.dot(keep, older_ref[s], preferred_element_type=jnp.float32)
        kept = recent * (-16.0 / 12.0 * step_size) + older * (5.0 / 12.0 * step_size)
        fields_ref[s] = (fields_ref[s] + kept) * live
        for block in range(2):
            faces = [
                ghosts_ref[s, :, w * FACE + block * LANES : w * FACE + (block + 1) * LANES]
                for w in (4, 5, 2, 3)
            ]
            for q in range(4):
                rim = faces[0]
                for n in range(4):
                    turned = pltpu.roll(faces[n], (n - q) % 4 * 2 * TE, 1) if n != q else faces[n]
                    rim = turned if n == 0 else jnp.where(quarter == n, turned, rim)
                high = rim.astype(jnp.bfloat16)
                low = (rim - high.astype(jnp.float32)).astype(jnp.bfloat16)
                start = (block * 4 + q) * 2 * LANES
                rims_ref[s, :, start : start + LANES] = high
                rims_ref[s, :, start + LANES : start + 2 * LANES] = low
        for copy in stores(s):
            copy.start()
        return carry

    lax.fori_loop(0, species, one, 0)
    for s in range(species):
        for copy in stores(s):
            copy.wait()


def plane_weights():
    weights = np.zeros((6 * LANES, 3 * FACE), np.float32)
    for cell in range(FACE):
        y, z = divmod(cell, TE)
        for d, at, step in ((0, y, TE), (1, z, 1)):
            for way in (-1, 1):
                if 0 <= at + way < TE:
                    rows = [cell + way * step, FACE + cell + way * step]
                else:
                    face = (2 + (way > 0)) if d == 0 else (way > 0)
                    spot = 2 * FACE + face * 2 * TE + (z if d == 0 else y)
                    rows = [spot, spot + TE, spot + LANES, spot + LANES + TE]
                weights[rows, cell] += 1.0
                weights[rows, (1 + d) * FACE + cell] += way
        weights[[cell, FACE + cell], cell] -= 6.0
    return weights


def main_kernel(
    live_ref,
    rate_ref,
    table_ref,
    tile_ref,
    speed_ref,
    weights_hbm,
    fields_hbm,
    ghosts_hbm,
    rims_hbm,
    base_hbm,
    new_fields_hbm,
    new_tend_hbm,
    weights_ref,
    fields_ref,
    rims_ref,
    base_ref,
    new_tend_ref,
    rates_ref,
    wide_ref,
    left_even_ref,
    left_odd_ref,
    sums_even_ref,
    sums_odd_ref,
    got,
    sent,
):
    species, slots, cells = base_ref.shape
    peers = table_ref.shape[0]
    chunk = PLANES * FACE
    chunks = cells // chunk

    def span(c, length, skipped=0):
        return pl.ds(pl.multiple_of(skipped + c * length, LANES), length)

    def bases(c):
        lanes = span(c, chunk)
        return pltpu.make_async_copy(
            base_hbm.at[:, :, lanes], base_ref.at[:, :, lanes], got.at[2, c]
        )

    def cells_in(c):
        lanes, rims, inner = span(c, chunk), span(c, chunk // 2), span(c, chunk, FACE)
        return (
            pltpu.make_async_copy(
                fields_hbm.at[:, :, lanes], fields_ref.at[:, :, inner], got.at[0, c]
            ),
            pltpu.make_async_copy(
                rims_hbm.at[:, :, rims], rims_ref.at[:, :, rims], got.at[1, c]
            ),
        )

    def ends():
        return (
            pltpu.make_async_copy(weights_hbm, weights_ref, got.at[3, 0]),
            pltpu.make_async_copy(
                ghosts_hbm.at[:, :, pl.ds(0, FACE)], fields_ref.at[:, :, pl.ds(0, FACE)], got.at[3, 1]
            ),
            pltpu.make_async_copy(
                ghosts_hbm.at[:, :, pl.ds(FACE, FACE)],
                fields_ref.at[:, :, pl.ds(FACE + cells, FACE)],
                got.at[3, 2],
            ),
        )

    def stores(c):
        lanes = span(c, chunk)
        return (
            pltpu.make_async_copy(
                base_ref.at[:, :, lanes], new_fields_hbm.at[:, :, lanes], sent.at[0, c]
            ),
            pltpu.make_async_copy(
                new_tend_ref.at[:, :, lanes], new_tend_hbm.at[:, :, lanes], sent.at[1, c]
            ),
        )

    for copy in ends():
        copy.start()
    for c in range(chunks):
        for copy in (*cells_in(c), bases(c)):
            copy.start()

    wanted = lax.broadcasted_iota(jnp.int32, (slots, peers), 1) == tile_ref[:, 0:1]
    picked = jnp.dot(
        wanted.astype(jnp.float32),
        table_ref[...],
        precision=lax.Precision.HIGHEST,
        preferred_element_type=jnp.float32,
    )
    lane = lax.broadcasted_iota(jnp.int32, picked.shape, 1)
    thick = jnp.sum(jnp.where(lane == tile_ref[:, 1:2], picked, 0.0), axis=1, keepdims=True)
    live = lax.broadcasted_iota(jnp.int32, (slots, 1), 0) < live_ref[0]
    live = jnp.where(live, 1.0, 0.0)
    parts = [viscous * thick * live, live / thick]
    parts += [0.5 * live * speed_ref[:, d : d + 1] for d in range(3)]
    for n, part in enumerate(parts):
        wide_ref[n] = jnp.broadcast_to(part, (slots, LANES))
    for s in range(species):
        for k in range(species):
            rates_ref[s * species + k] = jnp.full((8, LANES), rate_ref[s, k], jnp.float32)
    parity = lax.broadcasted_iota(jnp.int32, (slots, 2 * LANES), 1) // TE % 2

    def sums(pair, odd):
        left_ref, sums_ref = ((left_even_ref, sums_even_ref), (left_odd_ref, sums_odd_ref))[odd]
        rims = pl.ds(pl.multiple_of(pair * FACE, FACE), FACE)
        for s in range(species):
            both = rims_ref[s, :, rims]
            for p in range(2):
                lanes = pl.ds(pl.multiple_of((2 * pair + p + 1) * FACE, FACE), FACE)
                rows = slice((p * species + s) * slots, (p * species + s + 1) * slots)
                f = fields_ref[s, :, lanes]
                high = f.astype(jnp.bfloat16)
                left_ref[rows, 0:FACE] = high
                left_ref[rows, FACE : 2 * FACE] = (f - high.astype(jnp.float32)).astype(jnp.bfloat16)
                left_ref[rows, 2 * FACE :] = jnp.where(parity == p, both, jnp.zeros_like(both))
        sums_ref[...] = jnp.dot(left_ref[...], weights_ref[...], preferred_element_type=jnp.float32)

    def finish(pair, odd):
        sums_ref = (sums_even_ref, sums_odd_ref)[odd]
        for p in range(2):
            inner, before, here, after = (
                pl.ds(pl.multiple_of((2 * pair + p + n) * FACE, FACE), FACE) for n in (0, 0, 1, 2)
            )
            for g in range(slots // 8):
                rows = slice(g * 8, (g + 1) * 8)
                smooth, over, vx, vy, vz = (
                    jnp.concatenate([wide_ref[n, rows, :]] * 2, axis=1) for n in range(5)
                )
                fuel = [fields_ref[s, rows, here] for s in range(species)]
                burning = fuel[0] * fuel[1] * over
                fuel = [f * burning for f in fuel]
                for s in range(species):
                    react = None
                    for k in range(species):
                        rate = rates_ref[s * species + k]
                        term = jnp.concatenate([rate, rate], axis=1) * fuel[k]
                        react = term if react is None else react + term
                    low, high = fields_ref[s, rows, before], fields_ref[s, rows, after]
                    line = (p * species + s) * slots + g * 8
                    total, along_y, along_z = (
                        sums_ref[line : line + 8, d * FACE : (d + 1) * FACE] for d in range(3)
                    )
                    tend = smooth * (total + (low + high)) - vx * (high - low)
                    tend = (tend - vy * along_y) + (react - vz * along_z)
                    base_ref[s, rows, inner] += (step_size * 23.0 / 12.0) * tend
                    sums_ref[line : line + 8, 0:FACE] = tend
            for s in range(species):
                line = (p * species + s) * slots
                new_tend_ref[s, :, inner] = sums_ref[line : line + slots, 0:FACE].astype(jnp.bfloat16)

    for copy in (*ends(), *cells_in(0)):
        copy.wait()
    sums(0, 0)

    def four(c, carry):
        bases(c).wait()
        sums(2 * c + 1, 1)
        finish(2 * c, 0)

        @pl.when(c + 1 < chunks)
        def _():
            for copy in cells_in(c + 1):
                copy.wait()

        sums(jnp.minimum(2 * c + 2, 2 * (chunks - 1)), 0)
        finish(2 * c + 1, 1)
        for copy in stores(c):
            copy.start()
        return carry

    lax.fori_loop(0, chunks, four, 0)
    for c in range(chunks):
        for copy in stores(c):
            copy.wait()


def add_kernel(
    me_ref, live_ref, table_ref, fields_hbm, arrived_hbm, out_hbm, fields_ref, arrived_ref, got, sent
):
    species, peers = arrived_ref.shape[:2]
    slots = fields_ref.shape[1]

    def fetches(s):
        part = arrived_hbm.at[:, pl.ds(s * ROWS, ROWS)]
        return (
            pltpu.make_async_copy(part, arrived_ref.at[s], got.at[0, s]),
            pltpu.make_async_copy(fields_hbm.at[s], fields_ref.at[s], got.at[1, s]),
        )

    def store(s):
        return pltpu.make_async_copy(fields_ref.at[s], out_hbm.at[s], sent.at[s])

    for s in range(species):
        for copy in fetches(s):
            copy.start()
    me, first = me_ref[0], pl.multiple_of(me_ref[1] * LANES, LANES)
    notes = table_ref[:, pl.ds(first, LANES)]
    destination = notes[:, slots : 2 * slots]
    target = notes[:, 2 * slots : 3 * slots]
    peer = lax.broadcasted_iota(jnp.int32, (peers, slots), 0)
    mine = (destination == me.astype(jnp.float32)) & (peer != me)
    slot = jnp.max(jnp.where(mine, target, -1.0), axis=1, keepdims=True)
    index = lax.broadcasted_iota(jnp.int32, (peers, slots), 1)
    hot = (slot == index.astype(jnp.float32)) & (index < live_ref[0])
    hot = jnp.where(hot, step_size / SCALE, 0.0)
    hot = jnp.concatenate([hot, hot], axis=0).T.astype(jnp.bfloat16)
    for s in range(species):
        for copy in fetches(s):
            copy.wait()
        flat = arrived_ref.at[s].reshape(peers * ROWS, LANES)
        for c in range(ROWS // 2):
            lanes = slice(c * 2 * LANES, (c + 1) * 2 * LANES)
            arrived = jnp.concatenate(
                [flat[pl.ds(2 * c + k, peers, stride=ROWS), :] for k in range(2)], axis=1
            )
            high = arrived.astype(jnp.bfloat16)
            low = (arrived - high.astype(jnp.float32)).astype(jnp.bfloat16)
            fields_ref[s, :, lanes] += jnp.dot(
                hot, jnp.concatenate([high, low], axis=0), preferred_element_type=jnp.float32
            )
        store(s).start()
    for s in range(species):
        store(s).wait()


def smem():
    return pl.BlockSpec(memory_space=pltpu.SMEM)


def whole(shape):
    return pl.BlockSpec(shape, lambda i: (0,) * len(shape))


def params(mib, semantics=None):
    return pltpu.CompilerParams(vmem_limit_bytes=mib << 20, dimension_semantics=semantics)


def local(
    fields,
    ghosts,
    velocity,
    rate_matrix,
    recent_tend,
    older_tend,
    destination,
    target_slot,
    live_counts,
    tile_ids,
    sensor,
    flame_flags,
):
    slots, species, cells = fields.shape
    peers = lax.axis_size(TEAM)
    brick = sensor.shape[0]
    me = jnp.stack([lax.axis_index(TEAM), lax.axis_index("grp")]).astype(jnp.int32)
    fields, ghosts, recent, older = (
        a.transpose(1, 0, 2) for a in (fields, ghosts, recent_tend, older_tend)
    )
    moves = jnp.stack([destination, target_slot])

    raw = pl.pallas_call(
        raw_kernel,
        name="raw_sensor",
        out_shape=jax.ShapeDtypeStruct(sensor.shape, jnp.bfloat16),
        in_specs=[smem(), pl.BlockSpec(memory_space=pltpu.VMEM)],
        out_specs=pl.BlockSpec(memory_space=pltpu.VMEM),
        compiler_params=params(58),
    )(flame_flags, sensor)
    below = passed_along(raw, "pen", 1)
    above = passed_along(raw, "pen", -1)

    anywhere = pl.BlockSpec(memory_space=pl.ANY)
    in_hbm = pl.BlockSpec(memory_space=pltpu.HBM)
    vmem = pl.BlockSpec(memory_space=pltpu.VMEM)
    outgoing = pl.pallas_call(
        send_kernel,
        name="outgoing_histories",
        out_shape=jax.ShapeDtypeStruct((peers, species * ROWS, LANES), jnp.float32),
        in_specs=[smem(), vmem, in_hbm, in_hbm],
        out_specs=vmem,
        scratch_shapes=[
            pltpu.VMEM(recent.shape, jnp.bfloat16),
            pltpu.VMEM(older.shape, jnp.bfloat16),
            pltpu.SemaphoreType.DMA((2, species)),
        ],
        compiler_params=params(50),
        cost_estimate=pl.CostEstimate(flops=0, bytes_accessed=8 << 20, transcendentals=0),
    )(me, destination.reshape(1, slots), recent, older)
    outgoing = outgoing.astype(jnp.float16)

    shape = jax.ShapeDtypeStruct((species, slots, cells), jnp.float32)
    rims = jax.ShapeDtypeStruct((species, slots, TE * LANES), jnp.bfloat16)
    base, rims = pl.pallas_call(
        prepare_kernel,
        name="base_and_rims",
        out_shape=(shape, rims),
        in_specs=[smem(), smem(), vmem] + [anywhere] * 4,
        out_specs=(anywhere, anywhere),
        scratch_shapes=[
            pltpu.VMEM(shape.shape, jnp.float32),
            pltpu.VMEM(shape.shape, jnp.bfloat16),
            pltpu.VMEM(shape.shape, jnp.bfloat16),
            pltpu.VMEM(ghosts.shape, jnp.float32),
            pltpu.VMEM(rims.shape, jnp.bfloat16),
            pltpu.SemaphoreType.DMA((4, species)),
            pltpu.SemaphoreType.DMA((2, species)),
        ],
        compiler_params=params(58),
        cost_estimate=pl.CostEstimate(flops=0, bytes_accessed=24 << 20, transcendentals=0),
    )(me, live_counts, moves, fields, recent, older, ghosts)
    below, above, base, rims, outgoing = lax.optimization_barrier(
        (below, above, base, rims, outgoing)
    )

    notes = jnp.concatenate(
        [jnp.zeros((1, slots), jnp.float32), moves.astype(jnp.float32).reshape(1, 2 * slots)], axis=1
    )
    notes = jnp.pad(notes, ((0, 0), (0, LANES - 3 * slots)))
    filtered, row = pl.pallas_call(
        filter_kernel,
        name="filtered_sensor",
        out_shape=(
            jax.ShapeDtypeStruct(sensor.shape, jnp.float32),
            jax.ShapeDtypeStruct((1, LANES), jnp.float32),
        ),
        in_specs=[smem()] + [vmem] * 5,
        out_specs=(vmem, vmem),
        compiler_params=params(32),
        cost_estimate=pl.CostEstimate(flops=0, bytes_accessed=4 << 20, transcendentals=0),
    )(flame_flags, jnp.asarray(banded(brick, brick)), sensor, below, above, notes)
    owner, lane = tile_ids // slots, tile_ids % slots
    tile_place = jnp.stack([owner % peers, owner // peers * LANES + lane], axis=1)
    speed = jnp.pad(velocity.T, ((0, 0), (0, 5)))

    rows = gathered(row, ("pen",))
    rows, outgoing = lax.optimization_barrier((rows, outgoing))
    arrived = lax.all_to_all(outgoing, TEAM, split_axis=0, concat_axis=0, tiled=True)
    table = gathered(rows, ("grp", "mig"))
    arrived = arrived.astype(jnp.float32)

    weights = jnp.asarray(plane_weights(), jnp.bfloat16)
    left = pltpu.VMEM((2 * species * slots, 6 * LANES), jnp.bfloat16)
    sums = pltpu.VMEM((2 * species * slots, 3 * FACE), jnp.float32)
    new_fields, new_tend = pl.pallas_call(
        main_kernel,
        name="updates",
        out_shape=(shape, jax.ShapeDtypeStruct(shape.shape, jnp.bfloat16)),
        in_specs=[smem()] * 2 + [vmem] * 3 + [anywhere] * 5,
        out_specs=(anywhere, anywhere),
        scratch_shapes=[
            pltpu.VMEM(weights.shape, jnp.bfloat16),
            pltpu.VMEM((species, slots, cells + 2 * FACE), jnp.float32),
            pltpu.VMEM(rims.shape, jnp.bfloat16),
            pltpu.VMEM(shape.shape, jnp.float32),
            pltpu.VMEM(shape.shape, jnp.bfloat16),
            pltpu.VMEM((species * species, 8, LANES), jnp.float32),
            pltpu.VMEM((5, slots, LANES), jnp.float32),
            left,
            left,
            sums,
            sums,
            pltpu.SemaphoreType.DMA((4, TE // PLANES)),
            pltpu.SemaphoreType.DMA((2, TE // PLANES)),
        ],
        compiler_params=params(58),
        cost_estimate=pl.CostEstimate(flops=0, bytes_accessed=40 << 20, transcendentals=0),
    )(live_counts, rate_matrix, table, tile_place, speed, weights, fields, ghosts, rims, base)

    new_fields = pl.pallas_call(
        add_kernel,
        name="arrived_histories",
        out_shape=shape,
        in_specs=[smem(), smem(), vmem, anywhere, anywhere],
        out_specs=anywhere,
        scratch_shapes=[
            pltpu.VMEM(shape.shape, jnp.float32),
            pltpu.VMEM((species, peers, ROWS, LANES), jnp.float32),
            pltpu.SemaphoreType.DMA((2, species)),
            pltpu.SemaphoreType.DMA((species,)),
        ],
        compiler_params=params(58),
        cost_estimate=pl.CostEstimate(flops=0, bytes_accessed=12 << 20, transcendentals=0),
    )(me, live_counts, table, new_fields, arrived)
    return new_fields.transpose(1, 0, 2), new_tend.transpose(1, 0, 2), filtered


def gathered(row, axes):
    for axis in axes:
        count = lax.axis_size(axis)
        here = lax.axis_index(axis)
        rows = [row] + [passed_along(row, axis, by) for by in range(1, count)]
        height, width = row.shape
        if axis == "grp":
            table = jnp.zeros((height, count * width), row.dtype)
        else:
            table = jnp.zeros((count * height, width), row.dtype)
        for by, part in enumerate(rows):
            place = (here - by) % count
            place = (0, place * width) if axis == "grp" else (place * height, 0)
            table = lax.dynamic_update_slice(table, part, place)
        row = table
    return row


def solution(mesh):
    split = P(EVERY, None, None)
    return jax.shard_map(
        local,
        mesh=mesh,
        in_specs=(
            split,
            split,
            P(None, EVERY),
            P(),
            split,
            split,
            P(EVERY),
            P(EVERY),
            P(EVERY),
            P(EVERY),
            P("pen", ("grp", "mig")),
            P("pen", ("grp", "mig")),
        ),
        out_specs=(split, split, P("pen", ("grp", "mig"))),
        check_vma=False,
    )
```

```python
import jax
import jax.numpy as jnp
import numpy as np
from jax import lax
from jax.experimental import pallas as pl
from jax.experimental.pallas import tpu as pltpu
from jax.sharding import PartitionSpec as P

TE = 16
TZ = 2
TCOL = 16
FACE = TE * TE
CELLS = TE**3
LANES = 128
ROWS = CELLS // LANES

viscous = 0.05
step_size = 0.25
thicken = 5.0

SCALE = 4096.0
PLANES = 4
AHEAD = 4

EVERY = ("grp", "mig", "pen")
TEAM = ("mig", "pen")


def passed_along(x, axis, by):
    peers = lax.axis_size(axis)
    return lax.ppermute(x, axis, [(i, (i + by) % peers) for i in range(peers)])


def banded(brick_rows, reach):
    sigma = reach / 2.0
    offsets = np.arange(-reach, reach + 1, dtype=np.float64)
    total = np.sum(np.exp(-offsets * offsets / (2.0 * sigma * sigma)))
    row = np.arange(brick_rows)[:, None]
    col = np.arange(brick_rows + 2 * reach)[None, :]
    offset = (col - reach - row).astype(np.float64)
    weights = np.where(np.abs(offset) <= reach, np.exp(-offset * offset / (2.0 * sigma * sigma)), 0)
    return (weights / total).astype(np.float32)


def raw_kernel(flags_ref, sensor_ref, raw_ref):
    for r in range(TZ):
        for k in range(TCOL):
            rows, cols = slice(r * TE, (r + 1) * TE), slice(k * FACE, (k + 1) * FACE)
            flag = flags_ref[r, k].astype(jnp.float32)
            raw_ref[rows, cols] = (sensor_ref[rows, cols] * flag).astype(jnp.bfloat16)


def filter_kernel(
    flags_ref,
    weights_ref,
    sensor_ref,
    below_ref,
    above_ref,
    destination_ref,
    target_ref,
    filtered_ref,
    row_ref,
):
    lane = lax.broadcasted_iota(jnp.int32, (1, LANES), 1)
    slots = destination_ref.shape[1]
    row = jnp.concatenate(
        [
            jnp.zeros((1, slots), jnp.float32),
            destination_ref[...].astype(jnp.float32),
            target_ref[...].astype(jnp.float32),
            jnp.zeros((1, LANES - 3 * slots), jnp.float32),
        ],
        axis=1,
    )
    brick = sensor_ref.shape[0]
    for k in range(TCOL):
        cols = slice(k * FACE, (k + 1) * FACE)
        own = [
            sensor_ref[r * TE : (r + 1) * TE, cols] * flags_ref[r, k].astype(jnp.float32)
            for r in range(TZ)
        ]
        widened = jnp.concatenate(
            [below_ref[:, cols].astype(jnp.float32)] + own + [above_ref[:, cols].astype(jnp.float32)],
            axis=0,
        )
        filtered = jnp.dot(
            weights_ref[...],
            widened,
            precision=lax.Precision.HIGHEST,
            preferred_element_type=jnp.float32,
        )
        filtered_ref[:, cols] = filtered
        clipped = jnp.minimum(filtered, 1.0)
        for r in range(TZ):
            total = jnp.sum(
                jnp.sum(clipped[r * TE : (r + 1) * TE], axis=0, keepdims=True), axis=1, keepdims=True
            )
            thick = 1.0 + (thicken - 1.0) * (total / float(TE * FACE))
            row = jnp.where(lane == r * TCOL + k, thick, row)
    row_ref[...] = row


def send_kernel(
    destination_ref, recent_hbm, older_hbm, out_ref, recent_ref, older_ref, got
):
    species, slots, _ = recent_ref.shape
    peers = out_ref.shape[0]

    def fetches(s):
        return (
            pltpu.make_async_copy(recent_hbm.at[s], recent_ref.at[s], got.at[0, s]),
            pltpu.make_async_copy(older_hbm.at[s], older_ref.at[s], got.at[1, s]),
        )

    for s in range(AHEAD):
        for copy in fetches(s):
            copy.start()
    peer = lax.broadcasted_iota(jnp.int32, (peers, slots), 0)
    hot = ((destination_ref[...] == peer) & (peer != lax.axis_index(TEAM))).astype(jnp.bfloat16)
    flat = out_ref.reshape(peers * species * ROWS, LANES)
    for s in range(species):
        if s + AHEAD < species:
            for copy in fetches(s + AHEAD):
                copy.start()
        for copy in fetches(s):
            copy.wait()
        recent = jnp.dot(hot, recent_ref[s], preferred_element_type=jnp.float32)
        older = jnp.dot(hot, older_ref[s], preferred_element_type=jnp.float32)
        mixed = recent * (-16.0 / 12.0 * SCALE) + older * (5.0 / 12.0 * SCALE)
        for k in range(ROWS):
            flat[pl.ds(s * ROWS + k, peers, stride=species * ROWS), :] = mixed[
                :, k * LANES : (k + 1) * LANES
            ]


def prepare_kernel(
    live_ref,
    destination_ref,
    target_ref,
    fields_hbm,
    recent_hbm,
    older_hbm,
    ghosts_hbm,
    base_hbm,
    rims_hbm,
    fields_ref,
    recent_ref,
    older_ref,
    ghosts_ref,
    rims_ref,
    got,
    sent,
):
    species, slots, _ = fields_ref.shape

    def fetches(s):
        pairs = (
            (fields_hbm, fields_ref),
            (recent_hbm, recent_ref),
            (older_hbm, older_ref),
            (ghosts_hbm, ghosts_ref),
        )
        return [
            pltpu.make_async_copy(here.at[s], there.at[s], got.at[n, s])
            for n, (here, there) in enumerate(pairs)
        ]

    def stores(s):
        return (
            pltpu.make_async_copy(fields_ref.at[s], base_hbm.at[s], sent.at[0, s]),
            pltpu.make_async_copy(rims_ref.at[s], rims_hbm.at[s], sent.at[1, s]),
        )

    for s in range(AHEAD):
        for copy in fetches(s):
            copy.start()
    slot = lax.broadcasted_iota(jnp.int32, (slots, slots), 0)
    keep = (destination_ref[...] == lax.axis_index(TEAM)) & (target_ref[...] == slot)
    keep = keep.astype(jnp.bfloat16)
    live = lax.broadcasted_iota(jnp.int32, (slots, 1), 0) < live_ref[0]
    live = jnp.where(live, 1.0, 0.0)
    quarter = lax.broadcasted_iota(jnp.int32, (slots, LANES), 1) // (2 * TE)

    def one(s, carry):
        @pl.when(s + AHEAD < species)
        def _():
            for copy in fetches(s + AHEAD):
                copy.start()

        for copy in fetches(s):
            copy.wait()
        recent = jnp.dot(keep, recent_ref[s], preferred_element_type=jnp.float32)
        older = jnp.dot(keep, older_ref[s], preferred_element_type=jnp.float32)
        kept = recent * (-16.0 / 12.0 * step_size) + older * (5.0 / 12.0 * step_size)
        fields_ref[s] = (fields_ref[s] + kept) * live
        for block in range(2):
            faces = [
                ghosts_ref[s, :, w * FACE + block * LANES : w * FACE + (block + 1) * LANES]
                for w in (4, 5, 2, 3)
            ]
            for q in range(4):
                rim = faces[0]
                for n in range(4):
                    turned = pltpu.roll(faces[n], (n - q) % 4 * 2 * TE, 1) if n != q else faces[n]
                    rim = turned if n == 0 else jnp.where(quarter == n, turned, rim)
                high = rim.astype(jnp.bfloat16)
                low = (rim - high.astype(jnp.float32)).astype(jnp.bfloat16)
                start = (block * 4 + q) * 2 * LANES
                rims_ref[s, :, start : start + LANES] = high
                rims_ref[s, :, start + LANES : start + 2 * LANES] = low
        for copy in stores(s):
            copy.start()
        return carry

    lax.fori_loop(0, species, one, 0)
    for s in range(species):
        for copy in stores(s):
            copy.wait()


def plane_weights():
    weights = np.zeros((6 * LANES, 3 * FACE), np.float32)
    for cell in range(FACE):
        y, z = divmod(cell, TE)
        for d, at, step in ((0, y, TE), (1, z, 1)):
            for way in (-1, 1):
                if 0 <= at + way < TE:
                    rows = [cell + way * step, FACE + cell + way * step]
                else:
                    face = (2 + (way > 0)) if d == 0 else (way > 0)
                    spot = 2 * FACE + face * 2 * TE + (z if d == 0 else y)
                    rows = [spot, spot + TE, spot + LANES, spot + LANES + TE]
                weights[rows, cell] += 1.0
                weights[rows, (1 + d) * FACE + cell] += way
        weights[[cell, FACE + cell], cell] -= 6.0
    return weights


def main_kernel(
    live_ref,
    rate_ref,
    table_ref,
    tiles_ref,
    velocity_ref,
    weights_hbm,
    fields_hbm,
    ghosts_hbm,
    rims_hbm,
    base_hbm,
    new_fields_hbm,
    new_tend_hbm,
    weights_ref,
    fields_ref,
    rims_ref,
    base_ref,
    new_tend_ref,
    rates_ref,
    wide_ref,
    left_even_ref,
    left_odd_ref,
    sums_even_ref,
    sums_odd_ref,
    got,
    sent,
):
    species, slots, cells = base_ref.shape
    peers = table_ref.shape[0]
    chunk = PLANES * FACE
    chunks = cells // chunk

    def span(c, length, skipped=0):
        return pl.ds(pl.multiple_of(skipped + c * length, LANES), length)

    def bases(c):
        lanes = span(c, chunk)
        return pltpu.make_async_copy(
            base_hbm.at[:, :, lanes], base_ref.at[:, :, lanes], got.at[2, c]
        )

    def cells_in(c):
        lanes, rims, inner = span(c, chunk), span(c, chunk // 2), span(c, chunk, FACE)
        return (
            pltpu.make_async_copy(
                fields_hbm.at[:, :, lanes], fields_ref.at[:, :, inner], got.at[0, c]
            ),
            pltpu.make_async_copy(
                rims_hbm.at[:, :, rims], rims_ref.at[:, :, rims], got.at[1, c]
            ),
        )

    def ends():
        return (
            pltpu.make_async_copy(weights_hbm, weights_ref, got.at[3, 0]),
            pltpu.make_async_copy(
                ghosts_hbm.at[:, :, pl.ds(0, FACE)], fields_ref.at[:, :, pl.ds(0, FACE)], got.at[3, 1]
            ),
            pltpu.make_async_copy(
                ghosts_hbm.at[:, :, pl.ds(FACE, FACE)],
                fields_ref.at[:, :, pl.ds(FACE + cells, FACE)],
                got.at[3, 2],
            ),
        )

    def stores(c):
        lanes = span(c, chunk)
        return (
            pltpu.make_async_copy(
                base_ref.at[:, :, lanes], new_fields_hbm.at[:, :, lanes], sent.at[0, c]
            ),
            pltpu.make_async_copy(
                new_tend_ref.at[:, :, lanes], new_tend_hbm.at[:, :, lanes], sent.at[1, c]
            ),
        )

    for copy in ends():
        copy.start()
    for c in range(2):
        for copy in (*cells_in(c), bases(c)):
            copy.start()

    marks = jnp.concatenate(
        [velocity_ref[...], tiles_ref[...].astype(jnp.float32), jnp.zeros((4, slots), jnp.float32)], axis=0
    ).T
    tiles = marks[:, 3:4].astype(jnp.int32)
    owner = tiles // slots
    wanted = lax.broadcasted_iota(jnp.int32, (slots, peers), 1) == owner % peers
    picked = jnp.dot(
        wanted.astype(jnp.float32),
        table_ref[...],
        precision=lax.Precision.HIGHEST,
        preferred_element_type=jnp.float32,
    )
    lane = lax.broadcasted_iota(jnp.int32, picked.shape, 1)
    spot = owner // peers * LANES + tiles % slots
    thick = jnp.sum(jnp.where(lane == spot, picked, 0.0), axis=1, keepdims=True)
    live = lax.broadcasted_iota(jnp.int32, (slots, 1), 0) < live_ref[0]
    live = jnp.where(live, 1.0, 0.0)
    parts = [viscous * thick * live, live / thick]
    parts += [0.5 * live * marks[:, d : d + 1] for d in range(3)]
    for n, part in enumerate(parts):
        wide_ref[n] = jnp.broadcast_to(part, (slots, LANES))
    for s in range(species):
        for k in range(species):
            rates_ref[s * species + k] = jnp.full((8, LANES), rate_ref[s, k], jnp.float32)
    parity = lax.broadcasted_iota(jnp.int32, (slots, 2 * LANES), 1) // TE % 2

    def sums(pair, odd):
        left_ref, sums_ref = ((left_even_ref, sums_even_ref), (left_odd_ref, sums_odd_ref))[odd]
        rims = pl.ds(pl.multiple_of(pair * FACE, FACE), FACE)
        for s in range(species):
            both = rims_ref[s, :, rims]
            for p in range(2):
                lanes = pl.ds(pl.multiple_of((2 * pair + p + 1) * FACE, FACE), FACE)
                rows = slice((p * species + s) * slots, (p * species + s + 1) * slots)
                f = fields_ref[s, :, lanes]
                high = f.astype(jnp.bfloat16)
                left_ref[rows, 0:FACE] = high
                left_ref[rows, FACE : 2 * FACE] = (f - high.astype(jnp.float32)).astype(jnp.bfloat16)
                left_ref[rows, 2 * FACE :] = jnp.where(parity == p, both, jnp.zeros_like(both))
        sums_ref[...] = jnp.dot(left_ref[...], weights_ref[...], preferred_element_type=jnp.float32)

    def finish(pair, odd):
        sums_ref = (sums_even_ref, sums_odd_ref)[odd]
        for p in range(2):
            inner, before, here, after = (
                pl.ds(pl.multiple_of((2 * pair + p + n) * FACE, FACE), FACE) for n in (0, 0, 1, 2)
            )
            for g in range(slots // 8):
                rows = slice(g * 8, (g + 1) * 8)
                smooth, over, vx, vy, vz = (
                    jnp.concatenate([wide_ref[n, rows, :]] * 2, axis=1) for n in range(5)
                )
                fuel = [fields_ref[s, rows, here] for s in range(species)]
                burning = fuel[0] * fuel[1] * over
                fuel = [f * burning for f in fuel]
                for s in range(species):
                    react = None
                    for k in range(species):
                        rate = rates_ref[s * species + k]
                        term = jnp.concatenate([rate, rate], axis=1) * fuel[k]
                        react = term if react is None else react + term
                    low, high = fields_ref[s, rows, before], fields_ref[s, rows, after]
                    line = (p * species + s) * slots + g * 8
                    total, along_y, along_z = (
                        sums_ref[line : line + 8, d * FACE : (d + 1) * FACE] for d in range(3)
                    )
                    tend = smooth * (total + (low + high)) - vx * (high - low)
                    tend = (tend - vy * along_y) + (react - vz * along_z)
                    base_ref[s, rows, inner] += (step_size * 23.0 / 12.0) * tend
                    sums_ref[line : line + 8, 0:FACE] = tend
            for s in range(species):
                line = (p * species + s) * slots
                new_tend_ref[s, :, inner] = sums_ref[line : line + slots, 0:FACE].astype(jnp.bfloat16)

    for copy in (*ends(), *cells_in(0)):
        copy.wait()
    sums(0, 0)

    def four(c, carry):
        @pl.when(c + 2 < chunks)
        def _():
            for copy in (*cells_in(c + 2), bases(c + 2)):
                copy.start()

        bases(c).wait()
        sums(2 * c + 1, 1)
        finish(2 * c, 0)

        @pl.when(c + 1 < chunks)
        def _():
            for copy in cells_in(c + 1):
                copy.wait()

        sums(jnp.minimum(2 * c + 2, 2 * (chunks - 1)), 0)
        finish(2 * c + 1, 1)
        for copy in stores(c):
            copy.start()
        return carry

    lax.fori_loop(0, chunks, four, 0)
    for c in range(chunks):
        for copy in stores(c):
            copy.wait()


def add_kernel(
    live_ref, table_ref, fields_hbm, arrived_hbm, out_hbm, fields_ref, arrived_ref, got, sent
):
    species, peers = arrived_ref.shape[:2]
    slots = fields_ref.shape[1]

    def fetches(s):
        part = arrived_hbm.at[:, pl.ds(s * ROWS, ROWS)]
        return (
            pltpu.make_async_copy(part, arrived_ref.at[s], got.at[0, s]),
            pltpu.make_async_copy(fields_hbm.at[s], fields_ref.at[s], got.at[1, s]),
        )

    def store(s):
        return pltpu.make_async_copy(fields_ref.at[s], out_hbm.at[s], sent.at[s])

    for s in range(AHEAD):
        for copy in fetches(s):
            copy.start()
    me, first = lax.axis_index(TEAM), pl.multiple_of(lax.axis_index("grp") * LANES, LANES)
    notes = table_ref[:, pl.ds(first, LANES)]
    destination = notes[:, slots : 2 * slots]
    target = notes[:, 2 * slots : 3 * slots]
    peer = lax.broadcasted_iota(jnp.int32, (peers, slots), 0)
    mine = (destination == me.astype(jnp.float32)) & (peer != me)
    slot = jnp.max(jnp.where(mine, target, -1.0), axis=1, keepdims=True)
    index = lax.broadcasted_iota(jnp.int32, (peers, slots), 1)
    hot = (slot == index.astype(jnp.float32)) & (index < live_ref[0])
    hot = jnp.where(hot, step_size / SCALE, 0.0)
    hot = jnp.concatenate([hot, hot], axis=0).T.astype(jnp.bfloat16)
    for s in range(species):
        if s + AHEAD < species:
            for copy in fetches(s + AHEAD):
                copy.start()
        for copy in fetches(s):
            copy.wait()
        flat = arrived_ref.at[s].reshape(peers * ROWS, LANES)
        for c in range(ROWS // 2):
            lanes = slice(c * 2 * LANES, (c + 1) * 2 * LANES)
            arrived = jnp.concatenate(
                [flat[pl.ds(2 * c + k, peers, stride=ROWS), :] for k in range(2)], axis=1
            )
            high = arrived.astype(jnp.bfloat16)
            low = (arrived - high.astype(jnp.float32)).astype(jnp.bfloat16)
            fields_ref[s, :, lanes] += jnp.dot(
                hot, jnp.concatenate([high, low], axis=0), preferred_element_type=jnp.float32
            )
        store(s).start()
    for s in range(species):
        store(s).wait()


def smem():
    return pl.BlockSpec(memory_space=pltpu.SMEM)


def whole(shape):
    return pl.BlockSpec(shape, lambda i: (0,) * len(shape))


def params(mib, semantics=None):
    return pltpu.CompilerParams(vmem_limit_bytes=mib << 20, dimension_semantics=semantics)


def local(
    fields,
    ghosts,
    velocity,
    rate_matrix,
    recent_tend,
    older_tend,
    destination,
    target_slot,
    live_counts,
    tile_ids,
    sensor,
    flame_flags,
):
    slots, species, cells = fields.shape
    peers = lax.axis_size(TEAM)
    brick = sensor.shape[0]
    fields, ghosts, recent, older = (
        a.transpose(1, 0, 2) for a in (fields, ghosts, recent_tend, older_tend)
    )
    moves = (destination.reshape(1, slots), target_slot.reshape(1, slots))

    raw = pl.pallas_call(
        raw_kernel,
        name="raw_sensor",
        out_shape=jax.ShapeDtypeStruct(sensor.shape, jnp.bfloat16),
        in_specs=[smem(), pl.BlockSpec(memory_space=pltpu.VMEM)],
        out_specs=pl.BlockSpec(memory_space=pltpu.VMEM),
        compiler_params=params(58),
    )(flame_flags, sensor)
    below = passed_along(raw, "pen", 1)
    above = passed_along(raw, "pen", -1)

    anywhere = pl.BlockSpec(memory_space=pl.ANY)
    in_hbm = pl.BlockSpec(memory_space=pltpu.HBM)
    vmem = pl.BlockSpec(memory_space=pltpu.VMEM)
    outgoing = pl.pallas_call(
        send_kernel,
        name="outgoing_histories",
        out_shape=jax.ShapeDtypeStruct((peers, species * ROWS, LANES), jnp.float32),
        in_specs=[vmem, in_hbm, in_hbm],
        out_specs=vmem,
        scratch_shapes=[
            pltpu.VMEM(recent.shape, jnp.bfloat16),
            pltpu.VMEM(older.shape, jnp.bfloat16),
            pltpu.SemaphoreType.DMA((2, species)),
        ],
        compiler_params=params(50),
        cost_estimate=pl.CostEstimate(flops=0, bytes_accessed=8 << 20, transcendentals=0),
    )(destination.reshape(1, slots), recent, older)
    outgoing = outgoing.astype(jnp.float16)

    shape = jax.ShapeDtypeStruct((species, slots, cells), jnp.float32)
    rims = jax.ShapeDtypeStruct((species, slots, TE * LANES), jnp.bfloat16)
    base, rims = pl.pallas_call(
        prepare_kernel,
        name="base_and_rims",
        out_shape=(shape, rims),
        in_specs=[smem(), vmem, vmem] + [anywhere] * 4,
        out_specs=(anywhere, anywhere),
        scratch_shapes=[
            pltpu.VMEM(shape.shape, jnp.float32),
            pltpu.VMEM(shape.shape, jnp.bfloat16),
            pltpu.VMEM(shape.shape, jnp.bfloat16),
            pltpu.VMEM(ghosts.shape, jnp.float32),
            pltpu.VMEM(rims.shape, jnp.bfloat16),
            pltpu.SemaphoreType.DMA((4, species)),
            pltpu.SemaphoreType.DMA((2, species)),
        ],
        compiler_params=params(58),
        cost_estimate=pl.CostEstimate(flops=0, bytes_accessed=24 << 20, transcendentals=0),
    )(live_counts, *moves, fields, recent, older, ghosts)

    filtered, row = pl.pallas_call(
        filter_kernel,
        name="filtered_sensor",
        out_shape=(
            jax.ShapeDtypeStruct(sensor.shape, jnp.float32),
            jax.ShapeDtypeStruct((1, LANES), jnp.float32),
        ),
        in_specs=[smem()] + [vmem] * 6,
        out_specs=(vmem, vmem),
        compiler_params=params(32),
        cost_estimate=pl.CostEstimate(flops=0, bytes_accessed=4 << 20, transcendentals=0),
    )(flame_flags, jnp.asarray(banded(brick, brick)), sensor, below, above, *moves)
    rows = gathered(row, ("pen",))
    rows, outgoing, base, rims = lax.optimization_barrier((rows, outgoing, base, rims))
    arrived = lax.all_to_all(outgoing, TEAM, split_axis=0, concat_axis=0, tiled=True)
    table = gathered(rows, ("grp", "mig"))
    arrived = arrived.astype(jnp.float32)

    weights = jnp.asarray(plane_weights(), jnp.bfloat16)
    left = pltpu.VMEM((2 * species * slots, 6 * LANES), jnp.bfloat16)
    sums = pltpu.VMEM((2 * species * slots, 3 * FACE), jnp.float32)
    new_fields, new_tend = pl.pallas_call(
        main_kernel,
        name="updates",
        out_shape=(shape, jax.ShapeDtypeStruct(shape.shape, jnp.bfloat16)),
        in_specs=[smem()] * 2 + [vmem] * 3 + [anywhere] * 5,
        out_specs=(anywhere, anywhere),
        scratch_shapes=[
            pltpu.VMEM(weights.shape, jnp.bfloat16),
            pltpu.VMEM((species, slots, cells + 2 * FACE), jnp.float32),
            pltpu.VMEM(rims.shape, jnp.bfloat16),
            pltpu.VMEM(shape.shape, jnp.float32),
            pltpu.VMEM(shape.shape, jnp.bfloat16),
            pltpu.VMEM((species * species, 8, LANES), jnp.float32),
            pltpu.VMEM((5, slots, LANES), jnp.float32),
            left,
            left,
            sums,
            sums,
            pltpu.SemaphoreType.DMA((4, TE // PLANES)),
            pltpu.SemaphoreType.DMA((2, TE // PLANES)),
        ],
        compiler_params=params(58),
        cost_estimate=pl.CostEstimate(flops=0, bytes_accessed=40 << 20, transcendentals=0),
    )(
        live_counts,
        rate_matrix,
        table,
        tile_ids.reshape(1, slots),
        velocity,
        weights,
        fields,
        ghosts,
        rims,
        base,
    )

    new_fields = pl.pallas_call(
        add_kernel,
        name="arrived_histories",
        out_shape=shape,
        in_specs=[smem(), vmem, anywhere, anywhere],
        out_specs=anywhere,
        scratch_shapes=[
            pltpu.VMEM(shape.shape, jnp.float32),
            pltpu.VMEM((species, peers, ROWS, LANES), jnp.float32),
            pltpu.SemaphoreType.DMA((2, species)),
            pltpu.SemaphoreType.DMA((species,)),
        ],
        compiler_params=params(58),
        cost_estimate=pl.CostEstimate(flops=0, bytes_accessed=12 << 20, transcendentals=0),
    )(live_counts, table, new_fields, arrived)
    return new_fields.transpose(1, 0, 2), new_tend.transpose(1, 0, 2), filtered


def gathered(row, axes):
    for axis in axes:
        count = lax.axis_size(axis)
        here = lax.axis_index(axis)
        rows = [row] + [passed_along(row, axis, by) for by in range(1, count)]
        height, width = row.shape
        if axis == "grp":
            table = jnp.zeros((height, count * width), row.dtype)
        else:
            table = jnp.zeros((count * height, width), row.dtype)
        for by, part in enumerate(rows):
            place = (here - by) % count
            place = (0, place * width) if axis == "grp" else (place * height, 0)
            table = lax.dynamic_update_slice(table, part, place)
        row = table
    return row


def solution(mesh):
    split = P(EVERY, None, None)
    return jax.shard_map(
        local,
        mesh=mesh,
        in_specs=(
            split,
            split,
            P(None, EVERY),
            P(),
            split,
            split,
            P(EVERY),
            P(EVERY),
            P(EVERY),
            P(EVERY),
            P("pen", ("grp", "mig")),
            P("pen", ("grp", "mig")),
        ),
        out_specs=(split, split, P("pen", ("grp", "mig"))),
        check_vma=False,
    )
```

```python
import jax
import jax.numpy as jnp
import numpy as np
from jax import lax
from jax.experimental import pallas as pl
from jax.experimental.pallas import tpu as pltpu
from jax.sharding import PartitionSpec as P

TE = 16
TZ = 2
TCOL = 16
FACE = TE * TE
CELLS = TE**3
LANES = 128
ROWS = CELLS // LANES

viscous = 0.05
step_size = 0.25
thicken = 5.0

SCALE = 4096.0
PLANES = 4
AHEAD = 4

EVERY = ("grp", "mig", "pen")
TEAM = ("mig", "pen")


def passed_along(x, axis, by):
    peers = lax.axis_size(axis)
    return lax.ppermute(x, axis, [(i, (i + by) % peers) for i in range(peers)])


def banded(brick_rows, reach):
    sigma = reach / 2.0
    offsets = np.arange(-reach, reach + 1, dtype=np.float64)
    total = np.sum(np.exp(-offsets * offsets / (2.0 * sigma * sigma)))
    row = np.arange(brick_rows)[:, None]
    col = np.arange(brick_rows + 2 * reach)[None, :]
    offset = (col - reach - row).astype(np.float64)
    weights = np.where(np.abs(offset) <= reach, np.exp(-offset * offset / (2.0 * sigma * sigma)), 0)
    return (weights / total).astype(np.float32)


def raw_kernel(flags_ref, sensor_ref, raw_ref):
    for r in range(TZ):
        for k in range(TCOL):
            rows, cols = slice(r * TE, (r + 1) * TE), slice(k * FACE, (k + 1) * FACE)
            flag = flags_ref[r, k].astype(jnp.float32)
            raw_ref[rows, cols] = (sensor_ref[rows, cols] * flag).astype(jnp.bfloat16)


def filter_kernel(
    flags_ref,
    weights_ref,
    sensor_ref,
    below_ref,
    above_ref,
    destination_ref,
    target_ref,
    filtered_ref,
    row_ref,
):
    lane = lax.broadcasted_iota(jnp.int32, (1, LANES), 1)
    slots = destination_ref.shape[1]
    row = jnp.concatenate(
        [
            jnp.zeros((1, slots), jnp.float32),
            destination_ref[...].astype(jnp.float32),
            target_ref[...].astype(jnp.float32),
            jnp.zeros((1, LANES - 3 * slots), jnp.float32),
        ],
        axis=1,
    )
    brick = sensor_ref.shape[0]
    for k in range(TCOL):
        cols = slice(k * FACE, (k + 1) * FACE)
        own = [
            sensor_ref[r * TE : (r + 1) * TE, cols] * flags_ref[r, k].astype(jnp.float32)
            for r in range(TZ)
        ]
        widened = jnp.concatenate(
            [below_ref[:, cols].astype(jnp.float32)] + own + [above_ref[:, cols].astype(jnp.float32)],
            axis=0,
        )
        filtered = jnp.dot(
            weights_ref[...],
            widened,
            precision=lax.Precision.HIGHEST,
            preferred_element_type=jnp.float32,
        )
        filtered_ref[:, cols] = filtered
        clipped = jnp.minimum(filtered, 1.0)
        for r in range(TZ):
            total = jnp.sum(
                jnp.sum(clipped[r * TE : (r + 1) * TE], axis=0, keepdims=True), axis=1, keepdims=True
            )
            thick = 1.0 + (thicken - 1.0) * (total / float(TE * FACE))
            row = jnp.where(lane == r * TCOL + k, thick, row)
    row_ref[...] = row


def send_kernel(
    destination_ref, recent_hbm, older_hbm, out_ref, recent_ref, older_ref, got
):
    species, slots, _ = recent_ref.shape
    peers = out_ref.shape[0]

    def fetches(s):
        return (
            pltpu.make_async_copy(recent_hbm.at[s], recent_ref.at[s], got.at[0, s]),
            pltpu.make_async_copy(older_hbm.at[s], older_ref.at[s], got.at[1, s]),
        )

    for s in range(AHEAD):
        for copy in fetches(s):
            copy.start()
    peer = lax.broadcasted_iota(jnp.int32, (peers, slots), 0)
    hot = ((destination_ref[...] == peer) & (peer != lax.axis_index(TEAM))).astype(jnp.bfloat16)
    flat = out_ref.reshape(peers * species * ROWS, LANES)
    for s in range(species):
        if s + AHEAD < species:
            for copy in fetches(s + AHEAD):
                copy.start()
        for copy in fetches(s):
            copy.wait()
        recent = jnp.dot(hot, recent_ref[s], preferred_element_type=jnp.float32)
        older = jnp.dot(hot, older_ref[s], preferred_element_type=jnp.float32)
        mixed = recent * (-16.0 / 12.0 * SCALE) + older * (5.0 / 12.0 * SCALE)
        for k in range(ROWS):
            flat[pl.ds(s * ROWS + k, peers, stride=species * ROWS), :] = mixed[
                :, k * LANES : (k + 1) * LANES
            ]


def rims_kernel(ghosts_hbm, rims_hbm, ghosts_ref, rims_ref, got, sent):
    species, slots, _ = ghosts_ref.shape

    def fetch(s):
        return pltpu.make_async_copy(ghosts_hbm.at[s], ghosts_ref.at[s], got.at[s])

    def store(s):
        return pltpu.make_async_copy(rims_ref.at[s], rims_hbm.at[s], sent.at[s])

    for s in range(species):
        fetch(s).start()
    quarter = lax.broadcasted_iota(jnp.int32, (slots, LANES), 1) // (2 * TE)

    def one(s, carry):
        fetch(s).wait()
        for block in range(2):
            faces = [
                ghosts_ref[s, :, w * FACE + block * LANES : w * FACE + (block + 1) * LANES]
                for w in (4, 5, 2, 3)
            ]
            for q in range(4):
                rim = faces[0]
                for n in range(4):
                    turned = pltpu.roll(faces[n], (n - q) % 4 * 2 * TE, 1) if n != q else faces[n]
                    rim = turned if n == 0 else jnp.where(quarter == n, turned, rim)
                high = rim.astype(jnp.bfloat16)
                low = (rim - high.astype(jnp.float32)).astype(jnp.bfloat16)
                start = (block * 4 + q) * 2 * LANES
                rims_ref[s, :, start : start + LANES] = high
                rims_ref[s, :, start + LANES : start + 2 * LANES] = low
        store(s).start()
        return carry

    lax.fori_loop(0, species, one, 0)
    for s in range(species):
        store(s).wait()


def base_kernel(
    live_ref,
    destination_ref,
    target_ref,
    fields_hbm,
    recent_hbm,
    older_hbm,
    base_hbm,
    fields_ref,
    recent_ref,
    older_ref,
    got,
    sent,
):
    species, slots, _ = fields_ref.shape

    def fetches(s):
        pairs = ((fields_hbm, fields_ref), (recent_hbm, recent_ref), (older_hbm, older_ref))
        return [
            pltpu.make_async_copy(here.at[s], there.at[s], got.at[n, s])
            for n, (here, there) in enumerate(pairs)
        ]

    def store(s):
        return pltpu.make_async_copy(fields_ref.at[s], base_hbm.at[s], sent.at[s])

    for s in range(species):
        for copy in fetches(s):
            copy.start()
    slot = lax.broadcasted_iota(jnp.int32, (slots, slots), 0)
    keep = (destination_ref[...] == lax.axis_index(TEAM)) & (target_ref[...] == slot)
    keep = keep.astype(jnp.bfloat16)
    live = lax.broadcasted_iota(jnp.int32, (slots, 1), 0) < live_ref[0]
    live = jnp.where(live, 1.0, 0.0)

    def one(s, carry):
        for copy in fetches(s):
            copy.wait()
        recent = jnp.dot(keep, recent_ref[s], preferred_element_type=jnp.float32)
        older = jnp.dot(keep, older_ref[s], preferred_element_type=jnp.float32)
        kept = recent * (-16.0 / 12.0 * step_size) + older * (5.0 / 12.0 * step_size)
        fields_ref[s] = (fields_ref[s] + kept) * live
        store(s).start()
        return carry

    lax.fori_loop(0, species, one, 0)
    for s in range(species):
        store(s).wait()


def plane_weights():
    weights = np.zeros((6 * LANES, 3 * FACE), np.float32)
    for cell in range(FACE):
        y, z = divmod(cell, TE)
        for d, at, step in ((0, y, TE), (1, z, 1)):
            for way in (-1, 1):
                if 0 <= at + way < TE:
                    rows = [cell + way * step, FACE + cell + way * step]
                else:
                    face = (2 + (way > 0)) if d == 0 else (way > 0)
                    spot = 2 * FACE + face * 2 * TE + (z if d == 0 else y)
                    rows = [spot, spot + TE, spot + LANES, spot + LANES + TE]
                weights[rows, cell] += 1.0
                weights[rows, (1 + d) * FACE + cell] += way
        weights[[cell, FACE + cell], cell] -= 6.0
    return weights


def main_kernel(
    live_ref,
    rate_ref,
    table_ref,
    tiles_ref,
    velocity_ref,
    weights_hbm,
    fields_hbm,
    ghosts_hbm,
    rims_hbm,
    base_hbm,
    new_fields_hbm,
    new_tend_hbm,
    weights_ref,
    fields_ref,
    rims_ref,
    base_ref,
    new_tend_ref,
    mix_ref,
    wide_ref,
    left_even_ref,
    left_odd_ref,
    fuel_even_ref,
    fuel_odd_ref,
    sums_even_ref,
    sums_odd_ref,
    react_even_ref,
    react_odd_ref,
    got,
    sent,
):
    species, slots, cells = base_ref.shape
    peers = table_ref.shape[0]
    chunk = PLANES * FACE
    chunks = cells // chunk

    def span(c, length, skipped=0):
        return pl.ds(pl.multiple_of(skipped + c * length, LANES), length)

    def bases(c):
        lanes = span(c, chunk)
        return pltpu.make_async_copy(
            base_hbm.at[:, :, lanes], base_ref.at[:, :, lanes], got.at[2, c]
        )

    def cells_in(c):
        lanes, rims, inner = span(c, chunk), span(c, chunk // 2), span(c, chunk, FACE)
        return (
            pltpu.make_async_copy(
                fields_hbm.at[:, :, lanes], fields_ref.at[:, :, inner], got.at[0, c]
            ),
            pltpu.make_async_copy(
                rims_hbm.at[:, :, rims], rims_ref.at[:, :, rims], got.at[1, c]
            ),
        )

    def ends():
        return (
            pltpu.make_async_copy(weights_hbm, weights_ref, got.at[3, 0]),
            pltpu.make_async_copy(
                ghosts_hbm.at[:, :, pl.ds(0, FACE)], fields_ref.at[:, :, pl.ds(0, FACE)], got.at[3, 1]
            ),
            pltpu.make_async_copy(
                ghosts_hbm.at[:, :, pl.ds(FACE, FACE)],
                fields_ref.at[:, :, pl.ds(FACE + cells, FACE)],
                got.at[3, 2],
            ),
        )

    def stores(c):
        lanes = span(c, chunk)
        return (
            pltpu.make_async_copy(
                base_ref.at[:, :, lanes], new_fields_hbm.at[:, :, lanes], sent.at[0, c]
            ),
            pltpu.make_async_copy(
                new_tend_ref.at[:, :, lanes], new_tend_hbm.at[:, :, lanes], sent.at[1, c]
            ),
        )

    for copy in ends():
        copy.start()
    for c in range(2):
        for copy in (*cells_in(c), bases(c)):
            copy.start()

    marks = jnp.concatenate(
        [velocity_ref[...], tiles_ref[...].astype(jnp.float32), jnp.zeros((4, slots), jnp.float32)], axis=0
    ).T
    tiles = marks[:, 3:4].astype(jnp.int32)
    owner = tiles // slots
    wanted = lax.broadcasted_iota(jnp.int32, (slots, peers), 1) == owner % peers
    picked = jnp.dot(
        wanted.astype(jnp.float32),
        table_ref[...],
        precision=lax.Precision.HIGHEST,
        preferred_element_type=jnp.float32,
    )
    lane = lax.broadcasted_iota(jnp.int32, picked.shape, 1)
    spot = owner // peers * LANES + tiles % slots
    thick = jnp.sum(jnp.where(lane == spot, picked, 0.0), axis=1, keepdims=True)
    live = lax.broadcasted_iota(jnp.int32, (slots, 1), 0) < live_ref[0]
    live = jnp.where(live, 1.0, 0.0)
    parts = [viscous * thick * live, live / thick]
    parts += [0.5 * live * marks[:, d : d + 1] for d in range(3)]
    for n, part in enumerate(parts):
        wide_ref[n] = jnp.broadcast_to(part, (slots, LANES))
    main = (species - 1) * slots
    tail = lax.broadcasted_iota(jnp.int32, (slots, LANES), 1)
    main_lane = lax.broadcasted_iota(jnp.int32, (slots, main), 1)
    main_slot = lax.broadcasted_iota(jnp.int32, (slots, main), 0) == main_lane % slots
    tail_slot = lax.broadcasted_iota(jnp.int32, (slots, LANES), 0) == tail % slots
    for s in range(species):
        rows = slice(s * slots, (s + 1) * slots)
        rate = jnp.zeros((slots, main), jnp.float32)
        for k in range(species - 1):
            rate = jnp.where(main_lane // slots == k, rate_ref[s, k], rate)
        rate = jnp.where(main_slot, rate, 0.0)
        high = rate.astype(jnp.bfloat16)
        mix_ref[rows, 0:main] = high
        mix_ref[rows, main : 2 * main] = (rate - high.astype(jnp.float32)).astype(jnp.bfloat16)
        mix_ref[rows, 2 * main : 3 * main] = high
        rate = jnp.where(tail_slot & (tail < 3 * slots), rate_ref[s, species - 1], 0.0)
        high = rate.astype(jnp.bfloat16).astype(jnp.float32)
        rate = jnp.where(tail // slots == 1, rate - high, high)
        mix_ref[rows, 3 * main :] = rate.astype(jnp.bfloat16)
    for fuel_ref in (fuel_even_ref, fuel_odd_ref):
        fuel_ref[3 * main + 3 * slots :, :] = jnp.zeros((LANES - 3 * slots, 2 * FACE), jnp.bfloat16)

    parity = lax.broadcasted_iota(jnp.int32, (slots, 2 * LANES), 1) // TE % 2

    def sums(pair, odd):
        left_ref, sums_ref = ((left_even_ref, sums_even_ref), (left_odd_ref, sums_odd_ref))[odd]
        rims = pl.ds(pl.multiple_of(pair * FACE, FACE), FACE)
        for s in range(species):
            both = rims_ref[s, :, rims]
            for p in range(2):
                lanes = pl.ds(pl.multiple_of((2 * pair + p + 1) * FACE, FACE), FACE)
                rows = slice((p * species + s) * slots, (p * species + s + 1) * slots)
                f = fields_ref[s, :, lanes]
                high = f.astype(jnp.bfloat16)
                left_ref[rows, 0:FACE] = high
                left_ref[rows, FACE : 2 * FACE] = (f - high.astype(jnp.float32)).astype(jnp.bfloat16)
                left_ref[rows, 2 * FACE :] = jnp.where(parity == p, both, jnp.zeros_like(both))
        sums_ref[...] = jnp.dot(left_ref[...], weights_ref[...], preferred_element_type=jnp.float32)

        fuel_ref, react_ref = ((fuel_even_ref, react_even_ref), (fuel_odd_ref, react_odd_ref))[odd]
        both = pl.ds(pl.multiple_of((2 * pair + 1) * FACE, FACE), 2 * FACE)
        over = jnp.concatenate([wide_ref[1]] * 4, axis=1)
        burning = fields_ref[0, :, both] * fields_ref[1, :, both] * over
        for k in range(species):
            fuel = fields_ref[k, :, both] * burning
            high = fuel.astype(jnp.bfloat16)
            low = (fuel - high.astype(jnp.float32)).astype(jnp.bfloat16)
            for n, part in enumerate((high, high, low)):
                start = n * main + k * slots if k < species - 1 else 3 * main + n * slots
                fuel_ref[start : start + slots, :] = part
        react_ref[...] = jnp.dot(mix_ref[...], fuel_ref[...], preferred_element_type=jnp.float32)

    def finish(pair, odd):
        sums_ref, react_ref = ((sums_even_ref, react_even_ref), (sums_odd_ref, react_odd_ref))[odd]
        for p in range(2):
            inner, before, here, after = (
                pl.ds(pl.multiple_of((2 * pair + p + n) * FACE, FACE), FACE) for n in (0, 0, 1, 2)
            )
            for g in range(slots // 16):
                rows = slice(g * 16, (g + 1) * 16)
                smooth, vx, vy, vz = (
                    jnp.concatenate([wide_ref[n, rows, :]] * 2, axis=1) for n in (0, 2, 3, 4)
                )
                for s in range(species):
                    low, high = fields_ref[s, rows, before], fields_ref[s, rows, after]
                    line = s * slots + g * 16
                    react = react_ref[line : line + 16, p * FACE : (p + 1) * FACE]
                    line += p * species * slots
                    total, along_y, along_z = (
                        sums_ref[line : line + 16, d * FACE : (d + 1) * FACE] for d in range(3)
                    )
                    tend = smooth * (total + (low + high)) - vx * (high - low)
                    tend = (tend - vy * along_y) + (react - vz * along_z)
                    base_ref[s, rows, inner] += (step_size * 23.0 / 12.0) * tend
                    new_tend_ref[s, rows, inner] = tend.astype(jnp.bfloat16)

    for copy in (*ends(), *cells_in(0)):
        copy.wait()
    sums(0, 0)

    def four(c, carry):
        @pl.when(c + 2 < chunks)
        def _():
            for copy in (*cells_in(c + 2), bases(c + 2)):
                copy.start()

        bases(c).wait()
        sums(2 * c + 1, 1)
        finish(2 * c, 0)

        @pl.when(c + 1 < chunks)
        def _():
            for copy in cells_in(c + 1):
                copy.wait()

        sums(jnp.minimum(2 * c + 2, 2 * (chunks - 1)), 0)
        finish(2 * c + 1, 1)
        for copy in stores(c):
            copy.start()
        return carry

    lax.fori_loop(0, chunks, four, 0)
    for c in range(chunks):
        for copy in stores(c):
            copy.wait()


def add_kernel(
    live_ref, table_ref, fields_hbm, arrived_hbm, out_hbm, fields_ref, arrived_ref, got, sent
):
    species, peers = arrived_ref.shape[:2]
    slots = fields_ref.shape[1]

    def fetches(s):
        part = arrived_hbm.at[:, pl.ds(s * ROWS, ROWS)]
        return (
            pltpu.make_async_copy(part, arrived_ref.at[s], got.at[0, s]),
            pltpu.make_async_copy(fields_hbm.at[s], fields_ref.at[s], got.at[1, s]),
        )

    def store(s):
        return pltpu.make_async_copy(fields_ref.at[s], out_hbm.at[s], sent.at[s])

    for s in range(AHEAD):
        for copy in fetches(s):
            copy.start()
    me, first = lax.axis_index(TEAM), pl.multiple_of(lax.axis_index("grp") * LANES, LANES)
    notes = table_ref[:, pl.ds(first, LANES)]
    destination = notes[:, slots : 2 * slots]
    target = notes[:, 2 * slots : 3 * slots]
    peer = lax.broadcasted_iota(jnp.int32, (peers, slots), 0)
    mine = (destination == me.astype(jnp.float32)) & (peer != me)
    slot = jnp.max(jnp.where(mine, target, -1.0), axis=1, keepdims=True)
    index = lax.broadcasted_iota(jnp.int32, (peers, slots), 1)
    hot = (slot == index.astype(jnp.float32)) & (index < live_ref[0])
    hot = jnp.where(hot, step_size / SCALE, 0.0)
    hot = jnp.concatenate([hot, hot], axis=0).T.astype(jnp.bfloat16)
    for s in range(species):
        if s + AHEAD < species:
            for copy in fetches(s + AHEAD):
                copy.start()
        for copy in fetches(s):
            copy.wait()
        flat = arrived_ref.at[s].reshape(peers * ROWS, LANES)
        for c in range(ROWS // 2):
            lanes = slice(c * 2 * LANES, (c + 1) * 2 * LANES)
            arrived = jnp.concatenate(
                [flat[pl.ds(2 * c + k, peers, stride=ROWS), :] for k in range(2)], axis=1
            )
            high = arrived.astype(jnp.bfloat16)
            low = (arrived - high.astype(jnp.float32)).astype(jnp.bfloat16)
            fields_ref[s, :, lanes] += jnp.dot(
                hot, jnp.concatenate([high, low], axis=0), preferred_element_type=jnp.float32
            )
        store(s).start()
    for s in range(species):
        store(s).wait()


def smem():
    return pl.BlockSpec(memory_space=pltpu.SMEM)


def whole(shape):
    return pl.BlockSpec(shape, lambda i: (0,) * len(shape))


def params(mib, semantics=None):
    return pltpu.CompilerParams(vmem_limit_bytes=mib << 20, dimension_semantics=semantics)


def local(
    fields,
    ghosts,
    velocity,
    rate_matrix,
    recent_tend,
    older_tend,
    destination,
    target_slot,
    live_counts,
    tile_ids,
    sensor,
    flame_flags,
):
    slots, species, cells = fields.shape
    peers = lax.axis_size(TEAM)
    brick = sensor.shape[0]
    fields, ghosts, recent, older = (
        a.transpose(1, 0, 2) for a in (fields, ghosts, recent_tend, older_tend)
    )
    moves = (destination.reshape(1, slots), target_slot.reshape(1, slots))

    raw = pl.pallas_call(
        raw_kernel,
        name="raw_sensor",
        out_shape=jax.ShapeDtypeStruct(sensor.shape, jnp.bfloat16),
        in_specs=[smem(), pl.BlockSpec(memory_space=pltpu.VMEM)],
        out_specs=pl.BlockSpec(memory_space=pltpu.VMEM),
        compiler_params=params(58),
    )(flame_flags, sensor)
    below = passed_along(raw, "pen", 1)
    above = passed_along(raw, "pen", -1)

    anywhere = pl.BlockSpec(memory_space=pl.ANY)
    in_hbm = pl.BlockSpec(memory_space=pltpu.HBM)
    vmem = pl.BlockSpec(memory_space=pltpu.VMEM)
    outgoing = pl.pallas_call(
        send_kernel,
        name="outgoing_histories",
        out_shape=jax.ShapeDtypeStruct((peers, species * ROWS, LANES), jnp.float32),
        in_specs=[vmem, in_hbm, in_hbm],
        out_specs=vmem,
        scratch_shapes=[
            pltpu.VMEM(recent.shape, jnp.bfloat16),
            pltpu.VMEM(older.shape, jnp.bfloat16),
            pltpu.SemaphoreType.DMA((2, species)),
        ],
        compiler_params=params(50),
        cost_estimate=pl.CostEstimate(flops=0, bytes_accessed=8 << 20, transcendentals=0),
    )(destination.reshape(1, slots), recent, older)
    outgoing = outgoing.astype(jnp.float16)

    shape = jax.ShapeDtypeStruct((species, slots, cells), jnp.float32)
    rims = jax.ShapeDtypeStruct((species, slots, TE * LANES), jnp.bfloat16)
    base = pl.pallas_call(
        base_kernel,
        name="kept_histories",
        out_shape=shape,
        in_specs=[smem(), vmem, vmem] + [anywhere] * 3,
        out_specs=anywhere,
        scratch_shapes=[
            pltpu.VMEM(shape.shape, jnp.float32),
            pltpu.VMEM(shape.shape, jnp.bfloat16),
            pltpu.VMEM(shape.shape, jnp.bfloat16),
            pltpu.SemaphoreType.DMA((3, species)),
            pltpu.SemaphoreType.DMA((species,)),
        ],
        compiler_params=params(58),
        cost_estimate=pl.CostEstimate(flops=0, bytes_accessed=18 << 20, transcendentals=0),
    )(live_counts, *moves, fields, recent, older)
    rims = pl.pallas_call(
        rims_kernel,
        name="rims",
        out_shape=rims,
        in_specs=[anywhere],
        out_specs=anywhere,
        scratch_shapes=[
            pltpu.VMEM(ghosts.shape, jnp.float32),
            pltpu.VMEM(rims.shape, jnp.bfloat16),
            pltpu.SemaphoreType.DMA((species,)),
            pltpu.SemaphoreType.DMA((species,)),
        ],
        compiler_params=params(58),
        cost_estimate=pl.CostEstimate(flops=0, bytes_accessed=8 << 20, transcendentals=0),
    )(ghosts)
    below, above, rims = lax.optimization_barrier((below, above, rims))

    filtered, row = pl.pallas_call(
        filter_kernel,
        name="filtered_sensor",
        out_shape=(
            jax.ShapeDtypeStruct(sensor.shape, jnp.float32),
            jax.ShapeDtypeStruct((1, LANES), jnp.float32),
        ),
        in_specs=[smem()] + [vmem] * 6,
        out_specs=(vmem, vmem),
        compiler_params=params(32),
        cost_estimate=pl.CostEstimate(flops=0, bytes_accessed=4 << 20, transcendentals=0),
    )(flame_flags, jnp.asarray(banded(brick, brick)), sensor, below, above, *moves)
    rows = gathered(row, ("pen",))
    rows, outgoing, base = lax.optimization_barrier((rows, outgoing, base))
    arrived = lax.all_to_all(outgoing, TEAM, split_axis=0, concat_axis=0, tiled=True)
    table = gathered(rows, ("grp", "mig"))
    arrived = arrived.astype(jnp.float32)

    weights = jnp.asarray(plane_weights(), jnp.bfloat16)
    left = pltpu.VMEM((2 * species * slots, 6 * LANES), jnp.bfloat16)
    sums = pltpu.VMEM((2 * species * slots, 3 * FACE), jnp.float32)
    depth = 3 * (species - 1) * slots + LANES
    fuel = pltpu.VMEM((depth, 2 * FACE), jnp.bfloat16)
    react = pltpu.VMEM((species * slots, 2 * FACE), jnp.float32)
    new_fields, new_tend = pl.pallas_call(
        main_kernel,
        name="updates",
        out_shape=(shape, jax.ShapeDtypeStruct(shape.shape, jnp.bfloat16)),
        in_specs=[smem()] * 2 + [vmem] * 3 + [anywhere] * 5,
        out_specs=(anywhere, anywhere),
        scratch_shapes=[
            pltpu.VMEM(weights.shape, jnp.bfloat16),
            pltpu.VMEM((species, slots, cells + 2 * FACE), jnp.float32),
            pltpu.VMEM(rims.shape, jnp.bfloat16),
            pltpu.VMEM(shape.shape, jnp.float32),
            pltpu.VMEM(shape.shape, jnp.bfloat16),
            pltpu.VMEM((species * slots, depth), jnp.bfloat16),
            pltpu.VMEM((5, slots, LANES), jnp.float32),
            left,
            left,
            fuel,
            fuel,
            sums,
            sums,
            react,
            react,
            pltpu.SemaphoreType.DMA((4, TE // PLANES)),
            pltpu.SemaphoreType.DMA((2, TE // PLANES)),
        ],
        compiler_params=params(58),
        cost_estimate=pl.CostEstimate(flops=0, bytes_accessed=40 << 20, transcendentals=0),
    )(
        live_counts,
        rate_matrix,
        table,
        tile_ids.reshape(1, slots),
        velocity,
        weights,
        fields,
        ghosts,
        rims,
        base,
    )

    new_fields = pl.pallas_call(
        add_kernel,
        name="arrived_histories",
        out_shape=shape,
        in_specs=[smem(), vmem, anywhere, anywhere],
        out_specs=anywhere,
        scratch_shapes=[
            pltpu.VMEM(shape.shape, jnp.float32),
            pltpu.VMEM((species, peers, ROWS, LANES), jnp.float32),
            pltpu.SemaphoreType.DMA((2, species)),
            pltpu.SemaphoreType.DMA((species,)),
        ],
        compiler_params=params(58),
        cost_estimate=pl.CostEstimate(flops=0, bytes_accessed=12 << 20, transcendentals=0),
    )(live_counts, table, new_fields, arrived)
    return new_fields.transpose(1, 0, 2), new_tend.transpose(1, 0, 2), filtered


def gathered(row, axes):
    for axis in axes:
        count = lax.axis_size(axis)
        here = lax.axis_index(axis)
        rows = [row] + [passed_along(row, axis, by) for by in range(1, count)]
        height, width = row.shape
        if axis == "grp":
            table = jnp.zeros((height, count * width), row.dtype)
        else:
            table = jnp.zeros((count * height, width), row.dtype)
        for by, part in enumerate(rows):
            place = (here - by) % count
            place = (0, place * width) if axis == "grp" else (place * height, 0)
            table = lax.dynamic_update_slice(table, part, place)
        row = table
    return row


def solution(mesh):
    split = P(EVERY, None, None)
    return jax.shard_map(
        local,
        mesh=mesh,
        in_specs=(
            split,
            split,
            P(None, EVERY),
            P(),
            split,
            split,
            P(EVERY),
            P(EVERY),
            P(EVERY),
            P(EVERY),
            P("pen", ("grp", "mig")),
            P("pen", ("grp", "mig")),
        ),
        out_specs=(split, split, P("pen", ("grp", "mig"))),
        check_vma=False,
    )
```

```python
import jax
import jax.numpy as jnp
import numpy as np
from jax import lax
from jax.experimental import pallas as pl
from jax.experimental.pallas import tpu as pltpu
from jax.sharding import PartitionSpec as P

TE = 16
TZ = 2
TCOL = 16
FACE = TE * TE
CELLS = TE**3
LANES = 128
ROWS = CELLS // LANES

viscous = 0.05
step_size = 0.25
thicken = 5.0

SCALE = 4096.0
PLANES = 4
AHEAD = 4

EVERY = ("grp", "mig", "pen")
TEAM = ("mig", "pen")


def passed_along(x, axis, by):
    peers = lax.axis_size(axis)
    return lax.ppermute(x, axis, [(i, (i + by) % peers) for i in range(peers)])


def banded(brick_rows, reach):
    sigma = reach / 2.0
    offsets = np.arange(-reach, reach + 1, dtype=np.float64)
    total = np.sum(np.exp(-offsets * offsets / (2.0 * sigma * sigma)))
    row = np.arange(brick_rows)[:, None]
    col = np.arange(brick_rows + 2 * reach)[None, :]
    offset = (col - reach - row).astype(np.float64)
    weights = np.where(np.abs(offset) <= reach, np.exp(-offset * offset / (2.0 * sigma * sigma)), 0)
    return (weights / total).astype(np.float32)


def raw_kernel(flags_ref, sensor_ref, raw_ref):
    for r in range(TZ):
        for k in range(TCOL):
            rows, cols = slice(r * TE, (r + 1) * TE), slice(k * FACE, (k + 1) * FACE)
            flag = flags_ref[r, k].astype(jnp.float32)
            raw_ref[rows, cols] = (sensor_ref[rows, cols] * flag).astype(jnp.bfloat16)


def filter_kernel(
    flags_ref,
    weights_ref,
    sensor_ref,
    below_ref,
    above_ref,
    destination_ref,
    target_ref,
    filtered_ref,
    row_ref,
):
    lane = lax.broadcasted_iota(jnp.int32, (1, LANES), 1)
    slots = destination_ref.shape[1]
    row = jnp.concatenate(
        [
            jnp.zeros((1, slots), jnp.float32),
            destination_ref[...].astype(jnp.float32),
            target_ref[...].astype(jnp.float32),
            jnp.zeros((1, LANES - 3 * slots), jnp.float32),
        ],
        axis=1,
    )
    brick = sensor_ref.shape[0]
    for k in range(TCOL):
        cols = slice(k * FACE, (k + 1) * FACE)
        own = [
            sensor_ref[r * TE : (r + 1) * TE, cols] * flags_ref[r, k].astype(jnp.float32)
            for r in range(TZ)
        ]
        widened = jnp.concatenate(
            [below_ref[:, cols].astype(jnp.float32)] + own + [above_ref[:, cols].astype(jnp.float32)],
            axis=0,
        )
        filtered = jnp.dot(
            weights_ref[...],
            widened,
            precision=lax.Precision.HIGHEST,
            preferred_element_type=jnp.float32,
        )
        filtered_ref[:, cols] = filtered
        clipped = jnp.minimum(filtered, 1.0)
        for r in range(TZ):
            total = jnp.sum(
                jnp.sum(clipped[r * TE : (r + 1) * TE], axis=0, keepdims=True), axis=1, keepdims=True
            )
            thick = 1.0 + (thicken - 1.0) * (total / float(TE * FACE))
            row = jnp.where(lane == r * TCOL + k, thick, row)
    row_ref[...] = row


def send_kernel(
    destination_ref, recent_hbm, older_hbm, out_ref, recent_ref, older_ref, got
):
    species, slots, _ = recent_ref.shape
    peers = out_ref.shape[0]

    def fetches(s):
        return (
            pltpu.make_async_copy(recent_hbm.at[s], recent_ref.at[s], got.at[0, s]),
            pltpu.make_async_copy(older_hbm.at[s], older_ref.at[s], got.at[1, s]),
        )

    for s in range(AHEAD):
        for copy in fetches(s):
            copy.start()
    peer = lax.broadcasted_iota(jnp.int32, (peers, slots), 0)
    hot = ((destination_ref[...] == peer) & (peer != lax.axis_index(TEAM))).astype(jnp.bfloat16)
    flat = out_ref.reshape(peers * species * ROWS, LANES)
    for s in range(species):
        if s + AHEAD < species:
            for copy in fetches(s + AHEAD):
                copy.start()
        for copy in fetches(s):
            copy.wait()
        recent = jnp.dot(hot, recent_ref[s], preferred_element_type=jnp.float32)
        older = jnp.dot(hot, older_ref[s], preferred_element_type=jnp.float32)
        mixed = recent * (-16.0 / 12.0 * SCALE) + older * (5.0 / 12.0 * SCALE)
        for k in range(ROWS):
            flat[pl.ds(s * ROWS + k, peers, stride=species * ROWS), :] = mixed[
                :, k * LANES : (k + 1) * LANES
            ]


def rims_kernel(ghosts_hbm, rims_hbm, ghosts_ref, rims_ref, got, sent):
    species, slots, _ = ghosts_ref.shape

    def fetch(s):
        return pltpu.make_async_copy(ghosts_hbm.at[s], ghosts_ref.at[s], got.at[s])

    def store(s):
        return pltpu.make_async_copy(rims_ref.at[s], rims_hbm.at[s], sent.at[s])

    for s in range(species):
        fetch(s).start()
    quarter = lax.broadcasted_iota(jnp.int32, (slots, LANES), 1) // (2 * TE)

    def one(s, carry):
        fetch(s).wait()
        for block in range(2):
            faces = [
                ghosts_ref[s, :, w * FACE + block * LANES : w * FACE + (block + 1) * LANES]
                for w in (4, 5, 2, 3)
            ]
            for q in range(4):
                rim = faces[0]
                for n in range(4):
                    turned = pltpu.roll(faces[n], (n - q) % 4 * 2 * TE, 1) if n != q else faces[n]
                    rim = turned if n == 0 else jnp.where(quarter == n, turned, rim)
                high = rim.astype(jnp.bfloat16)
                low = (rim - high.astype(jnp.float32)).astype(jnp.bfloat16)
                start = (block * 4 + q) * 2 * LANES
                rims_ref[s, :, start : start + LANES] = high
                rims_ref[s, :, start + LANES : start + 2 * LANES] = low
        store(s).start()
        return carry

    lax.fori_loop(0, species, one, 0)
    for s in range(species):
        store(s).wait()


def base_kernel(
    live_ref,
    destination_ref,
    target_ref,
    fields_hbm,
    recent_hbm,
    older_hbm,
    base_hbm,
    fields_ref,
    recent_ref,
    older_ref,
    got,
    sent,
):
    species, slots, _ = fields_ref.shape

    def fetches(s):
        pairs = ((fields_hbm, fields_ref), (recent_hbm, recent_ref), (older_hbm, older_ref))
        return [
            pltpu.make_async_copy(here.at[s], there.at[s], got.at[n, s])
            for n, (here, there) in enumerate(pairs)
        ]

    def store(s):
        return pltpu.make_async_copy(fields_ref.at[s], base_hbm.at[s], sent.at[s])

    for s in range(species):
        for copy in fetches(s):
            copy.start()
    slot = lax.broadcasted_iota(jnp.int32, (slots, slots), 0)
    keep = (destination_ref[...] == lax.axis_index(TEAM)) & (target_ref[...] == slot)
    keep = keep.astype(jnp.bfloat16)
    live = lax.broadcasted_iota(jnp.int32, (slots, 1), 0) < live_ref[0]
    live = jnp.where(live, 1.0, 0.0)

    def one(s, carry):
        for copy in fetches(s):
            copy.wait()
        recent = jnp.dot(keep, recent_ref[s], preferred_element_type=jnp.float32)
        older = jnp.dot(keep, older_ref[s], preferred_element_type=jnp.float32)
        kept = recent * (-16.0 / 12.0 * step_size) + older * (5.0 / 12.0 * step_size)
        fields_ref[s] = (fields_ref[s] + kept) * live
        store(s).start()
        return carry

    lax.fori_loop(0, species, one, 0)
    for s in range(species):
        store(s).wait()


def plane_weights():
    weights = np.zeros((6 * LANES, 3 * FACE), np.float32)
    for cell in range(FACE):
        y, z = divmod(cell, TE)
        for d, at, step in ((0, y, TE), (1, z, 1)):
            for way in (-1, 1):
                if 0 <= at + way < TE:
                    rows = [cell + way * step, FACE + cell + way * step]
                else:
                    face = (2 + (way > 0)) if d == 0 else (way > 0)
                    spot = 2 * FACE + face * 2 * TE + (z if d == 0 else y)
                    rows = [spot, spot + TE, spot + LANES, spot + LANES + TE]
                weights[rows, cell] += 1.0
                weights[rows, (1 + d) * FACE + cell] += way
        weights[[cell, FACE + cell], cell] -= 6.0
    return weights


def main_kernel(
    live_ref,
    rate_ref,
    table_ref,
    tiles_ref,
    velocity_ref,
    weights_hbm,
    fields_hbm,
    ghosts_hbm,
    rims_hbm,
    base_hbm,
    new_fields_hbm,
    new_tend_hbm,
    weights_ref,
    fields_ref,
    rims_ref,
    base_ref,
    new_tend_ref,
    mix_ref,
    wide_ref,
    fuel_even_ref,
    fuel_odd_ref,
    react_even_ref,
    react_odd_ref,
    got,
    sent,
):
    species, slots, cells = base_ref.shape
    peers = table_ref.shape[0]
    chunk = PLANES * FACE
    chunks = cells // chunk

    def span(c, length, skipped=0):
        return pl.ds(pl.multiple_of(skipped + c * length, LANES), length)

    def bases(c):
        lanes = span(c, chunk)
        return pltpu.make_async_copy(
            base_hbm.at[:, :, lanes], base_ref.at[:, :, lanes], got.at[2, c]
        )

    def cells_in(c):
        lanes, rims, inner = span(c, chunk), span(c, chunk // 2), span(c, chunk, FACE)
        return (
            pltpu.make_async_copy(
                fields_hbm.at[:, :, lanes], fields_ref.at[:, :, inner], got.at[0, c]
            ),
            pltpu.make_async_copy(
                rims_hbm.at[:, :, rims], rims_ref.at[:, :, rims], got.at[1, c]
            ),
        )

    def ends():
        return (
            pltpu.make_async_copy(weights_hbm, weights_ref, got.at[3, 0]),
            pltpu.make_async_copy(
                ghosts_hbm.at[:, :, pl.ds(0, FACE)], fields_ref.at[:, :, pl.ds(0, FACE)], got.at[3, 1]
            ),
            pltpu.make_async_copy(
                ghosts_hbm.at[:, :, pl.ds(FACE, FACE)],
                fields_ref.at[:, :, pl.ds(FACE + cells, FACE)],
                got.at[3, 2],
            ),
        )

    def stores(c):
        lanes = span(c, chunk)
        return (
            pltpu.make_async_copy(
                base_ref.at[:, :, lanes], new_fields_hbm.at[:, :, lanes], sent.at[0, c]
            ),
            pltpu.make_async_copy(
                new_tend_ref.at[:, :, lanes], new_tend_hbm.at[:, :, lanes], sent.at[1, c]
            ),
        )

    for copy in ends():
        copy.start()
    for c in range(2):
        for copy in (*cells_in(c), bases(c)):
            copy.start()

    marks = jnp.concatenate(
        [velocity_ref[...], tiles_ref[...].astype(jnp.float32), jnp.zeros((4, slots), jnp.float32)], axis=0
    ).T
    tiles = marks[:, 3:4].astype(jnp.int32)
    owner = tiles // slots
    wanted = lax.broadcasted_iota(jnp.int32, (slots, peers), 1) == owner % peers
    picked = jnp.dot(
        wanted.astype(jnp.float32),
        table_ref[...],
        precision=lax.Precision.HIGHEST,
        preferred_element_type=jnp.float32,
    )
    lane = lax.broadcasted_iota(jnp.int32, picked.shape, 1)
    spot = owner // peers * LANES + tiles % slots
    thick = jnp.sum(jnp.where(lane == spot, picked, 0.0), axis=1, keepdims=True)
    live = lax.broadcasted_iota(jnp.int32, (slots, 1), 0) < live_ref[0]
    live = jnp.where(live, 1.0, 0.0)
    parts = [viscous * thick * live, live / thick]
    parts += [0.5 * live * marks[:, d : d + 1] for d in range(3)]
    for n, part in enumerate(parts):
        wide_ref[n] = jnp.broadcast_to(part, (slots, LANES))
    main = (species - 1) * slots
    tail = lax.broadcasted_iota(jnp.int32, (slots, LANES), 1)
    main_lane = lax.broadcasted_iota(jnp.int32, (slots, main), 1)
    main_slot = lax.broadcasted_iota(jnp.int32, (slots, main), 0) == main_lane % slots
    tail_slot = lax.broadcasted_iota(jnp.int32, (slots, LANES), 0) == tail % slots
    for s in range(species):
        rows = slice(s * slots, (s + 1) * slots)
        rate = jnp.zeros((slots, main), jnp.float32)
        for k in range(species - 1):
            rate = jnp.where(main_lane // slots == k, rate_ref[s, k], rate)
        rate = jnp.where(main_slot, rate, 0.0)
        high = rate.astype(jnp.bfloat16)
        mix_ref[rows, 0:main] = high
        mix_ref[rows, main : 2 * main] = (rate - high.astype(jnp.float32)).astype(jnp.bfloat16)
        mix_ref[rows, 2 * main : 3 * main] = high
        rate = jnp.where(tail_slot & (tail < 3 * slots), rate_ref[s, species - 1], 0.0)
        high = rate.astype(jnp.bfloat16).astype(jnp.float32)
        rate = jnp.where(tail // slots == 1, rate - high, high)
        mix_ref[rows, 3 * main :] = rate.astype(jnp.bfloat16)
    for fuel_ref in (fuel_even_ref, fuel_odd_ref):
        fuel_ref[3 * main + 3 * slots :, :] = jnp.zeros((LANES - 3 * slots, 2 * FACE), jnp.bfloat16)

    parity = lax.broadcasted_iota(jnp.int32, (slots, 2 * LANES), 1) // TE % 2

    def burn(pair, odd):
        fuel_ref, react_ref = ((fuel_even_ref, react_even_ref), (fuel_odd_ref, react_odd_ref))[odd]
        both = pl.ds(pl.multiple_of((2 * pair + 1) * FACE, FACE), 2 * FACE)
        over = jnp.concatenate([wide_ref[1]] * 4, axis=1)
        burning = fields_ref[0, :, both] * fields_ref[1, :, both] * over
        for k in range(species):
            fuel = fields_ref[k, :, both] * burning
            high = fuel.astype(jnp.bfloat16)
            low = (fuel - high.astype(jnp.float32)).astype(jnp.bfloat16)
            for n, part in enumerate((high, high, low)):
                start = n * main + k * slots if k < species - 1 else 3 * main + n * slots
                fuel_ref[start : start + slots, :] = part
        react_ref[...] = jnp.dot(mix_ref[...], fuel_ref[...], preferred_element_type=jnp.float32)

    def finish(pair, odd):
        react_ref = (react_even_ref, react_odd_ref)[odd]
        rims = pl.ds(pl.multiple_of(pair * FACE, FACE), FACE)
        planes = [pl.ds(pl.multiple_of((2 * pair + n) * FACE, FACE), FACE) for n in range(4)]
        for s in range(species):
            both = rims_ref[s, :, rims]
            none = jnp.zeros_like(both)
            rim = jnp.concatenate([jnp.where(parity == p, both, none) for p in range(2)], axis=0)
            f = jnp.concatenate([fields_ref[s, :, planes[1 + p]] for p in range(2)], axis=0)
            high = f.astype(jnp.bfloat16)
            low = (f - high.astype(jnp.float32)).astype(jnp.bfloat16)
            sums = jnp.dot(
                jnp.concatenate([high, low, rim], axis=1),
                weights_ref[...],
                preferred_element_type=jnp.float32,
            )
            for p in range(2):
                for g in range(slots // 16):
                    rows = slice(g * 16, (g + 1) * 16)
                    smooth, vx, vy, vz = (
                        jnp.concatenate([wide_ref[n, rows, :]] * 2, axis=1) for n in (0, 2, 3, 4)
                    )
                    before, after = (fields_ref[s, rows, planes[p + n]] for n in (0, 2))
                    line = p * slots + g * 16
                    total, along_y, along_z = (
                        sums[line : line + 16, d * FACE : (d + 1) * FACE] for d in range(3)
                    )
                    line = s * slots + g * 16
                    react = react_ref[line : line + 16, p * FACE : (p + 1) * FACE]
                    tend = smooth * (total + (before + after)) - vx * (after - before)
                    tend = (tend - vy * along_y) + (react - vz * along_z)
                    base_ref[s, rows, planes[p]] += (step_size * 23.0 / 12.0) * tend
                    new_tend_ref[s, rows, planes[p]] = tend.astype(jnp.bfloat16)

    for copy in (*ends(), *cells_in(0)):
        copy.wait()
    burn(0, 0)

    def four(c, carry):
        @pl.when(c + 2 < chunks)
        def _():
            for copy in (*cells_in(c + 2), bases(c + 2)):
                copy.start()

        bases(c).wait()
        burn(2 * c + 1, 1)
        finish(2 * c, 0)

        @pl.when(c + 1 < chunks)
        def _():
            for copy in cells_in(c + 1):
                copy.wait()

        burn(jnp.minimum(2 * c + 2, 2 * (chunks - 1)), 0)
        finish(2 * c + 1, 1)
        for copy in stores(c):
            copy.start()
        return carry

    lax.fori_loop(0, chunks, four, 0)
    for c in range(chunks):
        for copy in stores(c):
            copy.wait()


def add_kernel(
    live_ref, table_ref, fields_hbm, arrived_hbm, out_hbm, fields_ref, arrived_ref, got, sent
):
    species, peers = arrived_ref.shape[:2]
    slots = fields_ref.shape[1]

    def fetches(s):
        part = arrived_hbm.at[:, pl.ds(s * ROWS, ROWS)]
        return (
            pltpu.make_async_copy(part, arrived_ref.at[s], got.at[0, s]),
            pltpu.make_async_copy(fields_hbm.at[s], fields_ref.at[s], got.at[1, s]),
        )

    def store(s):
        return pltpu.make_async_copy(fields_ref.at[s], out_hbm.at[s], sent.at[s])

    for s in range(AHEAD):
        for copy in fetches(s):
            copy.start()
    me, first = lax.axis_index(TEAM), pl.multiple_of(lax.axis_index("grp") * LANES, LANES)
    notes = table_ref[:, pl.ds(first, LANES)]
    destination = notes[:, slots : 2 * slots]
    target = notes[:, 2 * slots : 3 * slots]
    peer = lax.broadcasted_iota(jnp.int32, (peers, slots), 0)
    mine = (destination == me.astype(jnp.float32)) & (peer != me)
    slot = jnp.max(jnp.where(mine, target, -1.0), axis=1, keepdims=True)
    index = lax.broadcasted_iota(jnp.int32, (peers, slots), 1)
    hot = (slot == index.astype(jnp.float32)) & (index < live_ref[0])
    hot = jnp.where(hot, step_size / SCALE, 0.0)
    hot = jnp.concatenate([hot, hot], axis=0).T.astype(jnp.bfloat16)
    for s in range(species):
        if s + AHEAD < species:
            for copy in fetches(s + AHEAD):
                copy.start()
        for copy in fetches(s):
            copy.wait()
        flat = arrived_ref.at[s].reshape(peers * ROWS, LANES)
        for c in range(ROWS // 2):
            lanes = slice(c * 2 * LANES, (c + 1) * 2 * LANES)
            arrived = jnp.concatenate(
                [flat[pl.ds(2 * c + k, peers, stride=ROWS), :] for k in range(2)], axis=1
            )
            high = arrived.astype(jnp.bfloat16)
            low = (arrived - high.astype(jnp.float32)).astype(jnp.bfloat16)
            fields_ref[s, :, lanes] += jnp.dot(
                hot, jnp.concatenate([high, low], axis=0), preferred_element_type=jnp.float32
            )
        store(s).start()
    for s in range(species):
        store(s).wait()


def smem():
    return pl.BlockSpec(memory_space=pltpu.SMEM)


def whole(shape):
    return pl.BlockSpec(shape, lambda i: (0,) * len(shape))


def params(mib, semantics=None):
    return pltpu.CompilerParams(vmem_limit_bytes=mib << 20, dimension_semantics=semantics)


def local(
    fields,
    ghosts,
    velocity,
    rate_matrix,
    recent_tend,
    older_tend,
    destination,
    target_slot,
    live_counts,
    tile_ids,
    sensor,
    flame_flags,
):
    slots, species, cells = fields.shape
    peers = lax.axis_size(TEAM)
    brick = sensor.shape[0]
    fields, ghosts, recent, older = (
        a.transpose(1, 0, 2) for a in (fields, ghosts, recent_tend, older_tend)
    )
    moves = (destination.reshape(1, slots), target_slot.reshape(1, slots))

    raw = pl.pallas_call(
        raw_kernel,
        name="raw_sensor",
        out_shape=jax.ShapeDtypeStruct(sensor.shape, jnp.bfloat16),
        in_specs=[smem(), pl.BlockSpec(memory_space=pltpu.VMEM)],
        out_specs=pl.BlockSpec(memory_space=pltpu.VMEM),
        compiler_params=params(58),
    )(flame_flags, sensor)
    below = passed_along(raw, "pen", 1)
    above = passed_along(raw, "pen", -1)

    anywhere = pl.BlockSpec(memory_space=pl.ANY)
    in_hbm = pl.BlockSpec(memory_space=pltpu.HBM)
    vmem = pl.BlockSpec(memory_space=pltpu.VMEM)
    outgoing = pl.pallas_call(
        send_kernel,
        name="outgoing_histories",
        out_shape=jax.ShapeDtypeStruct((peers, species * ROWS, LANES), jnp.float32),
        in_specs=[vmem, in_hbm, in_hbm],
        out_specs=vmem,
        scratch_shapes=[
            pltpu.VMEM(recent.shape, jnp.bfloat16),
            pltpu.VMEM(older.shape, jnp.bfloat16),
            pltpu.SemaphoreType.DMA((2, species)),
        ],
        compiler_params=params(50),
        cost_estimate=pl.CostEstimate(flops=0, bytes_accessed=8 << 20, transcendentals=0),
    )(destination.reshape(1, slots), recent, older)
    outgoing = outgoing.astype(jnp.float16)

    shape = jax.ShapeDtypeStruct((species, slots, cells), jnp.float32)
    rims = jax.ShapeDtypeStruct((species, slots, TE * LANES), jnp.bfloat16)
    rims = pl.pallas_call(
        rims_kernel,
        name="rims",
        out_shape=rims,
        in_specs=[anywhere],
        out_specs=anywhere,
        scratch_shapes=[
            pltpu.VMEM(ghosts.shape, jnp.float32),
            pltpu.VMEM(rims.shape, jnp.bfloat16),
            pltpu.SemaphoreType.DMA((species,)),
            pltpu.SemaphoreType.DMA((species,)),
        ],
        compiler_params=params(58),
        cost_estimate=pl.CostEstimate(flops=0, bytes_accessed=8 << 20, transcendentals=0),
    )(ghosts)
    below, above, rims = lax.optimization_barrier((below, above, rims))

    filtered, row = pl.pallas_call(
        filter_kernel,
        name="filtered_sensor",
        out_shape=(
            jax.ShapeDtypeStruct(sensor.shape, jnp.float32),
            jax.ShapeDtypeStruct((1, LANES), jnp.float32),
        ),
        in_specs=[smem()] + [vmem] * 6,
        out_specs=(vmem, vmem),
        compiler_params=params(32),
        cost_estimate=pl.CostEstimate(flops=0, bytes_accessed=4 << 20, transcendentals=0),
    )(flame_flags, jnp.asarray(banded(brick, brick)), sensor, below, above, *moves)
    rows = gathered(row, ("pen",))
    rows, outgoing, live = lax.optimization_barrier((rows, outgoing, live_counts))
    arrived = lax.all_to_all(outgoing, TEAM, split_axis=0, concat_axis=0, tiled=True)
    table = gathered(rows, ("grp", "mig"))
    arrived = arrived.astype(jnp.float32)
    base = pl.pallas_call(
        base_kernel,
        name="kept_histories",
        out_shape=shape,
        in_specs=[smem(), vmem, vmem] + [anywhere] * 3,
        out_specs=anywhere,
        scratch_shapes=[
            pltpu.VMEM(shape.shape, jnp.float32),
            pltpu.VMEM(shape.shape, jnp.bfloat16),
            pltpu.VMEM(shape.shape, jnp.bfloat16),
            pltpu.SemaphoreType.DMA((3, species)),
            pltpu.SemaphoreType.DMA((species,)),
        ],
        compiler_params=params(58),
        cost_estimate=pl.CostEstimate(flops=0, bytes_accessed=18 << 20, transcendentals=0),
    )(live, *moves, fields, recent, older)

    weights = jnp.asarray(plane_weights(), jnp.bfloat16)
    depth = 3 * (species - 1) * slots + LANES
    fuel = pltpu.VMEM((depth, 2 * FACE), jnp.bfloat16)
    react = pltpu.VMEM((species * slots, 2 * FACE), jnp.float32)
    new_fields, new_tend = pl.pallas_call(
        main_kernel,
        name="updates",
        out_shape=(shape, jax.ShapeDtypeStruct(shape.shape, jnp.bfloat16)),
        in_specs=[smem()] * 2 + [vmem] * 3 + [anywhere] * 5,
        out_specs=(anywhere, anywhere),
        scratch_shapes=[
            pltpu.VMEM(weights.shape, jnp.bfloat16),
            pltpu.VMEM((species, slots, cells + 2 * FACE), jnp.float32),
            pltpu.VMEM(rims.shape, jnp.bfloat16),
            pltpu.VMEM(shape.shape, jnp.float32),
            pltpu.VMEM(shape.shape, jnp.bfloat16),
            pltpu.VMEM((species * slots, depth), jnp.bfloat16),
            pltpu.VMEM((5, slots, LANES), jnp.float32),
            fuel,
            fuel,
            react,
            react,
            pltpu.SemaphoreType.DMA((4, TE // PLANES)),
            pltpu.SemaphoreType.DMA((2, TE // PLANES)),
        ],
        compiler_params=params(58),
        cost_estimate=pl.CostEstimate(flops=0, bytes_accessed=40 << 20, transcendentals=0),
    )(
        live_counts,
        rate_matrix,
        table,
        tile_ids.reshape(1, slots),
        velocity,
        weights,
        fields,
        ghosts,
        rims,
        base,
    )

    new_fields = pl.pallas_call(
        add_kernel,
        name="arrived_histories",
        out_shape=shape,
        in_specs=[smem(), vmem, anywhere, anywhere],
        out_specs=anywhere,
        scratch_shapes=[
            pltpu.VMEM(shape.shape, jnp.float32),
            pltpu.VMEM((species, peers, ROWS, LANES), jnp.float32),
            pltpu.SemaphoreType.DMA((2, species)),
            pltpu.SemaphoreType.DMA((species,)),
        ],
        compiler_params=params(58),
        cost_estimate=pl.CostEstimate(flops=0, bytes_accessed=12 << 20, transcendentals=0),
    )(live_counts, table, new_fields, arrived)
    return new_fields.transpose(1, 0, 2), new_tend.transpose(1, 0, 2), filtered


def gathered(row, axes):
    for axis in axes:
        count = lax.axis_size(axis)
        here = lax.axis_index(axis)
        rows = [row] + [passed_along(row, axis, by) for by in range(1, count)]
        height, width = row.shape
        if axis == "grp":
            table = jnp.zeros((height, count * width), row.dtype)
        else:
            table = jnp.zeros((count * height, width), row.dtype)
        for by, part in enumerate(rows):
            place = (here - by) % count
            place = (0, place * width) if axis == "grp" else (place * height, 0)
            table = lax.dynamic_update_slice(table, part, place)
        row = table
    return row


def solution(mesh):
    split = P(EVERY, None, None)
    return jax.shard_map(
        local,
        mesh=mesh,
        in_specs=(
            split,
            split,
            P(None, EVERY),
            P(),
            split,
            split,
            P(EVERY),
            P(EVERY),
            P(EVERY),
            P(EVERY),
            P("pen", ("grp", "mig")),
            P("pen", ("grp", "mig")),
        ),
        out_specs=(split, split, P("pen", ("grp", "mig"))),
        check_vma=False,
    )
```

```python
import jax
import jax.numpy as jnp
import numpy as np
from jax import lax
from jax.experimental import pallas as pl
from jax.experimental.pallas import tpu as pltpu
from jax.sharding import PartitionSpec as P

TE = 16
TZ = 2
TCOL = 16
FACE = TE * TE
CELLS = TE**3
LANES = 128
ROWS = CELLS // LANES

viscous = 0.05
step_size = 0.25
thicken = 5.0

SCALE = 4096.0
PLANES = 4
AHEAD = 4

EVERY = ("grp", "mig", "pen")
TEAM = ("mig", "pen")


def passed_along(x, axis, by):
    peers = lax.axis_size(axis)
    return lax.ppermute(x, axis, [(i, (i + by) % peers) for i in range(peers)])


def banded(brick_rows, reach):
    sigma = reach / 2.0
    offsets = np.arange(-reach, reach + 1, dtype=np.float64)
    total = np.sum(np.exp(-offsets * offsets / (2.0 * sigma * sigma)))
    row = np.arange(brick_rows)[:, None]
    col = np.arange(brick_rows + 2 * reach)[None, :]
    offset = (col - reach - row).astype(np.float64)
    weights = np.where(np.abs(offset) <= reach, np.exp(-offset * offset / (2.0 * sigma * sigma)), 0)
    return (weights / total).astype(np.float32)


def raw_kernel(flags_ref, sensor_ref, raw_ref):
    for r in range(TZ):
        for k in range(TCOL):
            rows, cols = slice(r * TE, (r + 1) * TE), slice(k * FACE, (k + 1) * FACE)
            flag = flags_ref[r, k].astype(jnp.float32)
            raw_ref[rows, cols] = (sensor_ref[rows, cols] * flag).astype(jnp.bfloat16)


def filter_kernel(
    flags_ref,
    weights_ref,
    sensor_ref,
    below_ref,
    above_ref,
    destination_ref,
    target_ref,
    filtered_ref,
    row_ref,
):
    lane = lax.broadcasted_iota(jnp.int32, (1, LANES), 1)
    slots = destination_ref.shape[1]
    row = jnp.concatenate(
        [
            jnp.zeros((1, slots), jnp.float32),
            destination_ref[...].astype(jnp.float32),
            target_ref[...].astype(jnp.float32),
            jnp.zeros((1, LANES - 3 * slots), jnp.float32),
        ],
        axis=1,
    )
    brick = sensor_ref.shape[0]
    for k in range(TCOL):
        cols = slice(k * FACE, (k + 1) * FACE)
        own = [
            sensor_ref[r * TE : (r + 1) * TE, cols] * flags_ref[r, k].astype(jnp.float32)
            for r in range(TZ)
        ]
        widened = jnp.concatenate(
            [below_ref[:, cols].astype(jnp.float32)] + own + [above_ref[:, cols].astype(jnp.float32)],
            axis=0,
        )
        filtered = jnp.dot(
            weights_ref[...],
            widened,
            precision=lax.Precision.HIGHEST,
            preferred_element_type=jnp.float32,
        )
        filtered_ref[:, cols] = filtered
        clipped = jnp.minimum(filtered, 1.0)
        for r in range(TZ):
            total = jnp.sum(
                jnp.sum(clipped[r * TE : (r + 1) * TE], axis=0, keepdims=True), axis=1, keepdims=True
            )
            thick = 1.0 + (thicken - 1.0) * (total / float(TE * FACE))
            row = jnp.where(lane == r * TCOL + k, thick, row)
    row_ref[...] = jnp.broadcast_to(row, row_ref.shape)


def send_kernel(
    destination_ref, recent_hbm, older_hbm, out_ref, recent_ref, older_ref, got
):
    species, slots, _ = recent_ref.shape
    peers = out_ref.shape[0]

    def fetches(s):
        return (
            pltpu.make_async_copy(recent_hbm.at[s], recent_ref.at[s], got.at[0, s]),
            pltpu.make_async_copy(older_hbm.at[s], older_ref.at[s], got.at[1, s]),
        )

    for s in range(AHEAD):
        for copy in fetches(s):
            copy.start()
    peer = lax.broadcasted_iota(jnp.int32, (peers, slots), 0)
    hot = ((destination_ref[...] == peer) & (peer != lax.axis_index(TEAM))).astype(jnp.bfloat16)
    flat = out_ref.reshape(peers * species * ROWS, LANES)
    for s in range(species):
        if s + AHEAD < species:
            for copy in fetches(s + AHEAD):
                copy.start()
        for copy in fetches(s):
            copy.wait()
        recent = jnp.dot(hot, recent_ref[s], preferred_element_type=jnp.float32)
        older = jnp.dot(hot, older_ref[s], preferred_element_type=jnp.float32)
        mixed = recent * (-16.0 / 12.0 * SCALE) + older * (5.0 / 12.0 * SCALE)
        for k in range(ROWS):
            flat[pl.ds(s * ROWS + k, peers, stride=species * ROWS), :] = mixed[
                :, k * LANES : (k + 1) * LANES
            ]


def rims_kernel(ghosts_hbm, rims_hbm, ghosts_ref, rims_ref, got, sent):
    species, slots, _ = ghosts_ref.shape

    def fetch(s):
        return pltpu.make_async_copy(ghosts_hbm.at[s], ghosts_ref.at[s], got.at[s])

    def store(s):
        return pltpu.make_async_copy(rims_ref.at[s], rims_hbm.at[s], sent.at[s])

    for s in range(species):
        fetch(s).start()
    quarter = lax.broadcasted_iota(jnp.int32, (slots, LANES), 1) // (2 * TE)

    def one(s, carry):
        fetch(s).wait()
        for block in range(2):
            faces = [
                ghosts_ref[s, :, w * FACE + block * LANES : w * FACE + (block + 1) * LANES]
                for w in (4, 5, 2, 3)
            ]
            for q in range(4):
                rim = faces[0]
                for n in range(4):
                    turned = pltpu.roll(faces[n], (n - q) % 4 * 2 * TE, 1) if n != q else faces[n]
                    rim = turned if n == 0 else jnp.where(quarter == n, turned, rim)
                high = rim.astype(jnp.bfloat16)
                low = (rim - high.astype(jnp.float32)).astype(jnp.bfloat16)
                start = (block * 4 + q) * 2 * LANES
                rims_ref[s, :, start : start + LANES] = high
                rims_ref[s, :, start + LANES : start + 2 * LANES] = low
        store(s).start()
        return carry

    lax.fori_loop(0, species, one, 0)
    for s in range(species):
        store(s).wait()


def plane_weights():
    weights = np.zeros((6 * LANES, 3 * FACE), np.float32)
    for cell in range(FACE):
        y, z = divmod(cell, TE)
        for d, at, step in ((0, y, TE), (1, z, 1)):
            for way in (-1, 1):
                if 0 <= at + way < TE:
                    rows = [cell + way * step, FACE + cell + way * step]
                else:
                    face = (2 + (way > 0)) if d == 0 else (way > 0)
                    spot = 2 * FACE + face * 2 * TE + (z if d == 0 else y)
                    rows = [spot, spot + TE, spot + LANES, spot + LANES + TE]
                weights[rows, cell] += 1.0
                weights[rows, (1 + d) * FACE + cell] += way
        weights[[cell, FACE + cell], cell] -= 6.0
    return weights


def main_kernel(
    live_ref,
    rate_ref,
    table_ref,
    tiles_ref,
    velocity_ref,
    destination_ref,
    target_ref,
    weights_hbm,
    fields_hbm,
    ghosts_hbm,
    rims_hbm,
    recent_hbm,
    older_hbm,
    new_fields_hbm,
    new_tend_hbm,
    weights_ref,
    fields_ref,
    rims_ref,
    recent_ref,
    older_ref,
    new_fields_ref,
    new_tend_ref,
    mix_ref,
    wide_ref,
    left_even_ref,
    left_odd_ref,
    fuel_even_ref,
    fuel_odd_ref,
    sums_even_ref,
    sums_odd_ref,
    react_even_ref,
    react_odd_ref,
    kept_even_ref,
    kept_odd_ref,
    got,
    sent,
):
    species, slots, cells = new_fields_ref.shape
    devices = table_ref.shape[0]
    chunk = PLANES * FACE
    chunks = cells // chunk

    def span(c, length, skipped=0):
        return pl.ds(pl.multiple_of(skipped + c * length, LANES), length)

    def cells_in(c):
        lanes, rims, inner = span(c, chunk), span(c, chunk // 2), span(c, chunk, FACE)
        return (
            pltpu.make_async_copy(
                fields_hbm.at[:, :, lanes], fields_ref.at[:, :, inner], got.at[0, c]
            ),
            pltpu.make_async_copy(
                rims_hbm.at[:, :, rims], rims_ref.at[:, :, rims], got.at[1, c]
            ),
            pltpu.make_async_copy(
                recent_hbm.at[:, :, lanes], recent_ref.at[:, :, lanes], got.at[2, c]
            ),
            pltpu.make_async_copy(
                older_hbm.at[:, :, lanes], older_ref.at[:, :, lanes], got.at[3, c]
            ),
        )

    def ends():
        return (
            pltpu.make_async_copy(weights_hbm, weights_ref, got.at[4, 0]),
            pltpu.make_async_copy(
                ghosts_hbm.at[:, :, pl.ds(0, FACE)], fields_ref.at[:, :, pl.ds(0, FACE)], got.at[4, 1]
            ),
            pltpu.make_async_copy(
                ghosts_hbm.at[:, :, pl.ds(FACE, FACE)],
                fields_ref.at[:, :, pl.ds(FACE + cells, FACE)],
                got.at[4, 2],
            ),
        )

    def stores(c):
        lanes = span(c, chunk)
        return (
            pltpu.make_async_copy(
                new_fields_ref.at[:, :, lanes], new_fields_hbm.at[:, :, lanes], sent.at[0, c]
            ),
            pltpu.make_async_copy(
                new_tend_ref.at[:, :, lanes], new_tend_hbm.at[:, :, lanes], sent.at[1, c]
            ),
        )

    for copy in ends():
        copy.start()
    for c in range(2):
        for copy in cells_in(c):
            copy.start()

    marks = jnp.concatenate(
        [velocity_ref[...], tiles_ref[...].astype(jnp.float32), jnp.zeros((4, slots), jnp.float32)], axis=0
    ).T
    tiles = marks[:, 3:4].astype(jnp.int32)
    wanted = lax.broadcasted_iota(jnp.int32, (slots, devices), 1) == tiles // slots
    picked = jnp.dot(
        wanted.astype(jnp.float32),
        table_ref[...],
        precision=lax.Precision.HIGHEST,
        preferred_element_type=jnp.float32,
    )
    lane = lax.broadcasted_iota(jnp.int32, picked.shape, 1)
    thick = jnp.sum(jnp.where(lane == tiles % slots, picked, 0.0), axis=1, keepdims=True)
    live = lax.broadcasted_iota(jnp.int32, (slots, 1), 0) < live_ref[0]
    live = jnp.where(live, 1.0, 0.0)
    parts = [viscous * thick * live, live / thick]
    parts += [0.5 * live * marks[:, d : d + 1] for d in range(3)] + [live]
    for n, part in enumerate(parts):
        wide_ref[n] = jnp.broadcast_to(part, (slots, LANES))
    main = (species - 1) * slots
    tail = lax.broadcasted_iota(jnp.int32, (slots, LANES), 1)
    main_lane = lax.broadcasted_iota(jnp.int32, (slots, main), 1)
    main_slot = lax.broadcasted_iota(jnp.int32, (slots, main), 0) == main_lane % slots
    tail_slot = lax.broadcasted_iota(jnp.int32, (slots, LANES), 0) == tail % slots
    for s in range(species):
        rows = slice(s * slots, (s + 1) * slots)
        rate = jnp.zeros((slots, main), jnp.float32)
        for k in range(species - 1):
            rate = jnp.where(main_lane // slots == k, rate_ref[s, k], rate)
        rate = jnp.where(main_slot, rate, 0.0)
        high = rate.astype(jnp.bfloat16)
        mix_ref[rows, 0:main] = high
        mix_ref[rows, main : 2 * main] = (rate - high.astype(jnp.float32)).astype(jnp.bfloat16)
        mix_ref[rows, 2 * main : 3 * main] = high
        rate = jnp.where(tail_slot & (tail < 3 * slots), rate_ref[s, species - 1], 0.0)
        high = rate.astype(jnp.bfloat16).astype(jnp.float32)
        rate = jnp.where(tail // slots == 1, rate - high, high)
        mix_ref[rows, 3 * main :] = rate.astype(jnp.bfloat16)
    for fuel_ref in (fuel_even_ref, fuel_odd_ref):
        fuel_ref[3 * main + 3 * slots :, :] = jnp.zeros((LANES - 3 * slots, 2 * FACE), jnp.bfloat16)

    parity = lax.broadcasted_iota(jnp.int32, (slots, 2 * LANES), 1) // TE % 2
    slot = lax.broadcasted_iota(jnp.int32, (slots, slots), 0)
    keep = (destination_ref[...] == lax.axis_index(TEAM)) & (target_ref[...] == slot)
    keep = keep.astype(jnp.bfloat16)

    def sums(pair, odd):
        left_ref, sums_ref = ((left_even_ref, sums_even_ref), (left_odd_ref, sums_odd_ref))[odd]
        rims = pl.ds(pl.multiple_of(pair * FACE, FACE), FACE)
        for s in range(species):
            both = rims_ref[s, :, rims]
            for p in range(2):
                lanes = pl.ds(pl.multiple_of((2 * pair + p + 1) * FACE, FACE), FACE)
                rows = slice((p * species + s) * slots, (p * species + s + 1) * slots)
                f = fields_ref[s, :, lanes]
                high = f.astype(jnp.bfloat16)
                left_ref[rows, 0:FACE] = high
                left_ref[rows, FACE : 2 * FACE] = (f - high.astype(jnp.float32)).astype(jnp.bfloat16)
                left_ref[rows, 2 * FACE :] = jnp.where(parity == p, both, jnp.zeros_like(both))
        sums_ref[...] = jnp.dot(left_ref[...], weights_ref[...], preferred_element_type=jnp.float32)

        kept_ref = (kept_even_ref, kept_odd_ref)[odd]
        both = pl.ds(pl.multiple_of(2 * pair * FACE, FACE), 2 * FACE)
        for s in range(species):
            recent = jnp.dot(keep, recent_ref[s, :, both], preferred_element_type=jnp.float32)
            older = jnp.dot(keep, older_ref[s, :, both], preferred_element_type=jnp.float32)
            kept_ref[s] = recent * (-16.0 / 12.0 * step_size) + older * (5.0 / 12.0 * step_size)

        fuel_ref, react_ref = ((fuel_even_ref, react_even_ref), (fuel_odd_ref, react_odd_ref))[odd]
        both = pl.ds(pl.multiple_of((2 * pair + 1) * FACE, FACE), 2 * FACE)
        over = jnp.concatenate([wide_ref[1]] * 4, axis=1)
        burning = fields_ref[0, :, both] * fields_ref[1, :, both] * over
        for k in range(species):
            fuel = fields_ref[k, :, both] * burning
            high = fuel.astype(jnp.bfloat16)
            low = (fuel - high.astype(jnp.float32)).astype(jnp.bfloat16)
            for n, part in enumerate((high, high, low)):
                start = n * main + k * slots if k < species - 1 else 3 * main + n * slots
                fuel_ref[start : start + slots, :] = part
        react_ref[...] = jnp.dot(mix_ref[...], fuel_ref[...], preferred_element_type=jnp.float32)

    def finish(pair, odd):
        kept_ref = (kept_even_ref, kept_odd_ref)[odd]
        sums_ref, react_ref = ((sums_even_ref, react_even_ref), (sums_odd_ref, react_odd_ref))[odd]
        for p in range(2):
            inner, before, here, after = (
                pl.ds(pl.multiple_of((2 * pair + p + n) * FACE, FACE), FACE) for n in (0, 0, 1, 2)
            )
            for g in range(slots // 16):
                rows = slice(g * 16, (g + 1) * 16)
                smooth, vx, vy, vz, live = (
                    jnp.concatenate([wide_ref[n, rows, :]] * 2, axis=1) for n in (0, 2, 3, 4, 5)
                )
                for s in range(species):
                    low, high = fields_ref[s, rows, before], fields_ref[s, rows, after]
                    line = s * slots + g * 16
                    react = react_ref[line : line + 16, p * FACE : (p + 1) * FACE]
                    line += p * species * slots
                    total, along_y, along_z = (
                        sums_ref[line : line + 16, d * FACE : (d + 1) * FACE] for d in range(3)
                    )
                    tend = smooth * (total + (low + high)) - vx * (high - low)
                    tend = (tend - vy * along_y) + (react - vz * along_z)
                    kept = kept_ref[s, rows, p * FACE : (p + 1) * FACE]
                    new = (fields_ref[s, rows, here] + kept) * live
                    new_fields_ref[s, rows, inner] = new + (step_size * 23.0 / 12.0) * tend
                    new_tend_ref[s, rows, inner] = tend.astype(jnp.bfloat16)

    for copy in (*ends(), *cells_in(0)):
        copy.wait()
    sums(0, 0)

    def four(c, carry):
        @pl.when(c + 2 < chunks)
        def _():
            for copy in cells_in(c + 2):
                copy.start()

        sums(2 * c + 1, 1)
        finish(2 * c, 0)

        @pl.when(c + 1 < chunks)
        def _():
            for copy in cells_in(c + 1):
                copy.wait()

        sums(jnp.minimum(2 * c + 2, 2 * (chunks - 1)), 0)
        finish(2 * c + 1, 1)
        for copy in stores(c):
            copy.start()
        return carry

    lax.fori_loop(0, chunks, four, 0)
    for c in range(chunks):
        for copy in stores(c):
            copy.wait()


def add_kernel(
    live_ref, table_ref, fields_hbm, arrived_hbm, out_hbm, fields_ref, arrived_ref, got, sent
):
    species, peers = arrived_ref.shape[:2]
    slots = fields_ref.shape[1]

    def fetches(s):
        part = arrived_hbm.at[:, pl.ds(s * ROWS, ROWS)]
        return (
            pltpu.make_async_copy(part, arrived_ref.at[s], got.at[0, s]),
            pltpu.make_async_copy(fields_hbm.at[s], fields_ref.at[s], got.at[1, s]),
        )

    def store(s):
        return pltpu.make_async_copy(fields_ref.at[s], out_hbm.at[s], sent.at[s])

    for s in range(AHEAD):
        for copy in fetches(s):
            copy.start()
    me, first = lax.axis_index(TEAM), pl.multiple_of(lax.axis_index("grp") * peers, peers)
    notes = table_ref[pl.ds(first, peers), :]
    destination = notes[:, slots : 2 * slots]
    target = notes[:, 2 * slots : 3 * slots]
    peer = lax.broadcasted_iota(jnp.int32, (peers, slots), 0)
    mine = (destination == me.astype(jnp.float32)) & (peer != me)
    slot = jnp.max(jnp.where(mine, target, -1.0), axis=1, keepdims=True)
    index = lax.broadcasted_iota(jnp.int32, (peers, slots), 1)
    hot = (slot == index.astype(jnp.float32)) & (index < live_ref[0])
    hot = jnp.where(hot, step_size / SCALE, 0.0)
    hot = jnp.concatenate([hot, hot], axis=0).T.astype(jnp.bfloat16)
    for s in range(species):
        if s + AHEAD < species:
            for copy in fetches(s + AHEAD):
                copy.start()
        for copy in fetches(s):
            copy.wait()
        flat = arrived_ref.at[s].reshape(peers * ROWS, LANES)
        for c in range(ROWS // 2):
            lanes = slice(c * 2 * LANES, (c + 1) * 2 * LANES)
            arrived = jnp.concatenate(
                [flat[pl.ds(2 * c + k, peers, stride=ROWS), :] for k in range(2)], axis=1
            )
            high = arrived.astype(jnp.bfloat16)
            low = (arrived - high.astype(jnp.float32)).astype(jnp.bfloat16)
            fields_ref[s, :, lanes] += jnp.dot(
                hot, jnp.concatenate([high, low], axis=0), preferred_element_type=jnp.float32
            )
        store(s).start()
    for s in range(species):
        store(s).wait()


def smem():
    return pl.BlockSpec(memory_space=pltpu.SMEM)


def whole(shape):
    return pl.BlockSpec(shape, lambda i: (0,) * len(shape))


def params(mib, semantics=None):
    return pltpu.CompilerParams(vmem_limit_bytes=mib << 20, dimension_semantics=semantics)


def local(
    fields,
    ghosts,
    velocity,
    rate_matrix,
    recent_tend,
    older_tend,
    destination,
    target_slot,
    live_counts,
    tile_ids,
    sensor,
    flame_flags,
):
    slots, species, cells = fields.shape
    peers = lax.axis_size(TEAM)
    devices = lax.axis_size(EVERY)
    brick = sensor.shape[0]
    fields, ghosts, recent, older = (
        a.transpose(1, 0, 2) for a in (fields, ghosts, recent_tend, older_tend)
    )
    moves = (destination.reshape(1, slots), target_slot.reshape(1, slots))

    raw = pl.pallas_call(
        raw_kernel,
        name="raw_sensor",
        out_shape=jax.ShapeDtypeStruct(sensor.shape, jnp.bfloat16),
        in_specs=[smem(), pl.BlockSpec(memory_space=pltpu.VMEM)],
        out_specs=pl.BlockSpec(memory_space=pltpu.VMEM),
        compiler_params=params(58),
    )(flame_flags, sensor)
    below = passed_along(raw, "pen", 1)
    above = passed_along(raw, "pen", -1)

    anywhere = pl.BlockSpec(memory_space=pl.ANY)
    in_hbm = pl.BlockSpec(memory_space=pltpu.HBM)
    vmem = pl.BlockSpec(memory_space=pltpu.VMEM)
    outgoing = pl.pallas_call(
        send_kernel,
        name="outgoing_histories",
        out_shape=jax.ShapeDtypeStruct((peers, species * ROWS, LANES), jnp.float32),
        in_specs=[vmem, in_hbm, in_hbm],
        out_specs=vmem,
        scratch_shapes=[
            pltpu.VMEM(recent.shape, jnp.bfloat16),
            pltpu.VMEM(older.shape, jnp.bfloat16),
            pltpu.SemaphoreType.DMA((2, species)),
        ],
        compiler_params=params(50),
        cost_estimate=pl.CostEstimate(flops=0, bytes_accessed=8 << 20, transcendentals=0),
    )(destination.reshape(1, slots), recent, older)
    outgoing = outgoing.astype(jnp.float16)

    shape = jax.ShapeDtypeStruct((species, slots, cells), jnp.float32)
    rims = jax.ShapeDtypeStruct((species, slots, TE * LANES), jnp.bfloat16)
    rims = pl.pallas_call(
        rims_kernel,
        name="rims",
        out_shape=rims,
        in_specs=[anywhere],
        out_specs=anywhere,
        scratch_shapes=[
            pltpu.VMEM(ghosts.shape, jnp.float32),
            pltpu.VMEM(rims.shape, jnp.bfloat16),
            pltpu.SemaphoreType.DMA((species,)),
            pltpu.SemaphoreType.DMA((species,)),
        ],
        compiler_params=params(58),
        cost_estimate=pl.CostEstimate(flops=0, bytes_accessed=8 << 20, transcendentals=0),
    )(ghosts)
    below, above, rims = lax.optimization_barrier((below, above, rims))

    filtered, rows = pl.pallas_call(
        filter_kernel,
        name="filtered_sensor",
        out_shape=(
            jax.ShapeDtypeStruct(sensor.shape, jnp.float32),
            jax.ShapeDtypeStruct((devices, LANES), jnp.float32),
        ),
        in_specs=[smem()] + [vmem] * 6,
        out_specs=(vmem, vmem),
        compiler_params=params(32),
        cost_estimate=pl.CostEstimate(flops=0, bytes_accessed=4 << 20, transcendentals=0),
    )(flame_flags, jnp.asarray(banded(brick, brick)), sensor, below, above, *moves)
    table = lax.all_to_all(rows, EVERY, split_axis=0, concat_axis=0, tiled=True)
    table, outgoing = lax.optimization_barrier((table, outgoing))
    arrived = lax.all_to_all(outgoing, TEAM, split_axis=0, concat_axis=0, tiled=True)
    arrived = arrived.astype(jnp.float32)

    weights = jnp.asarray(plane_weights(), jnp.bfloat16)
    left = pltpu.VMEM((2 * species * slots, 6 * LANES), jnp.bfloat16)
    sums = pltpu.VMEM((2 * species * slots, 3 * FACE), jnp.float32)
    depth = 3 * (species - 1) * slots + LANES
    fuel = pltpu.VMEM((depth, 2 * FACE), jnp.bfloat16)
    react = pltpu.VMEM((species * slots, 2 * FACE), jnp.float32)
    kept = pltpu.VMEM((species, slots, 2 * FACE), jnp.float32)
    new_fields, new_tend = pl.pallas_call(
        main_kernel,
        name="updates",
        out_shape=(shape, jax.ShapeDtypeStruct(shape.shape, jnp.bfloat16)),
        in_specs=[smem()] * 2 + [vmem] * 5 + [anywhere] * 6,
        out_specs=(anywhere, anywhere),
        scratch_shapes=[
            pltpu.VMEM(weights.shape, jnp.bfloat16),
            pltpu.VMEM((species, slots, cells + 2 * FACE), jnp.float32),
            pltpu.VMEM(rims.shape, jnp.bfloat16),
            pltpu.VMEM(shape.shape, jnp.bfloat16),
            pltpu.VMEM(shape.shape, jnp.bfloat16),
            pltpu.VMEM(shape.shape, jnp.float32),
            pltpu.VMEM(shape.shape, jnp.bfloat16),
            pltpu.VMEM((species * slots, depth), jnp.bfloat16),
            pltpu.VMEM((6, slots, LANES), jnp.float32),
            left,
            left,
            fuel,
            fuel,
            sums,
            sums,
            react,
            react,
            kept,
            kept,
            pltpu.SemaphoreType.DMA((5, TE // PLANES)),
            pltpu.SemaphoreType.DMA((2, TE // PLANES)),
        ],
        compiler_params=params(58),
        cost_estimate=pl.CostEstimate(flops=0, bytes_accessed=40 << 20, transcendentals=0),
    )(
        live_counts,
        rate_matrix,
        table,
        tile_ids.reshape(1, slots),
        velocity,
        *moves,
        weights,
        fields,
        ghosts,
        rims,
        recent,
        older,
    )

    new_fields = pl.pallas_call(
        add_kernel,
        name="arrived_histories",
        out_shape=shape,
        in_specs=[smem(), vmem, anywhere, anywhere],
        out_specs=anywhere,
        scratch_shapes=[
            pltpu.VMEM(shape.shape, jnp.float32),
            pltpu.VMEM((species, peers, ROWS, LANES), jnp.float32),
            pltpu.SemaphoreType.DMA((2, species)),
            pltpu.SemaphoreType.DMA((species,)),
        ],
        compiler_params=params(58),
        cost_estimate=pl.CostEstimate(flops=0, bytes_accessed=12 << 20, transcendentals=0),
    )(live_counts, table, new_fields, arrived)
    return new_fields.transpose(1, 0, 2), new_tend.transpose(1, 0, 2), filtered


def solution(mesh):
    split = P(EVERY, None, None)
    return jax.shard_map(
        local,
        mesh=mesh,
        in_specs=(
            split,
            split,
            P(None, EVERY),
            P(),
            split,
            split,
            P(EVERY),
            P(EVERY),
            P(EVERY),
            P(EVERY),
            P("pen", ("grp", "mig")),
            P("pen", ("grp", "mig")),
        ),
        out_specs=(split, split, P("pen", ("grp", "mig"))),
        check_vma=False,
    )
```

```python
import jax
import jax.numpy as jnp
import numpy as np
from jax import lax
from jax.experimental import pallas as pl
from jax.experimental.pallas import tpu as pltpu
from jax.sharding import PartitionSpec as P

TE = 16
TZ = 2
TCOL = 16
FACE = TE * TE
CELLS = TE**3
LANES = 128
ROWS = CELLS // LANES

viscous = 0.05
step_size = 0.25
thicken = 5.0

SCALE = 4096.0
PLANES = 4
AHEAD = 4

EVERY = ("grp", "mig", "pen")
TEAM = ("mig", "pen")


def passed_along(x, axis, by):
    peers = lax.axis_size(axis)
    return lax.ppermute(x, axis, [(i, (i + by) % peers) for i in range(peers)])


def banded(brick_rows, reach):
    sigma = reach / 2.0
    offsets = np.arange(-reach, reach + 1, dtype=np.float64)
    total = np.sum(np.exp(-offsets * offsets / (2.0 * sigma * sigma)))
    row = np.arange(brick_rows)[:, None]
    col = np.arange(brick_rows + 2 * reach)[None, :]
    offset = (col - reach - row).astype(np.float64)
    weights = np.where(np.abs(offset) <= reach, np.exp(-offset * offset / (2.0 * sigma * sigma)), 0)
    return (weights / total).astype(np.float32)


def raw_kernel(flags_ref, sensor_ref, raw_ref):
    for r in range(TZ):
        for k in range(TCOL):
            rows, cols = slice(r * TE, (r + 1) * TE), slice(k * FACE, (k + 1) * FACE)
            flag = flags_ref[r, k].astype(jnp.float32)
            raw_ref[rows, cols] = (sensor_ref[rows, cols] * flag).astype(jnp.bfloat16)


def filter_kernel(
    flags_ref,
    weights_ref,
    sensor_ref,
    below_ref,
    above_ref,
    destination_ref,
    target_ref,
    filtered_ref,
    row_ref,
):
    lane = lax.broadcasted_iota(jnp.int32, (1, LANES), 1)
    slots = destination_ref.shape[1]
    row = jnp.concatenate(
        [
            jnp.zeros((1, slots), jnp.float32),
            destination_ref[...].astype(jnp.float32),
            target_ref[...].astype(jnp.float32),
            jnp.zeros((1, LANES - 3 * slots), jnp.float32),
        ],
        axis=1,
    )
    brick = sensor_ref.shape[0]
    for k in range(TCOL):
        cols = slice(k * FACE, (k + 1) * FACE)
        own = [
            sensor_ref[r * TE : (r + 1) * TE, cols] * flags_ref[r, k].astype(jnp.float32)
            for r in range(TZ)
        ]
        widened = jnp.concatenate(
            [below_ref[:, cols].astype(jnp.float32)] + own + [above_ref[:, cols].astype(jnp.float32)],
            axis=0,
        )
        filtered = jnp.dot(
            weights_ref[...],
            widened,
            precision=lax.Precision.HIGHEST,
            preferred_element_type=jnp.float32,
        )
        filtered_ref[:, cols] = filtered
        clipped = jnp.minimum(filtered, 1.0)
        for r in range(TZ):
            total = jnp.sum(
                jnp.sum(clipped[r * TE : (r + 1) * TE], axis=0, keepdims=True), axis=1, keepdims=True
            )
            thick = 1.0 + (thicken - 1.0) * (total / float(TE * FACE))
            row = jnp.where(lane == r * TCOL + k, thick, row)
    row_ref[...] = jnp.broadcast_to(row, row_ref.shape)


def send_kernel(
    destination_ref, recent_hbm, older_hbm, out_ref, recent_ref, older_ref, got
):
    species, slots, _ = recent_ref.shape
    peers = out_ref.shape[0]

    def fetches(s):
        return (
            pltpu.make_async_copy(recent_hbm.at[s], recent_ref.at[s], got.at[0, s]),
            pltpu.make_async_copy(older_hbm.at[s], older_ref.at[s], got.at[1, s]),
        )

    for s in range(AHEAD):
        for copy in fetches(s):
            copy.start()
    peer = lax.broadcasted_iota(jnp.int32, (peers, slots), 0)
    hot = ((destination_ref[...] == peer) & (peer != lax.axis_index(TEAM))).astype(jnp.bfloat16)
    flat = out_ref.reshape(peers * species * ROWS, LANES)
    for s in range(species):
        if s + AHEAD < species:
            for copy in fetches(s + AHEAD):
                copy.start()
        for copy in fetches(s):
            copy.wait()
        recent = jnp.dot(hot, recent_ref[s], preferred_element_type=jnp.float32)
        older = jnp.dot(hot, older_ref[s], preferred_element_type=jnp.float32)
        mixed = recent * (-16.0 / 12.0 * SCALE) + older * (5.0 / 12.0 * SCALE)
        for k in range(ROWS):
            flat[pl.ds(s * ROWS + k, peers, stride=species * ROWS), :] = mixed[
                :, k * LANES : (k + 1) * LANES
            ]


def rims_kernel(ghosts_hbm, rims_hbm, ghosts_ref, rims_ref, got, sent):
    species, slots, _ = ghosts_ref.shape

    def fetch(s):
        return pltpu.make_async_copy(ghosts_hbm.at[s], ghosts_ref.at[s], got.at[s])

    def store(s):
        return pltpu.make_async_copy(rims_ref.at[s], rims_hbm.at[s], sent.at[s])

    for s in range(species):
        fetch(s).start()
    quarter = lax.broadcasted_iota(jnp.int32, (slots, LANES), 1) // (2 * TE)

    def one(s, carry):
        fetch(s).wait()
        for block in range(2):
            faces = [
                ghosts_ref[s, :, w * FACE + block * LANES : w * FACE + (block + 1) * LANES]
                for w in (4, 5, 2, 3)
            ]
            for q in range(4):
                rim = faces[0]
                for n in range(4):
                    turned = pltpu.roll(faces[n], (n - q) % 4 * 2 * TE, 1) if n != q else faces[n]
                    rim = turned if n == 0 else jnp.where(quarter == n, turned, rim)
                high = rim.astype(jnp.bfloat16)
                low = (rim - high.astype(jnp.float32)).astype(jnp.bfloat16)
                start = (block * 4 + q) * 2 * LANES
                rims_ref[s, :, start : start + LANES] = high
                rims_ref[s, :, start + LANES : start + 2 * LANES] = low
        store(s).start()
        return carry

    lax.fori_loop(0, species, one, 0)
    for s in range(species):
        store(s).wait()


def plane_weights():
    weights = np.zeros((6 * LANES, 3 * FACE), np.float32)
    for cell in range(FACE):
        y, z = divmod(cell, TE)
        for d, at, step in ((0, y, TE), (1, z, 1)):
            for way in (-1, 1):
                if 0 <= at + way < TE:
                    rows = [cell + way * step, FACE + cell + way * step]
                else:
                    face = (2 + (way > 0)) if d == 0 else (way > 0)
                    spot = 2 * FACE + face * 2 * TE + (z if d == 0 else y)
                    rows = [spot, spot + TE, spot + LANES, spot + LANES + TE]
                weights[rows, cell] += 1.0
                weights[rows, (1 + d) * FACE + cell] += way
        weights[[cell, FACE + cell], cell] -= 6.0
    return weights


def main_kernel(
    live_ref,
    rate_ref,
    table_ref,
    tiles_ref,
    velocity_ref,
    destination_ref,
    target_ref,
    weights_hbm,
    fields_hbm,
    ghosts_hbm,
    rims_hbm,
    recent_hbm,
    older_hbm,
    new_fields_hbm,
    new_tend_hbm,
    weights_ref,
    fields_ref,
    rims_ref,
    recent_ref,
    older_ref,
    new_fields_ref,
    new_tend_ref,
    mix_ref,
    wide_ref,
    left_even_ref,
    left_odd_ref,
    fuel_even_ref,
    fuel_odd_ref,
    sums_even_ref,
    sums_odd_ref,
    react_even_ref,
    react_odd_ref,
    kept_even_ref,
    kept_odd_ref,
    got,
    sent,
):
    species, slots, cells = new_fields_ref.shape
    devices = table_ref.shape[0]
    chunk = PLANES * FACE
    chunks = cells // chunk

    def span(c, length, skipped=0):
        return pl.ds(pl.multiple_of(skipped + c * length, LANES), length)

    def cells_in(c):
        lanes, rims, inner = span(c, chunk), span(c, chunk // 2), span(c, chunk, FACE)
        return (
            pltpu.make_async_copy(
                fields_hbm.at[:, :, lanes], fields_ref.at[:, :, inner], got.at[0, c]
            ),
            pltpu.make_async_copy(
                rims_hbm.at[:, :, rims], rims_ref.at[:, :, rims], got.at[1, c]
            ),
            pltpu.make_async_copy(
                recent_hbm.at[:, :, lanes], recent_ref.at[:, :, lanes], got.at[2, c]
            ),
            pltpu.make_async_copy(
                older_hbm.at[:, :, lanes], older_ref.at[:, :, lanes], got.at[3, c]
            ),
        )

    def ends():
        return (
            pltpu.make_async_copy(weights_hbm, weights_ref, got.at[4, 0]),
            pltpu.make_async_copy(
                ghosts_hbm.at[:, :, pl.ds(0, FACE)], fields_ref.at[:, :, pl.ds(0, FACE)], got.at[4, 1]
            ),
            pltpu.make_async_copy(
                ghosts_hbm.at[:, :, pl.ds(FACE, FACE)],
                fields_ref.at[:, :, pl.ds(FACE + cells, FACE)],
                got.at[4, 2],
            ),
        )

    def stores(c):
        lanes = span(c, chunk)
        return (
            pltpu.make_async_copy(
                new_fields_ref.at[:, :, lanes], new_fields_hbm.at[:, :, lanes], sent.at[0, c]
            ),
            pltpu.make_async_copy(
                new_tend_ref.at[:, :, lanes], new_tend_hbm.at[:, :, lanes], sent.at[1, c]
            ),
        )

    for copy in ends():
        copy.start()
    for c in range(2):
        for copy in cells_in(c):
            copy.start()

    marks = jnp.concatenate(
        [velocity_ref[...], tiles_ref[...].astype(jnp.float32), jnp.zeros((4, slots), jnp.float32)], axis=0
    ).T
    tiles = marks[:, 3:4].astype(jnp.int32)
    wanted = lax.broadcasted_iota(jnp.int32, (slots, devices), 1) == tiles // slots
    picked = jnp.dot(
        wanted.astype(jnp.float32),
        table_ref[...],
        precision=lax.Precision.HIGHEST,
        preferred_element_type=jnp.float32,
    )
    lane = lax.broadcasted_iota(jnp.int32, picked.shape, 1)
    thick = jnp.sum(jnp.where(lane == tiles % slots, picked, 0.0), axis=1, keepdims=True)
    live = lax.broadcasted_iota(jnp.int32, (slots, 1), 0) < live_ref[0]
    live = jnp.where(live, 1.0, 0.0)
    parts = [viscous * thick * live, live / thick]
    parts += [0.5 * live * marks[:, d : d + 1] for d in range(3)] + [live]
    for n, part in enumerate(parts):
        wide_ref[n] = jnp.broadcast_to(part, (slots, LANES))
    main = (species - 1) * slots
    tail = lax.broadcasted_iota(jnp.int32, (slots, LANES), 1)
    main_lane = lax.broadcasted_iota(jnp.int32, (slots, main), 1)
    main_slot = lax.broadcasted_iota(jnp.int32, (slots, main), 0) == main_lane % slots
    tail_slot = lax.broadcasted_iota(jnp.int32, (slots, LANES), 0) == tail % slots
    for s in range(species):
        rows = slice(s * slots, (s + 1) * slots)
        rate = jnp.zeros((slots, main), jnp.float32)
        for k in range(species - 1):
            rate = jnp.where(main_lane // slots == k, rate_ref[s, k], rate)
        rate = jnp.where(main_slot, rate, 0.0)
        high = rate.astype(jnp.bfloat16)
        mix_ref[rows, 0:main] = high
        mix_ref[rows, main : 2 * main] = (rate - high.astype(jnp.float32)).astype(jnp.bfloat16)
        mix_ref[rows, 2 * main : 3 * main] = high
        rate = jnp.where(tail_slot & (tail < 3 * slots), rate_ref[s, species - 1], 0.0)
        high = rate.astype(jnp.bfloat16).astype(jnp.float32)
        rate = jnp.where(tail // slots == 1, rate - high, high)
        mix_ref[rows, 3 * main :] = rate.astype(jnp.bfloat16)
    for fuel_ref in (fuel_even_ref, fuel_odd_ref):
        fuel_ref[3 * main + 3 * slots :, :] = jnp.zeros((LANES - 3 * slots, 2 * FACE), jnp.bfloat16)

    parity = lax.broadcasted_iota(jnp.int32, (slots, 2 * LANES), 1) // TE % 2
    slot = lax.broadcasted_iota(jnp.int32, (slots, slots), 0)
    keep = (destination_ref[...] == lax.axis_index(TEAM)) & (target_ref[...] == slot)
    keep = keep.astype(jnp.bfloat16)

    def sums(pair, odd):
        left_ref, sums_ref = ((left_even_ref, sums_even_ref), (left_odd_ref, sums_odd_ref))[odd]
        rims = pl.ds(pl.multiple_of(pair * FACE, FACE), FACE)
        for s in range(species):
            both = rims_ref[s, :, rims]
            for p in range(2):
                lanes = pl.ds(pl.multiple_of((2 * pair + p + 1) * FACE, FACE), FACE)
                rows = slice((p * species + s) * slots, (p * species + s + 1) * slots)
                f = fields_ref[s, :, lanes]
                high = f.astype(jnp.bfloat16)
                left_ref[rows, 0:FACE] = high
                left_ref[rows, FACE : 2 * FACE] = (f - high.astype(jnp.float32)).astype(jnp.bfloat16)
                left_ref[rows, 2 * FACE :] = jnp.where(parity == p, both, jnp.zeros_like(both))
        sums_ref[...] = jnp.dot(left_ref[...], weights_ref[...], preferred_element_type=jnp.float32)

        kept_ref = (kept_even_ref, kept_odd_ref)[odd]
        both = pl.ds(pl.multiple_of(2 * pair * FACE, FACE), 2 * FACE)
        for s in range(species):
            recent = jnp.dot(keep, recent_ref[s, :, both], preferred_element_type=jnp.float32)
            older = jnp.dot(keep, older_ref[s, :, both], preferred_element_type=jnp.float32)
            kept_ref[s] = recent * (-16.0 / 12.0 * step_size) + older * (5.0 / 12.0 * step_size)

        fuel_ref, react_ref = ((fuel_even_ref, react_even_ref), (fuel_odd_ref, react_odd_ref))[odd]
        both = pl.ds(pl.multiple_of((2 * pair + 1) * FACE, FACE), 2 * FACE)
        over = jnp.concatenate([wide_ref[1]] * 4, axis=1)
        burning = fields_ref[0, :, both] * fields_ref[1, :, both] * over
        for k in range(species):
            fuel = fields_ref[k, :, both] * burning
            high = fuel.astype(jnp.bfloat16)
            low = (fuel - high.astype(jnp.float32)).astype(jnp.bfloat16)
            for n, part in enumerate((high, high, low)):
                start = n * main + k * slots if k < species - 1 else 3 * main + n * slots
                fuel_ref[start : start + slots, :] = part
        react_ref[...] = jnp.dot(mix_ref[...], fuel_ref[...], preferred_element_type=jnp.float32)

    def finish(pair, odd):
        kept_ref = (kept_even_ref, kept_odd_ref)[odd]
        sums_ref, react_ref = ((sums_even_ref, react_even_ref), (sums_odd_ref, react_odd_ref))[odd]
        for p in range(2):
            inner, before, here, after = (
                pl.ds(pl.multiple_of((2 * pair + p + n) * FACE, FACE), FACE) for n in (0, 0, 1, 2)
            )
            for g in range(slots // 16):
                rows = slice(g * 16, (g + 1) * 16)
                smooth, vx, vy, vz, live = (
                    jnp.concatenate([wide_ref[n, rows, :]] * 2, axis=1) for n in (0, 2, 3, 4, 5)
                )
                for s in range(species):
                    low, high = fields_ref[s, rows, before], fields_ref[s, rows, after]
                    line = s * slots + g * 16
                    react = react_ref[line : line + 16, p * FACE : (p + 1) * FACE]
                    line += p * species * slots
                    total, along_y, along_z = (
                        sums_ref[line : line + 16, d * FACE : (d + 1) * FACE] for d in range(3)
                    )
                    tend = smooth * (total + (low + high)) - vx * (high - low)
                    tend = (tend - vy * along_y) + (react - vz * along_z)
                    kept = kept_ref[s, rows, p * FACE : (p + 1) * FACE]
                    new = (fields_ref[s, rows, here] + kept) * live
                    new_fields_ref[s, rows, inner] = new + (step_size * 23.0 / 12.0) * tend
                    new_tend_ref[s, rows, inner] = tend.astype(jnp.bfloat16)

    for copy in (*ends(), *cells_in(0)):
        copy.wait()
    sums(0, 0)

    def four(c, carry):
        @pl.when(c + 2 < chunks)
        def _():
            for copy in cells_in(c + 2):
                copy.start()

        sums(2 * c + 1, 1)
        finish(2 * c, 0)

        @pl.when(c + 1 < chunks)
        def _():
            for copy in cells_in(c + 1):
                copy.wait()

        sums(jnp.minimum(2 * c + 2, 2 * (chunks - 1)), 0)
        finish(2 * c + 1, 1)
        for copy in stores(c):
            copy.start()
        return carry

    lax.fori_loop(0, chunks, four, 0)
    for c in range(chunks):
        for copy in stores(c):
            copy.wait()


def add_kernel(
    live_ref,
    table_ref,
    fields_hbm,
    arrived_hbm,
    out_hbm,
    fields_ref,
    arrived_ref,
    hot_ref,
    parts_ref,
    got,
    sent,
):
    species, peers = arrived_ref.shape[:2]
    slots = fields_ref.shape[1]
    depth = peers * ROWS

    def fetches(s):
        part = arrived_hbm.at[:, pl.ds(s * ROWS, ROWS)]
        return (
            pltpu.make_async_copy(part, arrived_ref.at[s], got.at[0, s]),
            pltpu.make_async_copy(fields_hbm.at[s], fields_ref.at[s], got.at[1, s]),
        )

    def store(s):
        return pltpu.make_async_copy(fields_ref.at[s], out_hbm.at[s], sent.at[s])

    for s in range(species):
        for copy in fetches(s):
            copy.start()
    me, first = lax.axis_index(TEAM), pl.multiple_of(lax.axis_index("grp") * peers, peers)
    notes = table_ref[pl.ds(first, peers), :]
    destination = notes[:, slots : 2 * slots]
    target = notes[:, 2 * slots : 3 * slots]
    peer = lax.broadcasted_iota(jnp.int32, (peers, slots), 0)
    mine = (destination == me.astype(jnp.float32)) & (peer != me)
    slot = jnp.max(jnp.where(mine, target, -1.0), axis=1, keepdims=True)
    index = lax.broadcasted_iota(jnp.int32, (peers, slots), 1)
    hot = (slot == index.astype(jnp.float32)) & (index < live_ref[0])
    hot = jnp.where(hot, step_size / SCALE, 0.0).astype(jnp.bfloat16)
    spread = lax.broadcasted_iota(jnp.int32, (peers, depth), 1) // ROWS
    spread = (spread == lax.broadcasted_iota(jnp.int32, (peers, depth), 0)).astype(jnp.bfloat16)
    wide = lax.dot_general(hot, spread, (((0,), (0,)), ((), ())), preferred_element_type=jnp.float32)
    part = lax.broadcasted_iota(jnp.int32, (slots, depth), 1) % ROWS
    for k in range(ROWS):
        lines = jnp.where(part == k, wide, 0.0).astype(jnp.bfloat16)
        hot_ref[k * slots : (k + 1) * slots, 0:depth] = lines
        hot_ref[k * slots : (k + 1) * slots, depth:] = lines
    for first in range(0, species, 2):
        here = range(first, min(first + 2, species))
        for n, s in enumerate(here):
            for copy in fetches(s):
                copy.wait()
            arrived = arrived_ref.at[s].reshape(depth, LANES)[...]
            high = arrived.astype(jnp.bfloat16)
            lanes = slice(n * LANES, (n + 1) * LANES)
            parts_ref[0:depth, lanes] = high
            parts_ref[depth:, lanes] = (arrived - high.astype(jnp.float32)).astype(jnp.bfloat16)
        placed = jnp.dot(hot_ref[...], parts_ref[...], preferred_element_type=jnp.float32)
        for n, s in enumerate(here):
            for k in range(ROWS):
                lanes = slice(k * LANES, (k + 1) * LANES)
                fields_ref[s, :, lanes] += placed[
                    k * slots : (k + 1) * slots, n * LANES : (n + 1) * LANES
                ]
            store(s).start()
    for s in range(species):
        store(s).wait()


def smem():
    return pl.BlockSpec(memory_space=pltpu.SMEM)


def whole(shape):
    return pl.BlockSpec(shape, lambda i: (0,) * len(shape))


def params(mib, semantics=None):
    return pltpu.CompilerParams(vmem_limit_bytes=mib << 20, dimension_semantics=semantics)


def local(
    fields,
    ghosts,
    velocity,
    rate_matrix,
    recent_tend,
    older_tend,
    destination,
    target_slot,
    live_counts,
    tile_ids,
    sensor,
    flame_flags,
):
    slots, species, cells = fields.shape
    peers = lax.axis_size(TEAM)
    devices = lax.axis_size(EVERY)
    brick = sensor.shape[0]
    fields, ghosts, recent, older = (
        a.transpose(1, 0, 2) for a in (fields, ghosts, recent_tend, older_tend)
    )
    moves = (destination.reshape(1, slots), target_slot.reshape(1, slots))

    raw = pl.pallas_call(
        raw_kernel,
        name="raw_sensor",
        out_shape=jax.ShapeDtypeStruct(sensor.shape, jnp.bfloat16),
        in_specs=[smem(), pl.BlockSpec(memory_space=pltpu.VMEM)],
        out_specs=pl.BlockSpec(memory_space=pltpu.VMEM),
        compiler_params=params(58),
    )(flame_flags, sensor)
    below = passed_along(raw, "pen", 1)
    above = passed_along(raw, "pen", -1)

    anywhere = pl.BlockSpec(memory_space=pl.ANY)
    in_hbm = pl.BlockSpec(memory_space=pltpu.HBM)
    vmem = pl.BlockSpec(memory_space=pltpu.VMEM)
    outgoing = pl.pallas_call(
        send_kernel,
        name="outgoing_histories",
        out_shape=jax.ShapeDtypeStruct((peers, species * ROWS, LANES), jnp.float32),
        in_specs=[vmem, in_hbm, in_hbm],
        out_specs=vmem,
        scratch_shapes=[
            pltpu.VMEM(recent.shape, jnp.bfloat16),
            pltpu.VMEM(older.shape, jnp.bfloat16),
            pltpu.SemaphoreType.DMA((2, species)),
        ],
        compiler_params=params(50),
        cost_estimate=pl.CostEstimate(flops=0, bytes_accessed=8 << 20, transcendentals=0),
    )(destination.reshape(1, slots), recent, older)
    outgoing = outgoing.astype(jnp.float16)

    shape = jax.ShapeDtypeStruct((species, slots, cells), jnp.float32)
    rims = jax.ShapeDtypeStruct((species, slots, TE * LANES), jnp.bfloat16)
    rims = pl.pallas_call(
        rims_kernel,
        name="rims",
        out_shape=rims,
        in_specs=[anywhere],
        out_specs=anywhere,
        scratch_shapes=[
            pltpu.VMEM(ghosts.shape, jnp.float32),
            pltpu.VMEM(rims.shape, jnp.bfloat16),
            pltpu.SemaphoreType.DMA((species,)),
            pltpu.SemaphoreType.DMA((species,)),
        ],
        compiler_params=params(58),
        cost_estimate=pl.CostEstimate(flops=0, bytes_accessed=8 << 20, transcendentals=0),
    )(ghosts)
    below, above, rims, outgoing = lax.optimization_barrier((below, above, rims, outgoing))

    filtered, rows = pl.pallas_call(
        filter_kernel,
        name="filtered_sensor",
        out_shape=(
            jax.ShapeDtypeStruct(sensor.shape, jnp.float32),
            jax.ShapeDtypeStruct((devices, LANES), jnp.float32),
        ),
        in_specs=[smem()] + [vmem] * 6,
        out_specs=(vmem, vmem),
        compiler_params=params(32),
        cost_estimate=pl.CostEstimate(flops=0, bytes_accessed=4 << 20, transcendentals=0),
    )(flame_flags, jnp.asarray(banded(brick, brick)), sensor, below, above, *moves)
    table = lax.all_to_all(rows, EVERY, split_axis=0, concat_axis=0, tiled=True)
    table, outgoing = lax.optimization_barrier((table, outgoing))
    arrived = lax.all_to_all(outgoing, TEAM, split_axis=0, concat_axis=0, tiled=True)
    arrived = arrived.astype(jnp.float32)

    weights = jnp.asarray(plane_weights(), jnp.bfloat16)
    left = pltpu.VMEM((2 * species * slots, 6 * LANES), jnp.bfloat16)
    sums = pltpu.VMEM((2 * species * slots, 3 * FACE), jnp.float32)
    depth = 3 * (species - 1) * slots + LANES
    fuel = pltpu.VMEM((depth, 2 * FACE), jnp.bfloat16)
    react = pltpu.VMEM((species * slots, 2 * FACE), jnp.float32)
    kept = pltpu.VMEM((species, slots, 2 * FACE), jnp.float32)
    new_fields, new_tend = pl.pallas_call(
        main_kernel,
        name="updates",
        out_shape=(shape, jax.ShapeDtypeStruct(shape.shape, jnp.bfloat16)),
        in_specs=[smem()] * 2 + [vmem] * 5 + [anywhere] * 6,
        out_specs=(anywhere, anywhere),
        scratch_shapes=[
            pltpu.VMEM(weights.shape, jnp.bfloat16),
            pltpu.VMEM((species, slots, cells + 2 * FACE), jnp.float32),
            pltpu.VMEM(rims.shape, jnp.bfloat16),
            pltpu.VMEM(shape.shape, jnp.bfloat16),
            pltpu.VMEM(shape.shape, jnp.bfloat16),
            pltpu.VMEM(shape.shape, jnp.float32),
            pltpu.VMEM(shape.shape, jnp.bfloat16),
            pltpu.VMEM((species * slots, depth), jnp.bfloat16),
            pltpu.VMEM((6, slots, LANES), jnp.float32),
            left,
            left,
            fuel,
            fuel,
            sums,
            sums,
            react,
            react,
            kept,
            kept,
            pltpu.SemaphoreType.DMA((5, TE // PLANES)),
            pltpu.SemaphoreType.DMA((2, TE // PLANES)),
        ],
        compiler_params=params(58),
        cost_estimate=pl.CostEstimate(flops=0, bytes_accessed=40 << 20, transcendentals=0),
    )(
        live_counts,
        rate_matrix,
        table,
        tile_ids.reshape(1, slots),
        velocity,
        *moves,
        weights,
        fields,
        ghosts,
        rims,
        recent,
        older,
    )

    new_fields = pl.pallas_call(
        add_kernel,
        name="arrived_histories",
        out_shape=shape,
        in_specs=[smem(), vmem, anywhere, anywhere],
        out_specs=anywhere,
        scratch_shapes=[
            pltpu.VMEM(shape.shape, jnp.float32),
            pltpu.VMEM((species, peers, ROWS, LANES), jnp.float32),
            pltpu.VMEM((slots * ROWS, 2 * peers * ROWS), jnp.bfloat16),
            pltpu.VMEM((2 * peers * ROWS, 2 * LANES), jnp.bfloat16),
            pltpu.SemaphoreType.DMA((2, species)),
            pltpu.SemaphoreType.DMA((species,)),
        ],
        compiler_params=params(58),
        cost_estimate=pl.CostEstimate(flops=0, bytes_accessed=12 << 20, transcendentals=0),
    )(live_counts, table, new_fields, arrived)
    return new_fields.transpose(1, 0, 2), new_tend.transpose(1, 0, 2), filtered


def solution(mesh):
    split = P(EVERY, None, None)
    return jax.shard_map(
        local,
        mesh=mesh,
        in_specs=(
            split,
            split,
            P(None, EVERY),
            P(),
            split,
            split,
            P(EVERY),
            P(EVERY),
            P(EVERY),
            P(EVERY),
            P("pen", ("grp", "mig")),
            P("pen", ("grp", "mig")),
        ),
        out_specs=(split, split, P("pen", ("grp", "mig"))),
        check_vma=False,
    )
```

```python
import jax
import jax.numpy as jnp
import numpy as np
from jax import lax
from jax.experimental import pallas as pl
from jax.experimental.pallas import tpu as pltpu
from jax.sharding import PartitionSpec as P

TE = 16
TZ = 2
TCOL = 16
FACE = TE * TE
CELLS = TE**3
LANES = 128
ROWS = CELLS // LANES

viscous = 0.05
step_size = 0.25
thicken = 5.0

SCALE = 4096.0
PLANES = 4
AHEAD = 4

EVERY = ("grp", "mig", "pen")
TEAM = ("mig", "pen")


def passed_along(x, axis, by):
    peers = lax.axis_size(axis)
    return lax.ppermute(x, axis, [(i, (i + by) % peers) for i in range(peers)])


def banded(brick_rows, reach):
    sigma = reach / 2.0
    offsets = np.arange(-reach, reach + 1, dtype=np.float64)
    total = np.sum(np.exp(-offsets * offsets / (2.0 * sigma * sigma)))
    row = np.arange(brick_rows)[:, None]
    col = np.arange(brick_rows + 2 * reach)[None, :]
    offset = (col - reach - row).astype(np.float64)
    weights = np.where(np.abs(offset) <= reach, np.exp(-offset * offset / (2.0 * sigma * sigma)), 0)
    return (weights / total).astype(np.float32)


def raw_kernel(flags_ref, sensor_ref, raw_ref):
    for r in range(TZ):
        for k in range(TCOL):
            rows, cols = slice(r * TE, (r + 1) * TE), slice(k * FACE, (k + 1) * FACE)
            flag = flags_ref[r, k].astype(jnp.float32)
            raw_ref[rows, cols] = (sensor_ref[rows, cols] * flag).astype(jnp.bfloat16)


def filter_kernel(
    flags_ref,
    weights_ref,
    sensor_ref,
    below_ref,
    above_ref,
    destination_ref,
    target_ref,
    filtered_ref,
    row_ref,
):
    lane = lax.broadcasted_iota(jnp.int32, (1, LANES), 1)
    slots = destination_ref.shape[1]
    row = jnp.concatenate(
        [
            jnp.zeros((1, slots), jnp.float32),
            destination_ref[...].astype(jnp.float32),
            target_ref[...].astype(jnp.float32),
            jnp.zeros((1, LANES - 3 * slots), jnp.float32),
        ],
        axis=1,
    )
    brick = sensor_ref.shape[0]
    for k in range(TCOL):
        cols = slice(k * FACE, (k + 1) * FACE)
        own = [
            sensor_ref[r * TE : (r + 1) * TE, cols] * flags_ref[r, k].astype(jnp.float32)
            for r in range(TZ)
        ]
        widened = jnp.concatenate(
            [below_ref[:, cols].astype(jnp.float32)] + own + [above_ref[:, cols].astype(jnp.float32)],
            axis=0,
        )
        filtered = jnp.dot(
            weights_ref[...],
            widened,
            precision=lax.Precision.HIGHEST,
            preferred_element_type=jnp.float32,
        )
        filtered_ref[:, cols] = filtered
        clipped = jnp.minimum(filtered, 1.0)
        for r in range(TZ):
            total = jnp.sum(
                jnp.sum(clipped[r * TE : (r + 1) * TE], axis=0, keepdims=True), axis=1, keepdims=True
            )
            thick = 1.0 + (thicken - 1.0) * (total / float(TE * FACE))
            row = jnp.where(lane == r * TCOL + k, thick, row)
    row_ref[...] = row


def send_kernel(
    destination_ref, recent_hbm, older_hbm, out_ref, recent_ref, older_ref, got
):
    species, slots, _ = recent_ref.shape
    peers = out_ref.shape[0]

    def fetches(s):
        return (
            pltpu.make_async_copy(recent_hbm.at[s], recent_ref.at[s], got.at[0, s]),
            pltpu.make_async_copy(older_hbm.at[s], older_ref.at[s], got.at[1, s]),
        )

    for s in range(AHEAD):
        for copy in fetches(s):
            copy.start()
    peer = lax.broadcasted_iota(jnp.int32, (peers, slots), 0)
    hot = ((destination_ref[...] == peer) & (peer != lax.axis_index(TEAM))).astype(jnp.bfloat16)
    flat = out_ref.reshape(peers * species * ROWS, LANES)
    for s in range(species):
        if s + AHEAD < species:
            for copy in fetches(s + AHEAD):
                copy.start()
        for copy in fetches(s):
            copy.wait()
        recent = jnp.dot(hot, recent_ref[s], preferred_element_type=jnp.float32)
        older = jnp.dot(hot, older_ref[s], preferred_element_type=jnp.float32)
        mixed = recent * (-16.0 / 12.0 * SCALE) + older * (5.0 / 12.0 * SCALE)
        for k in range(ROWS):
            flat[pl.ds(s * ROWS + k, peers, stride=species * ROWS), :] = mixed[
                :, k * LANES : (k + 1) * LANES
            ]


def rims_kernel(ghosts_hbm, rims_hbm, ghosts_ref, rims_ref, got, sent):
    species, slots, _ = ghosts_ref.shape

    def fetch(s):
        return pltpu.make_async_copy(ghosts_hbm.at[s], ghosts_ref.at[s], got.at[s])

    def store(s):
        return pltpu.make_async_copy(rims_ref.at[s], rims_hbm.at[s], sent.at[s])

    for s in range(species):
        fetch(s).start()
    quarter = lax.broadcasted_iota(jnp.int32, (slots, LANES), 1) // (2 * TE)

    def one(s, carry):
        fetch(s).wait()
        for block in range(2):
            faces = [
                ghosts_ref[s, :, w * FACE + block * LANES : w * FACE + (block + 1) * LANES]
                for w in (4, 5, 2, 3)
            ]
            for q in range(4):
                rim = faces[0]
                for n in range(4):
                    turned = pltpu.roll(faces[n], (n - q) % 4 * 2 * TE, 1) if n != q else faces[n]
                    rim = turned if n == 0 else jnp.where(quarter == n, turned, rim)
                high = rim.astype(jnp.bfloat16)
                low = (rim - high.astype(jnp.float32)).astype(jnp.bfloat16)
                start = (block * 4 + q) * 2 * LANES
                rims_ref[s, :, start : start + LANES] = high
                rims_ref[s, :, start + LANES : start + 2 * LANES] = low
        store(s).start()
        return carry

    lax.fori_loop(0, species, one, 0)
    for s in range(species):
        store(s).wait()


def plane_weights():
    weights = np.zeros((6 * LANES, 3 * FACE), np.float32)
    for cell in range(FACE):
        y, z = divmod(cell, TE)
        for d, at, step in ((0, y, TE), (1, z, 1)):
            for way in (-1, 1):
                if 0 <= at + way < TE:
                    rows = [cell + way * step, FACE + cell + way * step]
                else:
                    face = (2 + (way > 0)) if d == 0 else (way > 0)
                    spot = 2 * FACE + face * 2 * TE + (z if d == 0 else y)
                    rows = [spot, spot + TE, spot + LANES, spot + LANES + TE]
                weights[rows, cell] += 1.0
                weights[rows, (1 + d) * FACE + cell] += way
        weights[[cell, FACE + cell], cell] -= 6.0
    return weights


def main_kernel(
    live_ref,
    rate_ref,
    table_ref,
    tiles_ref,
    velocity_ref,
    destination_ref,
    target_ref,
    weights_hbm,
    fields_hbm,
    ghosts_hbm,
    rims_hbm,
    recent_hbm,
    older_hbm,
    new_fields_hbm,
    new_tend_hbm,
    weights_ref,
    fields_ref,
    rims_ref,
    recent_ref,
    older_ref,
    new_fields_ref,
    new_tend_ref,
    mix_ref,
    wide_ref,
    mask_ref,
    left_even_ref,
    left_odd_ref,
    fuel_even_ref,
    fuel_odd_ref,
    sums_even_ref,
    sums_odd_ref,
    react_even_ref,
    react_odd_ref,
    kept_even_ref,
    kept_odd_ref,
    got,
    sent,
):
    species, slots, cells = new_fields_ref.shape
    peers = table_ref.shape[0]
    chunk = PLANES * FACE
    chunks = cells // chunk

    def span(c, length, skipped=0):
        return pl.ds(pl.multiple_of(skipped + c * length, LANES), length)

    def cells_in(c):
        lanes, rims, inner = span(c, chunk), span(c, chunk // 2), span(c, chunk, FACE)
        return (
            pltpu.make_async_copy(
                fields_hbm.at[:, :, lanes], fields_ref.at[:, :, inner], got.at[0, c]
            ),
            pltpu.make_async_copy(
                rims_hbm.at[:, :, rims], rims_ref.at[:, :, rims], got.at[1, c]
            ),
            pltpu.make_async_copy(
                recent_hbm.at[:, :, lanes], recent_ref.at[:, :, lanes], got.at[2, c]
            ),
            pltpu.make_async_copy(
                older_hbm.at[:, :, lanes], older_ref.at[:, :, lanes], got.at[3, c]
            ),
        )

    def ends():
        return (
            pltpu.make_async_copy(weights_hbm, weights_ref, got.at[4, 0]),
            pltpu.make_async_copy(
                ghosts_hbm.at[:, :, pl.ds(0, FACE)], fields_ref.at[:, :, pl.ds(0, FACE)], got.at[4, 1]
            ),
            pltpu.make_async_copy(
                ghosts_hbm.at[:, :, pl.ds(FACE, FACE)],
                fields_ref.at[:, :, pl.ds(FACE + cells, FACE)],
                got.at[4, 2],
            ),
        )

    def stores(c):
        lanes = span(c, chunk)
        return (
            pltpu.make_async_copy(
                new_fields_ref.at[:, :, lanes], new_fields_hbm.at[:, :, lanes], sent.at[0, c]
            ),
            pltpu.make_async_copy(
                new_tend_ref.at[:, :, lanes], new_tend_hbm.at[:, :, lanes], sent.at[1, c]
            ),
        )

    for copy in ends():
        copy.start()
    for c in range(2):
        for copy in cells_in(c):
            copy.start()

    marks = jnp.concatenate(
        [velocity_ref[...], tiles_ref[...].astype(jnp.float32), jnp.zeros((4, slots), jnp.float32)], axis=0
    ).T
    tiles = marks[:, 3:4].astype(jnp.int32)
    owner = tiles // slots
    wanted = lax.broadcasted_iota(jnp.int32, (slots, peers), 1) == owner % peers
    picked = jnp.dot(
        wanted.astype(jnp.float32),
        table_ref[...],
        precision=lax.Precision.HIGHEST,
        preferred_element_type=jnp.float32,
    )
    lane = lax.broadcasted_iota(jnp.int32, picked.shape, 1)
    spot = owner // peers * LANES + tiles % slots
    thick = jnp.sum(jnp.where(lane == spot, picked, 0.0), axis=1, keepdims=True)
    live = lax.broadcasted_iota(jnp.int32, (slots, 1), 0) < live_ref[0]
    live = jnp.where(live, 1.0, 0.0)
    parts = [viscous * thick * live, live / thick]
    parts += [0.5 * live * marks[:, d : d + 1] for d in range(3)] + [live]
    for n, part in enumerate(parts):
        wide_ref[n] = jnp.broadcast_to(part, (slots, LANES))
    main = (species - 1) * slots
    tail = lax.broadcasted_iota(jnp.int32, (slots, LANES), 1)
    main_lane = lax.broadcasted_iota(jnp.int32, (slots, main), 1)
    main_slot = lax.broadcasted_iota(jnp.int32, (slots, main), 0) == main_lane % slots
    tail_slot = lax.broadcasted_iota(jnp.int32, (slots, LANES), 0) == tail % slots
    for s in range(species):
        rows = slice(s * slots, (s + 1) * slots)
        rate = jnp.zeros((slots, main), jnp.float32)
        for k in range(species - 1):
            rate = jnp.where(main_lane // slots == k, rate_ref[s, k], rate)
        rate = jnp.where(main_slot, rate, 0.0)
        high = rate.astype(jnp.bfloat16)
        mix_ref[rows, 0:main] = high
        mix_ref[rows, main : 2 * main] = (rate - high.astype(jnp.float32)).astype(jnp.bfloat16)
        mix_ref[rows, 2 * main : 3 * main] = high
        rate = jnp.where(tail_slot & (tail < 3 * slots), rate_ref[s, species - 1], 0.0)
        high = rate.astype(jnp.bfloat16).astype(jnp.float32)
        rate = jnp.where(tail // slots == 1, rate - high, high)
        mix_ref[rows, 3 * main :] = rate.astype(jnp.bfloat16)
    for fuel_ref in (fuel_even_ref, fuel_odd_ref):
        fuel_ref[3 * main + 3 * slots :, :] = jnp.zeros((LANES - 3 * slots, 2 * FACE), jnp.bfloat16)

    parity = lax.broadcasted_iota(jnp.int32, (slots, 2 * LANES), 1) // TE % 2
    for p in range(2):
        mask_ref[p] = jnp.where(parity == p, 1.0, 0.0).astype(jnp.bfloat16)
    slot = lax.broadcasted_iota(jnp.int32, (slots, slots), 0)
    keep = (destination_ref[...] == lax.axis_index(TEAM)) & (target_ref[...] == slot)
    keep = keep.astype(jnp.bfloat16)

    def build(pair, odd, some):
        left_ref = (left_even_ref, left_odd_ref)[odd]
        rims = pl.ds(pl.multiple_of(pair * FACE, FACE), FACE)
        for s in some:
            both = rims_ref[s, :, rims]
            for p in range(2):
                lanes = pl.ds(pl.multiple_of((2 * pair + p + 1) * FACE, FACE), FACE)
                rows = slice((p * species + s) * slots, (p * species + s + 1) * slots)
                f = fields_ref[s, :, lanes]
                high = f.astype(jnp.bfloat16)
                left_ref[rows, 0:FACE] = high
                left_ref[rows, FACE : 2 * FACE] = (f - high.astype(jnp.float32)).astype(jnp.bfloat16)
                left_ref[rows, 2 * FACE :] = both * mask_ref[p]

    def multiply(pair, odd, d):
        left_ref, sums_ref = ((left_even_ref, sums_even_ref), (left_odd_ref, sums_odd_ref))[odd]
        columns = slice(d * FACE, (d + 1) * FACE)
        sums_ref[:, columns] = jnp.dot(
            left_ref[...], weights_ref[:, columns], preferred_element_type=jnp.float32
        )

    def burn(pair, odd):
        kept_ref = (kept_even_ref, kept_odd_ref)[odd]
        both = pl.ds(pl.multiple_of(2 * pair * FACE, FACE), 2 * FACE)
        for s in range(species):
            recent = jnp.dot(keep, recent_ref[s, :, both], preferred_element_type=jnp.float32)
            older = jnp.dot(keep, older_ref[s, :, both], preferred_element_type=jnp.float32)
            kept_ref[s] = recent * (-16.0 / 12.0 * step_size) + older * (5.0 / 12.0 * step_size)

        fuel_ref, react_ref = ((fuel_even_ref, react_even_ref), (fuel_odd_ref, react_odd_ref))[odd]
        both = pl.ds(pl.multiple_of((2 * pair + 1) * FACE, FACE), 2 * FACE)
        over = jnp.concatenate([wide_ref[1]] * 4, axis=1)
        burning = fields_ref[0, :, both] * fields_ref[1, :, both] * over
        for k in range(species):
            fuel = fields_ref[k, :, both] * burning
            high = fuel.astype(jnp.bfloat16)
            low = (fuel - high.astype(jnp.float32)).astype(jnp.bfloat16)
            for n, part in enumerate((high, high, low)):
                start = n * main + k * slots if k < species - 1 else 3 * main + n * slots
                fuel_ref[start : start + slots, :] = part
        react_ref[...] = jnp.dot(mix_ref[...], fuel_ref[...], preferred_element_type=jnp.float32)

    def finish(pair, odd, some):
        kept_ref = (kept_even_ref, kept_odd_ref)[odd]
        sums_ref, react_ref = ((sums_even_ref, react_even_ref), (sums_odd_ref, react_odd_ref))[odd]
        for p in range(2):
            inner, before, here, after = (
                pl.ds(pl.multiple_of((2 * pair + p + n) * FACE, FACE), FACE) for n in (0, 0, 1, 2)
            )
            for g in range(slots // 16):
                rows = slice(g * 16, (g + 1) * 16)
                smooth, vx, vy, vz, live = (
                    jnp.concatenate([wide_ref[n, rows, :]] * 2, axis=1) for n in (0, 2, 3, 4, 5)
                )
                for s in some:
                    low, high = fields_ref[s, rows, before], fields_ref[s, rows, after]
                    line = s * slots + g * 16
                    react = react_ref[line : line + 16, p * FACE : (p + 1) * FACE]
                    line += p * species * slots
                    total, along_y, along_z = (
                        sums_ref[line : line + 16, d * FACE : (d + 1) * FACE] for d in range(3)
                    )
                    tend = smooth * (total + (low + high)) - vx * (high - low)
                    tend = (tend - vy * along_y) + (react - vz * along_z)
                    kept = kept_ref[s, rows, p * FACE : (p + 1) * FACE]
                    new = (fields_ref[s, rows, here] + kept) * live
                    new_fields_ref[s, rows, inner] = new + (step_size * 23.0 / 12.0) * tend
                    new_tend_ref[s, rows, inner] = tend.astype(jnp.bfloat16)

    thirds = [range(n * species // 3, (n + 1) * species // 3) for n in range(3)]
    pairs = TE // 2

    def stage(pair, odd):
        after, later = jnp.minimum(pair + 1, pairs - 1), jnp.minimum(pair + 2, pairs - 1)
        burn(after, 1 - odd)
        for d, some in enumerate(thirds):
            multiply(after, 1 - odd, d)
            finish(pair, odd, some)
            build(later, odd, some)

    for copy in (*ends(), *cells_in(0)):
        copy.wait()
    build(0, 0, range(species))
    for d in range(3):
        multiply(0, 0, d)
    burn(0, 0)
    build(1, 1, range(species))

    def four(c, carry):
        @pl.when(c + 2 < chunks)
        def _():
            for copy in cells_in(c + 2):
                copy.start()

        @pl.when(c + 1 < chunks)
        def _():
            for copy in cells_in(c + 1):
                copy.wait()

        stage(2 * c, 0)
        stage(2 * c + 1, 1)
        for copy in stores(c):
            copy.start()
        return carry

    lax.fori_loop(0, chunks, four, 0)
    for c in range(chunks):
        for copy in stores(c):
            copy.wait()


def add_kernel(
    live_ref, table_ref, fields_hbm, arrived_hbm, out_hbm, fields_ref, arrived_ref, got, sent
):
    species, peers = arrived_ref.shape[:2]
    slots = fields_ref.shape[1]

    def fetches(s):
        part = arrived_hbm.at[:, pl.ds(s * ROWS, ROWS)]
        return (
            pltpu.make_async_copy(part, arrived_ref.at[s], got.at[0, s]),
            pltpu.make_async_copy(fields_hbm.at[s], fields_ref.at[s], got.at[1, s]),
        )

    def store(s):
        return pltpu.make_async_copy(fields_ref.at[s], out_hbm.at[s], sent.at[s])

    for s in range(AHEAD):
        for copy in fetches(s):
            copy.start()
    me, first = lax.axis_index(TEAM), pl.multiple_of(lax.axis_index("grp") * LANES, LANES)
    notes = table_ref[:, pl.ds(first, LANES)]
    destination = notes[:, slots : 2 * slots]
    target = notes[:, 2 * slots : 3 * slots]
    peer = lax.broadcasted_iota(jnp.int32, (peers, slots), 0)
    mine = (destination == me.astype(jnp.float32)) & (peer != me)
    slot = jnp.max(jnp.where(mine, target, -1.0), axis=1, keepdims=True)
    index = lax.broadcasted_iota(jnp.int32, (peers, slots), 1)
    hot = (slot == index.astype(jnp.float32)) & (index < live_ref[0])
    hot = jnp.where(hot, step_size / SCALE, 0.0)
    hot = jnp.concatenate([hot, hot], axis=0).T.astype(jnp.bfloat16)
    for s in range(species):
        if s + AHEAD < species:
            for copy in fetches(s + AHEAD):
                copy.start()
        for copy in fetches(s):
            copy.wait()
        flat = arrived_ref.at[s].reshape(peers * ROWS, LANES)
        for c in range(ROWS // 2):
            lanes = slice(c * 2 * LANES, (c + 1) * 2 * LANES)
            arrived = jnp.concatenate(
                [flat[pl.ds(2 * c + k, peers, stride=ROWS), :] for k in range(2)], axis=1
            )
            high = arrived.astype(jnp.bfloat16)
            low = (arrived - high.astype(jnp.float32)).astype(jnp.bfloat16)
            fields_ref[s, :, lanes] += jnp.dot(
                hot, jnp.concatenate([high, low], axis=0), preferred_element_type=jnp.float32
            )
        store(s).start()
    for s in range(species):
        store(s).wait()


def smem():
    return pl.BlockSpec(memory_space=pltpu.SMEM)


def whole(shape):
    return pl.BlockSpec(shape, lambda i: (0,) * len(shape))


def params(mib, semantics=None):
    return pltpu.CompilerParams(vmem_limit_bytes=mib << 20, dimension_semantics=semantics)


def local(
    fields,
    ghosts,
    velocity,
    rate_matrix,
    recent_tend,
    older_tend,
    destination,
    target_slot,
    live_counts,
    tile_ids,
    sensor,
    flame_flags,
):
    slots, species, cells = fields.shape
    peers = lax.axis_size(TEAM)
    brick = sensor.shape[0]
    fields, ghosts, recent, older = (
        a.transpose(1, 0, 2) for a in (fields, ghosts, recent_tend, older_tend)
    )
    moves = (destination.reshape(1, slots), target_slot.reshape(1, slots))

    raw = pl.pallas_call(
        raw_kernel,
        name="raw_sensor",
        out_shape=jax.ShapeDtypeStruct(sensor.shape, jnp.bfloat16),
        in_specs=[smem(), pl.BlockSpec(memory_space=pltpu.VMEM)],
        out_specs=pl.BlockSpec(memory_space=pltpu.VMEM),
        compiler_params=params(58),
    )(flame_flags, sensor)
    below = passed_along(raw, "pen", 1)
    above = passed_along(raw, "pen", -1)

    anywhere = pl.BlockSpec(memory_space=pl.ANY)
    in_hbm = pl.BlockSpec(memory_space=pltpu.HBM)
    vmem = pl.BlockSpec(memory_space=pltpu.VMEM)
    outgoing = pl.pallas_call(
        send_kernel,
        name="outgoing_histories",
        out_shape=jax.ShapeDtypeStruct((peers, species * ROWS, LANES), jnp.float32),
        in_specs=[vmem, in_hbm, in_hbm],
        out_specs=vmem,
        scratch_shapes=[
            pltpu.VMEM(recent.shape, jnp.bfloat16),
            pltpu.VMEM(older.shape, jnp.bfloat16),
            pltpu.SemaphoreType.DMA((2, species)),
        ],
        compiler_params=params(50),
        cost_estimate=pl.CostEstimate(flops=0, bytes_accessed=8 << 20, transcendentals=0),
    )(destination.reshape(1, slots), recent, older)
    outgoing = outgoing.astype(jnp.float16)

    shape = jax.ShapeDtypeStruct((species, slots, cells), jnp.float32)
    rims = jax.ShapeDtypeStruct((species, slots, TE * LANES), jnp.bfloat16)
    rims = pl.pallas_call(
        rims_kernel,
        name="rims",
        out_shape=rims,
        in_specs=[anywhere],
        out_specs=anywhere,
        scratch_shapes=[
            pltpu.VMEM(ghosts.shape, jnp.float32),
            pltpu.VMEM(rims.shape, jnp.bfloat16),
            pltpu.SemaphoreType.DMA((species,)),
            pltpu.SemaphoreType.DMA((species,)),
        ],
        compiler_params=params(58),
        cost_estimate=pl.CostEstimate(flops=0, bytes_accessed=8 << 20, transcendentals=0),
    )(ghosts)
    below, above, rims, outgoing = lax.optimization_barrier((below, above, rims, outgoing))

    filtered, row = pl.pallas_call(
        filter_kernel,
        name="filtered_sensor",
        out_shape=(
            jax.ShapeDtypeStruct(sensor.shape, jnp.float32),
            jax.ShapeDtypeStruct((1, LANES), jnp.float32),
        ),
        in_specs=[smem()] + [vmem] * 6,
        out_specs=(vmem, vmem),
        compiler_params=params(32),
        cost_estimate=pl.CostEstimate(flops=0, bytes_accessed=4 << 20, transcendentals=0),
    )(flame_flags, jnp.asarray(banded(brick, brick)), sensor, below, above, *moves)
    rows = gathered(row, ("pen",))
    rows, outgoing = lax.optimization_barrier((rows, outgoing))
    arrived = lax.all_to_all(outgoing, TEAM, split_axis=0, concat_axis=0, tiled=True)
    table = gathered(rows, ("grp", "mig"))
    arrived = arrived.astype(jnp.float32)

    weights = jnp.asarray(plane_weights(), jnp.bfloat16)
    left = pltpu.VMEM((2 * species * slots, 6 * LANES), jnp.bfloat16)
    sums = pltpu.VMEM((2 * species * slots, 3 * FACE), jnp.float32)
    depth = 3 * (species - 1) * slots + LANES
    fuel = pltpu.VMEM((depth, 2 * FACE), jnp.bfloat16)
    react = pltpu.VMEM((species * slots, 2 * FACE), jnp.float32)
    kept = pltpu.VMEM((species, slots, 2 * FACE), jnp.float32)
    new_fields, new_tend = pl.pallas_call(
        main_kernel,
        name="updates",
        out_shape=(shape, jax.ShapeDtypeStruct(shape.shape, jnp.bfloat16)),
        in_specs=[smem()] * 2 + [vmem] * 5 + [anywhere] * 6,
        out_specs=(anywhere, anywhere),
        scratch_shapes=[
            pltpu.VMEM(weights.shape, jnp.bfloat16),
            pltpu.VMEM((species, slots, cells + 2 * FACE), jnp.float32),
            pltpu.VMEM(rims.shape, jnp.bfloat16),
            pltpu.VMEM(shape.shape, jnp.bfloat16),
            pltpu.VMEM(shape.shape, jnp.bfloat16),
            pltpu.VMEM(shape.shape, jnp.float32),
            pltpu.VMEM(shape.shape, jnp.bfloat16),
            pltpu.VMEM((species * slots, depth), jnp.bfloat16),
            pltpu.VMEM((6, slots, LANES), jnp.float32),
            pltpu.VMEM((2, slots, FACE), jnp.bfloat16),
            left,
            left,
            fuel,
            fuel,
            sums,
            sums,
            react,
            react,
            kept,
            kept,
            pltpu.SemaphoreType.DMA((5, TE // PLANES)),
            pltpu.SemaphoreType.DMA((2, TE // PLANES)),
        ],
        compiler_params=params(58),
        cost_estimate=pl.CostEstimate(flops=0, bytes_accessed=40 << 20, transcendentals=0),
    )(
        live_counts,
        rate_matrix,
        table,
        tile_ids.reshape(1, slots),
        velocity,
        *moves,
        weights,
        fields,
        ghosts,
        rims,
        recent,
        older,
    )

    new_fields = pl.pallas_call(
        add_kernel,
        name="arrived_histories",
        out_shape=shape,
        in_specs=[smem(), vmem, anywhere, anywhere],
        out_specs=anywhere,
        scratch_shapes=[
            pltpu.VMEM(shape.shape, jnp.float32),
            pltpu.VMEM((species, peers, ROWS, LANES), jnp.float32),
            pltpu.SemaphoreType.DMA((2, species)),
            pltpu.SemaphoreType.DMA((species,)),
        ],
        compiler_params=params(58),
        cost_estimate=pl.CostEstimate(flops=0, bytes_accessed=12 << 20, transcendentals=0),
    )(live_counts, table, new_fields, arrived)
    return new_fields.transpose(1, 0, 2), new_tend.transpose(1, 0, 2), filtered


def gathered(row, axes):
    for axis in axes:
        count = lax.axis_size(axis)
        here = lax.axis_index(axis)
        rows = [row] + [passed_along(row, axis, by) for by in range(1, count)]
        height, width = row.shape
        if axis == "grp":
            table = jnp.zeros((height, count * width), row.dtype)
        else:
            table = jnp.zeros((count * height, width), row.dtype)
        for by, part in enumerate(rows):
            place = (here - by) % count
            place = (0, place * width) if axis == "grp" else (place * height, 0)
            table = lax.dynamic_update_slice(table, part, place)
        row = table
    return row


def solution(mesh):
    split = P(EVERY, None, None)
    return jax.shard_map(
        local,
        mesh=mesh,
        in_specs=(
            split,
            split,
            P(None, EVERY),
            P(),
            split,
            split,
            P(EVERY),
            P(EVERY),
            P(EVERY),
            P(EVERY),
            P("pen", ("grp", "mig")),
            P("pen", ("grp", "mig")),
        ),
        out_specs=(split, split, P("pen", ("grp", "mig"))),
        check_vma=False,
    )
```

```python
import jax
import jax.numpy as jnp
import numpy as np
from jax import lax
from jax.experimental import pallas as pl
from jax.experimental.pallas import tpu as pltpu
from jax.sharding import PartitionSpec as P

TE = 16
TZ = 2
TCOL = 16
FACE = TE * TE
CELLS = TE**3
LANES = 128
ROWS = CELLS // LANES

viscous = 0.05
step_size = 0.25
thicken = 5.0

SCALE = 4096.0
PLANES = 4
AHEAD = 4

EVERY = ("grp", "mig", "pen")
TEAM = ("mig", "pen")


def passed_along(x, axis, by):
    peers = lax.axis_size(axis)
    return lax.ppermute(x, axis, [(i, (i + by) % peers) for i in range(peers)])


def banded(brick_rows, reach):
    sigma = reach / 2.0
    offsets = np.arange(-reach, reach + 1, dtype=np.float64)
    total = np.sum(np.exp(-offsets * offsets / (2.0 * sigma * sigma)))
    row = np.arange(brick_rows)[:, None]
    col = np.arange(brick_rows + 2 * reach)[None, :]
    offset = (col - reach - row).astype(np.float64)
    weights = np.where(np.abs(offset) <= reach, np.exp(-offset * offset / (2.0 * sigma * sigma)), 0)
    return (weights / total).astype(np.float32)


def raw_kernel(flags_ref, sensor_ref, raw_ref):
    for r in range(TZ):
        for k in range(TCOL):
            rows, cols = slice(r * TE, (r + 1) * TE), slice(k * FACE, (k + 1) * FACE)
            flag = flags_ref[r, k].astype(jnp.float32)
            raw_ref[rows, cols] = (sensor_ref[rows, cols] * flag).astype(jnp.bfloat16)


def filter_kernel(
    flags_ref,
    weights_ref,
    sensor_ref,
    below_ref,
    above_ref,
    destination_ref,
    target_ref,
    filtered_ref,
    row_ref,
):
    lane = lax.broadcasted_iota(jnp.int32, (1, LANES), 1)
    slots = destination_ref.shape[1]
    row = jnp.concatenate(
        [
            jnp.zeros((1, slots), jnp.float32),
            destination_ref[...].astype(jnp.float32),
            target_ref[...].astype(jnp.float32),
            jnp.zeros((1, LANES - 3 * slots), jnp.float32),
        ],
        axis=1,
    )
    brick = sensor_ref.shape[0]
    for k in range(TCOL):
        cols = slice(k * FACE, (k + 1) * FACE)
        own = [
            sensor_ref[r * TE : (r + 1) * TE, cols] * flags_ref[r, k].astype(jnp.float32)
            for r in range(TZ)
        ]
        widened = jnp.concatenate(
            [below_ref[:, cols].astype(jnp.float32)] + own + [above_ref[:, cols].astype(jnp.float32)],
            axis=0,
        )
        filtered = jnp.dot(
            weights_ref[...],
            widened,
            precision=lax.Precision.HIGHEST,
            preferred_element_type=jnp.float32,
        )
        filtered_ref[:, cols] = filtered
        clipped = jnp.minimum(filtered, 1.0)
        for r in range(TZ):
            total = jnp.sum(
                jnp.sum(clipped[r * TE : (r + 1) * TE], axis=0, keepdims=True), axis=1, keepdims=True
            )
            thick = 1.0 + (thicken - 1.0) * (total / float(TE * FACE))
            row = jnp.where(lane == r * TCOL + k, thick, row)
    row_ref[...] = row


def send_kernel(
    destination_ref, recent_hbm, older_hbm, out_ref, recent_ref, older_ref, got
):
    species, slots, _ = recent_ref.shape
    peers = out_ref.shape[0]

    def fetches(s):
        return (
            pltpu.make_async_copy(recent_hbm.at[s], recent_ref.at[s], got.at[0, s]),
            pltpu.make_async_copy(older_hbm.at[s], older_ref.at[s], got.at[1, s]),
        )

    for s in range(AHEAD):
        for copy in fetches(s):
            copy.start()
    peer = lax.broadcasted_iota(jnp.int32, (peers, slots), 0)
    hot = ((destination_ref[...] == peer) & (peer != lax.axis_index(TEAM))).astype(jnp.bfloat16)
    flat = out_ref.reshape(peers * species * ROWS, LANES)
    for s in range(species):
        if s + AHEAD < species:
            for copy in fetches(s + AHEAD):
                copy.start()
        for copy in fetches(s):
            copy.wait()
        recent = jnp.dot(hot, recent_ref[s], preferred_element_type=jnp.float32)
        older = jnp.dot(hot, older_ref[s], preferred_element_type=jnp.float32)
        mixed = recent * (-16.0 / 12.0 * SCALE) + older * (5.0 / 12.0 * SCALE)
        for k in range(ROWS):
            flat[pl.ds(s * ROWS + k, peers, stride=species * ROWS), :] = mixed[
                :, k * LANES : (k + 1) * LANES
            ]


def lefts_kernel(
    fields_hbm, ghosts_hbm, lefts_hbm, fields_ref, ghosts_ref, lefts_ref, got, sent
):
    species, slots, _ = fields_ref.shape

    def fetches(s):
        return (
            pltpu.make_async_copy(ghosts_hbm.at[s], ghosts_ref.at[s], got.at[0, s]),
            pltpu.make_async_copy(fields_hbm.at[s], fields_ref.at[s], got.at[1, s]),
        )

    def store(s):
        return pltpu.make_async_copy(lefts_ref.at[s], lefts_hbm.at[:, :, s], sent.at[s])

    for s in range(species):
        for copy in fetches(s):
            copy.start()
    quarter = lax.broadcasted_iota(jnp.int32, (slots, LANES), 1) // (2 * TE)
    parity = lax.broadcasted_iota(jnp.int32, (slots, FACE), 1) // TE % 2
    masks = [jnp.where(parity == p, 1.0, 0.0).astype(jnp.bfloat16) for p in range(2)]

    def one(s, carry):
        for copy in fetches(s):
            copy.wait()
        for block in range(2):
            faces = [
                ghosts_ref[s, :, w * FACE + block * LANES : w * FACE + (block + 1) * LANES]
                for w in (4, 5, 2, 3)
            ]
            for q in range(4):
                rim = faces[0]
                for n in range(4):
                    turned = pltpu.roll(faces[n], (n - q) % 4 * 2 * TE, 1) if n != q else faces[n]
                    rim = turned if n == 0 else jnp.where(quarter == n, turned, rim)
                high = rim.astype(jnp.bfloat16)
                low = (rim - high.astype(jnp.float32)).astype(jnp.bfloat16)
                rim = jnp.concatenate([high, low], axis=1)
                pair = block * 4 + q
                for p in range(2):
                    f = fields_ref[s, :, (2 * pair + p) * FACE : (2 * pair + p + 1) * FACE]
                    high = f.astype(jnp.bfloat16)
                    low = (f - high.astype(jnp.float32)).astype(jnp.bfloat16)
                    lefts_ref[s, pair, p, :, 0:FACE] = high
                    lefts_ref[s, pair, p, :, FACE : 2 * FACE] = low
                    lefts_ref[s, pair, p, :, 2 * FACE :] = rim * masks[p]
        store(s).start()
        return carry

    lax.fori_loop(0, species, one, 0)
    for s in range(species):
        store(s).wait()


def plane_weights():
    weights = np.zeros((6 * LANES, 3 * FACE), np.float32)
    for cell in range(FACE):
        y, z = divmod(cell, TE)
        for d, at, step in ((0, y, TE), (1, z, 1)):
            for way in (-1, 1):
                if 0 <= at + way < TE:
                    rows = [cell + way * step, FACE + cell + way * step]
                else:
                    face = (2 + (way > 0)) if d == 0 else (way > 0)
                    spot = 2 * FACE + face * 2 * TE + (z if d == 0 else y)
                    rows = [spot, spot + TE, spot + LANES, spot + LANES + TE]
                weights[rows, cell] += 1.0
                weights[rows, (1 + d) * FACE + cell] += way
        weights[[cell, FACE + cell], cell] -= 6.0
    return weights


def main_kernel(
    live_ref,
    rate_ref,
    table_ref,
    tiles_ref,
    velocity_ref,
    destination_ref,
    target_ref,
    weights_hbm,
    fields_hbm,
    ghosts_hbm,
    lefts_hbm,
    recent_hbm,
    older_hbm,
    new_fields_hbm,
    new_tend_hbm,
    weights_ref,
    fields_ref,
    lefts_ref,
    recent_ref,
    older_ref,
    new_fields_ref,
    new_tend_ref,
    mix_ref,
    wide_ref,
    fuel_even_ref,
    fuel_odd_ref,
    sums_even_ref,
    sums_odd_ref,
    react_even_ref,
    react_odd_ref,
    kept_even_ref,
    kept_odd_ref,
    got,
    sent,
):
    species, slots, cells = new_fields_ref.shape
    peers = table_ref.shape[0]
    chunk = PLANES * FACE
    chunks = cells // chunk

    def span(c, length, skipped=0):
        return pl.ds(pl.multiple_of(skipped + c * length, LANES), length)

    def cells_in(c):
        lanes, inner, pairs = span(c, chunk), span(c, chunk, FACE), pl.ds(c * PLANES // 2, PLANES // 2)
        return (
            pltpu.make_async_copy(
                fields_hbm.at[:, :, lanes], fields_ref.at[:, :, inner], got.at[0, c]
            ),
            pltpu.make_async_copy(
                lefts_hbm.at[pairs], lefts_ref.at[pairs], got.at[1, c]
            ),
            pltpu.make_async_copy(
                recent_hbm.at[:, :, lanes], recent_ref.at[:, :, lanes], got.at[2, c]
            ),
            pltpu.make_async_copy(
                older_hbm.at[:, :, lanes], older_ref.at[:, :, lanes], got.at[3, c]
            ),
        )

    def ends():
        return (
            pltpu.make_async_copy(weights_hbm, weights_ref, got.at[4, 0]),
            pltpu.make_async_copy(
                ghosts_hbm.at[:, :, pl.ds(0, FACE)], fields_ref.at[:, :, pl.ds(0, FACE)], got.at[4, 1]
            ),
            pltpu.make_async_copy(
                ghosts_hbm.at[:, :, pl.ds(FACE, FACE)],
                fields_ref.at[:, :, pl.ds(FACE + cells, FACE)],
                got.at[4, 2],
            ),
        )

    def stores(c):
        lanes = span(c, chunk)
        return (
            pltpu.make_async_copy(
                new_fields_ref.at[:, :, lanes], new_fields_hbm.at[:, :, lanes], sent.at[0, c]
            ),
            pltpu.make_async_copy(
                new_tend_ref.at[:, :, lanes], new_tend_hbm.at[:, :, lanes], sent.at[1, c]
            ),
        )

    for copy in ends():
        copy.start()
    for c in range(2):
        for copy in cells_in(c):
            copy.start()

    marks = jnp.concatenate(
        [velocity_ref[...], tiles_ref[...].astype(jnp.float32), jnp.zeros((4, slots), jnp.float32)], axis=0
    ).T
    tiles = marks[:, 3:4].astype(jnp.int32)
    owner = tiles // slots
    wanted = lax.broadcasted_iota(jnp.int32, (slots, peers), 1) == owner % peers
    picked = jnp.dot(
        wanted.astype(jnp.float32),
        table_ref[...],
        precision=lax.Precision.HIGHEST,
        preferred_element_type=jnp.float32,
    )
    lane = lax.broadcasted_iota(jnp.int32, picked.shape, 1)
    spot = owner // peers * LANES + tiles % slots
    thick = jnp.sum(jnp.where(lane == spot, picked, 0.0), axis=1, keepdims=True)
    live = lax.broadcasted_iota(jnp.int32, (slots, 1), 0) < live_ref[0]
    live = jnp.where(live, 1.0, 0.0)
    parts = [viscous * thick * live, live / thick]
    parts += [0.5 * live * marks[:, d : d + 1] for d in range(3)] + [live]
    for n, part in enumerate(parts):
        wide_ref[n] = jnp.broadcast_to(part, (slots, LANES))
    main = (species - 1) * slots
    tail = lax.broadcasted_iota(jnp.int32, (slots, LANES), 1)
    main_lane = lax.broadcasted_iota(jnp.int32, (slots, main), 1)
    main_slot = lax.broadcasted_iota(jnp.int32, (slots, main), 0) == main_lane % slots
    tail_slot = lax.broadcasted_iota(jnp.int32, (slots, LANES), 0) == tail % slots
    for s in range(species):
        rows = slice(s * slots, (s + 1) * slots)
        rate = jnp.zeros((slots, main), jnp.float32)
        for k in range(species - 1):
            rate = jnp.where(main_lane // slots == k, rate_ref[s, k], rate)
        rate = jnp.where(main_slot, rate, 0.0)
        high = rate.astype(jnp.bfloat16)
        mix_ref[rows, 0:main] = high
        mix_ref[rows, main : 2 * main] = (rate - high.astype(jnp.float32)).astype(jnp.bfloat16)
        mix_ref[rows, 2 * main : 3 * main] = high
        rate = jnp.where(tail_slot & (tail < 3 * slots), rate_ref[s, species - 1], 0.0)
        high = rate.astype(jnp.bfloat16).astype(jnp.float32)
        rate = jnp.where(tail // slots == 1, rate - high, high)
        mix_ref[rows, 3 * main :] = rate.astype(jnp.bfloat16)
    for fuel_ref in (fuel_even_ref, fuel_odd_ref):
        fuel_ref[3 * main + 3 * slots :, :] = jnp.zeros((LANES - 3 * slots, 2 * FACE), jnp.bfloat16)

    slot = lax.broadcasted_iota(jnp.int32, (slots, slots), 0)
    keep = (destination_ref[...] == lax.axis_index(TEAM)) & (target_ref[...] == slot)
    keep = keep.astype(jnp.bfloat16)

    def multiply(pair, odd, d):
        sums_ref = (sums_even_ref, sums_odd_ref)[odd]
        columns = slice(d * FACE, (d + 1) * FACE)
        sums_ref[:, columns] = jnp.dot(
            lefts_ref[pair].reshape(sums_ref.shape[0], 6 * LANES),
            weights_ref[:, columns],
            preferred_element_type=jnp.float32,
        )

    def burn(pair, odd):
        kept_ref = (kept_even_ref, kept_odd_ref)[odd]
        both = pl.ds(pl.multiple_of(2 * pair * FACE, FACE), 2 * FACE)
        for s in range(species):
            recent = jnp.dot(keep, recent_ref[s, :, both], preferred_element_type=jnp.float32)
            older = jnp.dot(keep, older_ref[s, :, both], preferred_element_type=jnp.float32)
            kept_ref[s] = recent * (-16.0 / 12.0 * step_size) + older * (5.0 / 12.0 * step_size)

        fuel_ref, react_ref = ((fuel_even_ref, react_even_ref), (fuel_odd_ref, react_odd_ref))[odd]
        both = pl.ds(pl.multiple_of((2 * pair + 1) * FACE, FACE), 2 * FACE)
        over = jnp.concatenate([wide_ref[1]] * 4, axis=1)
        burning = fields_ref[0, :, both] * fields_ref[1, :, both] * over
        for k in range(species):
            fuel = fields_ref[k, :, both] * burning
            high = fuel.astype(jnp.bfloat16)
            low = (fuel - high.astype(jnp.float32)).astype(jnp.bfloat16)
            for n, part in enumerate((high, high, low)):
                start = n * main + k * slots if k < species - 1 else 3 * main + n * slots
                fuel_ref[start : start + slots, :] = part
        react_ref[...] = jnp.dot(mix_ref[...], fuel_ref[...], preferred_element_type=jnp.float32)

    def finish(pair, odd, some):
        kept_ref = (kept_even_ref, kept_odd_ref)[odd]
        sums_ref, react_ref = ((sums_even_ref, react_even_ref), (sums_odd_ref, react_odd_ref))[odd]
        for p in range(2):
            inner, before, here, after = (
                pl.ds(pl.multiple_of((2 * pair + p + n) * FACE, FACE), FACE) for n in (0, 0, 1, 2)
            )
            for g in range(slots // 16):
                rows = slice(g * 16, (g + 1) * 16)
                smooth, vx, vy, vz, live = (
                    jnp.concatenate([wide_ref[n, rows, :]] * 2, axis=1) for n in (0, 2, 3, 4, 5)
                )
                for s in some:
                    low, high = fields_ref[s, rows, before], fields_ref[s, rows, after]
                    line = s * slots + g * 16
                    react = react_ref[line : line + 16, p * FACE : (p + 1) * FACE]
                    line += p * species * slots
                    total, along_y, along_z = (
                        sums_ref[line : line + 16, d * FACE : (d + 1) * FACE] for d in range(3)
                    )
                    tend = smooth * (total + (low + high)) - vx * (high - low)
                    tend = (tend - vy * along_y) + (react - vz * along_z)
                    kept = kept_ref[s, rows, p * FACE : (p + 1) * FACE]
                    new = (fields_ref[s, rows, here] + kept) * live
                    new_fields_ref[s, rows, inner] = new + (step_size * 23.0 / 12.0) * tend
                    new_tend_ref[s, rows, inner] = tend.astype(jnp.bfloat16)

    thirds = [range(n * species // 3, (n + 1) * species // 3) for n in range(3)]
    pairs = TE // 2

    def stage(pair, odd):
        after = jnp.minimum(pair + 1, pairs - 1)
        burn(after, 1 - odd)
        for d, some in enumerate(thirds):
            multiply(after, 1 - odd, d)
            finish(pair, odd, some)

    for copy in (*ends(), *cells_in(0)):
        copy.wait()
    for d in range(3):
        multiply(0, 0, d)
    burn(0, 0)

    def four(c, carry):
        @pl.when(c + 2 < chunks)
        def _():
            for copy in cells_in(c + 2):
                copy.start()

        stage(2 * c, 0)

        @pl.when(c + 1 < chunks)
        def _():
            for copy in cells_in(c + 1):
                copy.wait()

        stage(2 * c + 1, 1)
        for copy in stores(c):
            copy.start()
        return carry

    lax.fori_loop(0, chunks, four, 0)
    for c in range(chunks):
        for copy in stores(c):
            copy.wait()


def add_kernel(
    live_ref, table_ref, fields_hbm, arrived_hbm, out_hbm, fields_ref, arrived_ref, got, sent
):
    species, peers = arrived_ref.shape[:2]
    slots = fields_ref.shape[1]

    def fetches(s):
        part = arrived_hbm.at[:, pl.ds(s * ROWS, ROWS)]
        return (
            pltpu.make_async_copy(part, arrived_ref.at[s], got.at[0, s]),
            pltpu.make_async_copy(fields_hbm.at[s], fields_ref.at[s], got.at[1, s]),
        )

    def store(s):
        return pltpu.make_async_copy(fields_ref.at[s], out_hbm.at[s], sent.at[s])

    for s in range(AHEAD):
        for copy in fetches(s):
            copy.start()
    me, first = lax.axis_index(TEAM), pl.multiple_of(lax.axis_index("grp") * LANES, LANES)
    notes = table_ref[:, pl.ds(first, LANES)]
    destination = notes[:, slots : 2 * slots]
    target = notes[:, 2 * slots : 3 * slots]
    peer = lax.broadcasted_iota(jnp.int32, (peers, slots), 0)
    mine = (destination == me.astype(jnp.float32)) & (peer != me)
    slot = jnp.max(jnp.where(mine, target, -1.0), axis=1, keepdims=True)
    index = lax.broadcasted_iota(jnp.int32, (peers, slots), 1)
    hot = (slot == index.astype(jnp.float32)) & (index < live_ref[0])
    hot = jnp.where(hot, step_size / SCALE, 0.0)
    hot = jnp.concatenate([hot, hot], axis=0).T.astype(jnp.bfloat16)
    for s in range(species):
        if s + AHEAD < species:
            for copy in fetches(s + AHEAD):
                copy.start()
        for copy in fetches(s):
            copy.wait()
        flat = arrived_ref.at[s].reshape(peers * ROWS, LANES)
        for c in range(ROWS // 2):
            lanes = slice(c * 2 * LANES, (c + 1) * 2 * LANES)
            arrived = jnp.concatenate(
                [flat[pl.ds(2 * c + k, peers, stride=ROWS), :] for k in range(2)], axis=1
            )
            high = arrived.astype(jnp.bfloat16)
            low = (arrived - high.astype(jnp.float32)).astype(jnp.bfloat16)
            fields_ref[s, :, lanes] += jnp.dot(
                hot, jnp.concatenate([high, low], axis=0), preferred_element_type=jnp.float32
            )
        store(s).start()
    for s in range(species):
        store(s).wait()


def smem():
    return pl.BlockSpec(memory_space=pltpu.SMEM)


def whole(shape):
    return pl.BlockSpec(shape, lambda i: (0,) * len(shape))


def params(mib, semantics=None):
    return pltpu.CompilerParams(vmem_limit_bytes=mib << 20, dimension_semantics=semantics)


def local(
    fields,
    ghosts,
    velocity,
    rate_matrix,
    recent_tend,
    older_tend,
    destination,
    target_slot,
    live_counts,
    tile_ids,
    sensor,
    flame_flags,
):
    slots, species, cells = fields.shape
    peers = lax.axis_size(TEAM)
    brick = sensor.shape[0]
    fields, ghosts, recent, older = (
        a.transpose(1, 0, 2) for a in (fields, ghosts, recent_tend, older_tend)
    )
    moves = (destination.reshape(1, slots), target_slot.reshape(1, slots))

    raw = pl.pallas_call(
        raw_kernel,
        name="raw_sensor",
        out_shape=jax.ShapeDtypeStruct(sensor.shape, jnp.bfloat16),
        in_specs=[smem(), pl.BlockSpec(memory_space=pltpu.VMEM)],
        out_specs=pl.BlockSpec(memory_space=pltpu.VMEM),
        compiler_params=params(58),
    )(flame_flags, sensor)
    below = passed_along(raw, "pen", 1)
    above = passed_along(raw, "pen", -1)

    anywhere = pl.BlockSpec(memory_space=pl.ANY)
    in_hbm = pl.BlockSpec(memory_space=pltpu.HBM)
    vmem = pl.BlockSpec(memory_space=pltpu.VMEM)
    outgoing = pl.pallas_call(
        send_kernel,
        name="outgoing_histories",
        out_shape=jax.ShapeDtypeStruct((peers, species * ROWS, LANES), jnp.float32),
        in_specs=[vmem, in_hbm, in_hbm],
        out_specs=vmem,
        scratch_shapes=[
            pltpu.VMEM(recent.shape, jnp.bfloat16),
            pltpu.VMEM(older.shape, jnp.bfloat16),
            pltpu.SemaphoreType.DMA((2, species)),
        ],
        compiler_params=params(50),
        cost_estimate=pl.CostEstimate(flops=0, bytes_accessed=8 << 20, transcendentals=0),
    )(destination.reshape(1, slots), recent, older)
    outgoing = outgoing.astype(jnp.float16)

    shape = jax.ShapeDtypeStruct((species, slots, cells), jnp.float32)
    lefts = (TE // 2, 2, species, slots, 6 * LANES)
    lefts = jax.ShapeDtypeStruct(lefts, jnp.bfloat16)
    lefts = pl.pallas_call(
        lefts_kernel,
        name="left_sides",
        out_shape=lefts,
        in_specs=[anywhere, anywhere],
        out_specs=anywhere,
        scratch_shapes=[
            pltpu.VMEM(shape.shape, jnp.float32),
            pltpu.VMEM(ghosts.shape, jnp.float32),
            pltpu.VMEM((species, TE // 2, 2, slots, 6 * LANES), jnp.bfloat16),
            pltpu.SemaphoreType.DMA((2, species)),
            pltpu.SemaphoreType.DMA((species,)),
        ],
        compiler_params=params(58),
        cost_estimate=pl.CostEstimate(flops=0, bytes_accessed=12 << 20, transcendentals=0),
    )(fields, ghosts)
    below, above, lefts, outgoing = lax.optimization_barrier((below, above, lefts, outgoing))

    filtered, row = pl.pallas_call(
        filter_kernel,
        name="filtered_sensor",
        out_shape=(
            jax.ShapeDtypeStruct(sensor.shape, jnp.float32),
            jax.ShapeDtypeStruct((1, LANES), jnp.float32),
        ),
        in_specs=[smem()] + [vmem] * 6,
        out_specs=(vmem, vmem),
        compiler_params=params(32),
        cost_estimate=pl.CostEstimate(flops=0, bytes_accessed=4 << 20, transcendentals=0),
    )(flame_flags, jnp.asarray(banded(brick, brick)), sensor, below, above, *moves)
    rows = gathered(row, ("pen",))
    rows, outgoing = lax.optimization_barrier((rows, outgoing))
    arrived = lax.all_to_all(outgoing, TEAM, split_axis=0, concat_axis=0, tiled=True)
    table = gathered(rows, ("grp", "mig"))
    arrived = arrived.astype(jnp.float32)

    weights = jnp.asarray(plane_weights(), jnp.bfloat16)
    sums = pltpu.VMEM((2 * species * slots, 3 * FACE), jnp.float32)
    depth = 3 * (species - 1) * slots + LANES
    fuel = pltpu.VMEM((depth, 2 * FACE), jnp.bfloat16)
    react = pltpu.VMEM((species * slots, 2 * FACE), jnp.float32)
    kept = pltpu.VMEM((species, slots, 2 * FACE), jnp.float32)
    new_fields, new_tend = pl.pallas_call(
        main_kernel,
        name="updates",
        out_shape=(shape, jax.ShapeDtypeStruct(shape.shape, jnp.bfloat16)),
        in_specs=[smem()] * 2 + [vmem] * 5 + [anywhere] * 6,
        out_specs=(anywhere, anywhere),
        scratch_shapes=[
            pltpu.VMEM(weights.shape, jnp.bfloat16),
            pltpu.VMEM((species, slots, cells + 2 * FACE), jnp.float32),
            pltpu.VMEM(lefts.shape, jnp.bfloat16),
            pltpu.VMEM(shape.shape, jnp.bfloat16),
            pltpu.VMEM(shape.shape, jnp.bfloat16),
            pltpu.VMEM(shape.shape, jnp.float32),
            pltpu.VMEM(shape.shape, jnp.bfloat16),
            pltpu.VMEM((species * slots, depth), jnp.bfloat16),
            pltpu.VMEM((6, slots, LANES), jnp.float32),
            fuel,
            fuel,
            sums,
            sums,
            react,
            react,
            kept,
            kept,
            pltpu.SemaphoreType.DMA((5, TE // PLANES)),
            pltpu.SemaphoreType.DMA((2, TE // PLANES)),
        ],
        compiler_params=params(58),
        cost_estimate=pl.CostEstimate(flops=0, bytes_accessed=40 << 20, transcendentals=0),
    )(
        live_counts,
        rate_matrix,
        table,
        tile_ids.reshape(1, slots),
        velocity,
        *moves,
        weights,
        fields,
        ghosts,
        lefts,
        recent,
        older,
    )

    new_fields = pl.pallas_call(
        add_kernel,
        name="arrived_histories",
        out_shape=shape,
        in_specs=[smem(), vmem, anywhere, anywhere],
        out_specs=anywhere,
        scratch_shapes=[
            pltpu.VMEM(shape.shape, jnp.float32),
            pltpu.VMEM((species, peers, ROWS, LANES), jnp.float32),
            pltpu.SemaphoreType.DMA((2, species)),
            pltpu.SemaphoreType.DMA((species,)),
        ],
        compiler_params=params(58),
        cost_estimate=pl.CostEstimate(flops=0, bytes_accessed=12 << 20, transcendentals=0),
    )(live_counts, table, new_fields, arrived)
    return new_fields.transpose(1, 0, 2), new_tend.transpose(1, 0, 2), filtered


def gathered(row, axes):
    for axis in axes:
        count = lax.axis_size(axis)
        here = lax.axis_index(axis)
        rows = [row] + [passed_along(row, axis, by) for by in range(1, count)]
        height, width = row.shape
        if axis == "grp":
            table = jnp.zeros((height, count * width), row.dtype)
        else:
            table = jnp.zeros((count * height, width), row.dtype)
        for by, part in enumerate(rows):
            place = (here - by) % count
            place = (0, place * width) if axis == "grp" else (place * height, 0)
            table = lax.dynamic_update_slice(table, part, place)
        row = table
    return row


def solution(mesh):
    split = P(EVERY, None, None)
    return jax.shard_map(
        local,
        mesh=mesh,
        in_specs=(
            split,
            split,
            P(None, EVERY),
            P(),
            split,
            split,
            P(EVERY),
            P(EVERY),
            P(EVERY),
            P(EVERY),
            P("pen", ("grp", "mig")),
            P("pen", ("grp", "mig")),
        ),
        out_specs=(split, split, P("pen", ("grp", "mig"))),
        check_vma=False,
    )
```

```python
import jax
import jax.numpy as jnp
import numpy as np
from jax import lax
from jax.experimental import pallas as pl
from jax.experimental.pallas import tpu as pltpu
from jax.sharding import PartitionSpec as P

TE = 16
TZ = 2
TCOL = 16
FACE = TE * TE
CELLS = TE**3
LANES = 128
ROWS = CELLS // LANES

viscous = 0.05
step_size = 0.25
thicken = 5.0

SCALE = 4096.0
PLANES = 4
AHEAD = 4

EVERY = ("grp", "mig", "pen")
TEAM = ("mig", "pen")


def passed_along(x, axis, by):
    peers = lax.axis_size(axis)
    return lax.ppermute(x, axis, [(i, (i + by) % peers) for i in range(peers)])


def banded(brick_rows, reach):
    sigma = reach / 2.0
    offsets = np.arange(-reach, reach + 1, dtype=np.float64)
    total = np.sum(np.exp(-offsets * offsets / (2.0 * sigma * sigma)))
    row = np.arange(brick_rows)[:, None]
    col = np.arange(brick_rows + 2 * reach)[None, :]
    offset = (col - reach - row).astype(np.float64)
    weights = np.where(np.abs(offset) <= reach, np.exp(-offset * offset / (2.0 * sigma * sigma)), 0)
    return (weights / total).astype(np.float32)


def raw_kernel(flags_ref, sensor_hbm, raw_hbm, sensor_ref, raw_ref, got, sent):
    parts = got.shape[0]
    tiles = TCOL // parts

    def fetch(c):
        columns = pl.ds(c * tiles * FACE, tiles * FACE)
        return pltpu.make_async_copy(sensor_hbm.at[:, columns], sensor_ref.at[:, columns], got.at[c])

    def store(c):
        columns = pl.ds(c * tiles * FACE, tiles * FACE)
        return pltpu.make_async_copy(raw_ref.at[:, columns], raw_hbm.at[:, columns], sent.at[c])

    for c in range(parts):
        fetch(c).start()
    for c in range(parts):
        fetch(c).wait()
        for r in range(TZ):
            for k in range(c * tiles, (c + 1) * tiles):
                rows, cols = slice(r * TE, (r + 1) * TE), slice(k * FACE, (k + 1) * FACE)
                flag = flags_ref[r, k].astype(jnp.float32)
                raw_ref[rows, cols] = (sensor_ref[rows, cols] * flag).astype(jnp.bfloat16)
        store(c).start()
    for c in range(parts):
        store(c).wait()


def filter_kernel(
    flags_ref,
    weights_ref,
    sensor_ref,
    below_ref,
    above_ref,
    destination_ref,
    target_ref,
    filtered_ref,
    row_ref,
):
    lane = lax.broadcasted_iota(jnp.int32, (1, LANES), 1)
    slots = destination_ref.shape[1]
    row = jnp.concatenate(
        [
            jnp.zeros((1, slots), jnp.float32),
            destination_ref[...].astype(jnp.float32),
            target_ref[...].astype(jnp.float32),
            jnp.zeros((1, LANES - 3 * slots), jnp.float32),
        ],
        axis=1,
    )
    brick = sensor_ref.shape[0]
    for k in range(TCOL):
        cols = slice(k * FACE, (k + 1) * FACE)
        own = [
            sensor_ref[r * TE : (r + 1) * TE, cols] * flags_ref[r, k].astype(jnp.float32)
            for r in range(TZ)
        ]
        widened = jnp.concatenate(
            [below_ref[:, cols].astype(jnp.float32)] + own + [above_ref[:, cols].astype(jnp.float32)],
            axis=0,
        )
        filtered = jnp.dot(
            weights_ref[...],
            widened,
            precision=lax.Precision.HIGHEST,
            preferred_element_type=jnp.float32,
        )
        filtered_ref[:, cols] = filtered
        clipped = jnp.minimum(filtered, 1.0)
        for r in range(TZ):
            total = jnp.sum(
                jnp.sum(clipped[r * TE : (r + 1) * TE], axis=0, keepdims=True), axis=1, keepdims=True
            )
            thick = 1.0 + (thicken - 1.0) * (total / float(TE * FACE))
            row = jnp.where(lane == r * TCOL + k, thick, row)
    row_ref[...] = row


def send_kernel(
    destination_ref, recent_hbm, older_hbm, out_ref, recent_ref, older_ref, got
):
    species, slots, _ = recent_ref.shape
    peers = out_ref.shape[0]

    def fetches(s):
        return (
            pltpu.make_async_copy(recent_hbm.at[s], recent_ref.at[s], got.at[0, s]),
            pltpu.make_async_copy(older_hbm.at[s], older_ref.at[s], got.at[1, s]),
        )

    for s in range(AHEAD):
        for copy in fetches(s):
            copy.start()
    peer = lax.broadcasted_iota(jnp.int32, (peers, slots), 0)
    hot = ((destination_ref[...] == peer) & (peer != lax.axis_index(TEAM))).astype(jnp.bfloat16)
    flat = out_ref.reshape(peers * species * ROWS, LANES)
    for s in range(species):
        if s + AHEAD < species:
            for copy in fetches(s + AHEAD):
                copy.start()
        for copy in fetches(s):
            copy.wait()
        recent = jnp.dot(hot, recent_ref[s], preferred_element_type=jnp.float32)
        older = jnp.dot(hot, older_ref[s], preferred_element_type=jnp.float32)
        mixed = recent * (-16.0 / 12.0 * SCALE) + older * (5.0 / 12.0 * SCALE)
        for k in range(ROWS):
            flat[pl.ds(s * ROWS + k, peers, stride=species * ROWS), :] = mixed[
                :, k * LANES : (k + 1) * LANES
            ]


def rims_kernel(ghosts_hbm, rims_hbm, ghosts_ref, rims_ref, got, sent):
    species, slots, _ = ghosts_ref.shape

    def fetch(s):
        return pltpu.make_async_copy(ghosts_hbm.at[s], ghosts_ref.at[s], got.at[s])

    def store(s):
        return pltpu.make_async_copy(rims_ref.at[s], rims_hbm.at[s], sent.at[s])

    for s in range(species):
        fetch(s).start()
    quarter = lax.broadcasted_iota(jnp.int32, (slots, LANES), 1) // (2 * TE)

    def one(s, carry):
        fetch(s).wait()
        for block in range(2):
            faces = [
                ghosts_ref[s, :, w * FACE + block * LANES : w * FACE + (block + 1) * LANES]
                for w in (4, 5, 2, 3)
            ]
            for q in range(4):
                rim = faces[0]
                for n in range(4):
                    turned = pltpu.roll(faces[n], (n - q) % 4 * 2 * TE, 1) if n != q else faces[n]
                    rim = turned if n == 0 else jnp.where(quarter == n, turned, rim)
                high = rim.astype(jnp.bfloat16)
                low = (rim - high.astype(jnp.float32)).astype(jnp.bfloat16)
                start = (block * 4 + q) * 2 * LANES
                rims_ref[s, :, start : start + LANES] = high
                rims_ref[s, :, start + LANES : start + 2 * LANES] = low
        store(s).start()
        return carry

    lax.fori_loop(0, species, one, 0)
    for s in range(species):
        store(s).wait()


def plane_weights():
    weights = np.zeros((6 * LANES, 3 * FACE), np.float32)
    for cell in range(FACE):
        y, z = divmod(cell, TE)
        for d, at, step in ((0, y, TE), (1, z, 1)):
            for way in (-1, 1):
                if 0 <= at + way < TE:
                    rows = [cell + way * step, FACE + cell + way * step]
                else:
                    face = (2 + (way > 0)) if d == 0 else (way > 0)
                    spot = 2 * FACE + face * 2 * TE + (z if d == 0 else y)
                    rows = [spot, spot + TE, spot + LANES, spot + LANES + TE]
                weights[rows, cell] += 1.0
                weights[rows, (1 + d) * FACE + cell] += way
        weights[[cell, FACE + cell], cell] -= 6.0
    return weights


def main_kernel(
    live_ref,
    rate_ref,
    table_ref,
    tiles_ref,
    velocity_ref,
    destination_ref,
    target_ref,
    weights_hbm,
    fields_hbm,
    ghosts_hbm,
    rims_hbm,
    recent_hbm,
    older_hbm,
    new_fields_hbm,
    new_tend_hbm,
    weights_ref,
    fields_ref,
    rims_ref,
    recent_ref,
    older_ref,
    new_fields_ref,
    new_tend_ref,
    mix_ref,
    wide_ref,
    mask_ref,
    left_even_ref,
    left_odd_ref,
    fuel_even_ref,
    fuel_odd_ref,
    sums_even_ref,
    sums_odd_ref,
    react_even_ref,
    react_odd_ref,
    kept_even_ref,
    kept_odd_ref,
    got,
    sent,
):
    species, slots, cells = new_fields_ref.shape
    peers = table_ref.shape[0]
    chunk = PLANES * FACE
    chunks = cells // chunk

    def span(c, length, skipped=0):
        return pl.ds(pl.multiple_of(skipped + c * length, LANES), length)

    def cells_in(c):
        lanes, rims, inner = span(c, chunk), span(c, chunk // 2), span(c, chunk, FACE)
        return (
            pltpu.make_async_copy(
                fields_hbm.at[:, :, lanes], fields_ref.at[:, :, inner], got.at[0, c]
            ),
            pltpu.make_async_copy(
                rims_hbm.at[:, :, rims], rims_ref.at[:, :, rims], got.at[1, c]
            ),
            pltpu.make_async_copy(
                recent_hbm.at[:, :, lanes], recent_ref.at[:, :, lanes], got.at[2, c]
            ),
            pltpu.make_async_copy(
                older_hbm.at[:, :, lanes], older_ref.at[:, :, lanes], got.at[3, c]
            ),
        )

    def ends():
        return (
            pltpu.make_async_copy(weights_hbm, weights_ref, got.at[4, 0]),
            pltpu.make_async_copy(
                ghosts_hbm.at[:, :, pl.ds(0, FACE)], fields_ref.at[:, :, pl.ds(0, FACE)], got.at[4, 1]
            ),
            pltpu.make_async_copy(
                ghosts_hbm.at[:, :, pl.ds(FACE, FACE)],
                fields_ref.at[:, :, pl.ds(FACE + cells, FACE)],
                got.at[4, 2],
            ),
        )

    def stores(c):
        lanes = span(c, chunk)
        return (
            pltpu.make_async_copy(
                new_fields_ref.at[:, :, lanes], new_fields_hbm.at[:, :, lanes], sent.at[0, c]
            ),
            pltpu.make_async_copy(
                new_tend_ref.at[:, :, lanes], new_tend_hbm.at[:, :, lanes], sent.at[1, c]
            ),
        )

    for copy in ends():
        copy.start()
    for c in range(2):
        for copy in cells_in(c):
            copy.start()

    marks = jnp.concatenate(
        [velocity_ref[...], tiles_ref[...].astype(jnp.float32), jnp.zeros((4, slots), jnp.float32)], axis=0
    ).T
    tiles = marks[:, 3:4].astype(jnp.int32)
    owner = tiles // slots
    wanted = lax.broadcasted_iota(jnp.int32, (slots, peers), 1) == owner % peers
    picked = jnp.dot(
        wanted.astype(jnp.float32),
        table_ref[...],
        precision=lax.Precision.HIGHEST,
        preferred_element_type=jnp.float32,
    )
    lane = lax.broadcasted_iota(jnp.int32, picked.shape, 1)
    spot = owner // peers * LANES + tiles % slots
    thick = jnp.sum(jnp.where(lane == spot, picked, 0.0), axis=1, keepdims=True)
    live = lax.broadcasted_iota(jnp.int32, (slots, 1), 0) < live_ref[0]
    live = jnp.where(live, 1.0, 0.0)
    parts = [viscous * thick * live, live / thick]
    parts += [0.5 * live * marks[:, d : d + 1] for d in range(3)] + [live]
    for n, part in enumerate(parts):
        wide_ref[n] = jnp.broadcast_to(part, (slots, LANES))
    main = (species - 1) * slots
    tail = lax.broadcasted_iota(jnp.int32, (slots, LANES), 1)
    main_lane = lax.broadcasted_iota(jnp.int32, (slots, main), 1)
    main_slot = lax.broadcasted_iota(jnp.int32, (slots, main), 0) == main_lane % slots
    tail_slot = lax.broadcasted_iota(jnp.int32, (slots, LANES), 0) == tail % slots
    for s in range(species):
        rows = slice(s * slots, (s + 1) * slots)
        rate = jnp.zeros((slots, main), jnp.float32)
        for k in range(species - 1):
            rate = jnp.where(main_lane // slots == k, rate_ref[s, k], rate)
        rate = jnp.where(main_slot, rate, 0.0)
        high = rate.astype(jnp.bfloat16)
        mix_ref[rows, 0:main] = high
        mix_ref[rows, main : 2 * main] = (rate - high.astype(jnp.float32)).astype(jnp.bfloat16)
        mix_ref[rows, 2 * main : 3 * main] = high
        rate = jnp.where(tail_slot & (tail < 3 * slots), rate_ref[s, species - 1], 0.0)
        high = rate.astype(jnp.bfloat16).astype(jnp.float32)
        rate = jnp.where(tail // slots == 1, rate - high, high)
        mix_ref[rows, 3 * main :] = rate.astype(jnp.bfloat16)
    for fuel_ref in (fuel_even_ref, fuel_odd_ref):
        fuel_ref[3 * main + 3 * slots :, :] = jnp.zeros((LANES - 3 * slots, 2 * FACE), jnp.bfloat16)

    parity = lax.broadcasted_iota(jnp.int32, (slots, 2 * LANES), 1) // TE % 2
    for p in range(2):
        mask_ref[p] = jnp.where(parity == p, 1.0, 0.0).astype(jnp.bfloat16)
    slot = lax.broadcasted_iota(jnp.int32, (slots, slots), 0)
    keep = (destination_ref[...] == lax.axis_index(TEAM)) & (target_ref[...] == slot)
    keep = keep.astype(jnp.bfloat16)

    def build(pair, odd, some):
        left_ref = (left_even_ref, left_odd_ref)[odd]
        rims = pl.ds(pl.multiple_of(pair * FACE, FACE), FACE)
        for s in some:
            both = rims_ref[s, :, rims]
            for p in range(2):
                lanes = pl.ds(pl.multiple_of((2 * pair + p + 1) * FACE, FACE), FACE)
                rows = slice((p * species + s) * slots, (p * species + s + 1) * slots)
                f = fields_ref[s, :, lanes]
                high = f.astype(jnp.bfloat16)
                left_ref[rows, 0:FACE] = high
                left_ref[rows, FACE : 2 * FACE] = (f - high.astype(jnp.float32)).astype(jnp.bfloat16)
                left_ref[rows, 2 * FACE :] = both * mask_ref[p]

    def multiply(pair, odd, d):
        left_ref, sums_ref = ((left_even_ref, sums_even_ref), (left_odd_ref, sums_odd_ref))[odd]
        columns = slice(d * FACE, (d + 1) * FACE)
        sums_ref[:, columns] = jnp.dot(
            left_ref[...], weights_ref[:, columns], preferred_element_type=jnp.float32
        )

    def burn(pair, odd):
        kept_ref = (kept_even_ref, kept_odd_ref)[odd]
        both = pl.ds(pl.multiple_of(2 * pair * FACE, FACE), 2 * FACE)
        for s in range(species):
            recent = jnp.dot(keep, recent_ref[s, :, both], preferred_element_type=jnp.float32)
            older = jnp.dot(keep, older_ref[s, :, both], preferred_element_type=jnp.float32)
            kept_ref[s] = recent * (-16.0 / 12.0 * step_size) + older * (5.0 / 12.0 * step_size)

        fuel_ref, react_ref = ((fuel_even_ref, react_even_ref), (fuel_odd_ref, react_odd_ref))[odd]
        both = pl.ds(pl.multiple_of((2 * pair + 1) * FACE, FACE), 2 * FACE)
        over = jnp.concatenate([wide_ref[1]] * 4, axis=1)
        burning = fields_ref[0, :, both] * fields_ref[1, :, both] * over
        for k in range(species):
            fuel = fields_ref[k, :, both] * burning
            high = fuel.astype(jnp.bfloat16)
            low = (fuel - high.astype(jnp.float32)).astype(jnp.bfloat16)
            for n, part in enumerate((high, high, low)):
                start = n * main + k * slots if k < species - 1 else 3 * main + n * slots
                fuel_ref[start : start + slots, :] = part
        react_ref[...] = jnp.dot(mix_ref[...], fuel_ref[...], preferred_element_type=jnp.float32)

    def finish(pair, odd, some):
        kept_ref = (kept_even_ref, kept_odd_ref)[odd]
        sums_ref, react_ref = ((sums_even_ref, react_even_ref), (sums_odd_ref, react_odd_ref))[odd]
        for p in range(2):
            inner, before, here, after = (
                pl.ds(pl.multiple_of((2 * pair + p + n) * FACE, FACE), FACE) for n in (0, 0, 1, 2)
            )
            for g in range(slots // 16):
                rows = slice(g * 16, (g + 1) * 16)
                smooth, vx, vy, vz, live = (
                    jnp.concatenate([wide_ref[n, rows, :]] * 2, axis=1) for n in (0, 2, 3, 4, 5)
                )
                for s in some:
                    low, high = fields_ref[s, rows, before], fields_ref[s, rows, after]
                    line = s * slots + g * 16
                    react = react_ref[line : line + 16, p * FACE : (p + 1) * FACE]
                    line += p * species * slots
                    total, along_y, along_z = (
                        sums_ref[line : line + 16, d * FACE : (d + 1) * FACE] for d in range(3)
                    )
                    tend = smooth * (total + (low + high)) - vx * (high - low)
                    tend = (tend - vy * along_y) + (react - vz * along_z)
                    kept = kept_ref[s, rows, p * FACE : (p + 1) * FACE]
                    new = (fields_ref[s, rows, here] + kept) * live
                    new_fields_ref[s, rows, inner] = new + (step_size * 23.0 / 12.0) * tend
                    new_tend_ref[s, rows, inner] = tend.astype(jnp.bfloat16)

    thirds = [range(n * species // 3, (n + 1) * species // 3) for n in range(3)]
    pairs = TE // 2

    def stage(pair, odd):
        after, later = jnp.minimum(pair + 1, pairs - 1), jnp.minimum(pair + 2, pairs - 1)
        burn(after, 1 - odd)
        for d, some in enumerate(thirds):
            multiply(after, 1 - odd, d)
            finish(pair, odd, some)
            build(later, odd, some)

    for copy in (*ends(), *cells_in(0)):
        copy.wait()
    build(0, 0, range(species))
    for d in range(3):
        multiply(0, 0, d)
    burn(0, 0)
    build(1, 1, range(species))

    def four(c, carry):
        @pl.when(c + 2 < chunks)
        def _():
            for copy in cells_in(c + 2):
                copy.start()

        @pl.when(c + 1 < chunks)
        def _():
            for copy in cells_in(c + 1):
                copy.wait()

        stage(2 * c, 0)
        stage(2 * c + 1, 1)
        for copy in stores(c):
            copy.start()
        return carry

    lax.fori_loop(0, chunks, four, 0)
    for c in range(chunks):
        for copy in stores(c):
            copy.wait()


def add_kernel(
    live_ref, table_ref, fields_hbm, arrived_hbm, out_hbm, fields_ref, arrived_ref, got, sent
):
    species, peers = arrived_ref.shape[:2]
    slots = fields_ref.shape[1]

    def fetches(s):
        part = arrived_hbm.at[:, pl.ds(s * ROWS, ROWS)]
        return (
            pltpu.make_async_copy(part, arrived_ref.at[s, :, pl.ds(0, ROWS)], got.at[0, s]),
            pltpu.make_async_copy(fields_hbm.at[s], fields_ref.at[s], got.at[1, s]),
        )

    def store(s):
        return pltpu.make_async_copy(fields_ref.at[s], out_hbm.at[s], sent.at[s])

    for s in range(AHEAD):
        for copy in fetches(s):
            copy.start()
    me, first = lax.axis_index(TEAM), pl.multiple_of(lax.axis_index("grp") * LANES, LANES)
    notes = table_ref[:, pl.ds(first, LANES)]
    destination = notes[:, slots : 2 * slots]
    target = notes[:, 2 * slots : 3 * slots]
    peer = lax.broadcasted_iota(jnp.int32, (peers, slots), 0)
    mine = (destination == me.astype(jnp.float32)) & (peer != me)
    slot = jnp.max(jnp.where(mine, target, -1.0), axis=1, keepdims=True)
    index = lax.broadcasted_iota(jnp.int32, (peers, slots), 1)
    hot = (slot == index.astype(jnp.float32)) & (index < live_ref[0])
    hot = jnp.where(hot, step_size / SCALE, 0.0)
    hot = jnp.concatenate([hot, hot], axis=0).T.astype(jnp.bfloat16)
    for s in range(species):
        if s + AHEAD < species:
            for copy in fetches(s + AHEAD):
                copy.start()
        for copy in fetches(s):
            copy.wait()
        apart = arrived_ref.shape[2]
        flat = arrived_ref.at[s].reshape(peers * apart, LANES)
        for c in range(ROWS // 2):
            lanes = slice(c * 2 * LANES, (c + 1) * 2 * LANES)
            arrived = jnp.concatenate(
                [flat[pl.ds(2 * c + k, peers, stride=apart), :] for k in range(2)], axis=1
            )
            high = arrived.astype(jnp.bfloat16)
            low = (arrived - high.astype(jnp.float32)).astype(jnp.bfloat16)
            fields_ref[s, :, lanes] += jnp.dot(
                hot, jnp.concatenate([high, low], axis=0), preferred_element_type=jnp.float32
            )
        store(s).start()
    for s in range(species):
        store(s).wait()


def smem():
    return pl.BlockSpec(memory_space=pltpu.SMEM)


def whole(shape):
    return pl.BlockSpec(shape, lambda i: (0,) * len(shape))


def params(mib, semantics=None):
    return pltpu.CompilerParams(vmem_limit_bytes=mib << 20, dimension_semantics=semantics)


def local(
    fields,
    ghosts,
    velocity,
    rate_matrix,
    recent_tend,
    older_tend,
    destination,
    target_slot,
    live_counts,
    tile_ids,
    sensor,
    flame_flags,
):
    slots, species, cells = fields.shape
    peers = lax.axis_size(TEAM)
    brick = sensor.shape[0]
    fields, ghosts, recent, older = (
        a.transpose(1, 0, 2) for a in (fields, ghosts, recent_tend, older_tend)
    )
    moves = (destination.reshape(1, slots), target_slot.reshape(1, slots))

    raw = pl.pallas_call(
        raw_kernel,
        name="raw_sensor",
        out_shape=jax.ShapeDtypeStruct(sensor.shape, jnp.bfloat16),
        in_specs=[smem(), pl.BlockSpec(memory_space=pl.ANY)],
        out_specs=pl.BlockSpec(memory_space=pl.ANY),
        scratch_shapes=[
            pltpu.VMEM(sensor.shape, jnp.float32),
            pltpu.VMEM(sensor.shape, jnp.bfloat16),
            pltpu.SemaphoreType.DMA((4,)),
            pltpu.SemaphoreType.DMA((4,)),
        ],
        compiler_params=params(58),
    )(flame_flags, sensor)
    below = passed_along(raw, "pen", 1)
    above = passed_along(raw, "pen", -1)

    anywhere = pl.BlockSpec(memory_space=pl.ANY)
    in_hbm = pl.BlockSpec(memory_space=pltpu.HBM)
    vmem = pl.BlockSpec(memory_space=pltpu.VMEM)
    outgoing = pl.pallas_call(
        send_kernel,
        name="outgoing_histories",
        out_shape=jax.ShapeDtypeStruct((peers, species * ROWS, LANES), jnp.float32),
        in_specs=[vmem, in_hbm, in_hbm],
        out_specs=vmem,
        scratch_shapes=[
            pltpu.VMEM(recent.shape, jnp.bfloat16),
            pltpu.VMEM(older.shape, jnp.bfloat16),
            pltpu.SemaphoreType.DMA((2, species)),
        ],
        compiler_params=params(50),
        cost_estimate=pl.CostEstimate(flops=0, bytes_accessed=8 << 20, transcendentals=0),
    )(destination.reshape(1, slots), recent, older)
    outgoing = outgoing.astype(jnp.float16)

    shape = jax.ShapeDtypeStruct((species, slots, cells), jnp.float32)
    rims = jax.ShapeDtypeStruct((species, slots, TE * LANES), jnp.bfloat16)
    rims = pl.pallas_call(
        rims_kernel,
        name="rims",
        out_shape=rims,
        in_specs=[anywhere],
        out_specs=anywhere,
        scratch_shapes=[
            pltpu.VMEM(ghosts.shape, jnp.float32),
            pltpu.VMEM(rims.shape, jnp.bfloat16),
            pltpu.SemaphoreType.DMA((species,)),
            pltpu.SemaphoreType.DMA((species,)),
        ],
        compiler_params=params(58),
        cost_estimate=pl.CostEstimate(flops=0, bytes_accessed=8 << 20, transcendentals=0),
    )(ghosts)
    below, above, rims, outgoing = lax.optimization_barrier((below, above, rims, outgoing))

    filtered, row = pl.pallas_call(
        filter_kernel,
        name="filtered_sensor",
        out_shape=(
            jax.ShapeDtypeStruct(sensor.shape, jnp.float32),
            jax.ShapeDtypeStruct((1, LANES), jnp.float32),
        ),
        in_specs=[smem()] + [vmem] * 6,
        out_specs=(vmem, vmem),
        compiler_params=params(32),
        cost_estimate=pl.CostEstimate(flops=0, bytes_accessed=4 << 20, transcendentals=0),
    )(flame_flags, jnp.asarray(banded(brick, brick)), sensor, below, above, *moves)
    rows = stacked(row)
    rows, outgoing = lax.optimization_barrier((rows, outgoing))
    arrived = lax.all_to_all(outgoing, TEAM, split_axis=0, concat_axis=0, tiled=True)
    table = spread(rows)
    arrived = arrived.astype(jnp.float32)

    weights = jnp.asarray(plane_weights(), jnp.bfloat16)
    left = pltpu.VMEM((2 * species * slots, 6 * LANES), jnp.bfloat16)
    sums = pltpu.VMEM((2 * species * slots, 3 * FACE), jnp.float32)
    depth = 3 * (species - 1) * slots + LANES
    fuel = pltpu.VMEM((depth, 2 * FACE), jnp.bfloat16)
    react = pltpu.VMEM((species * slots, 2 * FACE), jnp.float32)
    kept = pltpu.VMEM((species, slots, 2 * FACE), jnp.float32)
    new_fields, new_tend = pl.pallas_call(
        main_kernel,
        name="updates",
        out_shape=(shape, jax.ShapeDtypeStruct(shape.shape, jnp.bfloat16)),
        in_specs=[smem()] * 2 + [vmem] * 5 + [anywhere] * 6,
        out_specs=(anywhere, anywhere),
        scratch_shapes=[
            pltpu.VMEM(weights.shape, jnp.bfloat16),
            pltpu.VMEM((species, slots, cells + 2 * FACE), jnp.float32),
            pltpu.VMEM(rims.shape, jnp.bfloat16),
            pltpu.VMEM(shape.shape, jnp.bfloat16),
            pltpu.VMEM(shape.shape, jnp.bfloat16),
            pltpu.VMEM(shape.shape, jnp.float32),
            pltpu.VMEM(shape.shape, jnp.bfloat16),
            pltpu.VMEM((species * slots, depth), jnp.bfloat16),
            pltpu.VMEM((6, slots, LANES), jnp.float32),
            pltpu.VMEM((2, slots, FACE), jnp.bfloat16),
            left,
            left,
            fuel,
            fuel,
            sums,
            sums,
            react,
            react,
            kept,
            kept,
            pltpu.SemaphoreType.DMA((5, TE // PLANES)),
            pltpu.SemaphoreType.DMA((2, TE // PLANES)),
        ],
        compiler_params=params(58),
        cost_estimate=pl.CostEstimate(flops=0, bytes_accessed=40 << 20, transcendentals=0),
    )(
        live_counts,
        rate_matrix,
        table,
        tile_ids.reshape(1, slots),
        velocity,
        *moves,
        weights,
        fields,
        ghosts,
        rims,
        recent,
        older,
    )

    new_fields = pl.pallas_call(
        add_kernel,
        name="arrived_histories",
        out_shape=shape,
        in_specs=[smem(), vmem, anywhere, anywhere],
        out_specs=anywhere,
        scratch_shapes=[
            pltpu.VMEM(shape.shape, jnp.float32),
            pltpu.VMEM((species, peers, ROWS + 8, LANES), jnp.float32),
            pltpu.SemaphoreType.DMA((2, species)),
            pltpu.SemaphoreType.DMA((species,)),
        ],
        compiler_params=params(58),
        cost_estimate=pl.CostEstimate(flops=0, bytes_accessed=12 << 20, transcendentals=0),
    )(live_counts, table, new_fields, arrived)
    return new_fields.transpose(1, 0, 2), new_tend.transpose(1, 0, 2), filtered


def stacked(row):
    count, here = lax.axis_size("pen"), lax.axis_index("pen")
    table = jnp.zeros((count, row.shape[1]), row.dtype)
    for by in range(count):
        part = row if by == 0 else passed_along(row, "pen", by)
        table = lax.dynamic_update_slice(table, part, ((here - by) % count, 0))
    return table


def spread(rows):
    groups, migs = lax.axis_size("grp"), lax.axis_size("mig")
    group, mig = lax.axis_index("grp"), lax.axis_index("mig")
    height, width = rows.shape
    table = jnp.zeros((migs * height, groups * width), rows.dtype)
    for by_group in range(groups):
        for by_mig in range(migs):
            part = rows
            if by_group + by_mig > 0:
                pairs = [
                    (g * migs + m, (g + by_group) % groups * migs + (m + by_mig) % migs)
                    for g in range(groups)
                    for m in range(migs)
                ]
                part = lax.ppermute(rows, ("grp", "mig"), pairs)
            place = ((mig - by_mig) % migs * height, (group - by_group) % groups * width)
            table = lax.dynamic_update_slice(table, part, place)
    return table


def solution(mesh):
    split = P(EVERY, None, None)
    return jax.shard_map(
        local,
        mesh=mesh,
        in_specs=(
            split,
            split,
            P(None, EVERY),
            P(),
            split,
            split,
            P(EVERY),
            P(EVERY),
            P(EVERY),
            P(EVERY),
            P("pen", ("grp", "mig")),
            P("pen", ("grp", "mig")),
        ),
        out_specs=(split, split, P("pen", ("grp", "mig"))),
        check_vma=False,
    )
```

```python
import jax
import jax.numpy as jnp
import numpy as np
from jax import lax
from jax.experimental import pallas as pl
from jax.experimental.pallas import tpu as pltpu
from jax.sharding import PartitionSpec as P

TE = 16
TZ = 2
TCOL = 16
FACE = TE * TE
CELLS = TE**3
LANES = 128
ROWS = CELLS // LANES

viscous = 0.05
step_size = 0.25
thicken = 5.0

SCALE = 4096.0
PLANES = 4
AHEAD = 4

EVERY = ("grp", "mig", "pen")
TEAM = ("mig", "pen")


def passed_along(x, axis, by):
    peers = lax.axis_size(axis)
    return lax.ppermute(x, axis, [(i, (i + by) % peers) for i in range(peers)])


def banded(brick_rows, reach):
    sigma = reach / 2.0
    offsets = np.arange(-reach, reach + 1, dtype=np.float64)
    total = np.sum(np.exp(-offsets * offsets / (2.0 * sigma * sigma)))
    row = np.arange(brick_rows)[:, None]
    col = np.arange(brick_rows + 2 * reach)[None, :]
    offset = (col - reach - row).astype(np.float64)
    weights = np.where(np.abs(offset) <= reach, np.exp(-offset * offset / (2.0 * sigma * sigma)), 0)
    return (weights / total).astype(np.float32)


def raw_kernel(flags_ref, sensor_ref, raw_ref):
    for r in range(TZ):
        for k in range(TCOL):
            rows, cols = slice(r * TE, (r + 1) * TE), slice(k * FACE, (k + 1) * FACE)
            flag = flags_ref[r, k].astype(jnp.float32)
            raw_ref[rows, cols] = (sensor_ref[rows, cols] * flag).astype(jnp.bfloat16)


def filter_kernel(
    flags_ref,
    weights_ref,
    sensor_ref,
    below_ref,
    above_ref,
    destination_ref,
    target_ref,
    filtered_ref,
    row_ref,
):
    lane = lax.broadcasted_iota(jnp.int32, (1, LANES), 1)
    slots = destination_ref.shape[1]
    row = jnp.concatenate(
        [
            jnp.zeros((1, slots), jnp.float32),
            destination_ref[...].astype(jnp.float32),
            target_ref[...].astype(jnp.float32),
            jnp.zeros((1, LANES - 3 * slots), jnp.float32),
        ],
        axis=1,
    )
    brick = sensor_ref.shape[0]
    for k in range(TCOL):
        cols = slice(k * FACE, (k + 1) * FACE)
        own = [
            sensor_ref[r * TE : (r + 1) * TE, cols] * flags_ref[r, k].astype(jnp.float32)
            for r in range(TZ)
        ]
        widened = jnp.concatenate(
            [below_ref[:, cols].astype(jnp.float32)] + own + [above_ref[:, cols].astype(jnp.float32)],
            axis=0,
        )
        filtered = jnp.dot(
            weights_ref[...],
            widened,
            precision=lax.Precision.HIGHEST,
            preferred_element_type=jnp.float32,
        )
        filtered_ref[:, cols] = filtered
        clipped = jnp.minimum(filtered, 1.0)
        for r in range(TZ):
            total = jnp.sum(
                jnp.sum(clipped[r * TE : (r + 1) * TE], axis=0, keepdims=True), axis=1, keepdims=True
            )
            thick = 1.0 + (thicken - 1.0) * (total / float(TE * FACE))
            row = jnp.where(lane == r * TCOL + k, thick, row)
    row_ref[...] = row


def send_kernel(
    destination_ref, recent_hbm, older_hbm, out_ref, recent_ref, older_ref, got
):
    species, slots, _ = recent_ref.shape
    peers = out_ref.shape[0]

    def fetches(s):
        return (
            pltpu.make_async_copy(recent_hbm.at[s], recent_ref.at[s], got.at[0, s]),
            pltpu.make_async_copy(older_hbm.at[s], older_ref.at[s], got.at[1, s]),
        )

    for s in range(AHEAD):
        for copy in fetches(s):
            copy.start()
    peer = lax.broadcasted_iota(jnp.int32, (peers, slots), 0)
    hot = ((destination_ref[...] == peer) & (peer != lax.axis_index(TEAM))).astype(jnp.bfloat16)
    flat = out_ref.reshape(peers * species * ROWS, LANES)
    for s in range(species):
        if s + AHEAD < species:
            for copy in fetches(s + AHEAD):
                copy.start()
        for copy in fetches(s):
            copy.wait()
        recent = jnp.dot(hot, recent_ref[s], preferred_element_type=jnp.float32)
        older = jnp.dot(hot, older_ref[s], preferred_element_type=jnp.float32)
        mixed = recent * (-16.0 / 12.0 * SCALE) + older * (5.0 / 12.0 * SCALE)
        for k in range(ROWS):
            flat[pl.ds(s * ROWS + k, peers, stride=species * ROWS), :] = mixed[
                :, k * LANES : (k + 1) * LANES
            ]


def rims_kernel(ghosts_hbm, rims_hbm, ghosts_ref, rims_ref, got, sent):
    species, slots, _ = ghosts_ref.shape

    def fetch(s):
        return pltpu.make_async_copy(ghosts_hbm.at[s], ghosts_ref.at[s], got.at[s])

    def store(s):
        return pltpu.make_async_copy(rims_ref.at[s], rims_hbm.at[s], sent.at[s])

    for s in range(species):
        fetch(s).start()
    quarter = lax.broadcasted_iota(jnp.int32, (slots, LANES), 1) // (2 * TE)

    def one(s, carry):
        fetch(s).wait()
        for block in range(2):
            faces = [
                ghosts_ref[s, :, w * FACE + block * LANES : w * FACE + (block + 1) * LANES]
                for w in (4, 5, 2, 3)
            ]
            for q in range(4):
                rim = faces[0]
                for n in range(4):
                    turned = pltpu.roll(faces[n], (n - q) % 4 * 2 * TE, 1) if n != q else faces[n]
                    rim = turned if n == 0 else jnp.where(quarter == n, turned, rim)
                high = rim.astype(jnp.bfloat16)
                low = (rim - high.astype(jnp.float32)).astype(jnp.bfloat16)
                start = (block * 4 + q) * 2 * LANES
                rims_ref[s, :, start : start + LANES] = high
                rims_ref[s, :, start + LANES : start + 2 * LANES] = low
        store(s).start()
        return carry

    lax.fori_loop(0, species, one, 0)
    for s in range(species):
        store(s).wait()


def plane_weights():
    weights = np.zeros((6 * LANES, 3 * FACE), np.float32)
    for cell in range(FACE):
        y, z = divmod(cell, TE)
        for d, at, step in ((0, y, TE), (1, z, 1)):
            for way in (-1, 1):
                if 0 <= at + way < TE:
                    rows = [cell + way * step, FACE + cell + way * step]
                else:
                    face = (2 + (way > 0)) if d == 0 else (way > 0)
                    spot = 2 * FACE + face * 2 * TE + (z if d == 0 else y)
                    rows = [spot, spot + TE, spot + LANES, spot + LANES + TE]
                weights[rows, cell] += 1.0
                weights[rows, (1 + d) * FACE + cell] += way
        weights[[cell, FACE + cell], cell] -= 6.0
    return weights


def main_kernel(
    live_ref,
    rate_ref,
    table_ref,
    tiles_ref,
    velocity_ref,
    destination_ref,
    target_ref,
    weights_hbm,
    fields_hbm,
    ghosts_hbm,
    rims_hbm,
    recent_hbm,
    older_hbm,
    new_fields_hbm,
    new_tend_hbm,
    weights_ref,
    fields_ref,
    rims_ref,
    recent_ref,
    older_ref,
    new_fields_ref,
    new_tend_ref,
    mix_ref,
    wide_ref,
    mask_ref,
    left_even_ref,
    left_odd_ref,
    fuel_even_ref,
    fuel_odd_ref,
    sums_even_ref,
    sums_odd_ref,
    react_even_ref,
    react_odd_ref,
    kept_even_ref,
    kept_odd_ref,
    got,
    sent,
):
    species, slots, cells = new_fields_ref.shape
    peers = table_ref.shape[0]
    chunk = PLANES * FACE
    chunks = cells // chunk

    def span(c, length, skipped=0):
        return pl.ds(pl.multiple_of(skipped + c * length, LANES), length)

    def cells_in(c):
        lanes, rims, inner = span(c, chunk), span(c, chunk // 2), span(c, chunk, FACE)
        return (
            pltpu.make_async_copy(
                fields_hbm.at[:, :, lanes], fields_ref.at[:, :, inner], got.at[0, c]
            ),
            pltpu.make_async_copy(
                rims_hbm.at[:, :, rims], rims_ref.at[:, :, rims], got.at[1, c]
            ),
            pltpu.make_async_copy(
                recent_hbm.at[:, :, lanes], recent_ref.at[:, :, lanes], got.at[2, c]
            ),
            pltpu.make_async_copy(
                older_hbm.at[:, :, lanes], older_ref.at[:, :, lanes], got.at[3, c]
            ),
        )

    def ends():
        return (
            pltpu.make_async_copy(weights_hbm, weights_ref, got.at[4, 0]),
            pltpu.make_async_copy(
                ghosts_hbm.at[:, :, pl.ds(0, FACE)], fields_ref.at[:, :, pl.ds(0, FACE)], got.at[4, 1]
            ),
            pltpu.make_async_copy(
                ghosts_hbm.at[:, :, pl.ds(FACE, FACE)],
                fields_ref.at[:, :, pl.ds(FACE + cells, FACE)],
                got.at[4, 2],
            ),
        )

    def stores(c):
        lanes = span(c, chunk)
        return (
            pltpu.make_async_copy(
                new_fields_ref.at[:, :, lanes], new_fields_hbm.at[:, :, lanes], sent.at[0, c]
            ),
            pltpu.make_async_copy(
                new_tend_ref.at[:, :, lanes], new_tend_hbm.at[:, :, lanes], sent.at[1, c]
            ),
        )

    for copy in (*cells_in(0), *ends(), *cells_in(1)):
        copy.start()

    marks = jnp.concatenate(
        [velocity_ref[...], tiles_ref[...].astype(jnp.float32), jnp.zeros((4, slots), jnp.float32)], axis=0
    ).T
    tiles = marks[:, 3:4].astype(jnp.int32)
    owner = tiles // slots
    wanted = lax.broadcasted_iota(jnp.int32, (slots, peers), 1) == owner % peers
    picked = jnp.dot(
        wanted.astype(jnp.float32),
        table_ref[...],
        precision=lax.Precision.HIGHEST,
        preferred_element_type=jnp.float32,
    )
    lane = lax.broadcasted_iota(jnp.int32, picked.shape, 1)
    spot = owner // peers * LANES + tiles % slots
    thick = jnp.sum(jnp.where(lane == spot, picked, 0.0), axis=1, keepdims=True)
    live = lax.broadcasted_iota(jnp.int32, (slots, 1), 0) < live_ref[0]
    live = jnp.where(live, 1.0, 0.0)
    parts = [viscous * thick * live, live / thick]
    parts += [0.5 * live * marks[:, d : d + 1] for d in range(3)] + [live]
    for n, part in enumerate(parts):
        wide_ref[n] = jnp.broadcast_to(part, (slots, LANES))
    main = (species - 1) * slots
    tail = lax.broadcasted_iota(jnp.int32, (slots, LANES), 1)
    main_lane = lax.broadcasted_iota(jnp.int32, (slots, main), 1)
    main_slot = lax.broadcasted_iota(jnp.int32, (slots, main), 0) == main_lane % slots
    tail_slot = lax.broadcasted_iota(jnp.int32, (slots, LANES), 0) == tail % slots
    for s in range(species):
        rows = slice(s * slots, (s + 1) * slots)
        rate = jnp.zeros((slots, main), jnp.float32)
        for k in range(species - 1):
            rate = jnp.where(main_lane // slots == k, rate_ref[s, k], rate)
        rate = jnp.where(main_slot, rate, 0.0)
        high = rate.astype(jnp.bfloat16)
        mix_ref[rows, 0:main] = high
        mix_ref[rows, main : 2 * main] = (rate - high.astype(jnp.float32)).astype(jnp.bfloat16)
        mix_ref[rows, 2 * main : 3 * main] = high
        rate = jnp.where(tail_slot & (tail < 3 * slots), rate_ref[s, species - 1], 0.0)
        high = rate.astype(jnp.bfloat16).astype(jnp.float32)
        rate = jnp.where(tail // slots == 1, rate - high, high)
        mix_ref[rows, 3 * main :] = rate.astype(jnp.bfloat16)
    for fuel_ref in (fuel_even_ref, fuel_odd_ref):
        fuel_ref[3 * main + 3 * slots :, :] = jnp.zeros((LANES - 3 * slots, 2 * FACE), jnp.bfloat16)

    parity = lax.broadcasted_iota(jnp.int32, (slots, 2 * LANES), 1) // TE % 2
    for p in range(2):
        mask_ref[p] = jnp.where(parity == p, 1.0, 0.0).astype(jnp.bfloat16)
    slot = lax.broadcasted_iota(jnp.int32, (slots, slots), 0)
    keep = (destination_ref[...] == lax.axis_index(TEAM)) & (target_ref[...] == slot)
    keep = keep.astype(jnp.bfloat16)

    def build(pair, odd, some):
        left_ref = (left_even_ref, left_odd_ref)[odd]
        rims = pl.ds(pl.multiple_of(pair * FACE, FACE), FACE)
        for s in some:
            both = rims_ref[s, :, rims]
            for p in range(2):
                lanes = pl.ds(pl.multiple_of((2 * pair + p + 1) * FACE, FACE), FACE)
                rows = slice((p * species + s) * slots, (p * species + s + 1) * slots)
                f = fields_ref[s, :, lanes]
                high = f.astype(jnp.bfloat16)
                left_ref[rows, 0:FACE] = high
                left_ref[rows, FACE : 2 * FACE] = (f - high.astype(jnp.float32)).astype(jnp.bfloat16)
                left_ref[rows, 2 * FACE :] = both * mask_ref[p]

    def multiply(pair, odd, d):
        left_ref, sums_ref = ((left_even_ref, sums_even_ref), (left_odd_ref, sums_odd_ref))[odd]
        columns = slice(d * FACE, (d + 1) * FACE)
        sums_ref[:, columns] = jnp.dot(
            left_ref[...], weights_ref[:, columns], preferred_element_type=jnp.float32
        )

    def burn(pair, odd):
        kept_ref = (kept_even_ref, kept_odd_ref)[odd]
        both = pl.ds(pl.multiple_of(2 * pair * FACE, FACE), 2 * FACE)
        for s in range(species):
            recent = jnp.dot(keep, recent_ref[s, :, both], preferred_element_type=jnp.float32)
            older = jnp.dot(keep, older_ref[s, :, both], preferred_element_type=jnp.float32)
            kept_ref[s] = recent * (-16.0 / 12.0 * step_size) + older * (5.0 / 12.0 * step_size)

        fuel_ref, react_ref = ((fuel_even_ref, react_even_ref), (fuel_odd_ref, react_odd_ref))[odd]
        both = pl.ds(pl.multiple_of((2 * pair + 1) * FACE, FACE), 2 * FACE)
        over = jnp.concatenate([wide_ref[1]] * 4, axis=1)
        burning = fields_ref[0, :, both] * fields_ref[1, :, both] * over
        for k in range(species):
            fuel = fields_ref[k, :, both] * burning
            high = fuel.astype(jnp.bfloat16)
            low = (fuel - high.astype(jnp.float32)).astype(jnp.bfloat16)
            for n, part in enumerate((high, high, low)):
                start = n * main + k * slots if k < species - 1 else 3 * main + n * slots
                fuel_ref[start : start + slots, :] = part
        react_ref[...] = jnp.dot(mix_ref[...], fuel_ref[...], preferred_element_type=jnp.float32)

    def finish(pair, odd, some):
        kept_ref = (kept_even_ref, kept_odd_ref)[odd]
        sums_ref, react_ref = ((sums_even_ref, react_even_ref), (sums_odd_ref, react_odd_ref))[odd]
        for p in range(2):
            inner, before, here, after = (
                pl.ds(pl.multiple_of((2 * pair + p + n) * FACE, FACE), FACE) for n in (0, 0, 1, 2)
            )
            for g in range(slots // 16):
                rows = slice(g * 16, (g + 1) * 16)
                smooth, vx, vy, vz, live = (
                    jnp.concatenate([wide_ref[n, rows, :]] * 2, axis=1) for n in (0, 2, 3, 4, 5)
                )
                for s in some:
                    low, high = fields_ref[s, rows, before], fields_ref[s, rows, after]
                    line = s * slots + g * 16
                    react = react_ref[line : line + 16, p * FACE : (p + 1) * FACE]
                    line += p * species * slots
                    total, along_y, along_z = (
                        sums_ref[line : line + 16, d * FACE : (d + 1) * FACE] for d in range(3)
                    )
                    tend = smooth * (total + (low + high)) - vx * (high - low)
                    tend = (tend - vy * along_y) + (react - vz * along_z)
                    kept = kept_ref[s, rows, p * FACE : (p + 1) * FACE]
                    new = (fields_ref[s, rows, here] + kept) * live
                    new_fields_ref[s, rows, inner] = new + (step_size * 23.0 / 12.0) * tend
                    new_tend_ref[s, rows, inner] = tend.astype(jnp.bfloat16)

    thirds = [range(n * species // 3, (n + 1) * species // 3) for n in range(3)]
    pairs = TE // 2

    def stage(pair, odd):
        after, later = jnp.minimum(pair + 1, pairs - 1), jnp.minimum(pair + 2, pairs - 1)
        burn(after, 1 - odd)
        for d, some in enumerate(thirds):
            multiply(after, 1 - odd, d)
            finish(pair, odd, some)
            build(later, odd, some)

    for copy in (*ends(), *cells_in(0)):
        copy.wait()
    build(0, 0, range(species))
    for d in range(3):
        multiply(0, 0, d)
    burn(0, 0)
    build(1, 1, range(species))

    def four(c, carry):
        @pl.when(c + 2 < chunks)
        def _():
            for copy in cells_in(c + 2):
                copy.start()

        @pl.when(c + 1 < chunks)
        def _():
            for copy in cells_in(c + 1):
                copy.wait()

        stage(2 * c, 0)
        stage(2 * c + 1, 1)
        for copy in stores(c):
            copy.start()
        return carry

    lax.fori_loop(0, chunks, four, 0)
    for c in range(chunks):
        for copy in stores(c):
            copy.wait()


def add_kernel(
    live_ref, table_ref, fields_hbm, arrived_hbm, out_hbm, fields_ref, arrived_ref, got, sent
):
    species, peers = arrived_ref.shape[:2]
    slots = fields_ref.shape[1]

    def fetches(s):
        part = arrived_hbm.at[:, pl.ds(s * ROWS, ROWS)]
        return (
            pltpu.make_async_copy(part, arrived_ref.at[s, :, pl.ds(0, ROWS)], got.at[0, s]),
            pltpu.make_async_copy(fields_hbm.at[s], fields_ref.at[s], got.at[1, s]),
        )

    def store(s):
        return pltpu.make_async_copy(fields_ref.at[s], out_hbm.at[s], sent.at[s])

    for s in range(AHEAD):
        for copy in fetches(s):
            copy.start()
    me, first = lax.axis_index(TEAM), pl.multiple_of(lax.axis_index("grp") * LANES, LANES)
    notes = table_ref[:, pl.ds(first, LANES)]
    destination = notes[:, slots : 2 * slots]
    target = notes[:, 2 * slots : 3 * slots]
    peer = lax.broadcasted_iota(jnp.int32, (peers, slots), 0)
    mine = (destination == me.astype(jnp.float32)) & (peer != me)
    slot = jnp.max(jnp.where(mine, target, -1.0), axis=1, keepdims=True)
    index = lax.broadcasted_iota(jnp.int32, (peers, slots), 1)
    hot = (slot == index.astype(jnp.float32)) & (index < live_ref[0])
    hot = jnp.where(hot, step_size / SCALE, 0.0)
    hot = jnp.concatenate([hot, hot], axis=0).T.astype(jnp.bfloat16)
    for s in range(species):
        if s + AHEAD < species:
            for copy in fetches(s + AHEAD):
                copy.start()
        for copy in fetches(s):
            copy.wait()
        apart = arrived_ref.shape[2]
        flat = arrived_ref.at[s].reshape(peers * apart, LANES)
        for c in range(ROWS // 2):
            lanes = slice(c * 2 * LANES, (c + 1) * 2 * LANES)
            arrived = jnp.concatenate(
                [flat[pl.ds(2 * c + k, peers, stride=apart), :] for k in range(2)], axis=1
            )
            high = arrived.astype(jnp.bfloat16)
            low = (arrived - high.astype(jnp.float32)).astype(jnp.bfloat16)
            fields_ref[s, :, lanes] += jnp.dot(
                hot, jnp.concatenate([high, low], axis=0), preferred_element_type=jnp.float32
            )
        store(s).start()
    for s in range(species):
        store(s).wait()


def smem():
    return pl.BlockSpec(memory_space=pltpu.SMEM)


def whole(shape):
    return pl.BlockSpec(shape, lambda i: (0,) * len(shape))


def params(mib, semantics=None):
    return pltpu.CompilerParams(vmem_limit_bytes=mib << 20, dimension_semantics=semantics)


def local(
    fields,
    ghosts,
    velocity,
    rate_matrix,
    recent_tend,
    older_tend,
    destination,
    target_slot,
    live_counts,
    tile_ids,
    sensor,
    flame_flags,
):
    slots, species, cells = fields.shape
    peers = lax.axis_size(TEAM)
    brick = sensor.shape[0]
    fields, ghosts, recent, older = (
        a.transpose(1, 0, 2) for a in (fields, ghosts, recent_tend, older_tend)
    )
    moves = (destination.reshape(1, slots), target_slot.reshape(1, slots))

    raw = pl.pallas_call(
        raw_kernel,
        name="raw_sensor",
        out_shape=jax.ShapeDtypeStruct(sensor.shape, jnp.bfloat16),
        in_specs=[smem(), pl.BlockSpec(memory_space=pltpu.VMEM)],
        out_specs=pl.BlockSpec(memory_space=pltpu.VMEM),
        compiler_params=params(58),
    )(flame_flags, sensor)
    below = passed_along(raw, "pen", 1)
    above = passed_along(raw, "pen", -1)

    anywhere = pl.BlockSpec(memory_space=pl.ANY)
    in_hbm = pl.BlockSpec(memory_space=pltpu.HBM)
    vmem = pl.BlockSpec(memory_space=pltpu.VMEM)
    outgoing = pl.pallas_call(
        send_kernel,
        name="outgoing_histories",
        out_shape=jax.ShapeDtypeStruct((peers, species * ROWS, LANES), jnp.float32),
        in_specs=[vmem, in_hbm, in_hbm],
        out_specs=vmem,
        scratch_shapes=[
            pltpu.VMEM(recent.shape, jnp.bfloat16),
            pltpu.VMEM(older.shape, jnp.bfloat16),
            pltpu.SemaphoreType.DMA((2, species)),
        ],
        compiler_params=params(50),
        cost_estimate=pl.CostEstimate(flops=0, bytes_accessed=8 << 20, transcendentals=0),
    )(destination.reshape(1, slots), recent, older)
    outgoing = outgoing.astype(jnp.float16)

    shape = jax.ShapeDtypeStruct((species, slots, cells), jnp.float32)
    rims = jax.ShapeDtypeStruct((species, slots, TE * LANES), jnp.bfloat16)
    rims = pl.pallas_call(
        rims_kernel,
        name="rims",
        out_shape=rims,
        in_specs=[anywhere],
        out_specs=anywhere,
        scratch_shapes=[
            pltpu.VMEM(ghosts.shape, jnp.float32),
            pltpu.VMEM(rims.shape, jnp.bfloat16),
            pltpu.SemaphoreType.DMA((species,)),
            pltpu.SemaphoreType.DMA((species,)),
        ],
        compiler_params=params(58),
        cost_estimate=pl.CostEstimate(flops=0, bytes_accessed=8 << 20, transcendentals=0),
    )(ghosts)
    below, above, rims, outgoing = lax.optimization_barrier((below, above, rims, outgoing))

    filtered, row = pl.pallas_call(
        filter_kernel,
        name="filtered_sensor",
        out_shape=(
            jax.ShapeDtypeStruct(sensor.shape, jnp.float32),
            jax.ShapeDtypeStruct((1, LANES), jnp.float32),
        ),
        in_specs=[smem()] + [vmem] * 6,
        out_specs=(vmem, vmem),
        compiler_params=params(32),
        cost_estimate=pl.CostEstimate(flops=0, bytes_accessed=4 << 20, transcendentals=0),
    )(flame_flags, jnp.asarray(banded(brick, brick)), sensor, below, above, *moves)
    rows = gathered(row, ("pen",))
    rows, outgoing = lax.optimization_barrier((rows, outgoing))
    arrived = lax.all_to_all(outgoing, TEAM, split_axis=0, concat_axis=0, tiled=True)
    table = gathered(rows, ("grp", "mig"))
    arrived = arrived.astype(jnp.float32)

    weights = jnp.asarray(plane_weights(), jnp.bfloat16)
    left = pltpu.VMEM((2 * species * slots, 6 * LANES), jnp.bfloat16)
    sums = pltpu.VMEM((2 * species * slots, 3 * FACE), jnp.float32)
    depth = 3 * (species - 1) * slots + LANES
    fuel = pltpu.VMEM((depth, 2 * FACE), jnp.bfloat16)
    react = pltpu.VMEM((species * slots, 2 * FACE), jnp.float32)
    kept = pltpu.VMEM((species, slots, 2 * FACE), jnp.float32)
    new_fields, new_tend = pl.pallas_call(
        main_kernel,
        name="updates",
        out_shape=(shape, jax.ShapeDtypeStruct(shape.shape, jnp.bfloat16)),
        in_specs=[smem()] * 2 + [vmem] * 5 + [anywhere] * 6,
        out_specs=(anywhere, anywhere),
        scratch_shapes=[
            pltpu.VMEM(weights.shape, jnp.bfloat16),
            pltpu.VMEM((species, slots, cells + 2 * FACE), jnp.float32),
            pltpu.VMEM(rims.shape, jnp.bfloat16),
            pltpu.VMEM(shape.shape, jnp.bfloat16),
            pltpu.VMEM(shape.shape, jnp.bfloat16),
            pltpu.VMEM(shape.shape, jnp.float32),
            pltpu.VMEM(shape.shape, jnp.bfloat16),
            pltpu.VMEM((species * slots, depth), jnp.bfloat16),
            pltpu.VMEM((6, slots, LANES), jnp.float32),
            pltpu.VMEM((2, slots, FACE), jnp.bfloat16),
            left,
            left,
            fuel,
            fuel,
            sums,
            sums,
            react,
            react,
            kept,
            kept,
            pltpu.SemaphoreType.DMA((5, TE // PLANES)),
            pltpu.SemaphoreType.DMA((2, TE // PLANES)),
        ],
        compiler_params=params(52),
        cost_estimate=pl.CostEstimate(flops=0, bytes_accessed=40 << 20, transcendentals=0),
    )(
        live_counts,
        rate_matrix,
        table,
        tile_ids.reshape(1, slots),
        velocity,
        *moves,
        weights,
        fields,
        ghosts,
        rims,
        recent,
        older,
    )

    new_fields = pl.pallas_call(
        add_kernel,
        name="arrived_histories",
        out_shape=shape,
        in_specs=[smem(), vmem, anywhere, anywhere],
        out_specs=anywhere,
        scratch_shapes=[
            pltpu.VMEM(shape.shape, jnp.float32),
            pltpu.VMEM((species, peers, ROWS + 8, LANES), jnp.float32),
            pltpu.SemaphoreType.DMA((2, species)),
            pltpu.SemaphoreType.DMA((species,)),
        ],
        compiler_params=params(50),
        cost_estimate=pl.CostEstimate(flops=0, bytes_accessed=12 << 20, transcendentals=0),
    )(live_counts, table, new_fields, arrived)
    return new_fields.transpose(1, 0, 2), new_tend.transpose(1, 0, 2), filtered


def gathered(row, axes):
    for axis in axes:
        count = lax.axis_size(axis)
        here = lax.axis_index(axis)
        rows = [row] + [passed_along(row, axis, by) for by in range(1, count)]
        height, width = row.shape
        if axis == "grp":
            table = jnp.zeros((height, count * width), row.dtype)
        else:
            table = jnp.zeros((count * height, width), row.dtype)
        for by, part in enumerate(rows):
            place = (here - by) % count
            place = (0, place * width) if axis == "grp" else (place * height, 0)
            table = lax.dynamic_update_slice(table, part, place)
        row = table
    return row


def solution(mesh):
    split = P(EVERY, None, None)
    return jax.shard_map(
        local,
        mesh=mesh,
        in_specs=(
            split,
            split,
            P(None, EVERY),
            P(),
            split,
            split,
            P(EVERY),
            P(EVERY),
            P(EVERY),
            P(EVERY),
            P("pen", ("grp", "mig")),
            P("pen", ("grp", "mig")),
        ),
        out_specs=(split, split, P("pen", ("grp", "mig"))),
        check_vma=False,
    )
```

```python
import jax
import jax.numpy as jnp
import numpy as np
from jax import lax
from jax.experimental import pallas as pl
from jax.experimental.pallas import tpu as pltpu
from jax.sharding import PartitionSpec as P

TE = 16
TZ = 2
TCOL = 16
FACE = TE * TE
CELLS = TE**3
LANES = 128
ROWS = CELLS // LANES

viscous = 0.05
step_size = 0.25
thicken = 5.0

SCALE = 4096.0
PLANES = 4
AHEAD = 4

EVERY = ("grp", "mig", "pen")
TEAM = ("mig", "pen")


def passed_along(x, axis, by):
    peers = lax.axis_size(axis)
    return lax.ppermute(x, axis, [(i, (i + by) % peers) for i in range(peers)])


def banded(brick_rows, reach):
    sigma = reach / 2.0
    offsets = np.arange(-reach, reach + 1, dtype=np.float64)
    total = np.sum(np.exp(-offsets * offsets / (2.0 * sigma * sigma)))
    row = np.arange(brick_rows)[:, None]
    col = np.arange(brick_rows + 2 * reach)[None, :]
    offset = (col - reach - row).astype(np.float64)
    weights = np.where(np.abs(offset) <= reach, np.exp(-offset * offset / (2.0 * sigma * sigma)), 0)
    return (weights / total).astype(np.float32)


def raw_kernel(flags_ref, sensor_ref, raw_ref):
    for r in range(TZ):
        for k in range(TCOL):
            rows, cols = slice(r * TE, (r + 1) * TE), slice(k * FACE, (k + 1) * FACE)
            flag = flags_ref[r, k].astype(jnp.float32)
            raw_ref[rows, cols] = (sensor_ref[rows, cols] * flag).astype(jnp.bfloat16)


def filter_kernel(
    flags_ref,
    weights_ref,
    sensor_ref,
    below_ref,
    above_ref,
    destination_ref,
    target_ref,
    filtered_ref,
    row_ref,
):
    lane = lax.broadcasted_iota(jnp.int32, (1, LANES), 1)
    slots = destination_ref.shape[1]
    row = jnp.concatenate(
        [
            jnp.zeros((1, slots), jnp.float32),
            destination_ref[...].astype(jnp.float32),
            target_ref[...].astype(jnp.float32),
            jnp.zeros((1, LANES - 3 * slots), jnp.float32),
        ],
        axis=1,
    )
    brick = sensor_ref.shape[0]
    for k in range(TCOL):
        cols = slice(k * FACE, (k + 1) * FACE)
        own = [
            sensor_ref[r * TE : (r + 1) * TE, cols] * flags_ref[r, k].astype(jnp.float32)
            for r in range(TZ)
        ]
        widened = jnp.concatenate(
            [below_ref[:, cols].astype(jnp.float32)] + own + [above_ref[:, cols].astype(jnp.float32)],
            axis=0,
        )
        filtered = jnp.dot(
            weights_ref[...],
            widened,
            precision=lax.Precision.HIGHEST,
            preferred_element_type=jnp.float32,
        )
        filtered_ref[:, cols] = filtered
        clipped = jnp.minimum(filtered, 1.0)
        for r in range(TZ):
            total = jnp.sum(
                jnp.sum(clipped[r * TE : (r + 1) * TE], axis=0, keepdims=True), axis=1, keepdims=True
            )
            thick = 1.0 + (thicken - 1.0) * (total / float(TE * FACE))
            row = jnp.where(lane == r * TCOL + k, thick, row)
    row_ref[...] = row


def send_kernel(
    destination_ref, recent_hbm, older_hbm, out_ref, recent_ref, older_ref, got
):
    species, slots, _ = recent_ref.shape
    peers = out_ref.shape[0]

    def fetches(s):
        return (
            pltpu.make_async_copy(recent_hbm.at[s], recent_ref.at[s], got.at[0, s]),
            pltpu.make_async_copy(older_hbm.at[s], older_ref.at[s], got.at[1, s]),
        )

    for s in range(AHEAD):
        for copy in fetches(s):
            copy.start()
    peer = lax.broadcasted_iota(jnp.int32, (peers, slots), 0)
    hot = ((destination_ref[...] == peer) & (peer != lax.axis_index(TEAM))).astype(jnp.bfloat16)
    flat = out_ref.reshape(peers * species * ROWS, LANES)
    for s in range(species):
        if s + AHEAD < species:
            for copy in fetches(s + AHEAD):
                copy.start()
        for copy in fetches(s):
            copy.wait()
        recent = jnp.dot(hot, recent_ref[s], preferred_element_type=jnp.float32)
        older = jnp.dot(hot, older_ref[s], preferred_element_type=jnp.float32)
        mixed = recent * (-16.0 / 12.0 * SCALE) + older * (5.0 / 12.0 * SCALE)
        for k in range(ROWS):
            flat[pl.ds(s * ROWS + k, peers, stride=species * ROWS), :] = mixed[
                :, k * LANES : (k + 1) * LANES
            ]


def rims_kernel(ghosts_hbm, rims_hbm, ghosts_ref, rims_ref, got, sent):
    species, slots, _ = ghosts_ref.shape

    def fetch(s):
        return pltpu.make_async_copy(ghosts_hbm.at[s], ghosts_ref.at[s], got.at[s])

    def store(s):
        return pltpu.make_async_copy(rims_ref.at[s], rims_hbm.at[s], sent.at[s])

    for s in range(species):
        fetch(s).start()
    quarter = lax.broadcasted_iota(jnp.int32, (slots, LANES), 1) // (2 * TE)

    def one(s, carry):
        fetch(s).wait()
        for block in range(2):
            faces = [
                ghosts_ref[s, :, w * FACE + block * LANES : w * FACE + (block + 1) * LANES]
                for w in (4, 5, 2, 3)
            ]
            for q in range(4):
                rim = faces[0]
                for n in range(4):
                    turned = pltpu.roll(faces[n], (n - q) % 4 * 2 * TE, 1) if n != q else faces[n]
                    rim = turned if n == 0 else jnp.where(quarter == n, turned, rim)
                high = rim.astype(jnp.bfloat16)
                low = (rim - high.astype(jnp.float32)).astype(jnp.bfloat16)
                start = (block * 4 + q) * 2 * LANES
                rims_ref[s, :, start : start + LANES] = high
                rims_ref[s, :, start + LANES : start + 2 * LANES] = low
        store(s).start()
        return carry

    lax.fori_loop(0, species, one, 0)
    for s in range(species):
        store(s).wait()


def plane_weights():
    weights = np.zeros((6 * LANES, 3 * FACE), np.float32)
    for cell in range(FACE):
        y, z = divmod(cell, TE)
        for d, at, step in ((0, y, TE), (1, z, 1)):
            for way in (-1, 1):
                if 0 <= at + way < TE:
                    rows = [cell + way * step, FACE + cell + way * step]
                else:
                    face = (2 + (way > 0)) if d == 0 else (way > 0)
                    spot = 2 * FACE + face * 2 * TE + (z if d == 0 else y)
                    rows = [spot, spot + TE, spot + LANES, spot + LANES + TE]
                weights[rows, cell] += 1.0
                weights[rows, (1 + d) * FACE + cell] += way
        weights[[cell, FACE + cell], cell] -= 6.0
    return weights


def main_kernel(
    live_ref,
    rate_ref,
    table_ref,
    tiles_ref,
    velocity_ref,
    destination_ref,
    target_ref,
    weights_hbm,
    fields_hbm,
    ghosts_hbm,
    rims_hbm,
    recent_hbm,
    older_hbm,
    new_fields_hbm,
    new_tend_hbm,
    weights_ref,
    fields_ref,
    rims_ref,
    recent_ref,
    older_ref,
    new_fields_ref,
    new_tend_ref,
    mix_ref,
    wide_ref,
    mask_ref,
    left_even_ref,
    left_odd_ref,
    fuel_even_ref,
    fuel_odd_ref,
    sums_even_ref,
    sums_odd_ref,
    react_even_ref,
    react_odd_ref,
    kept_even_ref,
    kept_odd_ref,
    got,
    sent,
):
    species, slots, cells = new_fields_ref.shape
    peers = table_ref.shape[0]
    chunk = PLANES * FACE
    chunks = cells // chunk

    def span(c, length, skipped=0):
        return pl.ds(pl.multiple_of(skipped + c * length, LANES), length)

    def cells_in(c):
        lanes, rims, inner = span(c, chunk), span(c, chunk // 2), span(c, chunk, FACE)
        return (
            pltpu.make_async_copy(
                fields_hbm.at[:, :, lanes], fields_ref.at[:, :, inner], got.at[0, c]
            ),
            pltpu.make_async_copy(
                rims_hbm.at[:, :, rims], rims_ref.at[:, :, rims], got.at[1, c]
            ),
            pltpu.make_async_copy(
                recent_hbm.at[:, :, lanes], recent_ref.at[:, :, lanes], got.at[2, c]
            ),
            pltpu.make_async_copy(
                older_hbm.at[:, :, lanes], older_ref.at[:, :, lanes], got.at[3, c]
            ),
        )

    def ends():
        return (
            pltpu.make_async_copy(weights_hbm, weights_ref, got.at[4, 0]),
            pltpu.make_async_copy(
                ghosts_hbm.at[:, :, pl.ds(0, FACE)], fields_ref.at[:, :, pl.ds(0, FACE)], got.at[4, 1]
            ),
            pltpu.make_async_copy(
                ghosts_hbm.at[:, :, pl.ds(FACE, FACE)],
                fields_ref.at[:, :, pl.ds(FACE + cells, FACE)],
                got.at[4, 2],
            ),
        )

    def stores(c):
        lanes = span(c, chunk)
        return (
            pltpu.make_async_copy(
                new_fields_ref.at[:, :, lanes], new_fields_hbm.at[:, :, lanes], sent.at[0, c]
            ),
            pltpu.make_async_copy(
                new_tend_ref.at[:, :, lanes], new_tend_hbm.at[:, :, lanes], sent.at[1, c]
            ),
        )

    for copy in (*cells_in(0), *ends(), *cells_in(1)):
        copy.start()

    marks = jnp.concatenate(
        [velocity_ref[...], tiles_ref[...].astype(jnp.float32), jnp.zeros((4, slots), jnp.float32)], axis=0
    ).T
    tiles = marks[:, 3:4].astype(jnp.int32)
    owner = tiles // slots
    wanted = lax.broadcasted_iota(jnp.int32, (slots, peers), 1) == owner % peers
    picked = jnp.dot(
        wanted.astype(jnp.float32),
        table_ref[...],
        precision=lax.Precision.HIGHEST,
        preferred_element_type=jnp.float32,
    )
    lane = lax.broadcasted_iota(jnp.int32, picked.shape, 1)
    spot = owner // peers * LANES + tiles % slots
    thick = jnp.sum(jnp.where(lane == spot, picked, 0.0), axis=1, keepdims=True)
    live = lax.broadcasted_iota(jnp.int32, (slots, 1), 0) < live_ref[0]
    live = jnp.where(live, 1.0, 0.0)
    parts = [viscous * thick * live, live / thick]
    parts += [0.5 * live * marks[:, d : d + 1] for d in range(3)] + [live]
    for n, part in enumerate(parts):
        wide_ref[n] = jnp.broadcast_to(part, (slots, LANES))
    main = (species - 1) * slots
    tail = lax.broadcasted_iota(jnp.int32, (slots, LANES), 1)
    main_lane = lax.broadcasted_iota(jnp.int32, (slots, main), 1)
    main_slot = lax.broadcasted_iota(jnp.int32, (slots, main), 0) == main_lane % slots
    tail_slot = lax.broadcasted_iota(jnp.int32, (slots, LANES), 0) == tail % slots
    for s in range(species):
        rows = slice(s * slots, (s + 1) * slots)
        rate = jnp.zeros((slots, main), jnp.float32)
        for k in range(species - 1):
            rate = jnp.where(main_lane // slots == k, rate_ref[s, k], rate)
        rate = jnp.where(main_slot, rate, 0.0)
        high = rate.astype(jnp.bfloat16)
        mix_ref[rows, 0:main] = high
        mix_ref[rows, main : 2 * main] = (rate - high.astype(jnp.float32)).astype(jnp.bfloat16)
        mix_ref[rows, 2 * main : 3 * main] = high
        rate = jnp.where(tail_slot & (tail < 3 * slots), rate_ref[s, species - 1], 0.0)
        high = rate.astype(jnp.bfloat16).astype(jnp.float32)
        rate = jnp.where(tail // slots == 1, rate - high, high)
        mix_ref[rows, 3 * main :] = rate.astype(jnp.bfloat16)
    for fuel_ref in (fuel_even_ref, fuel_odd_ref):
        fuel_ref[3 * main + 3 * slots :, :] = jnp.zeros((LANES - 3 * slots, 2 * FACE), jnp.bfloat16)

    parity = lax.broadcasted_iota(jnp.int32, (slots, 2 * LANES), 1) // TE % 2
    for p in range(2):
        mask_ref[p] = jnp.where(parity == p, 1.0, 0.0).astype(jnp.bfloat16)
    slot = lax.broadcasted_iota(jnp.int32, (slots, slots), 0)
    keep = (destination_ref[...] == lax.axis_index(TEAM)) & (target_ref[...] == slot)
    keep = keep.astype(jnp.bfloat16)

    def build(pair, odd, some):
        left_ref = (left_even_ref, left_odd_ref)[odd]
        rims = pl.ds(pl.multiple_of(pair * FACE, FACE), FACE)
        for s in some:
            both = rims_ref[s, :, rims]
            for p in range(2):
                lanes = pl.ds(pl.multiple_of((2 * pair + p + 1) * FACE, FACE), FACE)
                rows = slice((p * species + s) * slots, (p * species + s + 1) * slots)
                f = fields_ref[s, :, lanes]
                high = f.astype(jnp.bfloat16)
                left_ref[rows, 0:FACE] = high
                left_ref[rows, FACE : 2 * FACE] = (f - high.astype(jnp.float32)).astype(jnp.bfloat16)
                left_ref[rows, 2 * FACE :] = both * mask_ref[p]

    def multiply(pair, odd, d):
        left_ref, sums_ref = ((left_even_ref, sums_even_ref), (left_odd_ref, sums_odd_ref))[odd]
        columns = slice(d * FACE, (d + 1) * FACE)
        sums_ref[:, columns] = jnp.dot(
            left_ref[...], weights_ref[:, columns], preferred_element_type=jnp.float32
        )

    def burn(pair, odd):
        kept_ref = (kept_even_ref, kept_odd_ref)[odd]
        both = pl.ds(pl.multiple_of(2 * pair * FACE, FACE), 2 * FACE)
        for s in range(species):
            recent = jnp.dot(keep, recent_ref[s, :, both], preferred_element_type=jnp.float32)
            older = jnp.dot(keep, older_ref[s, :, both], preferred_element_type=jnp.float32)
            kept_ref[s] = recent * (-16.0 / 12.0 * step_size) + older * (5.0 / 12.0 * step_size)

        fuel_ref, react_ref = ((fuel_even_ref, react_even_ref), (fuel_odd_ref, react_odd_ref))[odd]
        both = pl.ds(pl.multiple_of((2 * pair + 1) * FACE, FACE), 2 * FACE)
        over = jnp.concatenate([wide_ref[1]] * 4, axis=1)
        burning = fields_ref[0, :, both] * fields_ref[1, :, both] * over
        for k in range(species):
            fuel = fields_ref[k, :, both] * burning
            high = fuel.astype(jnp.bfloat16)
            low = (fuel - high.astype(jnp.float32)).astype(jnp.bfloat16)
            for n, part in enumerate((high, high, low)):
                start = n * main + k * slots if k < species - 1 else 3 * main + n * slots
                fuel_ref[start : start + slots, :] = part
        react_ref[...] = jnp.dot(mix_ref[...], fuel_ref[...], preferred_element_type=jnp.float32)

    def finish(pair, odd, some):
        kept_ref = (kept_even_ref, kept_odd_ref)[odd]
        sums_ref, react_ref = ((sums_even_ref, react_even_ref), (sums_odd_ref, react_odd_ref))[odd]
        for p in range(2):
            inner, before, here, after = (
                pl.ds(pl.multiple_of((2 * pair + p + n) * FACE, FACE), FACE) for n in (0, 0, 1, 2)
            )
            for g in range(slots // 16):
                rows = slice(g * 16, (g + 1) * 16)
                smooth, vx, vy, vz, live = (
                    jnp.concatenate([wide_ref[n, rows, :]] * 2, axis=1) for n in (0, 2, 3, 4, 5)
                )
                for s in some:
                    low, high = fields_ref[s, rows, before], fields_ref[s, rows, after]
                    line = s * slots + g * 16
                    react = react_ref[line : line + 16, p * FACE : (p + 1) * FACE]
                    line += p * species * slots
                    total, along_y, along_z = (
                        sums_ref[line : line + 16, d * FACE : (d + 1) * FACE] for d in range(3)
                    )
                    tend = smooth * (total + (low + high)) - vx * (high - low)
                    tend = (tend - vy * along_y) + (react - vz * along_z)
                    kept = kept_ref[s, rows, p * FACE : (p + 1) * FACE]
                    new = (fields_ref[s, rows, here] + kept) * live
                    new_fields_ref[s, rows, inner] = new + (step_size * 23.0 / 12.0) * tend
                    new_tend_ref[s, rows, inner] = tend.astype(jnp.bfloat16)

    thirds = [range(n * species // 3, (n + 1) * species // 3) for n in range(3)]
    pairs = TE // 2

    def stage(pair, odd):
        after, later = jnp.minimum(pair + 1, pairs - 1), jnp.minimum(pair + 2, pairs - 1)
        burn(after, 1 - odd)
        for d, some in enumerate(thirds):
            multiply(after, 1 - odd, d)
            finish(pair, odd, some)
            build(later, odd, some)

    for copy in (*ends(), *cells_in(0)):
        copy.wait()
    build(0, 0, range(species))
    for d in range(3):
        multiply(0, 0, d)
    burn(0, 0)
    build(1, 1, range(species))

    def four(c, carry):
        @pl.when(c + 2 < chunks)
        def _():
            for copy in cells_in(c + 2):
                copy.start()

        @pl.when(c + 1 < chunks)
        def _():
            for copy in cells_in(c + 1):
                copy.wait()

        stage(2 * c, 0)
        stage(2 * c + 1, 1)
        for copy in stores(c):
            copy.start()
        return carry

    lax.fori_loop(0, chunks, four, 0)
    for c in range(chunks):
        for copy in stores(c):
            copy.wait()


def add_kernel(
    live_ref, table_ref, fields_hbm, arrived_hbm, out_hbm, fields_ref, arrived_ref, got, sent
):
    species, peers = arrived_ref.shape[:2]
    slots = fields_ref.shape[1]

    def fetches(s):
        part = arrived_hbm.at[:, pl.ds(s * ROWS, ROWS)]
        return (
            pltpu.make_async_copy(part, arrived_ref.at[s, :, pl.ds(0, ROWS)], got.at[0, s]),
            pltpu.make_async_copy(fields_hbm.at[s], fields_ref.at[s], got.at[1, s]),
        )

    def store(s):
        return pltpu.make_async_copy(fields_ref.at[s], out_hbm.at[s], sent.at[s])

    for s in range(AHEAD):
        for copy in fetches(s):
            copy.start()
    me, first = lax.axis_index(TEAM), pl.multiple_of(lax.axis_index("grp") * LANES, LANES)
    notes = table_ref[:, pl.ds(first, LANES)]
    destination = notes[:, slots : 2 * slots]
    target = notes[:, 2 * slots : 3 * slots]
    peer = lax.broadcasted_iota(jnp.int32, (peers, slots), 0)
    mine = (destination == me.astype(jnp.float32)) & (peer != me)
    slot = jnp.max(jnp.where(mine, target, -1.0), axis=1, keepdims=True)
    index = lax.broadcasted_iota(jnp.int32, (peers, slots), 1)
    hot = (slot == index.astype(jnp.float32)) & (index < live_ref[0])
    hot = jnp.where(hot, step_size / SCALE, 0.0)
    hot = jnp.concatenate([hot, hot], axis=0).T.astype(jnp.bfloat16)
    for s in range(species):
        if s + AHEAD < species:
            for copy in fetches(s + AHEAD):
                copy.start()
        for copy in fetches(s):
            copy.wait()
        apart = arrived_ref.shape[2]
        flat = arrived_ref.at[s].reshape(peers * apart, LANES)
        for c in range(ROWS // 2):
            lanes = slice(c * 2 * LANES, (c + 1) * 2 * LANES)
            arrived = jnp.concatenate(
                [flat[pl.ds(2 * c + k, peers, stride=apart), :] for k in range(2)], axis=1
            )
            high = arrived.astype(jnp.bfloat16)
            low = (arrived - high.astype(jnp.float32)).astype(jnp.bfloat16)
            fields_ref[s, :, lanes] += jnp.dot(
                hot, jnp.concatenate([high, low], axis=0), preferred_element_type=jnp.float32
            )
        store(s).start()
    for s in range(species):
        store(s).wait()


def smem():
    return pl.BlockSpec(memory_space=pltpu.SMEM)


def whole(shape):
    return pl.BlockSpec(shape, lambda i: (0,) * len(shape))


def params(mib, semantics=None):
    return pltpu.CompilerParams(vmem_limit_bytes=mib << 20, dimension_semantics=semantics)


def local(
    fields,
    ghosts,
    velocity,
    rate_matrix,
    recent_tend,
    older_tend,
    destination,
    target_slot,
    live_counts,
    tile_ids,
    sensor,
    flame_flags,
):
    slots, species, cells = fields.shape
    peers = lax.axis_size(TEAM)
    brick = sensor.shape[0]
    fields, ghosts, recent, older = (
        a.transpose(1, 0, 2) for a in (fields, ghosts, recent_tend, older_tend)
    )
    moves = (destination.reshape(1, slots), target_slot.reshape(1, slots))

    raw = pl.pallas_call(
        raw_kernel,
        name="raw_sensor",
        out_shape=jax.ShapeDtypeStruct(sensor.shape, jnp.bfloat16),
        in_specs=[smem(), pl.BlockSpec(memory_space=pltpu.VMEM)],
        out_specs=pl.BlockSpec(memory_space=pltpu.VMEM),
        compiler_params=params(58),
    )(flame_flags, sensor)
    below = passed_along(raw, "pen", 1)
    above = passed_along(raw, "pen", -1)

    anywhere = pl.BlockSpec(memory_space=pl.ANY)
    in_hbm = pl.BlockSpec(memory_space=pltpu.HBM)
    vmem = pl.BlockSpec(memory_space=pltpu.VMEM)
    outgoing = pl.pallas_call(
        send_kernel,
        name="outgoing_histories",
        out_shape=jax.ShapeDtypeStruct((peers, species * ROWS, LANES), jnp.float32),
        in_specs=[vmem, in_hbm, in_hbm],
        out_specs=vmem,
        scratch_shapes=[
            pltpu.VMEM(recent.shape, jnp.bfloat16),
            pltpu.VMEM(older.shape, jnp.bfloat16),
            pltpu.SemaphoreType.DMA((2, species)),
        ],
        compiler_params=params(50),
        cost_estimate=pl.CostEstimate(flops=0, bytes_accessed=8 << 20, transcendentals=0),
    )(destination.reshape(1, slots), recent, older)
    outgoing = outgoing.astype(jnp.float16)

    shape = jax.ShapeDtypeStruct((species, slots, cells), jnp.float32)
    rims = jax.ShapeDtypeStruct((species, slots, TE * LANES), jnp.bfloat16)
    rims = pl.pallas_call(
        rims_kernel,
        name="rims",
        out_shape=rims,
        in_specs=[anywhere],
        out_specs=anywhere,
        scratch_shapes=[
            pltpu.VMEM(ghosts.shape, jnp.float32),
            pltpu.VMEM(rims.shape, jnp.bfloat16),
            pltpu.SemaphoreType.DMA((species,)),
            pltpu.SemaphoreType.DMA((species,)),
        ],
        compiler_params=params(58),
        cost_estimate=pl.CostEstimate(flops=0, bytes_accessed=8 << 20, transcendentals=0),
    )(ghosts)
    below, above, rims, outgoing = lax.optimization_barrier((below, above, rims, outgoing))

    filtered, row = pl.pallas_call(
        filter_kernel,
        name="filtered_sensor",
        out_shape=(
            jax.ShapeDtypeStruct(sensor.shape, jnp.float32),
            jax.ShapeDtypeStruct((1, LANES), jnp.float32),
        ),
        in_specs=[smem()] + [vmem] * 6,
        out_specs=(vmem, vmem),
        compiler_params=params(32),
        cost_estimate=pl.CostEstimate(flops=0, bytes_accessed=4 << 20, transcendentals=0),
    )(flame_flags, jnp.asarray(banded(brick, brick)), sensor, below, above, *moves)
    rows = gathered(row, ("pen",))
    rows, outgoing = lax.optimization_barrier((rows, outgoing))
    arrived = lax.all_to_all(outgoing, TEAM, split_axis=0, concat_axis=0, tiled=True)
    table = gathered(rows, ("grp", "mig"))
    arrived = arrived.astype(jnp.float32)

    weights = jnp.asarray(plane_weights(), jnp.bfloat16)
    left = pltpu.VMEM((2 * species * slots, 6 * LANES), jnp.bfloat16)
    sums = pltpu.VMEM((2 * species * slots, 3 * FACE), jnp.float32)
    depth = 3 * (species - 1) * slots + LANES
    fuel = pltpu.VMEM((depth, 2 * FACE), jnp.bfloat16)
    react = pltpu.VMEM((species * slots, 2 * FACE), jnp.float32)
    kept = pltpu.VMEM((species, slots, 2 * FACE), jnp.float32)
    new_fields, new_tend = pl.pallas_call(
        main_kernel,
        name="updates",
        out_shape=(shape, jax.ShapeDtypeStruct(shape.shape, jnp.bfloat16)),
        in_specs=[smem()] * 2 + [vmem] * 5 + [anywhere] * 6,
        out_specs=(anywhere, anywhere),
        scratch_shapes=[
            pltpu.VMEM(weights.shape, jnp.bfloat16),
            pltpu.VMEM((species, slots, cells + 2 * FACE), jnp.float32),
            pltpu.VMEM(rims.shape, jnp.bfloat16),
            pltpu.VMEM(shape.shape, jnp.bfloat16),
            pltpu.VMEM(shape.shape, jnp.bfloat16),
            pltpu.VMEM(shape.shape, jnp.float32),
            pltpu.VMEM(shape.shape, jnp.bfloat16),
            pltpu.VMEM((species * slots, depth), jnp.bfloat16),
            pltpu.VMEM((6, slots, LANES), jnp.float32),
            pltpu.VMEM((2, slots, FACE), jnp.bfloat16),
            left,
            left,
            fuel,
            fuel,
            sums,
            sums,
            react,
            react,
            kept,
            kept,
            pltpu.SemaphoreType.DMA((5, TE // PLANES)),
            pltpu.SemaphoreType.DMA((2, TE // PLANES)),
        ],
        compiler_params=params(47),
        cost_estimate=pl.CostEstimate(flops=0, bytes_accessed=40 << 20, transcendentals=0),
    )(
        live_counts,
        rate_matrix,
        table,
        tile_ids.reshape(1, slots),
        velocity,
        *moves,
        weights,
        fields,
        ghosts,
        rims,
        recent,
        older,
    )

    new_fields = pl.pallas_call(
        add_kernel,
        name="arrived_histories",
        out_shape=shape,
        in_specs=[smem(), vmem, anywhere, anywhere],
        out_specs=anywhere,
        scratch_shapes=[
            pltpu.VMEM(shape.shape, jnp.float32),
            pltpu.VMEM((species, peers, ROWS + 8, LANES), jnp.float32),
            pltpu.SemaphoreType.DMA((2, species)),
            pltpu.SemaphoreType.DMA((species,)),
        ],
        compiler_params=params(50),
        cost_estimate=pl.CostEstimate(flops=0, bytes_accessed=12 << 20, transcendentals=0),
    )(live_counts, table, new_fields, arrived)
    return new_fields.transpose(1, 0, 2), new_tend.transpose(1, 0, 2), filtered


def gathered(row, axes):
    for axis in axes:
        count = lax.axis_size(axis)
        here = lax.axis_index(axis)
        rows = [row] + [passed_along(row, axis, by) for by in range(1, count)]
        height, width = row.shape
        if axis == "grp":
            table = jnp.zeros((height, count * width), row.dtype)
        else:
            table = jnp.zeros((count * height, width), row.dtype)
        for by, part in enumerate(rows):
            place = (here - by) % count
            place = (0, place * width) if axis == "grp" else (place * height, 0)
            table = lax.dynamic_update_slice(table, part, place)
        row = table
    return row


def solution(mesh):
    split = P(EVERY, None, None)
    return jax.shard_map(
        local,
        mesh=mesh,
        in_specs=(
            split,
            split,
            P(None, EVERY),
            P(),
            split,
            split,
            P(EVERY),
            P(EVERY),
            P(EVERY),
            P(EVERY),
            P("pen", ("grp", "mig")),
            P("pen", ("grp", "mig")),
        ),
        out_specs=(split, split, P("pen", ("grp", "mig"))),
        check_vma=False,
    )
```

```python
import jax
import jax.numpy as jnp
import numpy as np
from jax import lax
from jax.experimental import pallas as pl
from jax.experimental.pallas import tpu as pltpu
from jax.sharding import PartitionSpec as P

TE = 16
TZ = 2
TCOL = 16
FACE = TE * TE
CELLS = TE**3
LANES = 128
ROWS = CELLS // LANES

viscous = 0.05
step_size = 0.25
thicken = 5.0

SCALE = 4096.0
PLANES = 4
AHEAD = 9

EVERY = ("grp", "mig", "pen")
TEAM = ("mig", "pen")


def passed_along(x, axis, by):
    peers = lax.axis_size(axis)
    return lax.ppermute(x, axis, [(i, (i + by) % peers) for i in range(peers)])


def banded(brick_rows, reach):
    sigma = reach / 2.0
    offsets = np.arange(-reach, reach + 1, dtype=np.float64)
    total = np.sum(np.exp(-offsets * offsets / (2.0 * sigma * sigma)))
    row = np.arange(brick_rows)[:, None]
    col = np.arange(brick_rows + 2 * reach)[None, :]
    offset = (col - reach - row).astype(np.float64)
    weights = np.where(np.abs(offset) <= reach, np.exp(-offset * offset / (2.0 * sigma * sigma)), 0)
    return (weights / total).astype(np.float32)


def raw_kernel(flags_ref, sensor_ref, raw_ref):
    for r in range(TZ):
        for k in range(TCOL):
            rows, cols = slice(r * TE, (r + 1) * TE), slice(k * FACE, (k + 1) * FACE)
            flag = flags_ref[r, k].astype(jnp.float32)
            raw_ref[rows, cols] = (sensor_ref[rows, cols] * flag).astype(jnp.bfloat16)


def filter_kernel(
    flags_ref,
    weights_ref,
    sensor_ref,
    below_ref,
    above_ref,
    destination_ref,
    target_ref,
    filtered_ref,
    row_ref,
):
    lane = lax.broadcasted_iota(jnp.int32, (1, LANES), 1)
    slots = destination_ref.shape[1]
    row = jnp.concatenate(
        [
            jnp.zeros((1, slots), jnp.float32),
            destination_ref[...].astype(jnp.float32),
            target_ref[...].astype(jnp.float32),
            jnp.zeros((1, LANES - 3 * slots), jnp.float32),
        ],
        axis=1,
    )
    brick = sensor_ref.shape[0]
    for k in range(TCOL):
        cols = slice(k * FACE, (k + 1) * FACE)
        own = [
            sensor_ref[r * TE : (r + 1) * TE, cols] * flags_ref[r, k].astype(jnp.float32)
            for r in range(TZ)
        ]
        widened = jnp.concatenate(
            [below_ref[:, cols].astype(jnp.float32)] + own + [above_ref[:, cols].astype(jnp.float32)],
            axis=0,
        )
        filtered = jnp.dot(
            weights_ref[...],
            widened,
            precision=lax.Precision.HIGHEST,
            preferred_element_type=jnp.float32,
        )
        filtered_ref[:, cols] = filtered
        clipped = jnp.minimum(filtered, 1.0)
        for r in range(TZ):
            total = jnp.sum(
                jnp.sum(clipped[r * TE : (r + 1) * TE], axis=0, keepdims=True), axis=1, keepdims=True
            )
            thick = 1.0 + (thicken - 1.0) * (total / float(TE * FACE))
            row = jnp.where(lane == r * TCOL + k, thick, row)
    row_ref[...] = row


def send_kernel(
    destination_ref, recent_hbm, older_hbm, out_ref, recent_ref, older_ref, got
):
    species, slots, _ = recent_ref.shape
    peers = out_ref.shape[0]

    def fetches(s):
        return (
            pltpu.make_async_copy(recent_hbm.at[s], recent_ref.at[s], got.at[0, s]),
            pltpu.make_async_copy(older_hbm.at[s], older_ref.at[s], got.at[1, s]),
        )

    for s in range(AHEAD):
        for copy in fetches(s):
            copy.start()
    peer = lax.broadcasted_iota(jnp.int32, (peers, slots), 0)
    hot = ((destination_ref[...] == peer) & (peer != lax.axis_index(TEAM))).astype(jnp.bfloat16)
    flat = out_ref.reshape(peers * species * ROWS, LANES)
    for s in range(species):
        if s + AHEAD < species:
            for copy in fetches(s + AHEAD):
                copy.start()
        for copy in fetches(s):
            copy.wait()
        recent = jnp.dot(hot, recent_ref[s], preferred_element_type=jnp.float32)
        older = jnp.dot(hot, older_ref[s], preferred_element_type=jnp.float32)
        mixed = recent * (-16.0 / 12.0 * SCALE) + older * (5.0 / 12.0 * SCALE)
        for k in range(ROWS):
            flat[pl.ds(s * ROWS + k, peers, stride=species * ROWS), :] = mixed[
                :, k * LANES : (k + 1) * LANES
            ]


def rims_kernel(ghosts_hbm, rims_hbm, ghosts_ref, rims_ref, got, sent):
    species, slots, _ = ghosts_ref.shape

    def fetch(s):
        return pltpu.make_async_copy(ghosts_hbm.at[s], ghosts_ref.at[s], got.at[s])

    def store(s):
        return pltpu.make_async_copy(rims_ref.at[s], rims_hbm.at[s], sent.at[s])

    for s in range(species):
        fetch(s).start()
    quarter = lax.broadcasted_iota(jnp.int32, (slots, LANES), 1) // (2 * TE)

    def one(s, carry):
        fetch(s).wait()
        for block in range(2):
            faces = [
                ghosts_ref[s, :, w * FACE + block * LANES : w * FACE + (block + 1) * LANES]
                for w in (4, 5, 2, 3)
            ]
            for q in range(4):
                rim = faces[0]
                for n in range(4):
                    turned = pltpu.roll(faces[n], (n - q) % 4 * 2 * TE, 1) if n != q else faces[n]
                    rim = turned if n == 0 else jnp.where(quarter == n, turned, rim)
                high = rim.astype(jnp.bfloat16)
                low = (rim - high.astype(jnp.float32)).astype(jnp.bfloat16)
                start = (block * 4 + q) * 2 * LANES
                rims_ref[s, :, start : start + LANES] = high
                rims_ref[s, :, start + LANES : start + 2 * LANES] = low
        store(s).start()
        return carry

    lax.fori_loop(0, species, one, 0)
    for s in range(species):
        store(s).wait()


def plane_weights():
    weights = np.zeros((6 * LANES, 3 * FACE), np.float32)
    for cell in range(FACE):
        y, z = divmod(cell, TE)
        for d, at, step in ((0, y, TE), (1, z, 1)):
            for way in (-1, 1):
                if 0 <= at + way < TE:
                    rows = [cell + way * step, FACE + cell + way * step]
                else:
                    face = (2 + (way > 0)) if d == 0 else (way > 0)
                    spot = 2 * FACE + face * 2 * TE + (z if d == 0 else y)
                    rows = [spot, spot + TE, spot + LANES, spot + LANES + TE]
                weights[rows, cell] += 1.0
                weights[rows, (1 + d) * FACE + cell] += way
        weights[[cell, FACE + cell], cell] -= 6.0
    return weights


def main_kernel(
    live_ref,
    rate_ref,
    table_ref,
    tiles_ref,
    velocity_ref,
    destination_ref,
    target_ref,
    weights_hbm,
    fields_hbm,
    ghosts_hbm,
    rims_hbm,
    recent_hbm,
    older_hbm,
    new_fields_hbm,
    new_tend_hbm,
    weights_ref,
    fields_ref,
    rims_ref,
    recent_ref,
    older_ref,
    new_fields_ref,
    new_tend_ref,
    mix_ref,
    wide_ref,
    mask_ref,
    left_even_ref,
    left_odd_ref,
    fuel_even_ref,
    fuel_odd_ref,
    sums_even_ref,
    sums_odd_ref,
    react_even_ref,
    react_odd_ref,
    kept_even_ref,
    kept_odd_ref,
    got,
    sent,
):
    species, slots, cells = new_fields_ref.shape
    peers = table_ref.shape[0]
    chunk = PLANES * FACE
    chunks = cells // chunk

    def span(c, length, skipped=0):
        return pl.ds(pl.multiple_of(skipped + c * length, LANES), length)

    def cells_in(c):
        lanes, rims, inner = span(c, chunk), span(c, chunk // 2), span(c, chunk, FACE)
        return (
            pltpu.make_async_copy(
                fields_hbm.at[:, :, lanes], fields_ref.at[:, :, inner], got.at[0, c]
            ),
            pltpu.make_async_copy(
                rims_hbm.at[:, :, rims], rims_ref.at[:, :, rims], got.at[1, c]
            ),
            pltpu.make_async_copy(
                recent_hbm.at[:, :, lanes], recent_ref.at[:, :, lanes], got.at[2, c]
            ),
            pltpu.make_async_copy(
                older_hbm.at[:, :, lanes], older_ref.at[:, :, lanes], got.at[3, c]
            ),
        )

    def ends():
        return (
            pltpu.make_async_copy(weights_hbm, weights_ref, got.at[4, 0]),
            pltpu.make_async_copy(
                ghosts_hbm.at[:, :, pl.ds(0, FACE)], fields_ref.at[:, :, pl.ds(0, FACE)], got.at[4, 1]
            ),
            pltpu.make_async_copy(
                ghosts_hbm.at[:, :, pl.ds(FACE, FACE)],
                fields_ref.at[:, :, pl.ds(FACE + cells, FACE)],
                got.at[4, 2],
            ),
        )

    def stores(c):
        lanes = span(c, 2 * FACE)
        return (
            pltpu.make_async_copy(
                new_fields_ref.at[:, :, lanes], new_fields_hbm.at[:, :, lanes], sent.at[0, c]
            ),
            pltpu.make_async_copy(
                new_tend_ref.at[:, :, lanes], new_tend_hbm.at[:, :, lanes], sent.at[1, c]
            ),
        )

    for copy in (*cells_in(0), *ends(), *cells_in(1)):
        copy.start()

    marks = jnp.concatenate(
        [velocity_ref[...], tiles_ref[...].astype(jnp.float32), jnp.zeros((4, slots), jnp.float32)], axis=0
    ).T
    tiles = marks[:, 3:4].astype(jnp.int32)
    owner = tiles // slots
    wanted = lax.broadcasted_iota(jnp.int32, (slots, peers), 1) == owner % peers
    picked = jnp.dot(
        wanted.astype(jnp.float32),
        table_ref[...],
        precision=lax.Precision.HIGHEST,
        preferred_element_type=jnp.float32,
    )
    lane = lax.broadcasted_iota(jnp.int32, picked.shape, 1)
    spot = owner // peers * LANES + tiles % slots
    thick = jnp.sum(jnp.where(lane == spot, picked, 0.0), axis=1, keepdims=True)
    live = lax.broadcasted_iota(jnp.int32, (slots, 1), 0) < live_ref[0]
    live = jnp.where(live, 1.0, 0.0)
    parts = [viscous * thick * live, live / thick]
    parts += [0.5 * live * marks[:, d : d + 1] for d in range(3)] + [live]
    for n, part in enumerate(parts):
        wide_ref[n] = jnp.broadcast_to(part, (slots, LANES))
    main = (species - 1) * slots
    tail = lax.broadcasted_iota(jnp.int32, (slots, LANES), 1)
    main_lane = lax.broadcasted_iota(jnp.int32, (slots, main), 1)
    main_slot = lax.broadcasted_iota(jnp.int32, (slots, main), 0) == main_lane % slots
    tail_slot = lax.broadcasted_iota(jnp.int32, (slots, LANES), 0) == tail % slots
    for s in range(species):
        rows = slice(s * slots, (s + 1) * slots)
        rate = jnp.zeros((slots, main), jnp.float32)
        for k in range(species - 1):
            rate = jnp.where(main_lane // slots == k, rate_ref[s, k], rate)
        rate = jnp.where(main_slot, rate, 0.0)
        high = rate.astype(jnp.bfloat16)
        mix_ref[rows, 0:main] = high
        mix_ref[rows, main : 2 * main] = (rate - high.astype(jnp.float32)).astype(jnp.bfloat16)
        mix_ref[rows, 2 * main : 3 * main] = high
        rate = jnp.where(tail_slot & (tail < 3 * slots), rate_ref[s, species - 1], 0.0)
        high = rate.astype(jnp.bfloat16).astype(jnp.float32)
        rate = jnp.where(tail // slots == 1, rate - high, high)
        mix_ref[rows, 3 * main :] = rate.astype(jnp.bfloat16)
    for fuel_ref in (fuel_even_ref, fuel_odd_ref):
        fuel_ref[3 * main + 3 * slots :, :] = jnp.zeros((LANES - 3 * slots, 2 * FACE), jnp.bfloat16)

    parity = lax.broadcasted_iota(jnp.int32, (slots, 2 * LANES), 1) // TE % 2
    for p in range(2):
        mask_ref[p] = jnp.where(parity == p, 1.0, 0.0).astype(jnp.bfloat16)
    slot = lax.broadcasted_iota(jnp.int32, (slots, slots), 0)
    keep = (destination_ref[...] == lax.axis_index(TEAM)) & (target_ref[...] == slot)
    keep = keep.astype(jnp.bfloat16)

    def build(pair, odd, some):
        left_ref = (left_even_ref, left_odd_ref)[odd]
        rims = pl.ds(pl.multiple_of(pair * FACE, FACE), FACE)
        for s in some:
            both = rims_ref[s, :, rims]
            for p in range(2):
                lanes = pl.ds(pl.multiple_of((2 * pair + p + 1) * FACE, FACE), FACE)
                rows = slice((p * species + s) * slots, (p * species + s + 1) * slots)
                f = fields_ref[s, :, lanes]
                high = f.astype(jnp.bfloat16)
                left_ref[rows, 0:FACE] = high
                left_ref[rows, FACE : 2 * FACE] = (f - high.astype(jnp.float32)).astype(jnp.bfloat16)
                left_ref[rows, 2 * FACE :] = both * mask_ref[p]

    def multiply(pair, odd, d):
        left_ref, sums_ref = ((left_even_ref, sums_even_ref), (left_odd_ref, sums_odd_ref))[odd]
        columns = slice(d * FACE, (d + 1) * FACE)
        sums_ref[:, columns] = jnp.dot(
            left_ref[...], weights_ref[:, columns], preferred_element_type=jnp.float32
        )

    def burn(pair, odd):
        kept_ref = (kept_even_ref, kept_odd_ref)[odd]
        both = pl.ds(pl.multiple_of(2 * pair * FACE, FACE), 2 * FACE)
        for s in range(species):
            recent = jnp.dot(keep, recent_ref[s, :, both], preferred_element_type=jnp.float32)
            older = jnp.dot(keep, older_ref[s, :, both], preferred_element_type=jnp.float32)
            kept_ref[s] = recent * (-16.0 / 12.0 * step_size) + older * (5.0 / 12.0 * step_size)

        fuel_ref, react_ref = ((fuel_even_ref, react_even_ref), (fuel_odd_ref, react_odd_ref))[odd]
        both = pl.ds(pl.multiple_of((2 * pair + 1) * FACE, FACE), 2 * FACE)
        over = jnp.concatenate([wide_ref[1]] * 4, axis=1)
        burning = fields_ref[0, :, both] * fields_ref[1, :, both] * over
        for k in range(species):
            fuel = fields_ref[k, :, both] * burning
            high = fuel.astype(jnp.bfloat16)
            low = (fuel - high.astype(jnp.float32)).astype(jnp.bfloat16)
            for n, part in enumerate((high, high, low)):
                start = n * main + k * slots if k < species - 1 else 3 * main + n * slots
                fuel_ref[start : start + slots, :] = part
        react_ref[...] = jnp.dot(mix_ref[...], fuel_ref[...], preferred_element_type=jnp.float32)

    def finish(pair, odd, some):
        kept_ref = (kept_even_ref, kept_odd_ref)[odd]
        sums_ref, react_ref = ((sums_even_ref, react_even_ref), (sums_odd_ref, react_odd_ref))[odd]
        for p in range(2):
            inner, before, here, after = (
                pl.ds(pl.multiple_of((2 * pair + p + n) * FACE, FACE), FACE) for n in (0, 0, 1, 2)
            )
            for g in range(slots // 16):
                rows = slice(g * 16, (g + 1) * 16)
                smooth, vx, vy, vz, live = (
                    jnp.concatenate([wide_ref[n, rows, :]] * 2, axis=1) for n in (0, 2, 3, 4, 5)
                )
                for s in some:
                    low, high = fields_ref[s, rows, before], fields_ref[s, rows, after]
                    line = s * slots + g * 16
                    react = react_ref[line : line + 16, p * FACE : (p + 1) * FACE]
                    line += p * species * slots
                    total, along_y, along_z = (
                        sums_ref[line : line + 16, d * FACE : (d + 1) * FACE] for d in range(3)
                    )
                    tend = smooth * (total + (low + high)) - vx * (high - low)
                    tend = (tend - vy * along_y) + (react - vz * along_z)
                    kept = kept_ref[s, rows, p * FACE : (p + 1) * FACE]
                    new = (fields_ref[s, rows, here] + kept) * live
                    new_fields_ref[s, rows, inner] = new + (step_size * 23.0 / 12.0) * tend
                    new_tend_ref[s, rows, inner] = tend.astype(jnp.bfloat16)

    thirds = [range(n * species // 3, (n + 1) * species // 3) for n in range(3)]
    pairs = TE // 2

    def stage(pair, odd):
        after, later = jnp.minimum(pair + 1, pairs - 1), jnp.minimum(pair + 2, pairs - 1)
        burn(after, 1 - odd)
        for d, some in enumerate(thirds):
            multiply(after, 1 - odd, d)
            finish(pair, odd, some)
            build(later, odd, some)

    for copy in (*ends(), *cells_in(0)):
        copy.wait()
    build(0, 0, range(species))
    for d in range(3):
        multiply(0, 0, d)
    burn(0, 0)
    build(1, 1, range(species))

    def four(c, carry):
        @pl.when(c + 2 < chunks)
        def _():
            for copy in cells_in(c + 2):
                copy.start()

        @pl.when(c + 1 < chunks)
        def _():
            for copy in cells_in(c + 1):
                copy.wait()

        stage(2 * c, 0)
        for copy in stores(2 * c):
            copy.start()
        stage(2 * c + 1, 1)
        for copy in stores(2 * c + 1):
            copy.start()
        return carry

    lax.fori_loop(0, chunks, four, 0)
    for pair in range(pairs):
        for copy in stores(pair):
            copy.wait()


def add_kernel(
    live_ref, table_ref, fields_hbm, arrived_hbm, out_hbm, fields_ref, arrived_ref, got, sent
):
    species, peers = arrived_ref.shape[:2]
    slots = fields_ref.shape[1]

    def fetches(s):
        part = arrived_hbm.at[:, pl.ds(s * ROWS, ROWS)]
        return (
            pltpu.make_async_copy(part, arrived_ref.at[s, :, pl.ds(0, ROWS)], got.at[0, s]),
            pltpu.make_async_copy(fields_hbm.at[s], fields_ref.at[s], got.at[1, s]),
        )

    def store(s):
        return pltpu.make_async_copy(fields_ref.at[s], out_hbm.at[s], sent.at[s])

    for s in range(AHEAD):
        for copy in fetches(s):
            copy.start()
    me, first = lax.axis_index(TEAM), pl.multiple_of(lax.axis_index("grp") * LANES, LANES)
    notes = table_ref[:, pl.ds(first, LANES)]
    destination = notes[:, slots : 2 * slots]
    target = notes[:, 2 * slots : 3 * slots]
    peer = lax.broadcasted_iota(jnp.int32, (peers, slots), 0)
    mine = (destination == me.astype(jnp.float32)) & (peer != me)
    slot = jnp.max(jnp.where(mine, target, -1.0), axis=1, keepdims=True)
    index = lax.broadcasted_iota(jnp.int32, (peers, slots), 1)
    hot = (slot == index.astype(jnp.float32)) & (index < live_ref[0])
    hot = jnp.where(hot, step_size / SCALE, 0.0)
    hot = jnp.concatenate([hot, hot], axis=0).T.astype(jnp.bfloat16)
    for s in range(species):
        if s + AHEAD < species:
            for copy in fetches(s + AHEAD):
                copy.start()
        for copy in fetches(s):
            copy.wait()
        apart = arrived_ref.shape[2]
        flat = arrived_ref.at[s].reshape(peers * apart, LANES)
        for c in range(ROWS // 2):
            lanes = slice(c * 2 * LANES, (c + 1) * 2 * LANES)
            arrived = jnp.concatenate(
                [flat[pl.ds(2 * c + k, peers, stride=apart), :] for k in range(2)], axis=1
            )
            high = arrived.astype(jnp.bfloat16)
            low = (arrived - high.astype(jnp.float32)).astype(jnp.bfloat16)
            fields_ref[s, :, lanes] += jnp.dot(
                hot, jnp.concatenate([high, low], axis=0), preferred_element_type=jnp.float32
            )
        store(s).start()
    for s in range(species):
        store(s).wait()


def smem():
    return pl.BlockSpec(memory_space=pltpu.SMEM)


def whole(shape):
    return pl.BlockSpec(shape, lambda i: (0,) * len(shape))


def params(mib, semantics=None):
    return pltpu.CompilerParams(vmem_limit_bytes=mib << 20, dimension_semantics=semantics)


def local(
    fields,
    ghosts,
    velocity,
    rate_matrix,
    recent_tend,
    older_tend,
    destination,
    target_slot,
    live_counts,
    tile_ids,
    sensor,
    flame_flags,
):
    slots, species, cells = fields.shape
    peers = lax.axis_size(TEAM)
    brick = sensor.shape[0]
    fields, ghosts, recent, older = (
        a.transpose(1, 0, 2) for a in (fields, ghosts, recent_tend, older_tend)
    )
    moves = (destination.reshape(1, slots), target_slot.reshape(1, slots))

    raw = pl.pallas_call(
        raw_kernel,
        name="raw_sensor",
        out_shape=jax.ShapeDtypeStruct(sensor.shape, jnp.bfloat16),
        in_specs=[smem(), pl.BlockSpec(memory_space=pltpu.VMEM)],
        out_specs=pl.BlockSpec(memory_space=pltpu.VMEM),
        compiler_params=params(58),
    )(flame_flags, sensor)
    below = passed_along(raw, "pen", 1)
    above = passed_along(raw, "pen", -1)

    anywhere = pl.BlockSpec(memory_space=pl.ANY)
    in_hbm = pl.BlockSpec(memory_space=pltpu.HBM)
    vmem = pl.BlockSpec(memory_space=pltpu.VMEM)
    outgoing = pl.pallas_call(
        send_kernel,
        name="outgoing_histories",
        out_shape=jax.ShapeDtypeStruct((peers, species * ROWS, LANES), jnp.float32),
        in_specs=[vmem, in_hbm, in_hbm],
        out_specs=vmem,
        scratch_shapes=[
            pltpu.VMEM(recent.shape, jnp.bfloat16),
            pltpu.VMEM(older.shape, jnp.bfloat16),
            pltpu.SemaphoreType.DMA((2, species)),
        ],
        compiler_params=params(50),
        cost_estimate=pl.CostEstimate(flops=0, bytes_accessed=8 << 20, transcendentals=0),
    )(destination.reshape(1, slots), recent, older)
    outgoing = outgoing.astype(jnp.float16)

    shape = jax.ShapeDtypeStruct((species, slots, cells), jnp.float32)
    rims = jax.ShapeDtypeStruct((species, slots, TE * LANES), jnp.bfloat16)
    rims = pl.pallas_call(
        rims_kernel,
        name="rims",
        out_shape=rims,
        in_specs=[anywhere],
        out_specs=anywhere,
        scratch_shapes=[
            pltpu.VMEM(ghosts.shape, jnp.float32),
            pltpu.VMEM(rims.shape, jnp.bfloat16),
            pltpu.SemaphoreType.DMA((species,)),
            pltpu.SemaphoreType.DMA((species,)),
        ],
        compiler_params=params(58),
        cost_estimate=pl.CostEstimate(flops=0, bytes_accessed=8 << 20, transcendentals=0),
    )(ghosts)
    below, above, rims, outgoing = lax.optimization_barrier((below, above, rims, outgoing))

    filtered, row = pl.pallas_call(
        filter_kernel,
        name="filtered_sensor",
        out_shape=(
            jax.ShapeDtypeStruct(sensor.shape, jnp.float32),
            jax.ShapeDtypeStruct((1, LANES), jnp.float32),
        ),
        in_specs=[smem()] + [vmem] * 6,
        out_specs=(vmem, vmem),
        compiler_params=params(32),
        cost_estimate=pl.CostEstimate(flops=0, bytes_accessed=4 << 20, transcendentals=0),
    )(flame_flags, jnp.asarray(banded(brick, brick)), sensor, below, above, *moves)
    rows = gathered(row, ("pen",))
    rows, outgoing = lax.optimization_barrier((rows, outgoing))
    arrived = lax.all_to_all(outgoing, TEAM, split_axis=0, concat_axis=0, tiled=True)
    table = gathered(rows, ("grp", "mig"))
    arrived = arrived.astype(jnp.float32)

    weights = jnp.asarray(plane_weights(), jnp.bfloat16)
    left = pltpu.VMEM((2 * species * slots, 6 * LANES), jnp.bfloat16)
    sums = pltpu.VMEM((2 * species * slots, 3 * FACE), jnp.float32)
    depth = 3 * (species - 1) * slots + LANES
    fuel = pltpu.VMEM((depth, 2 * FACE), jnp.bfloat16)
    react = pltpu.VMEM((species * slots, 2 * FACE), jnp.float32)
    kept = pltpu.VMEM((species, slots, 2 * FACE), jnp.float32)
    new_fields, new_tend = pl.pallas_call(
        main_kernel,
        name="updates",
        out_shape=(shape, jax.ShapeDtypeStruct(shape.shape, jnp.bfloat16)),
        in_specs=[smem()] * 2 + [vmem] * 5 + [anywhere] * 6,
        out_specs=(anywhere, anywhere),
        scratch_shapes=[
            pltpu.VMEM(weights.shape, jnp.bfloat16),
            pltpu.VMEM((species, slots, cells + 2 * FACE), jnp.float32),
            pltpu.VMEM(rims.shape, jnp.bfloat16),
            pltpu.VMEM(shape.shape, jnp.bfloat16),
            pltpu.VMEM(shape.shape, jnp.bfloat16),
            pltpu.VMEM(shape.shape, jnp.float32),
            pltpu.VMEM(shape.shape, jnp.bfloat16),
            pltpu.VMEM((species * slots, depth), jnp.bfloat16),
            pltpu.VMEM((6, slots, LANES), jnp.float32),
            pltpu.VMEM((2, slots, FACE), jnp.bfloat16),
            left,
            left,
            fuel,
            fuel,
            sums,
            sums,
            react,
            react,
            kept,
            kept,
            pltpu.SemaphoreType.DMA((5, TE // PLANES)),
            pltpu.SemaphoreType.DMA((2, TE // 2)),
        ],
        compiler_params=params(52),
        cost_estimate=pl.CostEstimate(flops=0, bytes_accessed=40 << 20, transcendentals=0),
    )(
        live_counts,
        rate_matrix,
        table,
        tile_ids.reshape(1, slots),
        velocity,
        *moves,
        weights,
        fields,
        ghosts,
        rims,
        recent,
        older,
    )

    new_fields = pl.pallas_call(
        add_kernel,
        name="arrived_histories",
        out_shape=shape,
        in_specs=[smem(), vmem, anywhere, anywhere],
        out_specs=anywhere,
        scratch_shapes=[
            pltpu.VMEM(shape.shape, jnp.float32),
            pltpu.VMEM((species, peers, ROWS + 8, LANES), jnp.float32),
            pltpu.SemaphoreType.DMA((2, species)),
            pltpu.SemaphoreType.DMA((species,)),
        ],
        compiler_params=params(50),
        cost_estimate=pl.CostEstimate(flops=0, bytes_accessed=12 << 20, transcendentals=0),
    )(live_counts, table, new_fields, arrived)
    return new_fields.transpose(1, 0, 2), new_tend.transpose(1, 0, 2), filtered


def gathered(row, axes):
    for axis in axes:
        count = lax.axis_size(axis)
        here = lax.axis_index(axis)
        rows = [row] + [passed_along(row, axis, by) for by in range(1, count)]
        height, width = row.shape
        if axis == "grp":
            table = jnp.zeros((height, count * width), row.dtype)
        else:
            table = jnp.zeros((count * height, width), row.dtype)
        for by, part in enumerate(rows):
            place = (here - by) % count
            place = (0, place * width) if axis == "grp" else (place * height, 0)
            table = lax.dynamic_update_slice(table, part, place)
        row = table
    return row


def solution(mesh):
    split = P(EVERY, None, None)
    return jax.shard_map(
        local,
        mesh=mesh,
        in_specs=(
            split,
            split,
            P(None, EVERY),
            P(),
            split,
            split,
            P(EVERY),
            P(EVERY),
            P(EVERY),
            P(EVERY),
            P("pen", ("grp", "mig")),
            P("pen", ("grp", "mig")),
        ),
        out_specs=(split, split, P("pen", ("grp", "mig"))),
        check_vma=False,
    )
```
